32 devices in a mesh: row: 8 (over y, x, core), col: 4 (over z).
Axes of the slice: x: 2, y: 2, z: 4, core: 2. Of those that a mesh axis runs over, the one named last changes fastest.
Arguments:
- tokens: bfloat16 [32, 128, 256], P('row', 'col'), may hold values from -6 to 6
- gain: float32 [256], replicated, may hold values from 0.25 to 1.75
- w_qkv: bfloat16 [256, 768], replicated, may hold values from -0.375 to 0.375
- head_scale: float32 [4], replicated, may hold values from 3 to 12
- w_out: bfloat16 [256, 256], replicated, may hold values from -0.375 to 0.375
- w_merge: bfloat16 [1024, 512], replicated, may hold values from -0.1875 to 0.1875
- d_merged: bfloat16 [16, 64, 512], P('row', 'col'), may hold values from -1 to 1
- d_skip: bfloat16 [32, 128, 256], P('row', 'col'), may hold values from -1 to 1
Outputs:
- skip_out: bfloat16 [32, 128, 256], P('row', 'col')
- merged: bfloat16 [16, 64, 512], P('row', 'col')
- grad_tokens: bfloat16 [32, 128, 256], P('row', 'col')
- grad_qkv: float32 [256, 768], P('row', 'col')
- grad_out: float32 [256, 256], P('row', 'col')
- grad_merge: float32 [1024, 512], P('row', 'col')
- grad_gain: float32 [256], replicated
- grad_scale: float32 [4], replicated
The draws below stay inside these ranges and needn't reach their ends.
All inputs are finite; a program needn't handle non-finite values.
Results may differ from the reference program's by a relative error of at most 0.012.
The reference program's roundings to bfloat16 on the way count: a program that leaves them out, or rounds other values in their place, can miss the bound.
Values may be sent and summed in bfloat16 or wider, within the bound.
No kernel may reach another device: no remote copies, remote signals or barrier semaphores. Data moves between devices by JAX's collectives and lax.ppermute only.
A program may use at most 64 MiB of HBM per device.

```python
import math
import jax
import jax.numpy as jnp
import numpy as np
from jax import lax

D = 256
DM = 512
HEAD_DIM = 64
RADIUS = 3
TILE_R = 4
TILE_C = 16
HEADS = 4
H = 32
IMAGE_ROWS = 32
W = 128
N_ROW = 8
N_COL = 4


def block_scale(key, dims, cuts, least, top_value):
    def one(axis_at, blocks):
        steps = jax.random.uniform(jax.random.fold_in(jax.random.fold_in(key, 6), axis_at), (blocks,), jnp.float32, least / len(cuts), top_value / len(cuts))
        return jnp.repeat(jnp.exp(steps), dims[axis_at] // blocks).reshape((-1,) + (1,) * (len(dims) - axis_at - 1))

    factor_of = one(*cuts[0])
    for cut in cuts[1:]:
        factor_of = factor_of * one(*cut)
    return factor_of


def centred(rng, extent, scale, most, cuts=(), kind=jnp.bfloat16):
    values = scale * jax.random.normal(rng, extent, jnp.float32)
    if cuts:
        values = values * block_scale(rng, extent, cuts, -0.22, 0.18)
    return jnp.clip(values, -most, most).astype(kind)


def setup_inputs(seed: int = 0) -> dict:
    key_list = jax.random.split(jax.random.key(seed), 9)
    return {
        "tokens": centred(key_list[0], (H, W, D), 1.0, 6.0, ((0, 8), (1, 4))),
        "gain": jnp.clip(1.0 + 0.15 * jax.random.normal(key_list[1], (D,), jnp.float32), 0.25, 1.75),
        "w_qkv": centred(key_list[2], (D, 3 * D), D ** -0.5, 0.375),
        "head_scale": jnp.clip(jnp.exp(jax.random.uniform(key_list[3], (HEADS,), jnp.float32, math.log(3.0), math.log(12.0))), 3.0, 12.0),
        "w_out": centred(key_list[4], (D, D), D ** -0.5, 0.375),
        "w_merge": centred(key_list[5], (4 * D, DM), (4 * D) ** -0.5, 0.1875),
        "d_merged": centred(key_list[6], (H // 2, W // 2, DM), (N_ROW * N_COL) ** -0.5, 1.0, ((0, 8), (1, 4))),
        "d_skip": centred(key_list[7], (H, W, D), (N_ROW * N_COL) ** -0.5, 1.0, ((0, 8), (1, 4))),
    }


EPS = 1e-06

def rounded(value):
    return lax.optimization_barrier(value.astype(jnp.bfloat16))

def split_queries(block):
    rows, cols, feats = block.shape
    part = block.reshape(rows // TILE_R, TILE_R, cols // TILE_C, TILE_C, feats).transpose(0, 2, 1, 3, 4)
    return part.reshape(rows // TILE_R, cols // TILE_C, TILE_R * TILE_C, feats)

def join_queries(tiles, rows, cols):
    feats = tiles.shape[-1]
    part = tiles.reshape(rows // TILE_R, cols // TILE_C, TILE_R, TILE_C, feats).transpose(0, 2, 1, 3, 4)
    return part.reshape(rows, cols, feats)

def tile_tables(rows, cols):
    span_r = TILE_R + 2 * RADIUS
    span_c = TILE_C + 2 * RADIUS
    row_table = (np.arange(rows // TILE_R)[:, None] * TILE_R + np.arange(span_r)[None, :]).reshape(-1)
    col_table = (np.arange(cols // TILE_C)[:, None] * TILE_C + np.arange(span_c)[None, :]).reshape(-1)
    return (row_table, col_table)

def cut_tiles(padded, rows, cols):
    span_r = TILE_R + 2 * RADIUS
    span_c = TILE_C + 2 * RADIUS
    row_table, col_table = tile_tables(rows, cols)
    feats = padded.shape[-1]
    part = jnp.take(padded, jnp.asarray(row_table, jnp.int32), axis=0)
    part = jnp.take(part, jnp.asarray(col_table, jnp.int32), axis=1)
    part = part.reshape(rows // TILE_R, span_r, cols // TILE_C, span_c, feats).transpose(0, 2, 1, 3, 4)
    return part.reshape(rows // TILE_R, cols // TILE_C, span_r * span_c, feats)

def add_tiles(tiles, rows, cols):
    span_r = TILE_R + 2 * RADIUS
    span_c = TILE_C + 2 * RADIUS
    row_table, col_table = tile_tables(rows, cols)
    feats = tiles.shape[-1]
    part = tiles.reshape(rows // TILE_R, cols // TILE_C, span_r, span_c, feats).transpose(0, 2, 1, 3, 4)
    part = part.reshape(row_table.shape[0], col_table.shape[0], feats)
    total = jnp.zeros((rows + 2 * RADIUS, cols + 2 * RADIUS, feats), tiles.dtype)
    return total.at[jnp.asarray(row_table, jnp.int32)[:, None], jnp.asarray(col_table, jnp.int32)[None, :]].add(part)

def window_mask():
    span_c = TILE_C + 2 * RADIUS
    count = (TILE_R + 2 * RADIUS) * span_c
    query_r = np.arange(TILE_R * TILE_C) // TILE_C
    query_c = np.arange(TILE_R * TILE_C) % TILE_C
    key_r = np.arange(count) // span_c
    key_c = np.arange(count) % span_c
    diff_r = key_r[None, :] - query_r[:, None]
    diff_c = key_c[None, :] - query_c[:, None]
    return jnp.asarray((diff_r >= 0) & (diff_r <= 2 * RADIUS) & (diff_c >= 0) & (diff_c <= 2 * RADIUS))

def attend(q_tiles, kv_tiles, valid_tiles, heads):
    nrow, ncol, nq, width = q_tiles.shape
    nk = kv_tiles.shape[2]
    dim = width // heads
    query = q_tiles.astype(jnp.float32).reshape(nrow, ncol, nq, heads, dim)
    keys = kv_tiles[..., :width].astype(jnp.float32).reshape(nrow, ncol, nk, heads, dim)
    values = kv_tiles[..., width:].astype(jnp.float32).reshape(nrow, ncol, nk, heads, dim)
    scores = jnp.einsum('abqhe,abkhe->abhqk', query, keys)
    allowed = window_mask()[None, None, None] & valid_tiles[:, :, None, None, :]
    expo = jnp.where(allowed, jnp.exp(scores), 0.0)
    prob = expo / lax.optimization_barrier(jnp.sum(expo, axis=-1, keepdims=True))
    weights = rounded(prob).astype(jnp.float32)
    out = jnp.einsum('abhqk,abkhe->abqhe', weights, values)
    return (out.reshape(nrow, ncol, nq, width).astype(jnp.bfloat16), prob)

def attend_back(q_tiles, kv_tiles, prob, grad_tiles, heads):
    nrow, ncol, nq, width = q_tiles.shape
    nk = kv_tiles.shape[2]
    dim = width // heads
    query = q_tiles.astype(jnp.float32).reshape(nrow, ncol, nq, heads, dim)
    keys = kv_tiles[..., :width].astype(jnp.float32).reshape(nrow, ncol, nk, heads, dim)
    values = kv_tiles[..., width:].astype(jnp.float32).reshape(nrow, ncol, nk, heads, dim)
    grads = grad_tiles.astype(jnp.float32).reshape(nrow, ncol, nq, heads, dim)
    d_weights = jnp.einsum('abqhe,abkhe->abhqk', grads, values)
    d_scores = prob * (d_weights - lax.optimization_barrier(jnp.sum(d_weights * prob, axis=-1, keepdims=True)))
    score_grad = rounded(d_scores).astype(jnp.float32)
    weights = rounded(prob).astype(jnp.float32)
    d_query = jnp.einsum('abhqk,abkhe->abqhe', score_grad, keys)
    d_keys = jnp.einsum('abhqk,abqhe->abkhe', score_grad, query)
    d_values = jnp.einsum('abhqk,abqhe->abkhe', weights, grads)
    kv_grad = jnp.concatenate([d_keys.reshape(nrow, ncol, nk, width), d_values.reshape(nrow, ncol, nk, width)], axis=-1)
    return (d_query.reshape(nrow, ncol, nq, width), kv_grad)

def reference(tokens, gain, w_qkv, head_scale, w_out, w_merge, d_merged, d_skip):
    span_r = TILE_R + 2 * RADIUS
    x = tokens.astype(jnp.float32)
    inverse = lax.rsqrt(lax.optimization_barrier(jnp.mean(x * x, axis=-1, keepdims=True)) + EPS)
    normed = (x * inverse * gain).astype(jnp.bfloat16)
    flat_normed = normed.reshape(H * W, D)
    qkv = jnp.dot(flat_normed, w_qkv, preferred_element_type=jnp.float32).reshape(H, W, 3, HEADS, HEAD_DIM)
    query, key_raw, value = (qkv[:, :, 0], qkv[:, :, 1], qkv[:, :, 2])
    q_norm = lax.rsqrt(lax.optimization_barrier(jnp.sum(query * query, axis=-1, keepdims=True)) + EPS)
    k_norm = lax.rsqrt(lax.optimization_barrier(jnp.sum(key_raw * key_raw, axis=-1, keepdims=True)) + EPS)
    q_unit = query * q_norm
    k_unit = key_raw * k_norm
    q_hat = rounded((q_unit * head_scale[:, None]).reshape(H, W, D))
    kv = rounded(jnp.concatenate([k_unit.reshape(H, W, D), value.reshape(H, W, D)], axis=-1))
    kv_pad = jnp.pad(kv, ((RADIUS, RADIUS), (RADIUS, RADIUS), (0, 0)))
    grid_c = jnp.arange(W + 2 * RADIUS, dtype=jnp.int32) - RADIUS
    col_ok = (grid_c >= 0) & (grid_c < W)
    starts = jnp.arange(H // TILE_R, dtype=jnp.int32) * TILE_R

    def pieces(start):
        q_block = lax.dynamic_slice_in_dim(q_hat, start, TILE_R, 0)
        kv_block = lax.dynamic_slice_in_dim(kv_pad, start, span_r, 0)
        row_ids = start - RADIUS + jnp.arange(span_r, dtype=jnp.int32)
        first = start // IMAGE_ROWS * IMAGE_ROWS
        row_ok = (row_ids >= first) & (row_ids < first + IMAGE_ROWS)
        in_block = row_ok[:, None] & col_ok[None, :]
        q_tiles = split_queries(q_block)
        kv_tiles = cut_tiles(kv_block, TILE_R, W)
        valid_tiles = cut_tiles(in_block[:, :, None], TILE_R, W)[..., 0]
        return (q_tiles, kv_tiles, valid_tiles)

    def forward_rows(start):
        q_tiles, kv_tiles, valid_tiles = pieces(start)
        out, prob = attend(q_tiles, kv_tiles, valid_tiles, HEADS)
        return join_queries(out, TILE_R, W)
    attn = lax.map(forward_rows, starts).reshape(H, W, D)
    flat_attn = attn.reshape(H * W, D)
    proj = jnp.dot(flat_attn, w_out, preferred_element_type=jnp.float32).reshape(H, W, D)
    skip_out = (x + proj).astype(jnp.bfloat16)
    merge_in = skip_out.reshape(H // 2, 2, W // 2, 2, D).transpose(0, 2, 1, 3, 4).reshape(H // 2 * (W // 2), 4 * D)
    merged = jnp.dot(merge_in, w_merge, preferred_element_type=jnp.float32).astype(jnp.bfloat16).reshape(H // 2, W // 2, DM)
    flat_dm = d_merged.reshape(H // 2 * (W // 2), DM)
    grad_merge = jnp.dot(merge_in.T, flat_dm, preferred_element_type=jnp.float32)
    d_in = jnp.dot(flat_dm, w_merge.T, preferred_element_type=jnp.float32)
    d_in = d_in.reshape(H // 2, W // 2, 2, 2, D).transpose(0, 2, 1, 3, 4).reshape(H, W, D)
    d_y = d_skip.astype(jnp.float32) + d_in
    dy_b = d_y.astype(jnp.bfloat16).reshape(H * W, D)
    grad_out = jnp.dot(flat_attn.T, dy_b, preferred_element_type=jnp.float32)
    d_attn = jnp.dot(dy_b, w_out.T, preferred_element_type=jnp.float32).astype(jnp.bfloat16).reshape(H, W, D)

    def backward_rows(start):
        q_tiles, kv_tiles, valid_tiles = pieces(start)
        out, prob = attend(q_tiles, kv_tiles, valid_tiles, HEADS)
        g_block = lax.dynamic_slice_in_dim(d_attn, start, TILE_R, 0)
        d_q_tiles, d_kv_tiles = attend_back(q_tiles, kv_tiles, prob, split_queries(g_block), HEADS)
        d_kv_block = add_tiles(d_kv_tiles, TILE_R, W)[:, RADIUS:RADIUS + W]
        top = d_kv_block[:RADIUS]
        middle = d_kv_block[RADIUS:RADIUS + TILE_R]
        bottom = d_kv_block[RADIUS + TILE_R:]
        return (join_queries(d_q_tiles, TILE_R, W), top, middle, bottom)
    d_qrows, top, middle, bottom = lax.map(backward_rows, starts)
    d_qhat = d_qrows.reshape(H, W, D)
    top_next = jnp.concatenate([top[1:], jnp.zeros_like(top[:1])], axis=0)
    bottom_prev = jnp.concatenate([jnp.zeros_like(bottom[:1]), bottom[:-1]], axis=0)
    full = middle + jnp.pad(top_next, ((0, 0), (TILE_R - RADIUS, 0), (0, 0), (0, 0)))
    full = full + jnp.pad(bottom_prev, ((0, 0), (0, TILE_R - RADIUS), (0, 0), (0, 0)))
    d_kv = full.reshape(H, W, 2 * D)
    g_qhat = d_qhat.reshape(H, W, HEADS, HEAD_DIM)
    grad_scale = lax.optimization_barrier(jnp.sum(q_unit * g_qhat, axis=(0, 1, 3)))
    g_unit = g_qhat * head_scale[:, None]
    d_query = q_norm * (g_unit - q_unit * lax.optimization_barrier(jnp.sum(q_unit * g_unit, axis=-1, keepdims=True)))
    g_key = d_kv[:, :, :D].reshape(H, W, HEADS, HEAD_DIM)
    d_key = k_norm * (g_key - k_unit * lax.optimization_barrier(jnp.sum(k_unit * g_key, axis=-1, keepdims=True)))
    d_value = d_kv[:, :, D:].reshape(H, W, HEADS, HEAD_DIM)
    d_qkv = jnp.stack([d_query, d_key, d_value], axis=2).reshape(H * W, 3 * D).astype(jnp.bfloat16)
    grad_qkv = jnp.dot(flat_normed.T, d_qkv, preferred_element_type=jnp.float32)
    d_normed = jnp.dot(d_qkv, w_qkv.T, preferred_element_type=jnp.float32).reshape(H, W, D)
    grad_gain = lax.optimization_barrier(jnp.sum(x * inverse * d_normed, axis=(0, 1)))
    scaled = gain * d_normed
    g_x = inverse * scaled - x * inverse ** 3 * lax.optimization_barrier(jnp.mean(x * scaled, axis=-1, keepdims=True))
    grad_tokens = (d_y + g_x).astype(jnp.bfloat16)
    return (skip_out, merged, grad_tokens, grad_qkv, grad_out, grad_merge, grad_gain, grad_scale)
```

```python
import functools
import jax
import jax.numpy as jnp
from jax import lax
from jax.experimental import pallas as pl
from jax.experimental.pallas import tpu as pltpu
from jax.sharding import PartitionSpec as P

RADIUS = 3
IMG_MAX = 512
EPS = 1e-06
EDGE = 4
SIDE = 8
LANES = 128
BF = jnp.bfloat16
F32 = jnp.float32


def mm(a, b):
    return lax.dot_general(a, b, (((1,), (0,)), ((), ())), preferred_element_type=F32)


def mm_t(a, b):
    return lax.dot_general(a, b, (((1,), (1,)), ((), ())), preferred_element_type=F32)


def split_two(value):
    high = value.astype(BF)
    return (high, (value - high.astype(F32)).astype(BF))


def by_side(axis, near, far):
    even = lax.rem(lax.axis_index(axis), 2) == 0
    return (jnp.where(even, far, near), jnp.where(even, near, far))


def own_edge_kernel(scale_ref, tok_ref, dm_ref, gain_ref, edges_ref, dm_own_ref, rows_ref):
    rows, cols, width = tok_ref.shape
    tok = tok_ref[...].astype(F32)
    left = tok[:, :EDGE].reshape(rows * EDGE, width)
    right = tok[:, cols - EDGE :].reshape(rows * EDGE, width)
    edges_ref[...] = jnp.concatenate([left, right], axis=0).astype(BF)
    dm_own_ref[...] = dm_ref[...].reshape(dm_own_ref.shape)
    lane = lax.broadcasted_iota(jnp.int32, (1, width), 1)
    heads = scale_ref.shape[0]
    scale_row = jnp.zeros((1, width), F32)
    for h in range(heads):
        scale_row = jnp.where(lane // (width // heads) == h, scale_ref[h], scale_row)
    blank = jnp.zeros((6, width), F32)
    rows_ref[...] = jnp.concatenate([gain_ref[...], scale_row, blank], axis=0)


def edge_kernel(edges_ref, near_ref, far_ref, edge_near_ref, edge_far_ref):
    rows, cols, width = near_ref.shape
    up, down = by_side("row", near_ref[...].astype(F32), far_ref[...].astype(F32))
    up = up[rows - RADIUS :]
    down = down[:RADIUS]
    own = edges_ref[...].astype(F32)
    sides = []
    for side, at in enumerate((0, cols - EDGE)):
        parts = [
            up[:, at : at + EDGE].reshape(RADIUS * EDGE, width),
            own[side * rows * EDGE : (side + 1) * rows * EDGE],
            down[:, at : at + EDGE].reshape(RADIUS * EDGE, width),
        ]
        sides.append(jnp.concatenate(parts, axis=0))
    far, near = by_side("col", sides[1], sides[0])
    edge_near_ref[...] = near.astype(BF)
    edge_far_ref[...] = far.astype(BF)


def pair_kernel(dm_ref, dm_near_ref, dm_pair_ref):
    size = dm_pair_ref.shape[0] // 2
    own, near = [ref[...].reshape(size, -1).astype(F32) for ref in (dm_ref, dm_near_ref)]
    dm_pair_ref[...] = jnp.concatenate(in_order("row", own, near), axis=0).astype(BF)


def in_order(axis, own, partner):
    even = lax.rem(lax.axis_index(axis), 2) == 0
    return (jnp.where(even, own, partner), jnp.where(even, partner, own))


def head_sum(value, heads):
    width = value.shape[1]
    head_dim = width // heads
    same_head = lax.broadcasted_iota(jnp.int32, (width, width), 0) // head_dim == (
        lax.broadcasted_iota(jnp.int32, (width, width), 1) // head_dim
    )
    ones_bd = jnp.where(same_head, 1.0, 0.0).astype(BF)
    high, low = split_two(value)
    return mm(high, ones_bd) + mm(low, ones_bd)


def own_kernel(
    heads, tok_ref, dm_ref, dskip_ref, rows_ref, wqkv_ref, wout_ref, wmerge_ref, *refs
):
    *dm_refs, q_norm_ref, q_unit_ref, dy_ref, d_attn_ref, dm_all_ref, dscr = refs
    dm_all_ref[...] = jnp.concatenate([ref[...] for ref in dm_refs], axis=0)
    rows, cols, width = tok_ref.shape
    tokens = rows * cols
    x = tok_ref[...].reshape(tokens, width).astype(F32)
    inverse = lax.rsqrt(jnp.mean(x * x, axis=1, keepdims=True) + EPS)
    normed = (x * inverse * rows_ref[0:1]).astype(BF)
    query = mm(normed, wqkv_ref[:, :width])
    q_norm = lax.rsqrt(head_sum(query * query, heads) + EPS)
    q_norm_ref[...] = q_norm
    q_unit_ref[...] = query * q_norm
    group_wide = cols // 2
    d_in = mm_t(dm_ref[...], wmerge_ref[...])
    for i in range(rows // 2):
        for pr in range(2):
            for pc in range(2):
                for part in range(width // LANES):
                    at = (2 * pr + pc) * width + part * LANES
                    dscr[part, 2 * i + pr, pl.ds(pc, group_wide, stride=2), :] = d_in[
                        i * group_wide : (i + 1) * group_wide, at : at + LANES
                    ]
    d_group = jnp.concatenate(
        [dscr[part].reshape(tokens, LANES) for part in range(width // LANES)], axis=1
    )
    d_y = dskip_ref[...].reshape(tokens, width).astype(F32) + d_group
    dy_ref[...] = d_y
    d_attn_ref[...] = mm_t(d_y.astype(BF), wout_ref[...]).astype(BF)


def layer_kernel(
    sizes,
    tok_ref,
    row_near_ref,
    row_far_ref,
    col_near_ref,
    col_far_ref,
    rows_ref,
    q_norm_ref,
    q_unit_ref,
    dy_ref,
    d_attn_ref,
    wqkv_ref,
    wout_ref,
    wmerge_ref,
    skip_ref,
    merged_ref,
    gx_ref,
    gx_near_ref,
    gx_far_ref,
    *refs,
):
    rows, cols, width, heads, n_row, n_col = sizes
    *sum_refs, yscr = refs
    head_dim = width // heads
    wide = cols + 2 * SIDE
    ext_rows = rows + 2 * RADIUS
    tokens = rows * cols
    image_rows = min(IMG_MAX, rows * n_row)
    row_start = lax.axis_index("row") * rows
    col_index = lax.axis_index("col")
    col_start = col_index * cols
    first = row_start // image_rows * image_rows

    def inner(value, at_row=RADIUS):
        pieces = []
        for i in range(at_row, at_row + rows):
            pieces.append(value[i * wide + SIDE : i * wide + SIDE + cols])
        return jnp.concatenate(pieces, axis=0)

    lane = lax.broadcasted_iota(jnp.int32, (1, width), 1)
    def blocks(value):
        zero = jnp.zeros_like(value)
        kept = [jnp.where(lane // head_dim == h, value, zero) for h in range(heads)]
        return jnp.concatenate(kept, axis=0).astype(BF)

    gain = rows_ref[0:1]
    scale_row = rows_ref[1:2]
    up, down = by_side("row", row_near_ref[...].astype(F32), row_far_ref[...].astype(F32))
    left, right = by_side("col", col_near_ref[...].astype(F32), col_far_ref[...].astype(F32))
    own = tok_ref[...].astype(F32)
    blank = jnp.zeros((SIDE - EDGE, width), F32)
    pieces = []
    for i in range(ext_rows):
        if i < RADIUS:
            row = up[rows - RADIUS + i]
        elif i < RADIUS + rows:
            row = own[i - RADIUS]
        else:
            row = down[i - RADIUS - rows]
        edge = slice(i * EDGE, (i + 1) * EDGE)
        pieces += [blank, left[edge], row, right[edge], blank]
    x = jnp.concatenate(pieces, axis=0)
    inverse = lax.rsqrt(jnp.mean(x * x, axis=1, keepdims=True) + EPS)
    unit = x * inverse
    normed32 = (unit * gain).astype(BF).astype(F32)
    normed = normed32.astype(BF)
    x_own = inner(x)
    normed_own32 = inner(normed32)
    kv = mm(normed, wqkv_ref[:, width:])
    key_raw = kv[:, :width]
    k_norm = lax.rsqrt(head_sum(key_raw * key_raw, heads) + EPS)
    k_unit = key_raw * k_norm
    keys = k_unit.astype(BF)
    values = kv[:, width:].astype(BF)
    q_norm = q_norm_ref[...]
    q_unit = q_unit_ref[...]
    q_hat = (q_unit * scale_row).astype(BF).astype(F32)
    d_y = dy_ref[...]
    dy_b = d_y.astype(BF)
    d_attn = d_attn_ref[...].astype(F32)

    index = lax.broadcasted_iota(jnp.int32, (1, tokens), 1)
    q_row = jnp.zeros_like(index)
    for i in range(1, rows):
        q_row = q_row + (index >= i * cols).astype(jnp.int32)
    q_col = index - q_row * cols
    key_col = lax.broadcasted_iota(jnp.int32, (wide, tokens), 0) - SIDE
    near = (key_col - q_col <= RADIUS) & (key_col - q_col >= -RADIUS)
    near = near & (key_col + col_start >= 0) & (key_col + col_start < cols * n_col)
    near = jnp.where(near, 1.0, 0.0)
    parts = []
    for i in range(-RADIUS, rows + RADIUS):
        ok = (q_row - i <= RADIUS) & (q_row - i >= -RADIUS)
        ok = ok & (row_start + i >= first) & (row_start + i < first + image_rows)
        parts.append(near * jnp.where(ok, 1.0, 0.0))
    allowed = jnp.concatenate([jnp.concatenate(parts, axis=0)] * heads, axis=1)
    q_blocks = blocks(q_hat)
    g_blocks = blocks(d_attn)
    expo = jnp.exp(mm_t(keys, q_blocks)) * allowed
    prob = expo * (1.0 / jnp.sum(expo, axis=0, keepdims=True))
    weights = prob.astype(BF)
    d_w = mm_t(values, g_blocks)
    delta = jnp.sum(d_w * prob, axis=0, keepdims=True)
    d_s = (prob * (d_w - delta)).astype(BF)
    values_t = values.astype(F32).T.astype(BF)
    keys_t = keys.astype(F32).T.astype(BF)
    attn_t = []
    d_qhat_t = []
    for h in range(heads):
        feats = slice(h * head_dim, (h + 1) * head_dim)
        lanes = slice(h * tokens, (h + 1) * tokens)
        attn_t.append(mm(values_t[feats], weights[:, lanes]))
        d_qhat_t.append(mm(keys_t[feats], d_s[:, lanes]))
    attn_t = jnp.concatenate(attn_t, axis=0)
    d_qhat = jnp.concatenate(d_qhat_t, axis=0).T
    d_k = mm(d_s, q_blocks)
    d_v = mm(weights, g_blocks)

    attn = attn_t.T.astype(BF)
    y = (x_own + mm(attn, wout_ref[...])).astype(BF)
    skip_ref[...] = y.reshape(rows, cols, width)
    y32 = y.astype(F32)
    for part in range(width // LANES):
        yscr[part] = y32[:, part * LANES : (part + 1) * LANES].reshape(rows, cols, LANES)
    lines = []
    for i in range(rows // 2):
        pieces = []
        for pr in range(2):
            for pc in range(2):
                for part in range(width // LANES):
                    pieces.append(yscr[part, 2 * i + pr, pl.ds(pc, cols // 2, stride=2), :])
        lines.append(jnp.concatenate(pieces, axis=1))
    group = jnp.concatenate(lines, axis=0).astype(BF)
    merged_ref[...] = mm(group, wmerge_ref[...]).astype(BF).reshape(merged_ref.shape)
    grad_out = mm(attn_t.astype(BF), dy_b)

    scale_part = jnp.sum(q_unit * d_qhat, axis=0, keepdims=True)
    g_unit = d_qhat * scale_row
    d_query = (q_norm * (g_unit - q_unit * head_sum(q_unit * g_unit, heads))).astype(BF)
    d_key = k_norm * (d_k - k_unit * head_sum(k_unit * d_k, heads))
    d_kv = jnp.concatenate([d_key, d_v], axis=1).astype(BF)
    grad_q = mm(normed_own32.T.astype(BF), d_query)
    grad_kv = mm(normed32.T.astype(BF), d_kv)
    sums = jnp.concatenate([grad_q, grad_kv, grad_out], axis=1)
    from_q = mm_t(d_query, wqkv_ref[:, :width])
    d_normed = mm_t(d_kv, wqkv_ref[:, width:])
    pieces = []
    side = jnp.zeros((SIDE, width), F32)
    for i in range(ext_rows):
        if RADIUS <= i < RADIUS + rows:
            at = (i - RADIUS) * cols
            pieces += [side, from_q[at : at + cols], side]
        else:
            pieces.append(jnp.zeros((wide, width), F32))
    d_normed = d_normed + jnp.concatenate(pieces, axis=0)
    gain_part = jnp.sum(unit * d_normed, axis=0, keepdims=True)
    scaled = gain * d_normed
    mean = jnp.mean(x * scaled, axis=1, keepdims=True)
    g_x = inverse * scaled - x * (inverse * inverse * inverse) * mean
    far, near = by_side("row", g_x[(RADIUS + rows) * wide :], g_x[: RADIUS * wide])
    gx_near_ref[...] = near.astype(BF)
    gx_far_ref[...] = far.astype(BF)
    pieces = []
    for i in range(rows):
        at = (RADIUS + i) * wide
        middle = g_x[at + SIDE : at + SIDE + cols] + d_y[i * cols : (i + 1) * cols]
        pieces += [g_x[at : at + SIDE], middle, g_x[at + SIDE + cols : at + wide]]
    gx_ref[...] = jnp.concatenate(pieces, axis=0)
    scale_lane = lax.broadcasted_iota(jnp.int32, (1, LANES), 1)
    scale_sums = jnp.zeros((1, LANES), F32)
    for h in range(heads):
        of_head = jnp.sum(jnp.where(lane // head_dim == h, scale_part, 0.0), axis=1, keepdims=True)
        scale_sums = jnp.where(scale_lane == h, of_head, scale_sums)
    small = [gain_part[:, i * LANES : (i + 1) * LANES] for i in range(width // LANES)] + [scale_sums]
    small = jnp.concatenate(small + [jnp.zeros((8 - len(small), LANES), F32)], axis=0)
    if len(sum_refs) == 3:
        sum_refs[0][...] = sums.astype(BF)
        sum_refs[1][...] = group
        sum_refs[2][...] = small
        return
    send_ref, keep_ref, keep_group_ref, small_ref = sum_refs
    small_ref[...] = small
    per = width // n_row
    feats = 4 * width // n_row
    small = small_rows(small, per)
    group = group.astype(F32)
    even = lax.rem(lax.axis_index("row"), 2) == 0
    for q in range(n_row // 2):
        parts = []
        for value, axis, size in ((sums, 0, per), (group, 1, feats)):
            first = lax.slice_in_dim(value, 2 * q * size, (2 * q + 1) * size, axis=axis)
            second = lax.slice_in_dim(value, (2 * q + 1) * size, (2 * q + 2) * size, axis=axis)
            parts.append((jnp.where(even, first, second), jnp.where(even, second, first)))
        (keep_ref[q], sums_send), (keep_group, group_send) = parts
        keep_group_ref[q] = keep_group.astype(BF)
        sent = jnp.concatenate([sums_send, group_send], axis=1).astype(BF)
        send_ref[q] = jnp.concatenate([sent, small], axis=1)


def small_rows(small, rows):
    high = small.astype(BF).astype(F32)
    blank = jnp.zeros((rows - 16, LANES), F32)
    return jnp.concatenate([high, small - high, blank], axis=0).astype(BF)


def small_value(rows):
    value = rows.astype(F32)
    return value[:8] + value[8:16]


def core_sum_kernel(got_ref, keep_ref, keep_group_ref, small_ref, *refs):
    *out_refs, own_ref, own_group_ref, small_sum_ref, blocks_ref = refs
    chips, per, width = keep_ref.shape
    feats = keep_group_ref.shape[2]
    end = width + feats
    small = small_value(small_rows(small_ref[...], per)) + small_value(got_ref[0, :, end:])
    small_sum_ref[...] = small
    small = small_rows(small, per)
    chip = lax.axis_index("row") // 2
    own_ref[...] = keep_ref[chip] + got_ref[chip, :, :width].astype(F32)
    for q in range(chips):
        sums = keep_ref[q] + got_ref[q, :, :width].astype(F32)
        kept = keep_group_ref[q].astype(F32)
        first, second = in_order("row", kept, got_ref[q, :, width:end].astype(F32))
        block = jnp.concatenate([sums, first, second], axis=1).astype(BF)
        blocks_ref[q] = jnp.concatenate([block, small], axis=1)
    own_group_ref[...] = blocks_ref[chip, :, width : width + 2 * feats]
    for step, out_ref in enumerate(out_refs, 1):
        out_ref[...] = blocks_ref[partner(chip, step)]


def row_sum_kernel(sizes, *refs):
    rows, cols, width, n_col = sizes
    own_ref, own_group_ref, small_ref, *refs = refs
    got_refs, dm_ref, refs = (refs[:3], refs[3], refs[4:])
    gx_ref, near_ref, far_ref, *out_refs, grad_ref, slots_ref = refs
    wide = cols + 2 * SIDE
    per = own_ref.shape[0]
    feats = own_group_ref.shape[1] // 2
    at = 4 * width
    end = at + 2 * feats

    def summed(first, part):
        second, third, fourth = [part(ref) for ref in got_refs]
        return (first + second) + (third + fourth)

    sums = summed(own_ref[...], lambda ref: ref[:, :at].astype(F32))
    small = small_value(small_rows(small_ref[...], per))
    small = summed(small, lambda ref: small_value(ref[:, end:]))
    group = [own_group_ref[...]] + [ref[:, at:end] for ref in got_refs]
    group = [part[:, i * feats : (i + 1) * feats].astype(F32) for part in group for i in range(2)]
    group = jnp.concatenate(group, axis=0)
    merge = mm(group.T.astype(BF), dm_ref[...])
    g_x = gx_ref[...]
    blank = jnp.zeros(((rows - RADIUS) * wide, width), F32)
    above, below = by_side("row", near_ref[...].astype(F32), far_ref[...].astype(F32))
    g_x = g_x + jnp.concatenate([above, blank], axis=0)
    g_x = g_x + jnp.concatenate([blank, below], axis=0)
    grad = []
    left = []
    right = []
    for i in range(rows):
        spot = i * wide + SIDE
        grad.append(g_x[spot : spot + cols])
        left.append(g_x[spot - SIDE : spot][SIDE - RADIUS :])
        right.append(g_x[spot + cols : spot + cols + SIDE][:RADIUS])
    grad_ref[...] = jnp.concatenate(grad, axis=0)
    left, right = [jnp.concatenate(part, axis=0) for part in (left, right)]
    left, right = [jnp.concatenate([v[:, :LANES], v[:, LANES:]], axis=0) for v in (left, right)]
    high = small.astype(BF).astype(F32)
    small = jnp.concatenate([high[:4], (small - high)[:4]], axis=0)
    col = lax.axis_index("col")
    third = 3 * width // n_col
    fourth = width // n_col
    depth = merge.shape[1] // n_col
    for slot in range(n_col):
        parts = [
            sums[:, slot * third : (slot + 1) * third],
            sums[:, 3 * width + slot * fourth : 3 * width + (slot + 1) * fourth],
        ]
        for k in range(feats // per):
            parts.append(merge[k * per : (k + 1) * per, slot * depth : (slot + 1) * depth])
        rim = jnp.where(slot < col, left, right)
        parts.append(jnp.concatenate([rim, small], axis=0))
        slots_ref[slot] = jnp.concatenate(parts, axis=1).astype(BF)
    for step, out_ref in enumerate(out_refs):
        out_ref[...] = slots_ref[partner(col, step)]


def partner(index, step):
    if step == 0:
        return index
    low = lax.rem(index, 2)
    if step == 1:
        return index + 1 - 2 * low
    if step == 2:
        return lax.rem(index + 2, 4)
    return 3 - index


def col_sum_kernel(
    sizes, a_ref, b_ref, c_ref, d_ref, grad_ref, gqkv_ref, gout_ref, gmerge_ref, ggain_ref, gscale_ref, gtok_ref
):
    rows, cols, width = sizes
    per, lanes = a_ref.shape
    third = gqkv_ref.shape[1]
    fourth = gout_ref.shape[1]
    depth = gmerge_ref.shape[1]
    end = lanes - LANES
    reach = per - 8

    def summed(part):
        first, second, third, fourth = [part(ref) for ref in (a_ref, b_ref, c_ref, d_ref)]
        return (first + second) + (third + fourth)

    def tiny(ref):
        value = ref[:, end:].astype(F32)
        return value[reach : reach + 4] + value[reach + 4 :]

    total = summed(lambda ref: ref[:, :end].astype(F32))
    small = summed(tiny)
    gqkv_ref[...] = total[:, :third]
    gout_ref[...] = total[:, third : third + fourth]
    for k in range(gmerge_ref.shape[0] // per):
        at = third + fourth + k * depth
        gmerge_ref[k * per : (k + 1) * per] = total[:, at : at + depth]
    ggain_ref[...] = jnp.concatenate([small[i : i + 1] for i in range(width // LANES)], axis=1)
    for h in range(gscale_ref.shape[0]):
        gscale_ref[h] = small[width // LANES, h]
    col = lax.axis_index("col")

    def rim(ref):
        value = ref[:, end:].astype(F32)
        half = reach // 2
        return jnp.concatenate([value[:half], value[half:reach]], axis=1)

    left, right = by_side("col", rim(b_ref), rim(d_ref))
    left = jnp.where(col > 0, left, 0.0)
    right = jnp.where(col < lax.axis_size("col") - 1, right, 0.0)
    blank = jnp.zeros((cols - 2 * RADIUS, width), F32)
    pieces = []
    for i in range(rows):
        edge = slice(i * RADIUS, (i + 1) * RADIUS)
        pieces += [left[edge], blank, right[edge]]
    grad = grad_ref[...] + jnp.concatenate(pieces, axis=0)
    gtok_ref[...] = grad.astype(BF).reshape(rows, cols, width)


def plain_sums(sizes, sums, group, small, dm, gx, above, below):
    rows, cols, width = sizes
    wide = cols + 2 * SIDE
    sums = sums.astype(F32)
    merge = jnp.dot(group.T, dm, preferred_element_type=F32)
    outs = []
    for part in (sums[:, : 3 * width], sums[:, 3 * width :], merge):
        part = lax.psum_scatter(part, "row", scatter_dimension=0, tiled=True)
        outs.append(lax.psum_scatter(part, "col", scatter_dimension=1, tiled=True))
    small = lax.psum(small, ("row", "col"))
    gx = gx.reshape(rows, wide, width)
    gx = gx.at[:RADIUS].add(above.astype(F32).reshape(RADIUS, wide, width))
    gx = gx.at[rows - RADIUS :].add(below.astype(F32).reshape(RADIUS, wide, width))
    from_right = shifted(gx[:, :SIDE].astype(BF), "col", -1).astype(F32)
    from_left = shifted(gx[:, SIDE + cols :].astype(BF), "col", 1).astype(F32)
    grad = gx[:, SIDE : SIDE + cols].at[:, :SIDE].add(from_left)
    grad = grad.at[:, cols - SIDE :].add(from_right)
    return (grad.astype(BF), *outs, small[: width // LANES].reshape(1, width), small[width // LANES])


def shifted(value, axis, step):
    count = lax.axis_size(axis)
    pairs = [(i, i + step) for i in range(count) if 0 <= i + step < count]
    return lax.ppermute(value, axis, pairs)


def swapped(near, far, axis):
    count = lax.axis_size(axis)
    first = [(i, i + 1) for i in range(0, count - 1, 2)]
    second = [(i, i + 1) for i in range(1, count - 1, 2)]
    first = first + [(j, i) for i, j in first]
    second = second + [(j, i) for i, j in second]
    return (lax.ppermute(near, axis, first), lax.ppermute(far, axis, second))


def swap(value, axis, step):
    count = lax.axis_size(axis)
    return lax.ppermute(value, axis, [(i, i ^ step) for i in range(count)])


def vmem(count):
    return [pl.BlockSpec(memory_space=pltpu.VMEM)] * count


def on_device(tokens, gain, w_qkv, head_scale, w_out, w_merge, d_merged, d_skip):
    rows, cols, width = tokens.shape
    heads = head_scale.shape[0]
    n_row, n_col = (lax.axis_size("row"), lax.axis_size("col"))
    g_rows, g_cols, depth = d_merged.shape
    groups = g_rows * g_cols
    wide = cols + 2 * SIDE
    ext_rows = rows + 2 * RADIUS
    shape = jax.ShapeDtypeStruct
    params = pltpu.CompilerParams(vmem_limit_bytes=24 * 1024 * 1024)
    less = pltpu.CompilerParams(vmem_limit_bytes=8 * 1024 * 1024)
    row_near, row_far = swapped(tokens, tokens, "row")
    edge = shape((ext_rows * EDGE, width), BF)
    dm_pair = pl.pallas_call(
        pair_kernel,
        out_shape=shape((2 * groups, depth), BF),
        in_specs=vmem(2),
        out_specs=vmem(1)[0],
        compiler_params=less,
    )(d_merged, swap(d_merged, "row", 1))
    dm_pairs = [dm_pair] + [swap(dm_pair, "row", 2 * step) for step in range(1, 4)]
    gathered = len(dm_pairs) * 2 * groups
    edges, dm_own, two_rows = pl.pallas_call(
        own_edge_kernel,
        out_shape=(
            shape((2 * rows * EDGE, width), BF),
            shape((groups, depth), BF),
            shape((8, width), F32),
        ),
        in_specs=[pl.BlockSpec(memory_space=pltpu.SMEM)] + vmem(3),
        out_specs=tuple(vmem(3)),
        compiler_params=less,
        cost_estimate=pl.CostEstimate(flops=10**10, bytes_accessed=10**6, transcendentals=0),
    )(head_scale, tokens, d_merged, gain.reshape(1, width))
    tile = shape((rows * cols, width), F32)
    q_norm, q_unit, d_y, d_attn, dm_all = pl.pallas_call(
        functools.partial(own_kernel, heads),
        out_shape=(tile, tile, tile, shape((rows * cols, width), BF), shape((gathered, depth), BF)),
        in_specs=vmem(11),
        out_specs=tuple(vmem(5)),
        scratch_shapes=[pltpu.VMEM((width // LANES, rows, cols, LANES), F32)],
        compiler_params=params,
        cost_estimate=pl.CostEstimate(flops=2 * 10**9, bytes_accessed=10**6, transcendentals=0),
    )(tokens, dm_own, d_skip, two_rows, w_qkv, w_out, w_merge, *dm_pairs)
    edge_near, edge_far = pl.pallas_call(
        edge_kernel,
        out_shape=(edge, edge),
        in_specs=vmem(3),
        out_specs=tuple(vmem(2)),
        compiler_params=less,
    )(edges, row_near, row_far)
    col_near, col_far = swapped(edge_near, edge_far, "col")

    per = width // n_row
    feats = 4 * width // n_row
    packed = per % 16 == 0 and feats % LANES == 0 and groups == per
    packed = packed and 2 * rows * RADIUS + 8 == per and width // LANES < 4 and depth // n_col == LANES and n_col == 4 and n_row == 8
    if packed:
        sum_shapes = (
            shape((n_row // 2, per, 4 * width + feats + LANES), BF),
            shape((n_row // 2, per, 4 * width), F32),
            shape((n_row // 2, per, feats), BF),
            shape((8, LANES), F32),
        )
    else:
        sum_shapes = (
            shape((width, 4 * width), BF),
            shape((groups, 4 * width), BF),
            shape((8, LANES), F32),
        )
    sizes = (rows, cols, width, heads, n_row, n_col)
    reach = RADIUS * wide
    skip_out, merged, gx, gx_near, gx_far, *sums = pl.pallas_call(
        functools.partial(layer_kernel, sizes),
        out_shape=(
            shape((rows, cols, width), BF),
            shape((g_rows, g_cols, depth), BF),
            shape((rows * wide, width), F32),
            shape((reach, width), BF),
            shape((reach, width), BF),
        )
        + sum_shapes,
        in_specs=vmem(13),
        out_specs=tuple(vmem(5 + len(sum_shapes))),
        scratch_shapes=[
            pltpu.VMEM((width // LANES, rows, cols, LANES), F32),
        ],
        compiler_params=params,
        cost_estimate=pl.CostEstimate(flops=4 * 10**9, bytes_accessed=10**6, transcendentals=0),
    )(
        tokens,
        row_near,
        row_far,
        col_near,
        col_far,
        two_rows,
        q_norm,
        q_unit,
        d_y,
        d_attn,
        w_qkv,
        w_out,
        w_merge,
    )
    if not packed:
        above, below = by_side("row", *swapped(gx_near, gx_far, "row"))
        grad_tokens, g_qkv, g_out, g_merge, g_gain, g_scale = plain_sums(
            (rows, cols, width), *sums, d_merged.reshape(groups, depth), gx, above, below
        )
    else:
        near, far = swapped(gx_near, gx_far, "row")
        send, *kept = sums
        block = shape((per, 4 * width + 2 * feats + LANES), BF)
        *blocks, own, own_group, small = pl.pallas_call(
            core_sum_kernel,
            out_shape=(block, block, block)
            + (shape((per, 4 * width), F32), shape((per, 2 * feats), BF), shape((8, LANES), F32)),
            in_specs=vmem(4),
            out_specs=tuple(vmem(6)),
            scratch_shapes=[pltpu.VMEM((n_row // 2,) + block.shape, BF)],
            compiler_params=less,
        )(swap(send, "row", 1), *kept)
        got = [swap(blocks[step - 1], "row", 2 * step) for step in (3, 2, 1)][::-1]
        lanes = 4 * width // n_col + feats // per * (depth // n_col) + LANES
        *slots, grad = pl.pallas_call(
            functools.partial(row_sum_kernel, (rows, cols, width, n_col)),
            out_shape=tuple([shape((per, lanes), BF)] * n_col)
            + (shape((rows * cols, width), F32),),
            in_specs=vmem(10),
            out_specs=tuple(vmem(n_col + 1)),
            scratch_shapes=[pltpu.VMEM((n_col, per, lanes), BF)],
            compiler_params=less,
        )(own, own_group, small, *got, dm_all, gx, near, far)
        got = [slots[0]]
        got += [swap(slots[step], "col", step) for step in (3, 2, 1)][::-1]
        g_qkv, g_out, g_merge, g_gain, g_scale, grad_tokens = pl.pallas_call(
            functools.partial(col_sum_kernel, (rows, cols, width)),
            out_shape=(
                shape((per, 3 * width // n_col), F32),
                shape((per, width // n_col), F32),
                shape((feats, depth // n_col), F32),
                shape((1, width), F32),
                shape((heads,), F32),
                shape((rows, cols, width), BF),
            ),
            in_specs=vmem(5),
            out_specs=tuple(vmem(4)) + (pl.BlockSpec(memory_space=pltpu.SMEM), vmem(1)[0]),
            compiler_params=less,
        )(*got, grad)
    return (
        skip_out,
        merged,
        grad_tokens,
        g_qkv,
        g_out,
        g_merge,
        g_gain.reshape(width),
        g_scale[:heads],
    )


def solution(mesh):
    block = P("row", "col", None)
    return jax.shard_map(
        on_device,
        mesh=mesh,
        in_specs=(block, P(), P(), P(), P(), P(), block, block),
        out_specs=(block, block, block, P("row", "col"), P("row", "col"), P("row", "col"), P(), P()),
        check_vma=False,
    )
```

```python
import functools
import jax
import jax.numpy as jnp
from jax import lax
from jax.experimental import pallas as pl
from jax.experimental.pallas import tpu as pltpu
from jax.sharding import PartitionSpec as P

RADIUS = 3
IMG_MAX = 512
EPS = 1e-06
EDGE = 4
SIDE = 8
LANES = 128
BF = jnp.bfloat16
F32 = jnp.float32


def mm(a, b):
    return lax.dot_general(a, b, (((1,), (0,)), ((), ())), preferred_element_type=F32)


def mm_t(a, b):
    return lax.dot_general(a, b, (((1,), (1,)), ((), ())), preferred_element_type=F32)


def split_two(value):
    high = value.astype(BF)
    return (high, (value - high.astype(F32)).astype(BF))


def by_side(axis, near, far):
    even = lax.rem(lax.axis_index(axis), 2) == 0
    return (jnp.where(even, far, near), jnp.where(even, near, far))


def first_kernel(ones_ref, parity_ref):
    width = ones_ref.shape[0]
    head_dim = width // (parity_ref.shape[0] // 2)
    same_head = lax.broadcasted_iota(jnp.int32, (width, width), 0) // head_dim == (
        lax.broadcasted_iota(jnp.int32, (width, width), 1) // head_dim
    )
    ones_ref[...] = jnp.where(same_head, 1.0, 0.0).astype(BF)
    half = (parity_ref.shape[0] // 2, parity_ref.shape[1])
    parts = [
        jnp.where(lax.rem(lax.axis_index(axis), 2) == 0, jnp.ones(half, F32), jnp.zeros(half, F32))
        for axis in ("row", "col")
    ]
    parity_ref[...] = jnp.concatenate(parts, axis=0)


def edge_kernel(edges_ref, near_ref, far_ref, edge_near_ref, edge_far_ref):
    rows, cols, width = near_ref.shape
    up, down = by_side("row", near_ref[...].astype(F32), far_ref[...].astype(F32))
    up = up[rows - RADIUS :]
    down = down[:RADIUS]
    halo = []
    for at in (0, cols - EDGE):
        parts = [part[:, at : at + EDGE].reshape(RADIUS * EDGE, width) for part in (up, down)]
        halo.append(jnp.concatenate(parts, axis=0))
    far, near = by_side("col", halo[1], halo[0])
    for out_ref, own_at, part in ((edge_near_ref, 0, near), (edge_far_ref, rows * EDGE, far)):
        own = edges_ref[own_at : own_at + rows * EDGE].astype(F32)
        size = RADIUS * EDGE
        out_ref[...] = jnp.concatenate([part[:size], own, part[size:]], axis=0).astype(BF)


def pair_kernel(parity_ref, dm_ref, dm_near_ref, dm_pair_ref):
    size = dm_pair_ref.shape[0] // 2
    own, near = [ref[...].reshape(size, -1).astype(F32) for ref in (dm_ref, dm_near_ref)]
    even = parity_ref[0:1, 0:1] > 0.5
    pair = [jnp.where(even, own, near), jnp.where(even, near, own)]
    dm_pair_ref[...] = jnp.concatenate(pair, axis=0).astype(BF)


def in_order(axis, own, partner):
    even = lax.rem(lax.axis_index(axis), 2) == 0
    return (jnp.where(even, own, partner), jnp.where(even, partner, own))


def head_sum(value, ones_ref):
    high, low = split_two(value)
    return mm(high, ones_ref[...]) + mm(low, ones_ref[...])


def own_kernel(
    ones_ref,
    parity_ref,
    scale_ref,
    tok_ref,
    dm_ref,
    dskip_ref,
    gain_ref,
    wqkv_ref,
    wout_ref,
    wmerge_ref,
    edges_ref,
    rows_ref,
    q_norm_ref,
    q_unit_ref,
    dy_ref,
    d_attn_ref,
    dscr,
):
    rows, cols, width = tok_ref.shape
    tokens = rows * cols
    tok = tok_ref[...].astype(F32)
    left = tok[:, :EDGE].reshape(rows * EDGE, width)
    right = tok[:, cols - EDGE :].reshape(rows * EDGE, width)
    heads = scale_ref.shape[1]
    even = parity_ref[heads : heads + 1, 0:1] > 0.5
    near, far = (jnp.where(even, right, left), jnp.where(even, left, right))
    edges_ref[...] = jnp.concatenate([near, far], axis=0).astype(BF)
    lane = lax.broadcasted_iota(jnp.int32, (1, width), 1)
    scale_row = jnp.zeros((1, width), F32)
    for h in range(heads):
        scale_row = jnp.where(lane // (width // heads) == h, scale_ref[:, h : h + 1], scale_row)
    blank = jnp.zeros((6, width), F32)
    rows_ref[...] = jnp.concatenate([gain_ref[...], scale_row, blank], axis=0)
    x = tok.reshape(tokens, width)
    inverse = lax.rsqrt(jnp.mean(x * x, axis=1, keepdims=True) + EPS)
    normed = (x * inverse * gain_ref[...]).astype(BF)
    query = mm(normed, wqkv_ref[:, :width])
    q_norm = lax.rsqrt(head_sum(query * query, ones_ref) + EPS)
    q_norm_ref[...] = q_norm
    q_unit_ref[...] = query * q_norm
    group_wide = cols // 2
    d_in = mm_t(dm_ref[...].reshape(-1, dm_ref.shape[2]), wmerge_ref[...])
    for i in range(rows // 2):
        for pr in range(2):
            for pc in range(2):
                for part in range(width // LANES):
                    at = (2 * pr + pc) * width + part * LANES
                    dscr[part, 2 * i + pr, pl.ds(pc, group_wide, stride=2), :] = d_in[
                        i * group_wide : (i + 1) * group_wide, at : at + LANES
                    ]
    d_group = jnp.concatenate(
        [dscr[part].reshape(tokens, LANES) for part in range(width // LANES)], axis=1
    )
    d_y = dskip_ref[...].reshape(tokens, width).astype(F32) + d_group
    dy_ref[...] = d_y
    d_attn_ref[...] = mm_t(d_y.astype(BF), wout_ref[...]).astype(BF)


def layer_kernel(
    sizes,
    ones_ref,
    tok_ref,
    row_near_ref,
    row_far_ref,
    col_near_ref,
    col_far_ref,
    rows_ref,
    q_norm_ref,
    q_unit_ref,
    dy_ref,
    d_attn_ref,
    wqkv_ref,
    wout_ref,
    x_ref,
    y_ref,
    d_query_ref,
    d_kv_ref,
    grad_out_ref,
    group_ref,
    scale_part_ref,
    yscr,
):
    rows, cols, width, heads, n_row, n_col = sizes
    head_dim = width // heads
    wide = cols + 2 * SIDE
    ext_rows = rows + 2 * RADIUS
    tokens = rows * cols
    image_rows = min(IMG_MAX, rows * n_row)
    row_start = lax.axis_index("row") * rows
    col_index = lax.axis_index("col")
    col_start = col_index * cols
    first = row_start // image_rows * image_rows

    lane = lax.broadcasted_iota(jnp.int32, (1, width), 1)
    def blocks(value):
        zero = jnp.zeros_like(value)
        kept = [jnp.where(lane // head_dim == h, value, zero) for h in range(heads)]
        return jnp.concatenate(kept, axis=0).astype(BF)

    gain = rows_ref[0:1]
    scale_row = rows_ref[1:2]
    up, down = by_side("row", row_near_ref[...].astype(F32), row_far_ref[...].astype(F32))
    left, right = by_side("col", col_near_ref[...].astype(F32), col_far_ref[...].astype(F32))
    own = tok_ref[...].astype(F32)
    blank = jnp.zeros((SIDE - EDGE, width), F32)
    pieces = []
    for i in range(ext_rows):
        if i < RADIUS:
            row = up[rows - RADIUS + i]
        elif i < RADIUS + rows:
            row = own[i - RADIUS]
        else:
            row = down[i - RADIUS - rows]
        edge = slice(i * EDGE, (i + 1) * EDGE)
        pieces += [blank, left[edge], row, right[edge], blank]
    x = jnp.concatenate(pieces, axis=0)
    x_ref[...] = x
    inverse = lax.rsqrt(jnp.mean(x * x, axis=1, keepdims=True) + EPS)
    unit = x * inverse
    normed32 = (unit * gain).astype(BF).astype(F32)
    normed = normed32.astype(BF)
    x_own = inner_tokens(x, rows, cols)
    kv = mm(normed, wqkv_ref[:, width:])
    key_raw = kv[:, :width]
    k_norm = lax.rsqrt(head_sum(key_raw * key_raw, ones_ref) + EPS)
    k_unit = key_raw * k_norm
    keys = k_unit.astype(BF)
    values = kv[:, width:].astype(BF)
    q_norm = q_norm_ref[...]
    q_unit = q_unit_ref[...]
    q_hat = (q_unit * scale_row).astype(BF).astype(F32)
    d_y = dy_ref[...]
    dy_b = d_y.astype(BF)
    d_attn = d_attn_ref[...].astype(F32)

    index = lax.broadcasted_iota(jnp.int32, (1, tokens), 1)
    q_row = jnp.zeros_like(index)
    for i in range(1, rows):
        q_row = q_row + (index >= i * cols).astype(jnp.int32)
    q_col = index - q_row * cols
    key_col = lax.broadcasted_iota(jnp.int32, (wide, tokens), 0) - SIDE
    near = (key_col - q_col <= RADIUS) & (key_col - q_col >= -RADIUS)
    near = near & (key_col + col_start >= 0) & (key_col + col_start < cols * n_col)
    near = jnp.where(near, 1.0, 0.0)
    parts = []
    for i in range(-RADIUS, rows + RADIUS):
        ok = (q_row - i <= RADIUS) & (q_row - i >= -RADIUS)
        ok = ok & (row_start + i >= first) & (row_start + i < first + image_rows)
        parts.append(near * jnp.where(ok, 1.0, 0.0))
    allowed = jnp.concatenate([jnp.concatenate(parts, axis=0)] * heads, axis=1)
    q_blocks = blocks(q_hat)
    g_blocks = blocks(d_attn)
    expo = jnp.exp(mm_t(keys, q_blocks)) * allowed
    prob = expo * (1.0 / jnp.sum(expo, axis=0, keepdims=True))
    weights = prob.astype(BF)
    d_w = mm_t(values, g_blocks)
    delta = jnp.sum(d_w * prob, axis=0, keepdims=True)
    d_s = (prob * (d_w - delta)).astype(BF)
    values_t = values.astype(F32).T.astype(BF)
    keys_t = keys.astype(F32).T.astype(BF)
    attn_t = []
    d_qhat_t = []
    for h in range(heads):
        feats = slice(h * head_dim, (h + 1) * head_dim)
        lanes = slice(h * tokens, (h + 1) * tokens)
        attn_t.append(mm(values_t[feats], weights[:, lanes]))
        d_qhat_t.append(mm(keys_t[feats], d_s[:, lanes]))
    attn_t = jnp.concatenate(attn_t, axis=0)
    d_qhat = jnp.concatenate(d_qhat_t, axis=0).T
    d_k = mm(d_s, q_blocks)
    d_v = mm(weights, g_blocks)

    attn = attn_t.T.astype(BF)
    y = (x_own + mm(attn, wout_ref[...])).astype(BF)
    y_ref[...] = y
    y32 = y.astype(F32)
    for part in range(width // LANES):
        yscr[part] = y32[:, part * LANES : (part + 1) * LANES].reshape(rows, cols, LANES)
    lines = []
    for i in range(rows // 2):
        pieces = []
        for pr in range(2):
            for pc in range(2):
                for part in range(width // LANES):
                    pieces.append(yscr[part, 2 * i + pr, pl.ds(pc, cols // 2, stride=2), :])
        lines.append(jnp.concatenate(pieces, axis=1))
    group = jnp.concatenate(lines, axis=0).astype(BF)
    group_ref[...] = group
    grad_out_ref[...] = mm(attn_t.astype(BF), dy_b)

    scale_part_ref[...] = jnp.broadcast_to(
        jnp.sum(q_unit * d_qhat, axis=0, keepdims=True), scale_part_ref.shape
    )
    g_unit = d_qhat * scale_row
    d_query_ref[...] = (q_norm * (g_unit - q_unit * head_sum(q_unit * g_unit, ones_ref))).astype(BF)
    d_key = k_norm * (d_k - k_unit * head_sum(k_unit * d_k, ones_ref))
    d_kv_ref[...] = jnp.concatenate([d_key, d_v], axis=1).astype(BF)


def inner_tokens(value, rows, cols):
    wide = cols + 2 * SIDE
    pieces = []
    for i in range(RADIUS, RADIUS + rows):
        pieces.append(value[i * wide + SIDE : i * wide + SIDE + cols])
    return jnp.concatenate(pieces, axis=0)


def output_kernel(y_ref, group_ref, wmerge_ref, skip_ref, merged_ref):
    skip_ref[...] = y_ref[...].reshape(skip_ref.shape)
    merged = mm(group_ref[...], wmerge_ref[...])
    merged_ref[...] = merged.astype(BF).reshape(merged_ref.shape)


def weights_kernel(
    sizes, x_ref, d_query_ref, d_kv_ref, grad_out_ref, group_ref, rows_ref, *refs
):
    rows, cols, width, n_row, n_dm = sizes
    dm_refs, dm_all_ref, sum_refs = (refs[:n_dm], refs[n_dm], refs[n_dm + 1 :])
    dm_all_ref[...] = jnp.concatenate([ref[...] for ref in dm_refs], axis=0)
    x = x_ref[...]
    inverse = lax.rsqrt(jnp.mean(x * x, axis=1, keepdims=True) + EPS)
    normed32 = (x * inverse * rows_ref[0:1]).astype(BF).astype(F32)
    grad_q = mm(inner_tokens(normed32, rows, cols).T.astype(BF), d_query_ref[...])
    grad_kv = mm(normed32.T.astype(BF), d_kv_ref[...])
    sums = jnp.concatenate([grad_q, grad_kv, grad_out_ref[...]], axis=1)
    group = group_ref[...]
    if len(sum_refs) == 2:
        sum_refs[0][...] = sums.astype(BF)
        sum_refs[1][...] = group
        return
    send_ref, keep_ref, keep_group_ref = sum_refs
    per = width // n_row
    feats = 4 * width // n_row
    group = group.astype(F32)
    even = lax.rem(lax.axis_index("row"), 2) == 0
    for q in range(n_row // 2):
        parts = []
        for value, axis, size in ((sums, 0, per), (group, 1, feats)):
            first = lax.slice_in_dim(value, 2 * q * size, (2 * q + 1) * size, axis=axis)
            second = lax.slice_in_dim(value, (2 * q + 1) * size, (2 * q + 2) * size, axis=axis)
            parts.append((jnp.where(even, first, second), jnp.where(even, second, first)))
        (keep_ref[q], sums_send), (keep_group, group_send) = parts
        keep_group_ref[q] = keep_group.astype(BF)
        send_ref[q] = jnp.concatenate([sums_send, group_send], axis=1).astype(BF)


def norm_kernel(
    sizes, x_ref, d_query_ref, d_kv_ref, scale_part_ref, rows_ref, dy_ref, wqkv_ref, *refs
):
    rows, cols, width, heads = sizes
    gx_ref, gx_near_ref, gx_far_ref, small_ref = refs
    head_dim = width // heads
    wide = cols + 2 * SIDE
    ext_rows = rows + 2 * RADIUS
    gain = rows_ref[0:1]
    lane = lax.broadcasted_iota(jnp.int32, (1, width), 1)
    x = x_ref[...]
    inverse = lax.rsqrt(jnp.mean(x * x, axis=1, keepdims=True) + EPS)
    unit = x * inverse
    d_y = dy_ref[...]
    from_q = mm_t(d_query_ref[...], wqkv_ref[:, :width])
    d_normed = mm_t(d_kv_ref[...], wqkv_ref[:, width:])
    pieces = []
    side = jnp.zeros((SIDE, width), F32)
    for i in range(ext_rows):
        if RADIUS <= i < RADIUS + rows:
            at = (i - RADIUS) * cols
            pieces += [side, from_q[at : at + cols], side]
        else:
            pieces.append(jnp.zeros((wide, width), F32))
    d_normed = d_normed + jnp.concatenate(pieces, axis=0)
    gain_part = jnp.sum(unit * d_normed, axis=0, keepdims=True)
    scaled = gain * d_normed
    mean = jnp.mean(x * scaled, axis=1, keepdims=True)
    g_x = inverse * scaled - x * (inverse * inverse * inverse) * mean

    def rim(first_row):
        parts = []
        for i in range(first_row, first_row + RADIUS):
            parts.append(g_x[i * wide : (i + 1) * wide][SIDE - EDGE : wide - SIDE + EDGE])
        return jnp.concatenate(parts, axis=0)

    far, near = by_side("row", rim(RADIUS + rows), rim(0))
    pieces = []
    for i in range(rows):
        at = (RADIUS + i) * wide
        middle = g_x[at + SIDE : at + SIDE + cols] + d_y[i * cols : (i + 1) * cols]
        pieces += [g_x[at : at + SIDE], middle, g_x[at + SIDE + cols : at + wide]]
    gx_ref[...] = jnp.concatenate(pieces, axis=0)
    scale_part = scale_part_ref[0:1]
    scale_lane = lax.broadcasted_iota(jnp.int32, (1, LANES), 1)
    scale_sums = jnp.zeros((1, LANES), F32)
    for h in range(heads):
        of_head = jnp.sum(jnp.where(lane // head_dim == h, scale_part, 0.0), axis=1, keepdims=True)
        scale_sums = jnp.where(scale_lane == h, of_head, scale_sums)
    small = [gain_part[:, i * LANES : (i + 1) * LANES] for i in range(width // LANES)] + [scale_sums]
    small = jnp.concatenate(small + [jnp.zeros((8 - len(small), LANES), F32)], axis=0)
    small_ref[...] = small
    high = small.astype(BF).astype(F32)
    small = jnp.concatenate([high, small - high], axis=1)
    gx_near_ref[...] = jnp.concatenate([near, small], axis=0).astype(BF)
    gx_far_ref[...] = far.astype(BF)


def small_rows(small, rows):
    high = small.astype(BF).astype(F32)
    blank = jnp.zeros((rows - 16, LANES), F32)
    return jnp.concatenate([high, small - high, blank], axis=0).astype(BF)


def wide_rim(ref, cols):
    size = cols + 2 * EDGE
    blank = jnp.zeros((SIDE - EDGE, ref.shape[1]), F32)
    pieces = []
    for i in range(RADIUS):
        pieces += [blank, ref[...][i * size : (i + 1) * size].astype(F32), blank]
    return jnp.concatenate(pieces, axis=0)


def small_value(rows):
    value = rows.astype(F32)
    return value[:8] + value[8:16]


def core_sum_kernel(got_ref, keep_ref, keep_group_ref, small_ref, near_ref, *refs):
    *out_refs, own_ref, own_group_ref, small_sum_ref, blocks_ref = refs
    chips, per, width = keep_ref.shape
    feats = keep_group_ref.shape[2]
    end = width + feats
    got_small = near_ref[...].astype(F32)[near_ref.shape[0] - 8 :]
    got_small = got_small[:, :LANES] + got_small[:, LANES:]
    small = small_value(small_rows(small_ref[...], per)) + got_small
    small_sum_ref[...] = small
    small = small_rows(small, per)
    chip = lax.axis_index("row") // 2
    own_ref[...] = keep_ref[chip] + got_ref[chip, :, :width].astype(F32)
    for q in range(chips):
        sums = keep_ref[q] + got_ref[q, :, :width].astype(F32)
        kept = keep_group_ref[q].astype(F32)
        first, second = in_order("row", kept, got_ref[q, :, width:end].astype(F32))
        block = jnp.concatenate([sums, first, second], axis=1).astype(BF)
        blocks_ref[q] = jnp.concatenate([block, small], axis=1)
    own_group_ref[...] = blocks_ref[chip, :, width : width + 2 * feats]
    for step, out_ref in enumerate(out_refs, 1):
        out_ref[...] = blocks_ref[partner(chip, step)]


def row_sum_kernel(sizes, *refs):
    rows, cols, width, n_col = sizes
    own_ref, own_group_ref, small_ref, *refs = refs
    got_refs, dm_ref, refs = (refs[:3], refs[3], refs[4:])
    gx_ref, near_ref, far_ref, *out_refs, grad_ref, slots_ref = refs
    wide = cols + 2 * SIDE
    per = own_ref.shape[0]
    feats = own_group_ref.shape[1] // 2
    at = 4 * width
    end = at + 2 * feats

    def summed(first, part):
        fourth, third, second = [part(ref) for ref in got_refs]
        return (first + second) + (third + fourth)

    sums = summed(own_ref[...], lambda ref: ref[:, :at].astype(F32))
    small = small_value(small_rows(small_ref[...], per))
    small = summed(small, lambda ref: small_value(ref[:, end:]))
    group = [own_group_ref[...]] + [ref[:, at:end] for ref in got_refs[::-1]]
    group = [part[:, i * feats : (i + 1) * feats].astype(F32) for part in group for i in range(2)]
    group = jnp.concatenate(group, axis=0)
    merge = mm(group.T.astype(BF), dm_ref[...])
    g_x = gx_ref[...]
    blank = jnp.zeros(((rows - RADIUS) * wide, width), F32)
    above, below = by_side("row", wide_rim(near_ref, cols), wide_rim(far_ref, cols))
    g_x = g_x + jnp.concatenate([above, blank], axis=0)
    g_x = g_x + jnp.concatenate([blank, below], axis=0)
    grad = []
    left = []
    right = []
    for i in range(rows):
        spot = i * wide + SIDE
        grad.append(g_x[spot : spot + cols])
        left.append(g_x[spot - SIDE : spot][SIDE - RADIUS :])
        right.append(g_x[spot + cols : spot + cols + SIDE][:RADIUS])
    grad_ref[...] = jnp.concatenate(grad, axis=0)
    left, right = [jnp.concatenate(part, axis=0) for part in (left, right)]
    left, right = [jnp.concatenate([v[:, :LANES], v[:, LANES:]], axis=0) for v in (left, right)]
    high = small.astype(BF).astype(F32)
    small = jnp.concatenate([high[:4], (small - high)[:4]], axis=0)
    col = lax.axis_index("col")
    third = 3 * width // n_col
    fourth = width // n_col
    depth = merge.shape[1] // n_col
    for slot in range(n_col):
        parts = [
            sums[:, slot * third : (slot + 1) * third],
            sums[:, 3 * width + slot * fourth : 3 * width + (slot + 1) * fourth],
        ]
        for k in range(feats // per):
            parts.append(merge[k * per : (k + 1) * per, slot * depth : (slot + 1) * depth])
        rim = jnp.where(slot < col, left, right)
        parts.append(jnp.concatenate([rim, small], axis=0))
        slots_ref[slot] = jnp.concatenate(parts, axis=1).astype(BF)
    for step, out_ref in enumerate(out_refs):
        out_ref[...] = slots_ref[partner(col, step)]


def partner(index, step):
    if step == 0:
        return index
    low = lax.rem(index, 2)
    if step == 1:
        return index + 1 - 2 * low
    if step == 2:
        return lax.rem(index + 2, 4)
    return 3 - index


def col_sum_kernel(
    sizes, a_ref, d_ref, c_ref, b_ref, grad_ref, gqkv_ref, gout_ref, gmerge_ref, ggain_ref, gscale_ref, gtok_ref
):
    rows, cols, width = sizes
    per, lanes = a_ref.shape
    third = gqkv_ref.shape[1]
    fourth = gout_ref.shape[1]
    depth = gmerge_ref.shape[1]
    end = lanes - LANES
    reach = per - 8

    def summed(part):
        first, second, third, fourth = [part(ref) for ref in (a_ref, b_ref, c_ref, d_ref)]
        return (first + second) + (third + fourth)

    def tiny(ref):
        value = ref[:, end:].astype(F32)
        return value[reach : reach + 4] + value[reach + 4 :]

    total = summed(lambda ref: ref[:, :end].astype(F32))
    small = summed(tiny)
    gqkv_ref[...] = total[:, :third]
    gout_ref[...] = total[:, third : third + fourth]
    for k in range(gmerge_ref.shape[0] // per):
        at = third + fourth + k * depth
        gmerge_ref[k * per : (k + 1) * per] = total[:, at : at + depth]
    ggain_ref[...] = jnp.concatenate([small[i : i + 1] for i in range(width // LANES)], axis=1)
    for h in range(gscale_ref.shape[0]):
        gscale_ref[h] = small[width // LANES, h]
    col = lax.axis_index("col")

    def rim(ref):
        value = ref[:, end:].astype(F32)
        half = reach // 2
        return jnp.concatenate([value[:half], value[half:reach]], axis=1)

    left, right = by_side("col", rim(b_ref), rim(d_ref))
    left = jnp.where(col > 0, left, 0.0)
    right = jnp.where(col < lax.axis_size("col") - 1, right, 0.0)
    blank = jnp.zeros((cols - 2 * RADIUS, width), F32)
    pieces = []
    for i in range(rows):
        edge = slice(i * RADIUS, (i + 1) * RADIUS)
        pieces += [left[edge], blank, right[edge]]
    grad = grad_ref[...] + jnp.concatenate(pieces, axis=0)
    gtok_ref[...] = grad.astype(BF).reshape(rows, cols, width)


def plain_sums(sizes, sums, group, small, dm, gx, above, below):
    rows, cols, width = sizes
    wide = cols + 2 * SIDE
    sums = sums.astype(F32)
    merge = jnp.dot(group.T, dm, preferred_element_type=F32)
    outs = []
    for part in (sums[:, : 3 * width], sums[:, 3 * width :], merge):
        part = lax.psum_scatter(part, "row", scatter_dimension=0, tiled=True)
        outs.append(lax.psum_scatter(part, "col", scatter_dimension=1, tiled=True))
    small = lax.psum(small, ("row", "col"))
    gx = gx.reshape(rows, wide, width)
    trim = slice(SIDE - EDGE, wide - SIDE + EDGE)
    gx = gx.at[:RADIUS, trim].add(above.astype(F32).reshape(RADIUS, -1, width))
    gx = gx.at[rows - RADIUS :, trim].add(below.astype(F32).reshape(RADIUS, -1, width))
    from_right = shifted(gx[:, :SIDE].astype(BF), "col", -1).astype(F32)
    from_left = shifted(gx[:, SIDE + cols :].astype(BF), "col", 1).astype(F32)
    grad = gx[:, SIDE : SIDE + cols].at[:, :SIDE].add(from_left)
    grad = grad.at[:, cols - SIDE :].add(from_right)
    return (grad.astype(BF), *outs, small[: width // LANES].reshape(1, width), small[width // LANES])


def shifted(value, axis, step):
    count = lax.axis_size(axis)
    pairs = [(i, i + step) for i in range(count) if 0 <= i + step < count]
    return lax.ppermute(value, axis, pairs)


def swapped(near, far, axis):
    count = lax.axis_size(axis)
    first = [(i, i + 1) for i in range(0, count, 2)]
    second = [(i, (i + 1) % count) for i in range(1, count, 2)]
    first = first + [(j, i) for i, j in first]
    second = second + [(j, i) for i, j in second]
    return (lax.ppermute(near, axis, first), lax.ppermute(far, axis, second))


def swap(value, axis, step):
    count = lax.axis_size(axis)
    return lax.ppermute(value, axis, [(i, i ^ step) for i in range(count)])


def vmem(count):
    return [pl.BlockSpec(memory_space=pltpu.VMEM)] * count


def on_device(tokens, gain, w_qkv, head_scale, w_out, w_merge, d_merged, d_skip):
    rows, cols, width = tokens.shape
    heads = head_scale.shape[0]
    n_row, n_col = (lax.axis_size("row"), lax.axis_size("col"))
    g_rows, g_cols, depth = d_merged.shape
    groups = g_rows * g_cols
    wide = cols + 2 * SIDE
    ext_rows = rows + 2 * RADIUS
    shape = jax.ShapeDtypeStruct
    params = pltpu.CompilerParams(vmem_limit_bytes=24 * 1024 * 1024)
    less = pltpu.CompilerParams(vmem_limit_bytes=8 * 1024 * 1024)
    row_near, row_far = swapped(tokens, tokens, "row")
    edge = shape((ext_rows * EDGE, width), BF)
    ones, parity = pl.pallas_call(
        first_kernel,
        out_shape=(shape((width, width), BF), shape((2 * heads, LANES), F32)),
        out_specs=tuple(vmem(2)),
        compiler_params=less,
        cost_estimate=pl.CostEstimate(flops=10**10, bytes_accessed=10**5, transcendentals=0),
    )()
    dm_pair = pl.pallas_call(
        pair_kernel,
        out_shape=shape((2 * groups, depth), BF),
        in_specs=vmem(3),
        out_specs=vmem(1)[0],
        compiler_params=less,
    )(parity, d_merged, swap(d_merged, "row", 1))
    dm_pairs = [dm_pair] + [swap(dm_pair, "row", 2 * step) for step in range(1, 4)]
    gathered = len(dm_pairs) * 2 * groups
    tile = shape((rows * cols, width), F32)
    half = shape((rows * cols, width), BF)
    edges, two_rows, q_norm, q_unit, d_y, d_attn = pl.pallas_call(
        own_kernel,
        out_shape=(shape((2 * rows * EDGE, width), BF), shape((8, width), F32), tile, tile, tile, half),
        in_specs=vmem(10),
        out_specs=tuple(vmem(6)),
        scratch_shapes=[pltpu.VMEM((width // LANES, rows, cols, LANES), F32)],
        compiler_params=params,
        cost_estimate=pl.CostEstimate(flops=10**9, bytes_accessed=10**6, transcendentals=0),
    )(
        ones,
        parity,
        head_scale.reshape(1, heads),
        tokens,
        d_merged,
        d_skip,
        gain.reshape(1, width),
        w_qkv,
        w_out,
        w_merge,
    )
    edge_near, edge_far = pl.pallas_call(
        edge_kernel,
        out_shape=(edge, edge),
        in_specs=vmem(3),
        out_specs=tuple(vmem(2)),
        compiler_params=less,
    )(edges, row_near, row_far)
    col_near, col_far = swapped(edge_near, edge_far, "col")

    per = width // n_row
    feats = 4 * width // n_row
    packed = per % 16 == 0 and feats % LANES == 0 and groups == per
    packed = packed and 2 * rows * RADIUS + 8 == per and width // LANES < 4 and depth // n_col == LANES and n_col == 4 and n_row == 8
    if packed:
        sum_shapes = (
            shape((n_row // 2, per, 4 * width + feats), BF),
            shape((n_row // 2, per, 4 * width), F32),
            shape((n_row // 2, per, feats), BF),
        )
    else:
        sum_shapes = (
            shape((width, 4 * width), BF),
            shape((groups, 4 * width), BF),
        )
    sizes = (rows, cols, width, heads, n_row, n_col)
    reach = RADIUS * (cols + 2 * EDGE)
    tall = ext_rows * wide
    x, y, d_query, d_kv, grad_out, group, scale_part = pl.pallas_call(
        functools.partial(layer_kernel, sizes),
        out_shape=(
            shape((tall, width), F32),
            half,
            half,
            shape((tall, 2 * width), BF),
            shape((width, width), F32),
            shape((groups, 4 * width), BF),
            shape((8, width), F32),
        ),
        in_specs=vmem(13),
        out_specs=tuple(vmem(7)),
        scratch_shapes=[pltpu.VMEM((width // LANES, rows, cols, LANES), F32)],
        compiler_params=params,
        cost_estimate=pl.CostEstimate(flops=4 * 10**9, bytes_accessed=10**6, transcendentals=0),
    )(
        ones,
        tokens,
        row_near,
        row_far,
        col_near,
        col_far,
        two_rows,
        q_norm,
        q_unit,
        d_y,
        d_attn,
        w_qkv,
        w_out,
    )
    dm_all, *sums = pl.pallas_call(
        functools.partial(weights_kernel, (rows, cols, width, n_row, len(dm_pairs))),
        out_shape=(shape((gathered, depth), BF),) + sum_shapes,
        in_specs=vmem(6 + len(dm_pairs)),
        out_specs=tuple(vmem(1 + len(sum_shapes))),
        compiler_params=params,
        cost_estimate=pl.CostEstimate(flops=10**9, bytes_accessed=10**6, transcendentals=0),
    )(x, d_query, d_kv, grad_out, group, two_rows, *dm_pairs)
    gx, gx_near, gx_far, small = pl.pallas_call(
        functools.partial(norm_kernel, (rows, cols, width, heads)),
        out_shape=(
            shape((rows * wide, width), F32),
            shape((reach + 8, width), BF),
            shape((reach, width), BF),
            shape((8, LANES), F32),
        ),
        in_specs=vmem(7),
        out_specs=tuple(vmem(4)),
        compiler_params=params,
        cost_estimate=pl.CostEstimate(flops=5 * 10**8, bytes_accessed=10**6, transcendentals=0),
    )(x, d_query, d_kv, scale_part, two_rows, d_y, w_qkv)
    skip_out, merged = pl.pallas_call(
        output_kernel,
        out_shape=(shape((rows, cols, width), BF), shape((g_rows, g_cols, depth), BF)),
        in_specs=vmem(3),
        out_specs=tuple(vmem(2)),
        compiler_params=less,
        cost_estimate=pl.CostEstimate(flops=10**9, bytes_accessed=10**6, transcendentals=0),
    )(y, group, w_merge)
    if not packed:
        above, below = by_side("row", *swapped(gx_near[:reach], gx_far, "row"))
        grad_tokens, g_qkv, g_out, g_merge, g_gain, g_scale = plain_sums(
            (rows, cols, width), *sums, small, d_merged.reshape(groups, depth), gx, above, below
        )
    else:
        near, far = swapped(gx_near, gx_far, "row")
        send, *kept = sums
        block = shape((per, 4 * width + 2 * feats + LANES), BF)
        *blocks, own, own_group, small = pl.pallas_call(
            core_sum_kernel,
            out_shape=(block, block, block)
            + (shape((per, 4 * width), F32), shape((per, 2 * feats), BF), shape((8, LANES), F32)),
            in_specs=vmem(5),
            out_specs=tuple(vmem(6)),
            scratch_shapes=[pltpu.VMEM((n_row // 2,) + block.shape, BF)],
            compiler_params=less,
            cost_estimate=pl.CostEstimate(flops=5 * 10**9, bytes_accessed=10**6, transcendentals=0),
        )(swap(send, "row", 1), *kept, small, near)
        got = [swap(blocks[step - 1], "row", 2 * step) for step in (3, 2, 1)]
        lanes = 4 * width // n_col + feats // per * (depth // n_col) + LANES
        *slots, grad = pl.pallas_call(
            functools.partial(row_sum_kernel, (rows, cols, width, n_col)),
            out_shape=tuple([shape((per, lanes), BF)] * n_col)
            + (shape((rows * cols, width), F32),),
            in_specs=vmem(10),
            out_specs=tuple(vmem(n_col + 1)),
            scratch_shapes=[pltpu.VMEM((n_col, per, lanes), BF)],
            compiler_params=less,
        )(own, own_group, small, *got, dm_all, gx, near, far)
        got = [slots[0]]
        got += [swap(slots[step], "col", step) for step in (3, 2, 1)]
        g_qkv, g_out, g_merge, g_gain, g_scale, grad_tokens = pl.pallas_call(
            functools.partial(col_sum_kernel, (rows, cols, width)),
            out_shape=(
                shape((per, 3 * width // n_col), F32),
                shape((per, width // n_col), F32),
                shape((feats, depth // n_col), F32),
                shape((1, width), F32),
                shape((heads,), F32),
                shape((rows, cols, width), BF),
            ),
            in_specs=vmem(5),
            out_specs=tuple(vmem(4)) + (pl.BlockSpec(memory_space=pltpu.SMEM), vmem(1)[0]),
            compiler_params=less,
        )(*got, grad)
    return (
        skip_out,
        merged,
        grad_tokens,
        g_qkv,
        g_out,
        g_merge,
        g_gain.reshape(width),
        g_scale[:heads],
    )


def solution(mesh):
    block = P("row", "col", None)
    return jax.shard_map(
        on_device,
        mesh=mesh,
        in_specs=(block, P(), P(), P(), P(), P(), block, block),
        out_specs=(block, block, block, P("row", "col"), P("row", "col"), P("row", "col"), P(), P()),
        check_vma=False,
    )
```

```python
import functools
import jax
import jax.numpy as jnp
from jax import lax
from jax.experimental import pallas as pl
from jax.experimental.pallas import tpu as pltpu
from jax.sharding import PartitionSpec as P

RADIUS = 3
IMG_MAX = 512
EPS = 1e-06
EDGE = 4
SIDE = 8
LANES = 128
BF = jnp.bfloat16
F32 = jnp.float32


def mm(a, b):
    return lax.dot_general(a, b, (((1,), (0,)), ((), ())), preferred_element_type=F32)


def mm_t(a, b):
    return lax.dot_general(a, b, (((1,), (1,)), ((), ())), preferred_element_type=F32)


def split_two(value):
    high = value.astype(BF)
    return (high, (value - high.astype(F32)).astype(BF))


def by_side(axis, near, far):
    even = lax.rem(lax.axis_index(axis), 2) == 0
    return (jnp.where(even, far, near), jnp.where(even, near, far))


def first_kernel(ones_ref, parity_ref):
    width = ones_ref.shape[0]
    head_dim = width // (parity_ref.shape[0] // 2)
    same_head = lax.broadcasted_iota(jnp.int32, (width, width), 0) // head_dim == (
        lax.broadcasted_iota(jnp.int32, (width, width), 1) // head_dim
    )
    ones_ref[...] = jnp.where(same_head, 1.0, 0.0).astype(BF)
    half = (parity_ref.shape[0] // 2, parity_ref.shape[1])
    parts = [
        jnp.where(lax.rem(lax.axis_index(axis), 2) == 0, jnp.ones(half, F32), jnp.zeros(half, F32))
        for axis in ("row", "col")
    ]
    parity_ref[...] = jnp.concatenate(parts, axis=0)


def edge_kernel(edges_ref, near_ref, far_ref, edge_near_ref, edge_far_ref):
    rows, cols, width = near_ref.shape
    up, down = by_side("row", near_ref[...].astype(F32), far_ref[...].astype(F32))
    up = up[rows - RADIUS :]
    down = down[:RADIUS]
    halo = []
    for at in (0, cols - EDGE):
        parts = [part[:, at : at + EDGE].reshape(RADIUS * EDGE, width) for part in (up, down)]
        halo.append(jnp.concatenate(parts, axis=0))
    far, near = by_side("col", halo[1], halo[0])
    for out_ref, own_at, part in ((edge_near_ref, 0, near), (edge_far_ref, rows * EDGE, far)):
        own = edges_ref[own_at : own_at + rows * EDGE].astype(F32)
        size = RADIUS * EDGE
        out_ref[...] = jnp.concatenate([part[:size], own, part[size:]], axis=0).astype(BF)


def pair_kernel(parity_ref, dm_ref, dm_near_ref, dm_pair_ref):
    size = dm_pair_ref.shape[0] // 2
    own, near = [ref[...].reshape(size, -1).astype(F32) for ref in (dm_ref, dm_near_ref)]
    even = parity_ref[0:1, 0:1] > 0.5
    pair = [jnp.where(even, own, near), jnp.where(even, near, own)]
    dm_pair_ref[...] = jnp.concatenate(pair, axis=0).astype(BF)


def in_order(axis, own, partner):
    even = lax.rem(lax.axis_index(axis), 2) == 0
    return (jnp.where(even, own, partner), jnp.where(even, partner, own))


def head_sum(value, ones_ref):
    high, low = split_two(value)
    return mm(high, ones_ref[...]) + mm(low, ones_ref[...])


def own_kernel(
    ones_ref,
    parity_ref,
    scale_ref,
    tok_ref,
    dm_ref,
    dskip_ref,
    gain_ref,
    wqkv_ref,
    wout_ref,
    wmerge_ref,
    edges_ref,
    rows_ref,
    q_norm_ref,
    q_unit_ref,
    dy_ref,
    d_attn_ref,
    dscr,
):
    rows, cols, width = tok_ref.shape
    tokens = rows * cols
    tok = tok_ref[...].astype(F32)
    left = tok[:, :EDGE].reshape(rows * EDGE, width)
    right = tok[:, cols - EDGE :].reshape(rows * EDGE, width)
    heads = scale_ref.shape[1]
    even = parity_ref[heads : heads + 1, 0:1] > 0.5
    near, far = (jnp.where(even, right, left), jnp.where(even, left, right))
    edges_ref[...] = jnp.concatenate([near, far], axis=0).astype(BF)
    lane = lax.broadcasted_iota(jnp.int32, (1, width), 1)
    scale_row = jnp.zeros((1, width), F32)
    for h in range(heads):
        scale_row = jnp.where(lane // (width // heads) == h, scale_ref[:, h : h + 1], scale_row)
    blank = jnp.zeros((6, width), F32)
    rows_ref[...] = jnp.concatenate([gain_ref[...], scale_row, blank], axis=0)
    x = tok.reshape(tokens, width)
    inverse = lax.rsqrt(jnp.mean(x * x, axis=1, keepdims=True) + EPS)
    normed = (x * inverse * gain_ref[...]).astype(BF)
    query = mm(normed, wqkv_ref[:, :width])
    q_norm = lax.rsqrt(head_sum(query * query, ones_ref) + EPS)
    q_norm_ref[...] = q_norm
    q_unit_ref[...] = query * q_norm
    group_wide = cols // 2
    d_in = mm_t(dm_ref[...].reshape(-1, dm_ref.shape[2]), wmerge_ref[...])
    for i in range(rows // 2):
        for pr in range(2):
            for pc in range(2):
                for part in range(width // LANES):
                    at = (2 * pr + pc) * width + part * LANES
                    dscr[part, 2 * i + pr, pl.ds(pc, group_wide, stride=2), :] = d_in[
                        i * group_wide : (i + 1) * group_wide, at : at + LANES
                    ]
    d_group = jnp.concatenate(
        [dscr[part].reshape(tokens, LANES) for part in range(width // LANES)], axis=1
    )
    d_y = dskip_ref[...].reshape(tokens, width).astype(F32) + d_group
    dy_ref[...] = d_y
    d_attn_ref[...] = mm_t(d_y.astype(BF), wout_ref[...]).astype(BF)


def layer_kernel(
    sizes,
    ones_ref,
    tok_ref,
    row_near_ref,
    row_far_ref,
    col_near_ref,
    col_far_ref,
    rows_ref,
    q_norm_ref,
    q_unit_ref,
    dy_ref,
    d_attn_ref,
    wqkv_ref,
    wout_ref,
    x_ref,
    y_ref,
    d_query_ref,
    d_kv_ref,
    grad_out_ref,
    group_ref,
    scale_part_ref,
    yscr,
):
    rows, cols, width, heads, n_row, n_col = sizes
    head_dim = width // heads
    wide = cols + 2 * SIDE
    ext_rows = rows + 2 * RADIUS
    tokens = rows * cols
    image_rows = min(IMG_MAX, rows * n_row)
    row_start = lax.axis_index("row") * rows
    col_index = lax.axis_index("col")
    col_start = col_index * cols
    first = row_start // image_rows * image_rows

    lane = lax.broadcasted_iota(jnp.int32, (1, width), 1)
    def blocks(value):
        zero = jnp.zeros_like(value)
        kept = [jnp.where(lane // head_dim == h, value, zero) for h in range(heads)]
        return jnp.concatenate(kept, axis=0).astype(BF)

    gain = rows_ref[0:1]
    scale_row = rows_ref[1:2]
    up, down = by_side("row", row_near_ref[...].astype(F32), row_far_ref[...].astype(F32))
    left, right = by_side("col", col_near_ref[...].astype(F32), col_far_ref[...].astype(F32))
    own = tok_ref[...].astype(F32)
    blank = jnp.zeros((SIDE - EDGE, width), F32)
    pieces = []
    for i in range(ext_rows):
        if i < RADIUS:
            row = up[rows - RADIUS + i]
        elif i < RADIUS + rows:
            row = own[i - RADIUS]
        else:
            row = down[i - RADIUS - rows]
        edge = slice(i * EDGE, (i + 1) * EDGE)
        pieces += [blank, left[edge], row, right[edge], blank]
    x = jnp.concatenate(pieces, axis=0)
    x_ref[...] = x
    inverse = lax.rsqrt(jnp.mean(x * x, axis=1, keepdims=True) + EPS)
    unit = x * inverse
    normed32 = (unit * gain).astype(BF).astype(F32)
    normed = normed32.astype(BF)
    x_own = inner_tokens(x, rows, cols)
    kv = mm(normed, wqkv_ref[:, width:])
    key_raw = kv[:, :width]
    k_norm = lax.rsqrt(head_sum(key_raw * key_raw, ones_ref) + EPS)
    k_unit = key_raw * k_norm
    keys = k_unit.astype(BF)
    values = kv[:, width:].astype(BF)
    q_norm = q_norm_ref[...]
    q_unit = q_unit_ref[...]
    q_hat = (q_unit * scale_row).astype(BF).astype(F32)
    d_y = dy_ref[...]
    dy_b = d_y.astype(BF)
    d_attn = d_attn_ref[...].astype(F32)

    index = lax.broadcasted_iota(jnp.int32, (1, tokens), 1)
    q_row = jnp.zeros_like(index)
    for i in range(1, rows):
        q_row = q_row + (index >= i * cols).astype(jnp.int32)
    q_col = index - q_row * cols
    key_col = lax.broadcasted_iota(jnp.int32, (wide, tokens), 0) - SIDE
    near = (key_col - q_col <= RADIUS) & (key_col - q_col >= -RADIUS)
    near = near & (key_col + col_start >= 0) & (key_col + col_start < cols * n_col)
    near = jnp.where(near, 1.0, 0.0)
    parts = []
    for i in range(-RADIUS, rows + RADIUS):
        ok = (q_row - i <= RADIUS) & (q_row - i >= -RADIUS)
        ok = ok & (row_start + i >= first) & (row_start + i < first + image_rows)
        parts.append(near * jnp.where(ok, 1.0, 0.0))
    allowed = jnp.concatenate([jnp.concatenate(parts, axis=0)] * heads, axis=1)
    q_blocks = blocks(q_hat)
    g_blocks = blocks(d_attn)
    expo = jnp.exp(mm_t(keys, q_blocks)) * allowed
    prob = expo * (1.0 / jnp.sum(expo, axis=0, keepdims=True))
    weights = prob.astype(BF)
    d_w = mm_t(values, g_blocks)
    delta = jnp.sum(d_w * prob, axis=0, keepdims=True)
    d_s = (prob * (d_w - delta)).astype(BF)
    values_t = values.astype(F32).T.astype(BF)
    keys_t = keys.astype(F32).T.astype(BF)
    attn_t = []
    d_qhat_t = []
    for h in range(heads):
        feats = slice(h * head_dim, (h + 1) * head_dim)
        lanes = slice(h * tokens, (h + 1) * tokens)
        attn_t.append(mm(values_t[feats], weights[:, lanes]))
        d_qhat_t.append(mm(keys_t[feats], d_s[:, lanes]))
    attn_t = jnp.concatenate(attn_t, axis=0)
    d_qhat = jnp.concatenate(d_qhat_t, axis=0).T
    d_k = mm(d_s, q_blocks)
    d_v = mm(weights, g_blocks)

    attn = attn_t.T.astype(BF)
    y = (x_own + mm(attn, wout_ref[...])).astype(BF)
    y_ref[...] = y
    y32 = y.astype(F32)
    for part in range(width // LANES):
        yscr[part] = y32[:, part * LANES : (part + 1) * LANES].reshape(rows, cols, LANES)
    lines = []
    for i in range(rows // 2):
        pieces = []
        for pr in range(2):
            for pc in range(2):
                for part in range(width // LANES):
                    pieces.append(yscr[part, 2 * i + pr, pl.ds(pc, cols // 2, stride=2), :])
        lines.append(jnp.concatenate(pieces, axis=1))
    group = jnp.concatenate(lines, axis=0).astype(BF)
    group_ref[...] = group
    grad_out_ref[...] = mm(attn_t.astype(BF), dy_b)

    scale_part_ref[...] = jnp.broadcast_to(
        jnp.sum(q_unit * d_qhat, axis=0, keepdims=True), scale_part_ref.shape
    )
    g_unit = d_qhat * scale_row
    d_query_ref[...] = (q_norm * (g_unit - q_unit * head_sum(q_unit * g_unit, ones_ref))).astype(BF)
    d_key = k_norm * (d_k - k_unit * head_sum(k_unit * d_k, ones_ref))
    d_kv_ref[...] = jnp.concatenate([d_key, d_v], axis=1).astype(BF)


def inner_tokens(value, rows, cols):
    wide = cols + 2 * SIDE
    pieces = []
    for i in range(RADIUS, RADIUS + rows):
        pieces.append(value[i * wide + SIDE : i * wide + SIDE + cols])
    return jnp.concatenate(pieces, axis=0)


def output_kernel(y_ref, group_ref, wmerge_ref, skip_ref, merged_ref):
    skip_ref[...] = y_ref[...].reshape(skip_ref.shape)
    merged = mm(group_ref[...], wmerge_ref[...])
    merged_ref[...] = merged.astype(BF).reshape(merged_ref.shape)


def weights_kernel(
    sizes, x_ref, d_query_ref, d_kv_ref, grad_out_ref, group_ref, rows_ref, *refs
):
    rows, cols, width, n_row, n_dm = sizes
    dm_refs, dm_all_ref, sum_refs = (refs[:n_dm], refs[n_dm], refs[n_dm + 1 :])
    dm_all_ref[...] = jnp.concatenate([ref[...] for ref in dm_refs[::-1]], axis=0)
    x = x_ref[...]
    inverse = lax.rsqrt(jnp.mean(x * x, axis=1, keepdims=True) + EPS)
    normed32 = (x * inverse * rows_ref[0:1]).astype(BF).astype(F32)
    grad_q = mm(inner_tokens(normed32, rows, cols).T.astype(BF), d_query_ref[...])
    grad_kv = mm(normed32.T.astype(BF), d_kv_ref[...])
    sums = jnp.concatenate([grad_q, grad_kv, grad_out_ref[...]], axis=1)
    group = group_ref[...]
    if len(sum_refs) == 2:
        sum_refs[0][...] = sums.astype(BF)
        sum_refs[1][...] = group
        return
    send_ref, keep_ref, keep_group_ref = sum_refs
    per = width // n_row
    feats = 4 * width // n_row
    group = group.astype(F32)
    even = lax.rem(lax.axis_index("row"), 2) == 0
    for q in range(n_row // 2):
        parts = []
        for value, axis, size in ((sums, 0, per), (group, 1, feats)):
            first = lax.slice_in_dim(value, 2 * q * size, (2 * q + 1) * size, axis=axis)
            second = lax.slice_in_dim(value, (2 * q + 1) * size, (2 * q + 2) * size, axis=axis)
            parts.append((jnp.where(even, first, second), jnp.where(even, second, first)))
        (keep_ref[q], sums_send), (keep_group, group_send) = parts
        keep_group_ref[q] = keep_group.astype(BF)
        send_ref[q] = jnp.concatenate([sums_send, group_send], axis=1).astype(BF)


def norm_kernel(
    sizes, x_ref, d_query_ref, d_kv_ref, scale_part_ref, rows_ref, dy_ref, wqkv_ref, *refs
):
    rows, cols, width, heads = sizes
    gx_ref, gx_near_ref, gx_far_ref, small_ref = refs
    head_dim = width // heads
    wide = cols + 2 * SIDE
    ext_rows = rows + 2 * RADIUS
    gain = rows_ref[0:1]
    lane = lax.broadcasted_iota(jnp.int32, (1, width), 1)
    x = x_ref[...]
    inverse = lax.rsqrt(jnp.mean(x * x, axis=1, keepdims=True) + EPS)
    unit = x * inverse
    d_y = dy_ref[...]
    from_q = mm_t(d_query_ref[...], wqkv_ref[:, :width])
    d_normed = mm_t(d_kv_ref[...], wqkv_ref[:, width:])
    pieces = []
    side = jnp.zeros((SIDE, width), F32)
    for i in range(ext_rows):
        if RADIUS <= i < RADIUS + rows:
            at = (i - RADIUS) * cols
            pieces += [side, from_q[at : at + cols], side]
        else:
            pieces.append(jnp.zeros((wide, width), F32))
    d_normed = d_normed + jnp.concatenate(pieces, axis=0)
    gain_part = jnp.sum(unit * d_normed, axis=0, keepdims=True)
    scaled = gain * d_normed
    mean = jnp.mean(x * scaled, axis=1, keepdims=True)
    g_x = inverse * scaled - x * (inverse * inverse * inverse) * mean

    def rim(first_row):
        parts = []
        for i in range(first_row, first_row + RADIUS):
            parts.append(g_x[i * wide : (i + 1) * wide][SIDE - EDGE : wide - SIDE + EDGE])
        return jnp.concatenate(parts, axis=0)

    far, near = by_side("row", rim(RADIUS + rows), rim(0))
    pieces = []
    for i in range(rows):
        at = (RADIUS + i) * wide
        middle = g_x[at + SIDE : at + SIDE + cols] + d_y[i * cols : (i + 1) * cols]
        pieces += [g_x[at : at + SIDE], middle, g_x[at + SIDE + cols : at + wide]]
    gx_ref[...] = jnp.concatenate(pieces, axis=0)
    scale_part = scale_part_ref[0:1]
    scale_lane = lax.broadcasted_iota(jnp.int32, (1, LANES), 1)
    scale_sums = jnp.zeros((1, LANES), F32)
    for h in range(heads):
        of_head = jnp.sum(jnp.where(lane // head_dim == h, scale_part, 0.0), axis=1, keepdims=True)
        scale_sums = jnp.where(scale_lane == h, of_head, scale_sums)
    small = [gain_part[:, i * LANES : (i + 1) * LANES] for i in range(width // LANES)] + [scale_sums]
    small = jnp.concatenate(small + [jnp.zeros((8 - len(small), LANES), F32)], axis=0)
    small_ref[...] = small
    high = small.astype(BF).astype(F32)
    small = jnp.concatenate([high, small - high], axis=1)
    gx_near_ref[...] = jnp.concatenate([near, small], axis=0).astype(BF)
    gx_far_ref[...] = far.astype(BF)


def small_rows(small, rows):
    high = small.astype(BF).astype(F32)
    blank = jnp.zeros((rows - 16, LANES), F32)
    return jnp.concatenate([high, small - high, blank], axis=0).astype(BF)


def wide_rim(ref, cols):
    size = cols + 2 * EDGE
    blank = jnp.zeros((SIDE - EDGE, ref.shape[1]), F32)
    pieces = []
    for i in range(RADIUS):
        pieces += [blank, ref[...][i * size : (i + 1) * size].astype(F32), blank]
    return jnp.concatenate(pieces, axis=0)


def small_value(rows):
    value = rows.astype(F32)
    return value[:8] + value[8:16]


def core_sum_kernel(got_ref, keep_ref, keep_group_ref, small_ref, near_ref, *refs):
    *out_refs, own_ref, own_group_ref, small_sum_ref, blocks_ref = refs
    chips, per, width = keep_ref.shape
    feats = keep_group_ref.shape[2]
    end = width + feats
    got_small = near_ref[...].astype(F32)[near_ref.shape[0] - 8 :]
    got_small = got_small[:, :LANES] + got_small[:, LANES:]
    small = small_value(small_rows(small_ref[...], per)) + got_small
    small_sum_ref[...] = small
    small = small_rows(small, per)
    chip = lax.axis_index("row") // 2
    own_ref[...] = keep_ref[chip] + got_ref[chip, :, :width].astype(F32)
    for q in range(chips):
        sums = keep_ref[q] + got_ref[q, :, :width].astype(F32)
        kept = keep_group_ref[q].astype(F32)
        first, second = in_order("row", kept, got_ref[q, :, width:end].astype(F32))
        block = jnp.concatenate([sums, first, second], axis=1).astype(BF)
        blocks_ref[q] = jnp.concatenate([block, small], axis=1)
    own_group_ref[...] = blocks_ref[chip, :, width : width + 2 * feats]
    for step, out_ref in enumerate(out_refs, 1):
        out_ref[...] = blocks_ref[partner(chip, step)]


def row_sum_kernel(sizes, *refs):
    rows, cols, width, n_col = sizes
    own_ref, own_group_ref, small_ref, *refs = refs
    got_refs, dm_ref, gx_ref, near_ref, *refs = (refs[:3], *refs[3:])
    *out_refs, gx_sum_ref, slots_ref = refs
    wide = cols + 2 * SIDE
    blank = jnp.zeros(((rows - RADIUS) * wide, width), F32)
    near = wide_rim(near_ref, cols)
    above, below = (jnp.concatenate([near, blank], axis=0), jnp.concatenate([blank, near], axis=0))
    even = lax.rem(lax.axis_index("row"), 2) == 0
    gx_sum_ref[...] = gx_ref[...] + jnp.where(even, below, above)
    per = own_ref.shape[0]
    feats = own_group_ref.shape[1] // 2
    at = 4 * width
    end = at + 2 * feats

    def summed(first, part):
        fourth, third, second = [part(ref) for ref in got_refs]
        return (first + second) + (third + fourth)

    sums = summed(own_ref[...], lambda ref: ref[:, :at].astype(F32))
    small = small_value(small_rows(small_ref[...], per))
    small = summed(small, lambda ref: small_value(ref[:, end:]))
    group = [own_group_ref[...]] + [ref[:, at:end] for ref in got_refs[::-1]]
    group = [part[:, i * feats : (i + 1) * feats].astype(F32) for part in group for i in range(2)]
    group = jnp.concatenate(group, axis=0)
    merge = mm(group.T.astype(BF), dm_ref[...])
    high = small.astype(BF).astype(F32)
    small = jnp.concatenate([high[:4], (small - high)[:4], jnp.zeros((per - 8, LANES), F32)], axis=0)
    col = lax.axis_index("col")
    third = 3 * width // n_col
    fourth = width // n_col
    depth = merge.shape[1] // n_col
    for slot in range(n_col):
        parts = [
            sums[:, slot * third : (slot + 1) * third],
            sums[:, 3 * width + slot * fourth : 3 * width + (slot + 1) * fourth],
        ]
        for k in range(feats // per):
            parts.append(merge[k * per : (k + 1) * per, slot * depth : (slot + 1) * depth])
        parts.append(small)
        slots_ref[slot] = jnp.concatenate(parts, axis=1).astype(BF)
    for step, out_ref in enumerate(out_refs):
        out_ref[...] = slots_ref[partner(col, step)]


def partner(index, step):
    if step == 0:
        return index
    low = lax.rem(index, 2)
    if step == 1:
        return index + 1 - 2 * low
    if step == 2:
        return lax.rem(index + 2, 4)
    return 3 - index


def side_kernel(sizes, gx_ref, far_ref, grad_ref, side_near_ref, side_far_ref):
    rows, cols, width = sizes
    wide = cols + 2 * SIDE
    blank = jnp.zeros(((rows - RADIUS) * wide, width), F32)
    far = wide_rim(far_ref, cols)
    above, below = (jnp.concatenate([far, blank], axis=0), jnp.concatenate([blank, far], axis=0))
    even = lax.rem(lax.axis_index("row"), 2) == 0
    g_x = gx_ref[...] + jnp.where(even, above, below)
    grad = []
    left = []
    right = []
    for i in range(rows):
        spot = i * wide + SIDE
        grad.append(g_x[spot : spot + cols])
        left.append(g_x[spot - SIDE : spot][SIDE - EDGE :])
        right.append(g_x[spot + cols : spot + cols + SIDE][:EDGE])
    grad_ref[...] = jnp.concatenate(grad, axis=0)
    left, right = [jnp.concatenate(part, axis=0) for part in (left, right)]
    far, near = by_side("col", right, left)
    side_near_ref[...] = near.astype(BF)
    side_far_ref[...] = far.astype(BF)


def col_sum_kernel(
    sizes, a_ref, d_ref, c_ref, b_ref, grad_ref, near_ref, far_ref, gqkv_ref, gout_ref, gmerge_ref, ggain_ref, gscale_ref, gtok_ref
):
    rows, cols, width = sizes
    per, lanes = a_ref.shape
    third = gqkv_ref.shape[1]
    fourth = gout_ref.shape[1]
    depth = gmerge_ref.shape[1]
    end = lanes - LANES

    def summed(part):
        first, second, third, fourth = [part(ref) for ref in (a_ref, b_ref, c_ref, d_ref)]
        return (first + second) + (third + fourth)

    def tiny(ref):
        value = ref[:, end:].astype(F32)
        return value[:4] + value[4:8]

    total = summed(lambda ref: ref[:, :end].astype(F32))
    small = summed(tiny)
    gqkv_ref[...] = total[:, :third]
    gout_ref[...] = total[:, third : third + fourth]
    for k in range(gmerge_ref.shape[0] // per):
        at = third + fourth + k * depth
        gmerge_ref[k * per : (k + 1) * per] = total[:, at : at + depth]
    ggain_ref[...] = jnp.concatenate([small[i : i + 1] for i in range(width // LANES)], axis=1)
    for h in range(gscale_ref.shape[0]):
        gscale_ref[h] = small[width // LANES, h]
    col = lax.axis_index("col")

    left, right = by_side("col", near_ref[...].astype(F32), far_ref[...].astype(F32))
    left = jnp.where(col > 0, left, 0.0)
    right = jnp.where(col < lax.axis_size("col") - 1, right, 0.0)
    blank = jnp.zeros((cols - 2 * EDGE, width), F32)
    pieces = []
    for i in range(rows):
        edge = slice(i * EDGE, (i + 1) * EDGE)
        pieces += [left[edge], blank, right[edge]]
    grad = grad_ref[...] + jnp.concatenate(pieces, axis=0)
    gtok_ref[...] = grad.astype(BF).reshape(rows, cols, width)


def plain_sums(sizes, sums, group, small, dm, gx, above, below):
    rows, cols, width = sizes
    wide = cols + 2 * SIDE
    sums = sums.astype(F32)
    merge = jnp.dot(group.T, dm, preferred_element_type=F32)
    outs = []
    for part in (sums[:, : 3 * width], sums[:, 3 * width :], merge):
        part = lax.psum_scatter(part, "row", scatter_dimension=0, tiled=True)
        outs.append(lax.psum_scatter(part, "col", scatter_dimension=1, tiled=True))
    small = lax.psum(small, ("row", "col"))
    gx = gx.reshape(rows, wide, width)
    trim = slice(SIDE - EDGE, wide - SIDE + EDGE)
    gx = gx.at[:RADIUS, trim].add(above.astype(F32).reshape(RADIUS, -1, width))
    gx = gx.at[rows - RADIUS :, trim].add(below.astype(F32).reshape(RADIUS, -1, width))
    from_right = shifted(gx[:, :SIDE].astype(BF), "col", -1).astype(F32)
    from_left = shifted(gx[:, SIDE + cols :].astype(BF), "col", 1).astype(F32)
    grad = gx[:, SIDE : SIDE + cols].at[:, :SIDE].add(from_left)
    grad = grad.at[:, cols - SIDE :].add(from_right)
    return (grad.astype(BF), *outs, small[: width // LANES].reshape(1, width), small[width // LANES])


def shifted(value, axis, step):
    count = lax.axis_size(axis)
    pairs = [(i, i + step) for i in range(count) if 0 <= i + step < count]
    return lax.ppermute(value, axis, pairs)


def swapped(near, far, axis):
    count = lax.axis_size(axis)
    first = [(i, i + 1) for i in range(0, count, 2)]
    second = [(i, (i + 1) % count) for i in range(1, count, 2)]
    first = first + [(j, i) for i, j in first]
    second = second + [(j, i) for i, j in second]
    return (lax.ppermute(near, axis, first), lax.ppermute(far, axis, second))


def swap(value, axis, step):
    count = lax.axis_size(axis)
    return lax.ppermute(value, axis, [(i, i ^ step) for i in range(count)])


def vmem(count):
    return [pl.BlockSpec(memory_space=pltpu.VMEM)] * count


def on_device(tokens, gain, w_qkv, head_scale, w_out, w_merge, d_merged, d_skip):
    rows, cols, width = tokens.shape
    heads = head_scale.shape[0]
    n_row, n_col = (lax.axis_size("row"), lax.axis_size("col"))
    g_rows, g_cols, depth = d_merged.shape
    groups = g_rows * g_cols
    wide = cols + 2 * SIDE
    ext_rows = rows + 2 * RADIUS
    shape = jax.ShapeDtypeStruct
    params = pltpu.CompilerParams(vmem_limit_bytes=24 * 1024 * 1024)
    less = pltpu.CompilerParams(vmem_limit_bytes=8 * 1024 * 1024)
    row_near, row_far = swapped(tokens, tokens, "row")
    edge = shape((ext_rows * EDGE, width), BF)
    ones, parity = pl.pallas_call(
        first_kernel,
        out_shape=(shape((width, width), BF), shape((2 * heads, LANES), F32)),
        out_specs=tuple(vmem(2)),
        compiler_params=less,
        cost_estimate=pl.CostEstimate(flops=10**10, bytes_accessed=10**5, transcendentals=0),
    )()
    dm_pair = pl.pallas_call(
        pair_kernel,
        out_shape=shape((2 * groups, depth), BF),
        in_specs=vmem(3),
        out_specs=vmem(1)[0],
        compiler_params=less,
    )(parity, d_merged, swap(d_merged, "row", 1))
    dm_pairs = [swap(dm_pair, "row", 2 * step) for step in (3, 2, 1)] + [dm_pair]
    gathered = len(dm_pairs) * 2 * groups
    tile = shape((rows * cols, width), F32)
    half = shape((rows * cols, width), BF)
    edges, two_rows, q_norm, q_unit, d_y, d_attn = pl.pallas_call(
        own_kernel,
        out_shape=(shape((2 * rows * EDGE, width), BF), shape((8, width), F32), tile, tile, tile, half),
        in_specs=vmem(10),
        out_specs=tuple(vmem(6)),
        scratch_shapes=[pltpu.VMEM((width // LANES, rows, cols, LANES), F32)],
        compiler_params=params,
        cost_estimate=pl.CostEstimate(flops=10**9, bytes_accessed=10**6, transcendentals=0),
    )(
        ones,
        parity,
        head_scale.reshape(1, heads),
        tokens,
        d_merged,
        d_skip,
        gain.reshape(1, width),
        w_qkv,
        w_out,
        w_merge,
    )
    edge_near, edge_far = pl.pallas_call(
        edge_kernel,
        out_shape=(edge, edge),
        in_specs=vmem(3),
        out_specs=tuple(vmem(2)),
        compiler_params=less,
    )(edges, row_near, row_far)
    col_near, col_far = swapped(edge_near, edge_far, "col")

    per = width // n_row
    feats = 4 * width // n_row
    packed = per % 16 == 0 and feats % LANES == 0 and groups == per
    packed = packed and width // LANES < 4 and depth // n_col == LANES and n_col == 4 and n_row == 8
    if packed:
        sum_shapes = (
            shape((n_row // 2, per, 4 * width + feats), BF),
            shape((n_row // 2, per, 4 * width), F32),
            shape((n_row // 2, per, feats), BF),
        )
    else:
        sum_shapes = (
            shape((width, 4 * width), BF),
            shape((groups, 4 * width), BF),
        )
    sizes = (rows, cols, width, heads, n_row, n_col)
    reach = RADIUS * (cols + 2 * EDGE)
    tall = ext_rows * wide
    x, y, d_query, d_kv, grad_out, group, scale_part = pl.pallas_call(
        functools.partial(layer_kernel, sizes),
        out_shape=(
            shape((tall, width), F32),
            half,
            half,
            shape((tall, 2 * width), BF),
            shape((width, width), F32),
            shape((groups, 4 * width), BF),
            shape((8, width), F32),
        ),
        in_specs=vmem(13),
        out_specs=tuple(vmem(7)),
        scratch_shapes=[pltpu.VMEM((width // LANES, rows, cols, LANES), F32)],
        compiler_params=params,
        cost_estimate=pl.CostEstimate(flops=4 * 10**9, bytes_accessed=10**6, transcendentals=0),
    )(
        ones,
        tokens,
        row_near,
        row_far,
        col_near,
        col_far,
        two_rows,
        q_norm,
        q_unit,
        d_y,
        d_attn,
        w_qkv,
        w_out,
    )
    dm_all, *sums = pl.pallas_call(
        functools.partial(weights_kernel, (rows, cols, width, n_row, len(dm_pairs))),
        out_shape=(shape((gathered, depth), BF),) + sum_shapes,
        in_specs=vmem(6 + len(dm_pairs)),
        out_specs=tuple(vmem(1 + len(sum_shapes))),
        compiler_params=params,
        cost_estimate=pl.CostEstimate(flops=10**9, bytes_accessed=10**6, transcendentals=0),
    )(x, d_query, d_kv, grad_out, group, two_rows, *dm_pairs)
    gx, gx_near, gx_far, small = pl.pallas_call(
        functools.partial(norm_kernel, (rows, cols, width, heads)),
        out_shape=(
            shape((rows * wide, width), F32),
            shape((reach + 8, width), BF),
            shape((reach, width), BF),
            shape((8, LANES), F32),
        ),
        in_specs=vmem(7),
        out_specs=tuple(vmem(4)),
        compiler_params=params,
        cost_estimate=pl.CostEstimate(flops=5 * 10**8, bytes_accessed=10**6, transcendentals=0),
    )(x, d_query, d_kv, scale_part, two_rows, d_y, w_qkv)
    skip_out, merged = pl.pallas_call(
        output_kernel,
        out_shape=(shape((rows, cols, width), BF), shape((g_rows, g_cols, depth), BF)),
        in_specs=vmem(3),
        out_specs=tuple(vmem(2)),
        compiler_params=less,
        cost_estimate=pl.CostEstimate(flops=10**9, bytes_accessed=10**6, transcendentals=0),
    )(y, group, w_merge)
    if not packed:
        above, below = by_side("row", *swapped(gx_near[:reach], gx_far, "row"))
        grad_tokens, g_qkv, g_out, g_merge, g_gain, g_scale = plain_sums(
            (rows, cols, width), *sums, small, d_merged.reshape(groups, depth), gx, above, below
        )
    else:
        near, far = swapped(gx_near, gx_far, "row")
        send, *kept = sums
        block = shape((per, 4 * width + 2 * feats + LANES), BF)
        *blocks, own, own_group, small = pl.pallas_call(
            core_sum_kernel,
            out_shape=(block, block, block)
            + (shape((per, 4 * width), F32), shape((per, 2 * feats), BF), shape((8, LANES), F32)),
            in_specs=vmem(5),
            out_specs=tuple(vmem(6)),
            scratch_shapes=[pltpu.VMEM((n_row // 2,) + block.shape, BF)],
            compiler_params=less,
            cost_estimate=pl.CostEstimate(flops=5 * 10**9, bytes_accessed=10**6, transcendentals=0),
        )(swap(send, "row", 1), *kept, small, near)
        got = [swap(blocks[step - 1], "row", 2 * step) for step in (3, 2, 1)]
        lanes = 4 * width // n_col + feats // per * (depth // n_col) + LANES
        *slots, gx = pl.pallas_call(
            functools.partial(row_sum_kernel, (rows, cols, width, n_col)),
            out_shape=tuple([shape((per, lanes), BF)] * n_col) + (shape(gx.shape, F32),),
            in_specs=vmem(9),
            out_specs=tuple(vmem(n_col + 1)),
            scratch_shapes=[pltpu.VMEM((n_col, per, lanes), BF)],
            compiler_params=less,
        )(own, own_group, small, *got, dm_all, gx, near)
        side = shape((rows * EDGE, width), BF)
        grad, *sides = pl.pallas_call(
            functools.partial(side_kernel, (rows, cols, width)),
            out_shape=(shape((rows * cols, width), F32), side, side),
            in_specs=vmem(2),
            out_specs=tuple(vmem(3)),
            compiler_params=less,
        )(gx, far)
        sides = swapped(*sides, "col")
        got = [slots[0]]
        got += [swap(slots[step], "col", step) for step in (3, 2, 1)]
        g_qkv, g_out, g_merge, g_gain, g_scale, grad_tokens = pl.pallas_call(
            functools.partial(col_sum_kernel, (rows, cols, width)),
            out_shape=(
                shape((per, 3 * width // n_col), F32),
                shape((per, width // n_col), F32),
                shape((feats, depth // n_col), F32),
                shape((1, width), F32),
                shape((heads,), F32),
                shape((rows, cols, width), BF),
            ),
            in_specs=vmem(7),
            out_specs=tuple(vmem(4)) + (pl.BlockSpec(memory_space=pltpu.SMEM), vmem(1)[0]),
            compiler_params=less,
        )(*got, grad, *sides)
    return (
        skip_out,
        merged,
        grad_tokens,
        g_qkv,
        g_out,
        g_merge,
        g_gain.reshape(width),
        g_scale[:heads],
    )


def solution(mesh):
    block = P("row", "col", None)
    return jax.shard_map(
        on_device,
        mesh=mesh,
        in_specs=(block, P(), P(), P(), P(), P(), block, block),
        out_specs=(block, block, block, P("row", "col"), P("row", "col"), P("row", "col"), P(), P()),
        check_vma=False,
    )
```

```python
import functools
import jax
import jax.numpy as jnp
from jax import lax
from jax.experimental import pallas as pl
from jax.experimental.pallas import tpu as pltpu
from jax.sharding import PartitionSpec as P

RADIUS = 3
IMG_MAX = 512
EPS = 1e-06
EDGE = 4
SIDE = 8
LANES = 128
BF = jnp.bfloat16
F32 = jnp.float32


def mm(a, b):
    return lax.dot_general(a, b, (((1,), (0,)), ((), ())), preferred_element_type=F32)


def mm_t(a, b):
    return lax.dot_general(a, b, (((1,), (1,)), ((), ())), preferred_element_type=F32)


def split_two(value):
    high = value.astype(BF)
    return (high, (value - high.astype(F32)).astype(BF))


def by_side(axis, near, far):
    even = lax.rem(lax.axis_index(axis), 2) == 0
    return (jnp.where(even, far, near), jnp.where(even, near, far))


def first_kernel(ones_ref, parity_ref):
    width = ones_ref.shape[0]
    head_dim = width // (parity_ref.shape[0] // 2)
    same_head = lax.broadcasted_iota(jnp.int32, (width, width), 0) // head_dim == (
        lax.broadcasted_iota(jnp.int32, (width, width), 1) // head_dim
    )
    ones_ref[...] = jnp.where(same_head, 1.0, 0.0).astype(BF)
    half = (parity_ref.shape[0] // 2, parity_ref.shape[1])
    parts = [
        jnp.where(lax.rem(lax.axis_index(axis), 2) == 0, jnp.ones(half, F32), jnp.zeros(half, F32))
        for axis in ("row", "col")
    ]
    parity_ref[...] = jnp.concatenate(parts, axis=0)


def edge_kernel(edges_ref, near_ref, far_ref, edge_near_ref, edge_far_ref):
    rows, cols, width = near_ref.shape
    up, down = by_side("row", near_ref[...].astype(F32), far_ref[...].astype(F32))
    up = up[rows - RADIUS :]
    down = down[:RADIUS]
    halo = []
    for at in (0, cols - EDGE):
        parts = [part[:, at : at + EDGE].reshape(RADIUS * EDGE, width) for part in (up, down)]
        halo.append(jnp.concatenate(parts, axis=0))
    far, near = by_side("col", halo[1], halo[0])
    for out_ref, own_at, part in ((edge_near_ref, 0, near), (edge_far_ref, rows * EDGE, far)):
        own = edges_ref[own_at : own_at + rows * EDGE].astype(F32)
        size = RADIUS * EDGE
        out_ref[...] = jnp.concatenate([part[:size], own, part[size:]], axis=0).astype(BF)


def in_order(axis, own, partner):
    even = lax.rem(lax.axis_index(axis), 2) == 0
    return (jnp.where(even, own, partner), jnp.where(even, partner, own))


def head_sum(value, ones_ref):
    high, low = split_two(value)
    return mm(high, ones_ref[...]) + mm(low, ones_ref[...])


def own_kernel(
    ones_ref,
    parity_ref,
    scale_ref,
    tok_ref,
    dm_ref,
    dskip_ref,
    gain_ref,
    wqkv_ref,
    wout_ref,
    wmerge_ref,
    edges_ref,
    rows_ref,
    q_norm_ref,
    q_unit_ref,
    dy_ref,
    d_attn_ref,
    dscr,
):
    rows, cols, width = tok_ref.shape
    tokens = rows * cols
    tok = tok_ref[...].astype(F32)
    left = tok[:, :EDGE].reshape(rows * EDGE, width)
    right = tok[:, cols - EDGE :].reshape(rows * EDGE, width)
    heads = scale_ref.shape[1]
    even = parity_ref[heads : heads + 1, 0:1] > 0.5
    near, far = (jnp.where(even, right, left), jnp.where(even, left, right))
    edges_ref[...] = jnp.concatenate([near, far], axis=0).astype(BF)
    lane = lax.broadcasted_iota(jnp.int32, (1, width), 1)
    scale_row = jnp.zeros((1, width), F32)
    for h in range(heads):
        scale_row = jnp.where(lane // (width // heads) == h, scale_ref[:, h : h + 1], scale_row)
    blank = jnp.zeros((6, width), F32)
    rows_ref[...] = jnp.concatenate([gain_ref[...], scale_row, blank], axis=0)
    x = tok.reshape(tokens, width)
    inverse = lax.rsqrt(jnp.mean(x * x, axis=1, keepdims=True) + EPS)
    normed = (x * inverse * gain_ref[...]).astype(BF)
    query = mm(normed, wqkv_ref[:, :width])
    q_norm = lax.rsqrt(head_sum(query * query, ones_ref) + EPS)
    q_norm_ref[...] = q_norm
    q_unit_ref[...] = query * q_norm
    group_wide = cols // 2
    d_in = mm_t(dm_ref[...].reshape(-1, dm_ref.shape[2]), wmerge_ref[...])
    for i in range(rows // 2):
        for pr in range(2):
            for pc in range(2):
                for part in range(width // LANES):
                    at = (2 * pr + pc) * width + part * LANES
                    dscr[part, 2 * i + pr, pl.ds(pc, group_wide, stride=2), :] = d_in[
                        i * group_wide : (i + 1) * group_wide, at : at + LANES
                    ]
    d_group = jnp.concatenate(
        [dscr[part].reshape(tokens, LANES) for part in range(width // LANES)], axis=1
    )
    d_y = dskip_ref[...].reshape(tokens, width).astype(F32) + d_group
    dy_ref[...] = d_y
    d_attn_ref[...] = mm_t(d_y.astype(BF), wout_ref[...]).astype(BF)


def layer_kernel(
    sizes,
    ones_ref,
    tok_ref,
    row_near_ref,
    row_far_ref,
    col_near_ref,
    col_far_ref,
    rows_ref,
    q_norm_ref,
    q_unit_ref,
    dy_ref,
    d_attn_ref,
    wqkv_ref,
    wout_ref,
    x_ref,
    y_ref,
    d_query_ref,
    d_kv_ref,
    grad_out_ref,
    group_ref,
    scale_part_ref,
    yscr,
):
    rows, cols, width, heads, n_row, n_col = sizes
    head_dim = width // heads
    wide = cols + 2 * SIDE
    ext_rows = rows + 2 * RADIUS
    tokens = rows * cols
    image_rows = min(IMG_MAX, rows * n_row)
    row_start = lax.axis_index("row") * rows
    col_index = lax.axis_index("col")
    col_start = col_index * cols
    first = row_start // image_rows * image_rows

    lane = lax.broadcasted_iota(jnp.int32, (1, width), 1)
    def blocks(value):
        zero = jnp.zeros_like(value)
        kept = [jnp.where(lane // head_dim == h, value, zero) for h in range(heads)]
        return jnp.concatenate(kept, axis=0).astype(BF)

    gain = rows_ref[0:1]
    scale_row = rows_ref[1:2]
    up, down = by_side("row", row_near_ref[...].astype(F32), row_far_ref[...].astype(F32))
    left, right = by_side("col", col_near_ref[...].astype(F32), col_far_ref[...].astype(F32))
    own = tok_ref[...].astype(F32)
    blank = jnp.zeros((SIDE - EDGE, width), F32)
    pieces = []
    for i in range(ext_rows):
        if i < RADIUS:
            row = up[rows - RADIUS + i]
        elif i < RADIUS + rows:
            row = own[i - RADIUS]
        else:
            row = down[i - RADIUS - rows]
        edge = slice(i * EDGE, (i + 1) * EDGE)
        pieces += [blank, left[edge], row, right[edge], blank]
    x = jnp.concatenate(pieces, axis=0)
    x_ref[...] = x
    inverse = lax.rsqrt(jnp.mean(x * x, axis=1, keepdims=True) + EPS)
    unit = x * inverse
    normed32 = (unit * gain).astype(BF).astype(F32)
    normed = normed32.astype(BF)
    x_own = inner_tokens(x, rows, cols)
    kv = mm(normed, wqkv_ref[:, width:])
    key_raw = kv[:, :width]
    k_norm = lax.rsqrt(head_sum(key_raw * key_raw, ones_ref) + EPS)
    k_unit = key_raw * k_norm
    keys = k_unit.astype(BF)
    values = kv[:, width:].astype(BF)
    q_norm = q_norm_ref[...]
    q_unit = q_unit_ref[...]
    q_hat = (q_unit * scale_row).astype(BF).astype(F32)
    d_y = dy_ref[...]
    dy_b = d_y.astype(BF)
    d_attn = d_attn_ref[...].astype(F32)

    index = lax.broadcasted_iota(jnp.int32, (1, tokens), 1)
    q_row = jnp.zeros_like(index)
    for i in range(1, rows):
        q_row = q_row + (index >= i * cols).astype(jnp.int32)
    q_col = index - q_row * cols
    key_col = lax.broadcasted_iota(jnp.int32, (wide, tokens), 0) - SIDE
    near = (key_col - q_col <= RADIUS) & (key_col - q_col >= -RADIUS)
    near = near & (key_col + col_start >= 0) & (key_col + col_start < cols * n_col)
    near = jnp.where(near, 1.0, 0.0)
    parts = []
    for i in range(-RADIUS, rows + RADIUS):
        ok = (q_row - i <= RADIUS) & (q_row - i >= -RADIUS)
        ok = ok & (row_start + i >= first) & (row_start + i < first + image_rows)
        parts.append(near * jnp.where(ok, 1.0, 0.0))
    allowed = jnp.concatenate([jnp.concatenate(parts, axis=0)] * heads, axis=1)
    q_blocks = blocks(q_hat)
    g_blocks = blocks(d_attn)
    expo = jnp.exp(mm_t(keys, q_blocks)) * allowed
    prob = expo * (1.0 / jnp.sum(expo, axis=0, keepdims=True))
    weights = prob.astype(BF)
    d_w = mm_t(values, g_blocks)
    delta = jnp.sum(d_w * prob, axis=0, keepdims=True)
    d_s = (prob * (d_w - delta)).astype(BF)
    values_t = values.astype(F32).T.astype(BF)
    keys_t = keys.astype(F32).T.astype(BF)
    attn_t = []
    d_qhat_t = []
    for h in range(heads):
        feats = slice(h * head_dim, (h + 1) * head_dim)
        lanes = slice(h * tokens, (h + 1) * tokens)
        attn_t.append(mm(values_t[feats], weights[:, lanes]))
        d_qhat_t.append(mm(keys_t[feats], d_s[:, lanes]))
    attn_t = jnp.concatenate(attn_t, axis=0)
    d_qhat = jnp.concatenate(d_qhat_t, axis=0).T
    d_k = mm(d_s, q_blocks)
    d_v = mm(weights, g_blocks)

    attn = attn_t.T.astype(BF)
    y = (x_own + mm(attn, wout_ref[...])).astype(BF)
    y_ref[...] = y
    y32 = y.astype(F32)
    for part in range(width // LANES):
        yscr[part] = y32[:, part * LANES : (part + 1) * LANES].reshape(rows, cols, LANES)
    lines = []
    for i in range(rows // 2):
        pieces = []
        for pr in range(2):
            for pc in range(2):
                for part in range(width // LANES):
                    pieces.append(yscr[part, 2 * i + pr, pl.ds(pc, cols // 2, stride=2), :])
        lines.append(jnp.concatenate(pieces, axis=1))
    group = jnp.concatenate(lines, axis=0).astype(BF)
    group_ref[...] = group
    grad_out_ref[...] = mm(attn_t.astype(BF), dy_b)

    scale_part_ref[...] = jnp.broadcast_to(
        jnp.sum(q_unit * d_qhat, axis=0, keepdims=True), scale_part_ref.shape
    )
    g_unit = d_qhat * scale_row
    d_query_ref[...] = (q_norm * (g_unit - q_unit * head_sum(q_unit * g_unit, ones_ref))).astype(BF)
    d_key = k_norm * (d_k - k_unit * head_sum(k_unit * d_k, ones_ref))
    d_kv_ref[...] = jnp.concatenate([d_key, d_v], axis=1).astype(BF)


def inner_tokens(value, rows, cols):
    wide = cols + 2 * SIDE
    pieces = []
    for i in range(RADIUS, RADIUS + rows):
        pieces.append(value[i * wide + SIDE : i * wide + SIDE + cols])
    return jnp.concatenate(pieces, axis=0)


def output_kernel(y_ref, group_ref, wmerge_ref, skip_ref, merged_ref):
    skip_ref[...] = y_ref[...].reshape(skip_ref.shape)
    merged = mm(group_ref[...], wmerge_ref[...])
    merged_ref[...] = merged.astype(BF).reshape(merged_ref.shape)


def weights_kernel(
    sizes, x_ref, d_query_ref, d_kv_ref, grad_out_ref, group_ref, rows_ref, *refs
):
    rows, cols, width, n_row, n_dm = sizes
    dm_refs, dm_all_ref, sum_refs = (refs[:n_dm], refs[n_dm], refs[n_dm + 1 :])
    size = dm_all_ref.shape[0] // n_dm
    dm = [ref[...].reshape(size, dm_all_ref.shape[1]) for ref in dm_refs]
    dm_all_ref[...] = jnp.concatenate(dm[::-1], axis=0)
    x = x_ref[...]
    inverse = lax.rsqrt(jnp.mean(x * x, axis=1, keepdims=True) + EPS)
    normed32 = (x * inverse * rows_ref[0:1]).astype(BF).astype(F32)
    grad_q = mm(inner_tokens(normed32, rows, cols).T.astype(BF), d_query_ref[...])
    grad_kv = mm(normed32.T.astype(BF), d_kv_ref[...])
    sums = jnp.concatenate([grad_q, grad_kv, grad_out_ref[...]], axis=1)
    group = group_ref[...]
    if len(sum_refs) == 2:
        sum_refs[0][...] = sums.astype(BF)
        sum_refs[1][...] = group
        return
    send_ref, keep_ref, keep_group_ref = sum_refs
    per = width // n_row
    feats = 4 * width // n_row
    group = group.astype(F32)
    even = lax.rem(lax.axis_index("row"), 2) == 0
    for q in range(n_row // 2):
        parts = []
        for value, axis, size in ((sums, 0, per), (group, 1, feats)):
            first = lax.slice_in_dim(value, 2 * q * size, (2 * q + 1) * size, axis=axis)
            second = lax.slice_in_dim(value, (2 * q + 1) * size, (2 * q + 2) * size, axis=axis)
            parts.append((jnp.where(even, first, second), jnp.where(even, second, first)))
        (keep_ref[q], sums_send), (keep_group, group_send) = parts
        keep_group_ref[q] = keep_group.astype(BF)
        send_ref[q] = jnp.concatenate([sums_send, group_send], axis=1).astype(BF)


def norm_kernel(
    sizes, x_ref, d_query_ref, d_kv_ref, scale_part_ref, rows_ref, dy_ref, wqkv_ref, *refs
):
    rows, cols, width, heads = sizes
    gx_ref, side_near_ref, side_far_ref, small_ref = refs
    head_dim = width // heads
    wide = cols + 2 * SIDE
    ext_rows = rows + 2 * RADIUS
    gain = rows_ref[0:1]
    lane = lax.broadcasted_iota(jnp.int32, (1, width), 1)
    x = x_ref[...]
    inverse = lax.rsqrt(jnp.mean(x * x, axis=1, keepdims=True) + EPS)
    unit = x * inverse
    d_y = dy_ref[...]
    from_q = mm_t(d_query_ref[...], wqkv_ref[:, :width])
    d_normed = mm_t(d_kv_ref[...], wqkv_ref[:, width:])
    pieces = []
    side = jnp.zeros((SIDE, width), F32)
    for i in range(ext_rows):
        if RADIUS <= i < RADIUS + rows:
            at = (i - RADIUS) * cols
            pieces += [side, from_q[at : at + cols], side]
        else:
            pieces.append(jnp.zeros((wide, width), F32))
    d_normed = d_normed + jnp.concatenate(pieces, axis=0)
    gain_part = jnp.sum(unit * d_normed, axis=0, keepdims=True)
    scaled = gain * d_normed
    mean = jnp.mean(x * scaled, axis=1, keepdims=True)
    g_x = inverse * scaled - x * (inverse * inverse * inverse) * mean

    pieces = []
    left = []
    right = []
    for i in range(ext_rows):
        row = g_x[i * wide : (i + 1) * wide]
        middle = row[SIDE : SIDE + cols]
        if RADIUS <= i < RADIUS + rows:
            middle = middle + d_y[(i - RADIUS) * cols : (i - RADIUS + 1) * cols]
        pieces.append(middle)
        left.append(row[:SIDE][SIDE - EDGE :])
        right.append(row[SIDE + cols :][:EDGE])
    gx_ref[...] = jnp.concatenate(pieces, axis=0)
    left, right = [jnp.concatenate(part, axis=0) for part in (left, right)]
    far, near = by_side("col", right, left)
    side_near_ref[...] = near.astype(BF)
    side_far_ref[...] = far.astype(BF)
    scale_part = scale_part_ref[0:1]
    scale_lane = lax.broadcasted_iota(jnp.int32, (1, LANES), 1)
    scale_sums = jnp.zeros((1, LANES), F32)
    for h in range(heads):
        of_head = jnp.sum(jnp.where(lane // head_dim == h, scale_part, 0.0), axis=1, keepdims=True)
        scale_sums = jnp.where(scale_lane == h, of_head, scale_sums)
    small = [gain_part[:, i * LANES : (i + 1) * LANES] for i in range(width // LANES)] + [scale_sums]
    small = jnp.concatenate(small + [jnp.zeros((8 - len(small), LANES), F32)], axis=0)
    small_ref[...] = small


def small_rows(small):
    high = small.astype(BF).astype(F32)
    return jnp.concatenate([high[:4], (small - high)[:4]], axis=0)


def small_value(rows):
    value = rows.astype(BF).astype(F32)
    return value[:4] + value[4:]


def stacked(value):
    return jnp.concatenate(
        [value[:, i : i + LANES] for i in range(0, value.shape[1], LANES)], axis=0
    )


def unstacked(value, rows):
    return jnp.concatenate([value[i : i + rows] for i in range(0, value.shape[0], rows)], axis=1)


def core_sum_kernel(got_ref, keep_ref, keep_group_ref, small_ref, small_near_ref, *refs):
    *out_refs, own_ref, own_group_ref, small_sum_ref, blocks_ref = refs
    chips, per, width = keep_ref.shape
    feats = keep_group_ref.shape[2]
    small = small_ref[...] + small_near_ref[...]
    small_sum_ref[...] = small
    small = small_rows(small)
    chip = lax.axis_index("row") // 2
    own_ref[...] = keep_ref[chip] + got_ref[chip, :, :width].astype(F32)
    for q in range(chips):
        sums = keep_ref[q] + got_ref[q, :, :width].astype(F32)
        kept = keep_group_ref[q].astype(F32)
        first, second = in_order("row", kept, got_ref[q, :, width:].astype(F32))
        block = [stacked(sums), first, second, small]
        blocks_ref[q] = jnp.concatenate(block, axis=0).astype(BF)
    size = width // LANES * per
    own_group_ref[...] = blocks_ref[chip][size : size + 2 * per]
    for step, out_ref in enumerate(out_refs, 1):
        out_ref[...] = blocks_ref[partner(chip, step)]


def row_sum_kernel(sizes, *refs):
    rows, cols, width, n_col = sizes
    own_ref, own_group_ref, small_ref, *refs = refs
    got_refs, dm_ref, dm_near_ref, gx_ref, *refs = (refs[:3], *refs[3:])
    *out_refs, gx_sum_ref, slots_ref = refs
    gx_sum_ref[...] = gx_ref[...]
    per = own_ref.shape[0]
    feats = own_group_ref.shape[1]
    size = 4 * width // LANES * per

    def summed(first, part):
        fourth, third, second = [part(ref[...].astype(F32)) for ref in got_refs]
        return (first + second) + (third + fourth)

    sums = summed(stacked(own_ref[...]), lambda value: value[:size])
    sums = unstacked(sums, per)
    small = summed(small_value(small_rows(small_ref[...])), lambda value: small_value(value[size + 2 * per :]))
    group = [own_group_ref[...].astype(F32)]
    group += [ref[...].astype(F32)[size : size + 2 * per] for ref in got_refs[::-1]]
    group = [part[i * per : (i + 1) * per] for i in range(2) for part in group]
    group = jnp.concatenate(group, axis=0)
    own, near = (dm_ref[...].astype(F32), dm_near_ref[...].astype(F32))
    dm = jnp.concatenate(in_order("row", own, near), axis=0).astype(BF)
    merge = mm(group.T.astype(BF), dm)
    small = small_rows(small)
    col = lax.axis_index("col")
    third = 3 * width // n_col
    fourth = width // n_col
    depth = merge.shape[1] // n_col
    for slot in range(n_col):
        parts = [
            sums[:, slot * third : (slot + 1) * third],
            sums[:, 3 * width + slot * fourth : 3 * width + (slot + 1) * fourth],
        ]
        parts = [stacked(jnp.concatenate(parts, axis=1))]
        parts += [merge[:, slot * depth : (slot + 1) * depth], small]
        slots_ref[slot] = jnp.concatenate(parts, axis=0).astype(BF)
    for step, out_ref in enumerate(out_refs):
        out_ref[...] = slots_ref[partner(col, step)]


def partner(index, step):
    if step == 0:
        return index
    low = lax.rem(index, 2)
    if step == 1:
        return index + 1 - 2 * low
    if step == 2:
        return lax.rem(index + 2, 4)
    return 3 - index


def side_kernel(sizes, gx_ref, near_ref, far_ref, grad_ref, row_near_ref, row_far_ref):
    rows, cols, width = sizes
    ends = lax.axis_index("col")
    left, right = by_side("col", near_ref[...].astype(F32), far_ref[...].astype(F32))
    left = jnp.where(ends > 0, left, 0.0)
    right = jnp.where(ends < lax.axis_size("col") - 1, right, 0.0)
    blank = jnp.zeros((cols - 2 * EDGE, width), F32)
    pieces = []
    for i in range(rows + 2 * RADIUS):
        edge = slice(i * EDGE, (i + 1) * EDGE)
        pieces += [left[edge], blank, right[edge]]
    g_x = gx_ref[...] + jnp.concatenate(pieces, axis=0)
    reach = RADIUS * cols
    far, near = by_side("row", g_x[reach + rows * cols :], g_x[:reach])
    grad_ref[...] = g_x[reach : reach + rows * cols]
    row_near_ref[...] = near.astype(BF)
    row_far_ref[...] = far.astype(BF)


def col_sum_kernel(
    sizes,
    a_ref,
    d_ref,
    c_ref,
    b_ref,
    grad_ref,
    near_ref,
    far_ref,
    gqkv_ref,
    gout_ref,
    gmerge_ref,
    ggain_ref,
    gscale_ref,
    gtok_ref,
):
    rows, cols, width = sizes
    per, third = gqkv_ref.shape
    size = a_ref.shape[0] - 8

    def summed(part):
        first, second, third, fourth = [
            part(ref[...].astype(F32)) for ref in (a_ref, b_ref, c_ref, d_ref)
        ]
        return (first + second) + (third + fourth)

    total = summed(lambda value: value[:size])
    small = summed(lambda value: small_value(value[size:]))
    merge_at = size - gmerge_ref.shape[0]
    sums = unstacked(total[:merge_at], per)
    gqkv_ref[...] = sums[:, :third]
    gout_ref[...] = sums[:, third:]
    gmerge_ref[...] = total[merge_at:]
    ggain_ref[...] = jnp.concatenate([small[i : i + 1] for i in range(width // LANES)], axis=1)
    for h in range(gscale_ref.shape[0]):
        gscale_ref[h] = small[width // LANES, h]
    blank = jnp.zeros(((rows - RADIUS) * cols, width), F32)
    above, below = by_side("row", near_ref[...].astype(F32), far_ref[...].astype(F32))
    grad = grad_ref[...] + jnp.concatenate([above, blank], axis=0)
    grad = grad + jnp.concatenate([blank, below], axis=0)
    gtok_ref[...] = grad.astype(BF).reshape(rows, cols, width)


def plain_sums(width, sums, group, small, dm):
    sums = sums.astype(F32)
    merge = jnp.dot(group.T, dm, preferred_element_type=F32)
    outs = []
    for part in (sums[:, : 3 * width], sums[:, 3 * width :], merge):
        part = lax.psum_scatter(part, "row", scatter_dimension=0, tiled=True)
        outs.append(lax.psum_scatter(part, "col", scatter_dimension=1, tiled=True))
    small = lax.psum(small, ("row", "col"))
    return (*outs, small[: width // LANES].reshape(1, width), small[width // LANES])


def add_rows(grad, near, far, rows, cols):
    above, below = by_side("row", near.astype(F32), far.astype(F32))
    size = RADIUS * cols
    grad = grad.at[:size].add(above).at[rows * cols - size :].add(below)
    return grad.astype(BF).reshape(rows, cols, -1)


def swapped(near, far, axis):
    count = lax.axis_size(axis)
    first = [(i, i + 1) for i in range(0, count, 2)]
    second = [(i, (i + 1) % count) for i in range(1, count, 2)]
    first = first + [(j, i) for i, j in first]
    second = second + [(j, i) for i, j in second]
    return (lax.ppermute(near, axis, first), lax.ppermute(far, axis, second))


def swap(value, axis, step):
    count = lax.axis_size(axis)
    return lax.ppermute(value, axis, [(i, i ^ step) for i in range(count)])


def vmem(count):
    return [pl.BlockSpec(memory_space=pltpu.VMEM)] * count


def on_device(tokens, gain, w_qkv, head_scale, w_out, w_merge, d_merged, d_skip):
    rows, cols, width = tokens.shape
    heads = head_scale.shape[0]
    n_row, n_col = (lax.axis_size("row"), lax.axis_size("col"))
    g_rows, g_cols, depth = d_merged.shape
    groups = g_rows * g_cols
    wide = cols + 2 * SIDE
    ext_rows = rows + 2 * RADIUS
    shape = jax.ShapeDtypeStruct
    params = pltpu.CompilerParams(vmem_limit_bytes=24 * 1024 * 1024)
    less = pltpu.CompilerParams(vmem_limit_bytes=8 * 1024 * 1024)
    row_near, row_far = swapped(tokens, tokens, "row")
    edge = shape((ext_rows * EDGE, width), BF)
    ones, parity = pl.pallas_call(
        first_kernel,
        out_shape=(shape((width, width), BF), shape((2 * heads, LANES), F32)),
        out_specs=tuple(vmem(2)),
        compiler_params=less,
        cost_estimate=pl.CostEstimate(flops=10**10, bytes_accessed=10**5, transcendentals=0),
    )()
    dm = d_merged.reshape(groups, depth)
    dms = [swap(dm, "row", 2 * step) for step in (3, 2, 1)] + [dm]
    tile = shape((rows * cols, width), F32)
    half = shape((rows * cols, width), BF)
    edges, two_rows, q_norm, q_unit, d_y, d_attn = pl.pallas_call(
        own_kernel,
        out_shape=(shape((2 * rows * EDGE, width), BF), shape((8, width), F32), tile, tile, tile, half),
        in_specs=vmem(10),
        out_specs=tuple(vmem(6)),
        scratch_shapes=[pltpu.VMEM((width // LANES, rows, cols, LANES), F32)],
        compiler_params=params,
        cost_estimate=pl.CostEstimate(flops=10**9, bytes_accessed=10**6, transcendentals=0),
    )(
        ones,
        parity,
        head_scale.reshape(1, heads),
        tokens,
        d_merged,
        d_skip,
        gain.reshape(1, width),
        w_qkv,
        w_out,
        w_merge,
    )
    edge_near, edge_far = pl.pallas_call(
        edge_kernel,
        out_shape=(edge, edge),
        in_specs=vmem(3),
        out_specs=tuple(vmem(2)),
        compiler_params=less,
    )(edges, row_near, row_far)
    col_near, col_far = swapped(edge_near, edge_far, "col")

    per = width // n_row
    feats = 4 * width // n_row
    packed = per % 16 == 0 and feats % LANES == 0 and groups == per
    packed = packed and width // LANES < 4 and feats == LANES and depth // n_col == LANES and n_col == 4 and n_row == 8
    if packed:
        sum_shapes = (
            shape((n_row // 2, per, 4 * width + feats), BF),
            shape((n_row // 2, per, 4 * width), F32),
            shape((n_row // 2, per, feats), BF),
        )
    else:
        sum_shapes = (
            shape((width, 4 * width), BF),
            shape((groups, 4 * width), BF),
        )
    sizes = (rows, cols, width, heads, n_row, n_col)
    tall = ext_rows * wide
    x, y, d_query, d_kv, grad_out, group, scale_part = pl.pallas_call(
        functools.partial(layer_kernel, sizes),
        out_shape=(
            shape((tall, width), F32),
            half,
            half,
            shape((tall, 2 * width), BF),
            shape((width, width), F32),
            shape((groups, 4 * width), BF),
            shape((8, width), F32),
        ),
        in_specs=vmem(13),
        out_specs=tuple(vmem(7)),
        scratch_shapes=[pltpu.VMEM((width // LANES, rows, cols, LANES), F32)],
        compiler_params=params,
        cost_estimate=pl.CostEstimate(flops=4 * 10**9, bytes_accessed=10**6, transcendentals=0),
    )(
        ones,
        tokens,
        row_near,
        row_far,
        col_near,
        col_far,
        two_rows,
        q_norm,
        q_unit,
        d_y,
        d_attn,
        w_qkv,
        w_out,
    )
    dm_core, *sums = pl.pallas_call(
        functools.partial(weights_kernel, (rows, cols, width, n_row, len(dms))),
        out_shape=(shape((len(dms) * groups, depth), BF),) + sum_shapes,
        in_specs=vmem(6 + len(dms)),
        out_specs=tuple(vmem(1 + len(sum_shapes))),
        compiler_params=params,
        cost_estimate=pl.CostEstimate(flops=10**9, bytes_accessed=10**6, transcendentals=0),
    )(x, d_query, d_kv, grad_out, group, two_rows, *dms)
    gx, *sides = pl.pallas_call(
        functools.partial(norm_kernel, (rows, cols, width, heads)),
        out_shape=(shape((ext_rows * cols, width), F32), edge, edge, shape((8, LANES), F32)),
        in_specs=vmem(7),
        out_specs=tuple(vmem(4)),
        compiler_params=params,
        cost_estimate=pl.CostEstimate(flops=5 * 10**8, bytes_accessed=10**6, transcendentals=0),
    )(x, d_query, d_kv, scale_part, two_rows, d_y, w_qkv)
    *sides, small = sides
    sides = swapped(*sides, "col")
    skip_out, merged = pl.pallas_call(
        output_kernel,
        out_shape=(shape((rows, cols, width), BF), shape((g_rows, g_cols, depth), BF)),
        in_specs=vmem(3),
        out_specs=tuple(vmem(2)),
        compiler_params=less,
        cost_estimate=pl.CostEstimate(flops=10**9, bytes_accessed=10**6, transcendentals=0),
    )(y, group, w_merge)
    reach = shape((RADIUS * cols, width), BF)
    side_call = pl.pallas_call(
        functools.partial(side_kernel, (rows, cols, width)),
        out_shape=(tile, reach, reach),
        in_specs=vmem(3),
        out_specs=tuple(vmem(3)),
        compiler_params=less,
    )
    if not packed:
        grad, *rims = side_call(gx, *sides)
        grad_tokens = add_rows(grad, *swapped(*rims, "row"), rows, cols)
        g_qkv, g_out, g_merge, g_gain, g_scale = plain_sums(width, *sums, small, dm)
    else:
        send, *kept = sums
        block = shape((4 * width // LANES * per + 2 * per + 8, LANES), BF)
        *blocks, own, own_group, small = pl.pallas_call(
            core_sum_kernel,
            out_shape=(block, block, block)
            + (shape((per, 4 * width), F32), shape((2 * per, LANES), BF), shape((8, LANES), F32)),
            in_specs=vmem(5),
            out_specs=tuple(vmem(6)),
            scratch_shapes=[pltpu.VMEM((n_row // 2,) + block.shape, BF)],
            compiler_params=less,
            cost_estimate=pl.CostEstimate(flops=5 * 10**9, bytes_accessed=10**6, transcendentals=0),
        )(swap(send, "row", 1), *kept, small, swap(small, "row", 1))
        got = [swap(blocks[step - 1], "row", 2 * step) for step in (3, 2, 1)]
        slot = shape((4 * width // n_col // LANES * per + feats + 8, LANES), BF)
        *slots, gx = pl.pallas_call(
            functools.partial(row_sum_kernel, (rows, cols, width, n_col)),
            out_shape=(slot,) * n_col + (shape(gx.shape, F32),),
            in_specs=vmem(9),
            out_specs=tuple(vmem(n_col + 1)),
            scratch_shapes=[pltpu.VMEM((n_col,) + slot.shape, BF)],
            compiler_params=less,
        )(own, own_group, small, *got, dm_core, swap(dm_core, "row", 1), gx)
        got = [slots[0]] + [swap(slots[step], "col", step) for step in (3, 2, 1)]
        grad, *rims = side_call(gx, *sides)
        rims = swapped(*rims, "row")
        g_qkv, g_out, g_merge, g_gain, g_scale, grad_tokens = pl.pallas_call(
            functools.partial(col_sum_kernel, (rows, cols, width)),
            out_shape=(
                shape((per, 3 * width // n_col), F32),
                shape((per, width // n_col), F32),
                shape((feats, depth // n_col), F32),
                shape((1, width), F32),
                shape((heads,), F32),
                shape((rows, cols, width), BF),
            ),
            in_specs=vmem(7),
            out_specs=tuple(vmem(4)) + (pl.BlockSpec(memory_space=pltpu.SMEM), vmem(1)[0]),
            compiler_params=less,
        )(*got, grad, *rims)
    return (
        skip_out,
        merged,
        grad_tokens,
        g_qkv,
        g_out,
        g_merge,
        g_gain.reshape(width),
        g_scale[:heads],
    )


def solution(mesh):
    block = P("row", "col", None)
    return jax.shard_map(
        on_device,
        mesh=mesh,
        in_specs=(block, P(), P(), P(), P(), P(), block, block),
        out_specs=(block, block, block, P("row", "col"), P("row", "col"), P("row", "col"), P(), P()),
        check_vma=False,
    )
```

```python
import functools
import jax
import jax.numpy as jnp
from jax import lax
from jax.experimental import pallas as pl
from jax.experimental.pallas import tpu as pltpu
from jax.sharding import PartitionSpec as P

RADIUS = 3
IMG_MAX = 512
EPS = 1e-06
EDGE = 4
SIDE = 8
LANES = 128
BF = jnp.bfloat16
F32 = jnp.float32


def mm(a, b):
    return lax.dot_general(a, b, (((1,), (0,)), ((), ())), preferred_element_type=F32)


def mm_t(a, b):
    return lax.dot_general(a, b, (((1,), (1,)), ((), ())), preferred_element_type=F32)


def split_two(value):
    high = value.astype(BF)
    return (high, (value - high.astype(F32)).astype(BF))


def by_side(axis, near, far):
    even = lax.rem(lax.axis_index(axis), 2) == 0
    return (jnp.where(even, far, near), jnp.where(even, near, far))


def first_kernel(ones_ref, parity_ref):
    width = ones_ref.shape[0]
    head_dim = width // (parity_ref.shape[0] // 2)
    same_head = lax.broadcasted_iota(jnp.int32, (width, width), 0) // head_dim == (
        lax.broadcasted_iota(jnp.int32, (width, width), 1) // head_dim
    )
    ones_ref[...] = jnp.where(same_head, 1.0, 0.0).astype(BF)
    half = (parity_ref.shape[0] // 2, parity_ref.shape[1])
    parts = [
        jnp.where(lax.rem(lax.axis_index(axis), 2) == 0, jnp.ones(half, F32), jnp.zeros(half, F32))
        for axis in ("row", "col")
    ]
    parity_ref[...] = jnp.concatenate(parts, axis=0)


def edge_kernel(edges_ref, far_ref, near_ref, dm_ref, edge_near_ref, edge_far_ref, dm_out_ref):
    rows, cols, width = near_ref.shape
    dm_out_ref[...] = dm_ref[...]
    up, down = by_side("row", near_ref[...].astype(F32), far_ref[...].astype(F32))
    up = up[rows - RADIUS :]
    down = down[:RADIUS]
    halo = []
    for at in (0, cols - EDGE):
        parts = [part[:, at : at + EDGE].reshape(RADIUS * EDGE, width) for part in (up, down)]
        halo.append(jnp.concatenate(parts, axis=0))
    far, near = by_side("col", halo[1], halo[0])
    for out_ref, own_at, part in ((edge_near_ref, 0, near), (edge_far_ref, rows * EDGE, far)):
        own = edges_ref[own_at : own_at + rows * EDGE].astype(F32)
        size = RADIUS * EDGE
        out_ref[...] = jnp.concatenate([part[:size], own, part[size:]], axis=0).astype(BF)


def in_order(axis, own, partner):
    even = lax.rem(lax.axis_index(axis), 2) == 0
    return (jnp.where(even, own, partner), jnp.where(even, partner, own))


def head_sum(value, ones_ref):
    high, low = split_two(value)
    return mm(high, ones_ref[...]) + mm(low, ones_ref[...])


def own_kernel(
    ones_ref,
    parity_ref,
    scale_ref,
    tok_ref,
    dm_ref,
    dskip_ref,
    gain_ref,
    wqkv_ref,
    wout_ref,
    wmerge_ref,
    edges_ref,
    rows_ref,
    q_norm_ref,
    q_unit_ref,
    dy_ref,
    d_attn_ref,
    dscr,
):
    rows, cols, width = tok_ref.shape
    tokens = rows * cols
    tok = tok_ref[...].astype(F32)
    left = tok[:, :EDGE].reshape(rows * EDGE, width)
    right = tok[:, cols - EDGE :].reshape(rows * EDGE, width)
    heads = scale_ref.shape[1]
    even = parity_ref[heads : heads + 1, 0:1] > 0.5
    near, far = (jnp.where(even, right, left), jnp.where(even, left, right))
    edges_ref[...] = jnp.concatenate([near, far], axis=0).astype(BF)
    lane = lax.broadcasted_iota(jnp.int32, (1, width), 1)
    scale_row = jnp.zeros((1, width), F32)
    for h in range(heads):
        scale_row = jnp.where(lane // (width // heads) == h, scale_ref[:, h : h + 1], scale_row)
    blank = jnp.zeros((6, width), F32)
    rows_ref[...] = jnp.concatenate([gain_ref[...], scale_row, blank], axis=0)
    x = tok.reshape(tokens, width)
    inverse = lax.rsqrt(jnp.mean(x * x, axis=1, keepdims=True) + EPS)
    normed = (x * inverse * gain_ref[...]).astype(BF)
    query = mm(normed, wqkv_ref[:, :width])
    q_norm = lax.rsqrt(head_sum(query * query, ones_ref) + EPS)
    q_norm_ref[...] = q_norm
    q_unit_ref[...] = query * q_norm
    group_wide = cols // 2
    d_in = mm_t(dm_ref[...].reshape(-1, dm_ref.shape[2]), wmerge_ref[...])
    for i in range(rows // 2):
        for pr in range(2):
            for pc in range(2):
                for part in range(width // LANES):
                    at = (2 * pr + pc) * width + part * LANES
                    dscr[part, 2 * i + pr, pl.ds(pc, group_wide, stride=2), :] = d_in[
                        i * group_wide : (i + 1) * group_wide, at : at + LANES
                    ]
    d_group = jnp.concatenate(
        [dscr[part].reshape(tokens, LANES) for part in range(width // LANES)], axis=1
    )
    d_y = dskip_ref[...].reshape(tokens, width).astype(F32) + d_group
    dy_ref[...] = d_y
    d_attn_ref[...] = mm_t(d_y.astype(BF), wout_ref[...]).astype(BF)


def layer_kernel(
    sizes,
    ones_ref,
    tok_ref,
    row_far_ref,
    row_near_ref,
    col_far_ref,
    col_near_ref,
    rows_ref,
    q_norm_ref,
    q_unit_ref,
    dy_ref,
    d_attn_ref,
    wqkv_ref,
    wout_ref,
    x_ref,
    y_ref,
    d_query_ref,
    d_kv_ref,
    grad_out_ref,
    group_ref,
    scale_part_ref,
    yscr,
):
    rows, cols, width, heads, n_row, n_col = sizes
    head_dim = width // heads
    wide = cols + 2 * SIDE
    ext_rows = rows + 2 * RADIUS
    tokens = rows * cols
    image_rows = min(IMG_MAX, rows * n_row)
    row_start = lax.axis_index("row") * rows
    col_index = lax.axis_index("col")
    col_start = col_index * cols
    first = row_start // image_rows * image_rows

    lane = lax.broadcasted_iota(jnp.int32, (1, width), 1)
    def blocks(value):
        zero = jnp.zeros_like(value)
        kept = [jnp.where(lane // head_dim == h, value, zero) for h in range(heads)]
        return jnp.concatenate(kept, axis=0).astype(BF)

    gain = rows_ref[0:1]
    scale_row = rows_ref[1:2]
    up, down = by_side("row", row_near_ref[...].astype(F32), row_far_ref[...].astype(F32))
    left, right = by_side("col", col_near_ref[...].astype(F32), col_far_ref[...].astype(F32))
    own = tok_ref[...].astype(F32)
    blank = jnp.zeros((SIDE - EDGE, width), F32)
    pieces = []
    for i in range(ext_rows):
        if i < RADIUS:
            row = up[rows - RADIUS + i]
        elif i < RADIUS + rows:
            row = own[i - RADIUS]
        else:
            row = down[i - RADIUS - rows]
        edge = slice(i * EDGE, (i + 1) * EDGE)
        pieces += [blank, left[edge], row, right[edge], blank]
    x = jnp.concatenate(pieces, axis=0)
    x_ref[...] = x
    inverse = lax.rsqrt(jnp.mean(x * x, axis=1, keepdims=True) + EPS)
    unit = x * inverse
    normed32 = (unit * gain).astype(BF).astype(F32)
    normed = normed32.astype(BF)
    x_own = inner_tokens(x, rows, cols)
    kv = mm(normed, wqkv_ref[:, width:])
    key_raw = kv[:, :width]
    k_norm = lax.rsqrt(head_sum(key_raw * key_raw, ones_ref) + EPS)
    k_unit = key_raw * k_norm
    keys = k_unit.astype(BF)
    values = kv[:, width:].astype(BF)
    q_norm = q_norm_ref[...]
    q_unit = q_unit_ref[...]
    q_hat = (q_unit * scale_row).astype(BF).astype(F32)
    d_y = dy_ref[...]
    dy_b = d_y.astype(BF)
    d_attn = d_attn_ref[...].astype(F32)

    index = lax.broadcasted_iota(jnp.int32, (1, tokens), 1)
    q_row = jnp.zeros_like(index)
    for i in range(1, rows):
        q_row = q_row + (index >= i * cols).astype(jnp.int32)
    q_col = index - q_row * cols
    key_col = lax.broadcasted_iota(jnp.int32, (wide, tokens), 0) - SIDE
    near = (key_col - q_col <= RADIUS) & (key_col - q_col >= -RADIUS)
    near = near & (key_col + col_start >= 0) & (key_col + col_start < cols * n_col)
    near = jnp.where(near, 1.0, 0.0)
    parts = []
    for i in range(-RADIUS, rows + RADIUS):
        ok = (q_row - i <= RADIUS) & (q_row - i >= -RADIUS)
        ok = ok & (row_start + i >= first) & (row_start + i < first + image_rows)
        parts.append(near * jnp.where(ok, 1.0, 0.0))
    allowed = jnp.concatenate([jnp.concatenate(parts, axis=0)] * heads, axis=1)
    q_blocks = blocks(q_hat)
    g_blocks = blocks(d_attn)
    expo = jnp.exp(mm_t(keys, q_blocks)) * allowed
    prob = expo * (1.0 / jnp.sum(expo, axis=0, keepdims=True))
    weights = prob.astype(BF)
    d_w = mm_t(values, g_blocks)
    delta = jnp.sum(d_w * prob, axis=0, keepdims=True)
    d_s = (prob * (d_w - delta)).astype(BF)
    values_t = values.astype(F32).T.astype(BF)
    keys_t = keys.astype(F32).T.astype(BF)
    attn_t = []
    d_qhat_t = []
    for h in range(heads):
        feats = slice(h * head_dim, (h + 1) * head_dim)
        lanes = slice(h * tokens, (h + 1) * tokens)
        attn_t.append(mm(values_t[feats], weights[:, lanes]))
        d_qhat_t.append(mm(keys_t[feats], d_s[:, lanes]))
    attn_t = jnp.concatenate(attn_t, axis=0)
    d_qhat = jnp.concatenate(d_qhat_t, axis=0).T
    d_k = mm(d_s, q_blocks)
    d_v = mm(weights, g_blocks)

    attn = attn_t.T.astype(BF)
    y = (x_own + mm(attn, wout_ref[...])).astype(BF)
    y_ref[...] = y
    y32 = y.astype(F32)
    for part in range(width // LANES):
        yscr[part] = y32[:, part * LANES : (part + 1) * LANES].reshape(rows, cols, LANES)
    lines = []
    for i in range(rows // 2):
        pieces = []
        for pr in range(2):
            for pc in range(2):
                for part in range(width // LANES):
                    pieces.append(yscr[part, 2 * i + pr, pl.ds(pc, cols // 2, stride=2), :])
        lines.append(jnp.concatenate(pieces, axis=1))
    group = jnp.concatenate(lines, axis=0).astype(BF)
    group_ref[...] = group
    grad_out_ref[...] = mm(attn_t.astype(BF), dy_b)

    scale_part_ref[...] = jnp.broadcast_to(
        jnp.sum(q_unit * d_qhat, axis=0, keepdims=True), scale_part_ref.shape
    )
    g_unit = d_qhat * scale_row
    d_query_ref[...] = (q_norm * (g_unit - q_unit * head_sum(q_unit * g_unit, ones_ref))).astype(BF)
    d_key = k_norm * (d_k - k_unit * head_sum(k_unit * d_k, ones_ref))
    d_kv_ref[...] = jnp.concatenate([d_key, d_v], axis=1).astype(BF)


def inner_tokens(value, rows, cols):
    wide = cols + 2 * SIDE
    pieces = []
    for i in range(RADIUS, RADIUS + rows):
        pieces.append(value[i * wide + SIDE : i * wide + SIDE + cols])
    return jnp.concatenate(pieces, axis=0)


def output_kernel(y_ref, group_ref, wmerge_ref, skip_ref, merged_ref):
    skip_ref[...] = y_ref[...].reshape(skip_ref.shape)
    merged = mm(group_ref[...], wmerge_ref[...])
    merged_ref[...] = merged.astype(BF).reshape(merged_ref.shape)


def weights_kernel(
    sizes, x_ref, d_query_ref, d_kv_ref, grad_out_ref, group_ref, rows_ref, *refs
):
    rows, cols, width, n_row, n_dm = sizes
    dm_refs, dm_all_ref, sum_refs = (refs[:n_dm], refs[n_dm], refs[n_dm + 1 :])
    size = dm_all_ref.shape[0] // n_dm
    dm = [ref[...].reshape(size, dm_all_ref.shape[1]) for ref in dm_refs]
    dm_all_ref[...] = jnp.concatenate(dm[::-1], axis=0)
    x = x_ref[...]
    inverse = lax.rsqrt(jnp.mean(x * x, axis=1, keepdims=True) + EPS)
    normed32 = (x * inverse * rows_ref[0:1]).astype(BF).astype(F32)
    grad_q = mm(inner_tokens(normed32, rows, cols).T.astype(BF), d_query_ref[...])
    grad_kv = mm(normed32.T.astype(BF), d_kv_ref[...])
    sums = jnp.concatenate([grad_q, grad_kv, grad_out_ref[...]], axis=1)
    group = group_ref[...]
    if len(sum_refs) == 2:
        sum_refs[0][...] = sums.astype(BF)
        sum_refs[1][...] = group
        return
    send_ref, keep_ref, keep_group_ref = sum_refs
    per = width // n_row
    feats = 4 * width // n_row
    group = group.astype(F32)
    even = lax.rem(lax.axis_index("row"), 2) == 0
    for q in range(n_row // 2):
        parts = []
        for value, axis, size in ((sums, 0, per), (group, 1, feats)):
            first = lax.slice_in_dim(value, 2 * q * size, (2 * q + 1) * size, axis=axis)
            second = lax.slice_in_dim(value, (2 * q + 1) * size, (2 * q + 2) * size, axis=axis)
            parts.append((jnp.where(even, first, second), jnp.where(even, second, first)))
        (keep_ref[q], sums_send), (keep_group, group_send) = parts
        keep_group_ref[q] = keep_group.astype(BF)
        send_ref[q] = jnp.concatenate([sums_send, group_send], axis=1).astype(BF)


def norm_kernel(
    sizes, x_ref, d_query_ref, d_kv_ref, scale_part_ref, rows_ref, dy_ref, wqkv_ref, *refs
):
    rows, cols, width, heads = sizes
    gx_ref, side_near_ref, side_far_ref, small_ref = refs
    head_dim = width // heads
    wide = cols + 2 * SIDE
    ext_rows = rows + 2 * RADIUS
    gain = rows_ref[0:1]
    lane = lax.broadcasted_iota(jnp.int32, (1, width), 1)
    x = x_ref[...]
    inverse = lax.rsqrt(jnp.mean(x * x, axis=1, keepdims=True) + EPS)
    unit = x * inverse
    d_y = dy_ref[...]
    from_q = mm_t(d_query_ref[...], wqkv_ref[:, :width])
    d_normed = mm_t(d_kv_ref[...], wqkv_ref[:, width:])
    pieces = []
    side = jnp.zeros((SIDE, width), F32)
    for i in range(ext_rows):
        if RADIUS <= i < RADIUS + rows:
            at = (i - RADIUS) * cols
            pieces += [side, from_q[at : at + cols], side]
        else:
            pieces.append(jnp.zeros((wide, width), F32))
    d_normed = d_normed + jnp.concatenate(pieces, axis=0)
    gain_part = jnp.sum(unit * d_normed, axis=0, keepdims=True)
    scaled = gain * d_normed
    mean = jnp.mean(x * scaled, axis=1, keepdims=True)
    g_x = inverse * scaled - x * (inverse * inverse * inverse) * mean

    pieces = []
    left = []
    right = []
    for i in range(ext_rows):
        row = g_x[i * wide : (i + 1) * wide]
        middle = row[SIDE : SIDE + cols]
        if RADIUS <= i < RADIUS + rows:
            middle = middle + d_y[(i - RADIUS) * cols : (i - RADIUS + 1) * cols]
        pieces.append(middle)
        left.append(row[:SIDE][SIDE - EDGE :])
        right.append(row[SIDE + cols :][:EDGE])
    gx_ref[...] = jnp.concatenate(pieces, axis=0)
    left, right = [jnp.concatenate(part, axis=0) for part in (left, right)]
    far, near = by_side("col", right, left)
    side_near_ref[...] = near.astype(BF)
    side_far_ref[...] = far.astype(BF)
    scale_part = scale_part_ref[0:1]
    scale_lane = lax.broadcasted_iota(jnp.int32, (1, LANES), 1)
    scale_sums = jnp.zeros((1, LANES), F32)
    for h in range(heads):
        of_head = jnp.sum(jnp.where(lane // head_dim == h, scale_part, 0.0), axis=1, keepdims=True)
        scale_sums = jnp.where(scale_lane == h, of_head, scale_sums)
    small = [gain_part[:, i * LANES : (i + 1) * LANES] for i in range(width // LANES)] + [scale_sums]
    small = jnp.concatenate(small + [jnp.zeros((8 - len(small), LANES), F32)], axis=0)
    small_ref[...] = small


def small_rows(small):
    high = small.astype(BF).astype(F32)
    return jnp.concatenate([high[:4], (small - high)[:4]], axis=0)


def small_value(rows):
    value = rows.astype(BF).astype(F32)
    return value[:4] + value[4:]


def stacked(value):
    return jnp.concatenate(
        [value[:, i : i + LANES] for i in range(0, value.shape[1], LANES)], axis=0
    )


def unstacked(value, rows):
    return jnp.concatenate([value[i : i + rows] for i in range(0, value.shape[0], rows)], axis=1)


def core_sum_kernel(got_ref, keep_ref, keep_group_ref, small_ref, small_near_ref, *refs):
    *out_refs, own_ref, own_group_ref, small_sum_ref, blocks_ref = refs
    chips, per, width = keep_ref.shape
    feats = keep_group_ref.shape[2]
    small = small_ref[...] + small_near_ref[...]
    small_sum_ref[...] = small
    small = small_rows(small)
    chip = lax.axis_index("row") // 2
    own_ref[...] = keep_ref[chip] + got_ref[chip, :, :width].astype(F32)
    for q in range(chips):
        sums = keep_ref[q] + got_ref[q, :, :width].astype(F32)
        kept = keep_group_ref[q].astype(F32)
        first, second = in_order("row", kept, got_ref[q, :, width:].astype(F32))
        block = [stacked(sums), first, second, small]
        blocks_ref[q] = jnp.concatenate(block, axis=0).astype(BF)
    size = width // LANES * per
    own_group_ref[...] = blocks_ref[chip][size : size + 2 * per]
    for step, out_ref in enumerate(out_refs, 1):
        out_ref[...] = blocks_ref[partner(chip, step)]


def row_sum_kernel(sizes, *refs):
    rows, cols, width, n_col = sizes
    own_ref, own_group_ref, small_ref, *refs = refs
    got_refs, dm_ref, dm_near_ref, gx_ref, *refs = (refs[:3], *refs[3:])
    *out_refs, gx_sum_ref, slots_ref = refs
    gx_sum_ref[...] = gx_ref[...]
    per = own_ref.shape[0]
    feats = own_group_ref.shape[1]
    size = 4 * width // LANES * per

    def summed(first, part):
        fourth, third, second = [part(ref[...].astype(F32)) for ref in got_refs]
        return (first + second) + (third + fourth)

    sums = summed(stacked(own_ref[...]), lambda value: value[:size])
    sums = unstacked(sums, per)
    small = summed(small_value(small_rows(small_ref[...])), lambda value: small_value(value[size + 2 * per :]))
    group = [own_group_ref[...].astype(F32)]
    group += [ref[...].astype(F32)[size : size + 2 * per] for ref in got_refs[::-1]]
    group = [part[i * per : (i + 1) * per] for i in range(2) for part in group]
    group = jnp.concatenate(group, axis=0)
    own, near = (dm_ref[...].astype(F32), dm_near_ref[...].astype(F32))
    dm = jnp.concatenate(in_order("row", own, near), axis=0).astype(BF)
    merge = mm(group.T.astype(BF), dm)
    small = small_rows(small)
    col = lax.axis_index("col")
    third = 3 * width // n_col
    fourth = width // n_col
    depth = merge.shape[1] // n_col
    for slot in range(n_col):
        parts = [
            sums[:, slot * third : (slot + 1) * third],
            sums[:, 3 * width + slot * fourth : 3 * width + (slot + 1) * fourth],
        ]
        parts = [stacked(jnp.concatenate(parts, axis=1))]
        parts += [merge[:, slot * depth : (slot + 1) * depth], small]
        slots_ref[slot] = jnp.concatenate(parts, axis=0).astype(BF)
    for step, out_ref in enumerate(out_refs):
        out_ref[...] = slots_ref[partner(col, step)]


def partner(index, step):
    if step == 0:
        return index
    low = lax.rem(index, 2)
    if step == 1:
        return index + 1 - 2 * low
    if step == 2:
        return lax.rem(index + 2, 4)
    return 3 - index


def side_kernel(sizes, gx_ref, far_ref, near_ref, grad_ref, row_near_ref, row_far_ref):
    rows, cols, width = sizes
    ends = lax.axis_index("col")
    left, right = by_side("col", near_ref[...].astype(F32), far_ref[...].astype(F32))
    left = jnp.where(ends > 0, left, 0.0)
    right = jnp.where(ends < lax.axis_size("col") - 1, right, 0.0)
    blank = jnp.zeros((cols - 2 * EDGE, width), F32)
    pieces = []
    for i in range(rows + 2 * RADIUS):
        edge = slice(i * EDGE, (i + 1) * EDGE)
        pieces += [left[edge], blank, right[edge]]
    g_x = gx_ref[...] + jnp.concatenate(pieces, axis=0)
    reach = RADIUS * cols
    far, near = by_side("row", g_x[reach + rows * cols :], g_x[:reach])
    grad_ref[...] = g_x[reach : reach + rows * cols]
    row_near_ref[...] = near.astype(BF)
    row_far_ref[...] = far.astype(BF)


def col_sum_kernel(
    sizes,
    a_ref,
    d_ref,
    c_ref,
    b_ref,
    grad_ref,
    far_ref,
    near_ref,
    gqkv_ref,
    gout_ref,
    gmerge_ref,
    ggain_ref,
    gscale_ref,
    gtok_ref,
):
    rows, cols, width = sizes
    per, third = gqkv_ref.shape
    size = a_ref.shape[0] - 8

    def summed(part):
        first, second, third, fourth = [
            part(ref[...].astype(F32)) for ref in (a_ref, b_ref, c_ref, d_ref)
        ]
        return (first + second) + (third + fourth)

    total = summed(lambda value: value[:size])
    small = summed(lambda value: small_value(value[size:]))
    merge_at = size - gmerge_ref.shape[0]
    sums = unstacked(total[:merge_at], per)
    gqkv_ref[...] = sums[:, :third]
    gout_ref[...] = sums[:, third:]
    gmerge_ref[...] = total[merge_at:]
    ggain_ref[...] = jnp.concatenate([small[i : i + 1] for i in range(width // LANES)], axis=1)
    for h in range(gscale_ref.shape[0]):
        gscale_ref[h] = small[width // LANES, h]
    blank = jnp.zeros(((rows - RADIUS) * cols, width), F32)
    above, below = by_side("row", near_ref[...].astype(F32), far_ref[...].astype(F32))
    grad = grad_ref[...] + jnp.concatenate([above, blank], axis=0)
    grad = grad + jnp.concatenate([blank, below], axis=0)
    gtok_ref[...] = grad.astype(BF).reshape(rows, cols, width)


def plain_sums(width, sums, group, small, dm):
    sums = sums.astype(F32)
    merge = jnp.dot(group.T, dm, preferred_element_type=F32)
    outs = []
    for part in (sums[:, : 3 * width], sums[:, 3 * width :], merge):
        part = lax.psum_scatter(part, "row", scatter_dimension=0, tiled=True)
        outs.append(lax.psum_scatter(part, "col", scatter_dimension=1, tiled=True))
    small = lax.psum(small, ("row", "col"))
    return (*outs, small[: width // LANES].reshape(1, width), small[width // LANES])


def add_rows(grad, near, far, rows, cols):
    above, below = by_side("row", near.astype(F32), far.astype(F32))
    size = RADIUS * cols
    grad = grad.at[:size].add(above).at[rows * cols - size :].add(below)
    return grad.astype(BF).reshape(rows, cols, -1)


def swapped(near, far, axis):
    count = lax.axis_size(axis)
    first = [(i, i + 1) for i in range(0, count, 2)]
    second = [(i, i + 1) for i in range(1, count - 1, 2)]
    first = first + [(j, i) for i, j in first]
    second = second + [(j, i) for i, j in second] + [(0, 0), (count - 1, count - 1)]
    return (lax.ppermute(near, axis, first), lax.ppermute(far, axis, second))


def swap(value, axis, step):
    count = lax.axis_size(axis)
    return lax.ppermute(value, axis, [(i, i ^ step) for i in range(count)])


def vmem(count):
    return [pl.BlockSpec(memory_space=pltpu.VMEM)] * count


def on_device(tokens, gain, w_qkv, head_scale, w_out, w_merge, d_merged, d_skip):
    rows, cols, width = tokens.shape
    heads = head_scale.shape[0]
    n_row, n_col = (lax.axis_size("row"), lax.axis_size("col"))
    g_rows, g_cols, depth = d_merged.shape
    groups = g_rows * g_cols
    wide = cols + 2 * SIDE
    ext_rows = rows + 2 * RADIUS
    shape = jax.ShapeDtypeStruct
    params = pltpu.CompilerParams(vmem_limit_bytes=24 * 1024 * 1024)
    less = pltpu.CompilerParams(vmem_limit_bytes=8 * 1024 * 1024)
    row_near, row_far = swapped(tokens, tokens, "row")
    edge = shape((ext_rows * EDGE, width), BF)
    ones, parity = pl.pallas_call(
        first_kernel,
        out_shape=(shape((width, width), BF), shape((2 * heads, LANES), F32)),
        out_specs=tuple(vmem(2)),
        compiler_params=less,
        cost_estimate=pl.CostEstimate(flops=10**10, bytes_accessed=10**5, transcendentals=0),
    )()
    dm = d_merged.reshape(groups, depth)
    dms = [swap(dm, "row", 2 * step) for step in (3, 2, 1)] + [dm]
    tile = shape((rows * cols, width), F32)
    half = shape((rows * cols, width), BF)
    edges, two_rows, q_norm, q_unit, d_y, d_attn = pl.pallas_call(
        own_kernel,
        out_shape=(shape((2 * rows * EDGE, width), BF), shape((8, width), F32), tile, tile, tile, half),
        in_specs=vmem(10),
        out_specs=tuple(vmem(6)),
        scratch_shapes=[pltpu.VMEM((width // LANES, rows, cols, LANES), F32)],
        compiler_params=params,
        cost_estimate=pl.CostEstimate(flops=10**9, bytes_accessed=10**6, transcendentals=0),
    )(
        ones,
        parity,
        head_scale.reshape(1, heads),
        tokens,
        d_merged,
        d_skip,
        gain.reshape(1, width),
        w_qkv,
        w_out,
        w_merge,
    )
    edge_near, edge_far, dms[0] = pl.pallas_call(
        edge_kernel,
        out_shape=(edge, edge, shape(dm.shape, BF)),
        in_specs=vmem(4),
        out_specs=tuple(vmem(3)),
        compiler_params=less,
    )(edges, row_far, row_near, dms[0])
    col_near, col_far = swapped(edge_near, edge_far, "col")

    per = width // n_row
    feats = 4 * width // n_row
    packed = per % 16 == 0 and feats % LANES == 0 and groups == per
    packed = packed and width // LANES < 4 and feats == LANES and depth // n_col == LANES and n_col == 4 and n_row == 8
    if packed:
        sum_shapes = (
            shape((n_row // 2, per, 4 * width + feats), BF),
            shape((n_row // 2, per, 4 * width), F32),
            shape((n_row // 2, per, feats), BF),
        )
    else:
        sum_shapes = (
            shape((width, 4 * width), BF),
            shape((groups, 4 * width), BF),
        )
    sizes = (rows, cols, width, heads, n_row, n_col)
    tall = ext_rows * wide
    x, y, d_query, d_kv, grad_out, group, scale_part = pl.pallas_call(
        functools.partial(layer_kernel, sizes),
        out_shape=(
            shape((tall, width), F32),
            half,
            half,
            shape((tall, 2 * width), BF),
            shape((width, width), F32),
            shape((groups, 4 * width), BF),
            shape((8, width), F32),
        ),
        in_specs=vmem(13),
        out_specs=tuple(vmem(7)),
        scratch_shapes=[pltpu.VMEM((width // LANES, rows, cols, LANES), F32)],
        compiler_params=params,
        cost_estimate=pl.CostEstimate(flops=4 * 10**9, bytes_accessed=10**6, transcendentals=0),
    )(
        ones,
        tokens,
        row_far,
        row_near,
        col_far,
        col_near,
        two_rows,
        q_norm,
        q_unit,
        d_y,
        d_attn,
        w_qkv,
        w_out,
    )
    dm_core, *sums = pl.pallas_call(
        functools.partial(weights_kernel, (rows, cols, width, n_row, len(dms))),
        out_shape=(shape((len(dms) * groups, depth), BF),) + sum_shapes,
        in_specs=vmem(6 + len(dms)),
        out_specs=tuple(vmem(1 + len(sum_shapes))),
        compiler_params=params,
        cost_estimate=pl.CostEstimate(flops=10**9, bytes_accessed=10**6, transcendentals=0),
    )(x, d_query, d_kv, grad_out, group, two_rows, *dms)
    gx, *sides = pl.pallas_call(
        functools.partial(norm_kernel, (rows, cols, width, heads)),
        out_shape=(shape((ext_rows * cols, width), F32), edge, edge, shape((8, LANES), F32)),
        in_specs=vmem(7),
        out_specs=tuple(vmem(4)),
        compiler_params=params,
        cost_estimate=pl.CostEstimate(flops=5 * 10**8, bytes_accessed=10**6, transcendentals=0),
    )(x, d_query, d_kv, scale_part, two_rows, d_y, w_qkv)
    *sides, small = sides
    sides = swapped(*sides, "col")
    skip_out, merged = pl.pallas_call(
        output_kernel,
        out_shape=(shape((rows, cols, width), BF), shape((g_rows, g_cols, depth), BF)),
        in_specs=vmem(3),
        out_specs=tuple(vmem(2)),
        compiler_params=less,
        cost_estimate=pl.CostEstimate(flops=10**9, bytes_accessed=10**6, transcendentals=0),
    )(y, group, w_merge)
    reach = shape((RADIUS * cols, width), BF)
    side_call = pl.pallas_call(
        functools.partial(side_kernel, (rows, cols, width)),
        out_shape=(tile, reach, reach),
        in_specs=vmem(3),
        out_specs=tuple(vmem(3)),
        compiler_params=less,
    )
    if not packed:
        grad, *rims = side_call(gx, *sides[::-1])
        grad_tokens = add_rows(grad, *swapped(*rims, "row"), rows, cols)
        g_qkv, g_out, g_merge, g_gain, g_scale = plain_sums(width, *sums, small, dm)
    else:
        send, *kept = sums
        block = shape((4 * width // LANES * per + 2 * per + 8, LANES), BF)
        *blocks, own, own_group, small = pl.pallas_call(
            core_sum_kernel,
            out_shape=(block, block, block)
            + (shape((per, 4 * width), F32), shape((2 * per, LANES), BF), shape((8, LANES), F32)),
            in_specs=vmem(5),
            out_specs=tuple(vmem(6)),
            scratch_shapes=[pltpu.VMEM((n_row // 2,) + block.shape, BF)],
            compiler_params=less,
            cost_estimate=pl.CostEstimate(flops=5 * 10**9, bytes_accessed=10**6, transcendentals=0),
        )(swap(send, "row", 1), *kept, small, swap(small, "row", 1))
        got = [swap(blocks[step - 1], "row", 2 * step) for step in (3, 2, 1)]
        slot = shape((4 * width // n_col // LANES * per + feats + 8, LANES), BF)
        *slots, gx = pl.pallas_call(
            functools.partial(row_sum_kernel, (rows, cols, width, n_col)),
            out_shape=(slot,) * n_col + (shape(gx.shape, F32),),
            in_specs=vmem(9),
            out_specs=tuple(vmem(n_col + 1)),
            scratch_shapes=[pltpu.VMEM((n_col,) + slot.shape, BF)],
            compiler_params=less,
        )(own, own_group, small, *got, dm_core, swap(dm_core, "row", 1), gx)
        got = [slots[0]] + [swap(slots[step], "col", step) for step in (3, 2, 1)]
        grad, *rims = side_call(gx, *sides[::-1])
        rims = swapped(*rims, "row")
        g_qkv, g_out, g_merge, g_gain, g_scale, grad_tokens = pl.pallas_call(
            functools.partial(col_sum_kernel, (rows, cols, width)),
            out_shape=(
                shape((per, 3 * width // n_col), F32),
                shape((per, width // n_col), F32),
                shape((feats, depth // n_col), F32),
                shape((1, width), F32),
                shape((heads,), F32),
                shape((rows, cols, width), BF),
            ),
            in_specs=vmem(7),
            out_specs=tuple(vmem(4)) + (pl.BlockSpec(memory_space=pltpu.SMEM), vmem(1)[0]),
            compiler_params=less,
        )(*got, grad, *rims[::-1])
    return (
        skip_out,
        merged,
        grad_tokens,
        g_qkv,
        g_out,
        g_merge,
        g_gain.reshape(width),
        g_scale[:heads],
    )


def solution(mesh):
    block = P("row", "col", None)
    return jax.shard_map(
        on_device,
        mesh=mesh,
        in_specs=(block, P(), P(), P(), P(), P(), block, block),
        out_specs=(block, block, block, P("row", "col"), P("row", "col"), P("row", "col"), P(), P()),
        check_vma=False,
    )
```

```python
import functools
import jax
import jax.numpy as jnp
from jax import lax
from jax.experimental import pallas as pl
from jax.experimental.pallas import tpu as pltpu
from jax.sharding import PartitionSpec as P

RADIUS = 3
IMG_MAX = 512
EPS = 1e-06
EDGE = 4
SIDE = 8
LANES = 128
BF = jnp.bfloat16
F32 = jnp.float32


def mm(a, b):
    return lax.dot_general(a, b, (((1,), (0,)), ((), ())), preferred_element_type=F32)


def mm_t(a, b):
    return lax.dot_general(a, b, (((1,), (1,)), ((), ())), preferred_element_type=F32)


def split_two(value):
    high = value.astype(BF)
    return (high, (value - high.astype(F32)).astype(BF))


def by_side(axis, near, far):
    even = lax.rem(lax.axis_index(axis), 2) == 0
    return (jnp.where(even, far, near), jnp.where(even, near, far))


def first_kernel(ones_ref, parity_ref):
    width = ones_ref.shape[0]
    head_dim = width // (parity_ref.shape[0] // 2)
    same_head = lax.broadcasted_iota(jnp.int32, (width, width), 0) // head_dim == (
        lax.broadcasted_iota(jnp.int32, (width, width), 1) // head_dim
    )
    ones_ref[...] = jnp.where(same_head, 1.0, 0.0).astype(BF)
    half = (parity_ref.shape[0] // 2, parity_ref.shape[1])
    parts = [
        jnp.where(lax.rem(lax.axis_index(axis), 2) == 0, jnp.ones(half, F32), jnp.zeros(half, F32))
        for axis in ("row", "col")
    ]
    parity_ref[...] = jnp.concatenate(parts, axis=0)


def edge_kernel(
    edges_ref, far_ref, near_ref, dm_ref, dm_next_ref, edge_near_ref, edge_far_ref, dm_pair_ref
):
    rows, cols, width = near_ref.shape
    size = dm_next_ref.shape[0]
    dm_pair_ref[...] = jnp.concatenate([dm_ref[...].reshape(size, -1), dm_next_ref[...]], axis=0)
    up, down = by_side("row", near_ref[...].astype(F32), far_ref[...].astype(F32))
    up = up[rows - RADIUS :]
    down = down[:RADIUS]
    halo = []
    for at in (0, cols - EDGE):
        parts = [part[:, at : at + EDGE].reshape(RADIUS * EDGE, width) for part in (up, down)]
        halo.append(jnp.concatenate(parts, axis=0))
    far, near = by_side("col", halo[1], halo[0])
    for out_ref, own_at, part in ((edge_near_ref, 0, near), (edge_far_ref, rows * EDGE, far)):
        own = edges_ref[own_at : own_at + rows * EDGE].astype(F32)
        size = RADIUS * EDGE
        out_ref[...] = jnp.concatenate([part[:size], own, part[size:]], axis=0).astype(BF)


def in_order(axis, own, partner):
    even = lax.rem(lax.axis_index(axis), 2) == 0
    return (jnp.where(even, own, partner), jnp.where(even, partner, own))


def head_sum(value, ones_ref):
    high, low = split_two(value)
    return mm(high, ones_ref[...]) + mm(low, ones_ref[...])


def own_kernel(
    ones_ref,
    parity_ref,
    scale_ref,
    tok_ref,
    dm_ref,
    dskip_ref,
    gain_ref,
    wqkv_ref,
    wout_ref,
    wmerge_ref,
    edges_ref,
    rows_ref,
    q_norm_ref,
    q_unit_ref,
    dy_ref,
    d_attn_ref,
    dscr,
):
    rows, cols, width = tok_ref.shape
    tokens = rows * cols
    tok = tok_ref[...].astype(F32)
    left = tok[:, :EDGE].reshape(rows * EDGE, width)
    right = tok[:, cols - EDGE :].reshape(rows * EDGE, width)
    heads = scale_ref.shape[1]
    even = parity_ref[heads : heads + 1, 0:1] > 0.5
    near, far = (jnp.where(even, right, left), jnp.where(even, left, right))
    edges_ref[...] = jnp.concatenate([near, far], axis=0).astype(BF)
    lane = lax.broadcasted_iota(jnp.int32, (1, width), 1)
    scale_row = jnp.zeros((1, width), F32)
    for h in range(heads):
        scale_row = jnp.where(lane // (width // heads) == h, scale_ref[:, h : h + 1], scale_row)
    blank = jnp.zeros((6, width), F32)
    rows_ref[...] = jnp.concatenate([gain_ref[...], scale_row, blank], axis=0)
    x = tok.reshape(tokens, width)
    inverse = lax.rsqrt(jnp.mean(x * x, axis=1, keepdims=True) + EPS)
    normed = (x * inverse * gain_ref[...]).astype(BF)
    query = mm(normed, wqkv_ref[:, :width])
    q_norm = lax.rsqrt(head_sum(query * query, ones_ref) + EPS)
    q_norm_ref[...] = q_norm
    q_unit_ref[...] = query * q_norm
    group_wide = cols // 2
    d_in = mm_t(dm_ref[...].reshape(-1, dm_ref.shape[2]), wmerge_ref[...])
    for i in range(rows // 2):
        for pr in range(2):
            for pc in range(2):
                for part in range(width // LANES):
                    at = (2 * pr + pc) * width + part * LANES
                    dscr[part, 2 * i + pr, pl.ds(pc, group_wide, stride=2), :] = d_in[
                        i * group_wide : (i + 1) * group_wide, at : at + LANES
                    ]
    d_group = jnp.concatenate(
        [dscr[part].reshape(tokens, LANES) for part in range(width // LANES)], axis=1
    )
    d_y = dskip_ref[...].reshape(tokens, width).astype(F32) + d_group
    dy_ref[...] = d_y
    d_attn_ref[...] = mm_t(d_y.astype(BF), wout_ref[...]).astype(BF)


def layer_kernel(
    sizes,
    ones_ref,
    tok_ref,
    row_far_ref,
    row_near_ref,
    col_near_ref,
    col_far_ref,
    rows_ref,
    q_norm_ref,
    q_unit_ref,
    dy_ref,
    d_attn_ref,
    wqkv_ref,
    wout_ref,
    x_ref,
    y_ref,
    d_query_ref,
    d_kv_ref,
    grad_out_ref,
    group_ref,
    scale_part_ref,
    yscr,
):
    rows, cols, width, heads, n_row, n_col = sizes
    head_dim = width // heads
    wide = cols + 2 * SIDE
    ext_rows = rows + 2 * RADIUS
    tokens = rows * cols
    image_rows = min(IMG_MAX, rows * n_row)
    row_start = lax.axis_index("row") * rows
    col_index = lax.axis_index("col")
    col_start = col_index * cols
    first = row_start // image_rows * image_rows

    lane = lax.broadcasted_iota(jnp.int32, (1, width), 1)
    def blocks(value):
        zero = jnp.zeros_like(value)
        kept = [jnp.where(lane // head_dim == h, value, zero) for h in range(heads)]
        return jnp.concatenate(kept, axis=0).astype(BF)

    gain = rows_ref[0:1]
    scale_row = rows_ref[1:2]
    up, down = by_side("row", row_near_ref[...].astype(F32), row_far_ref[...].astype(F32))
    left, right = by_side("col", col_near_ref[...].astype(F32), col_far_ref[...].astype(F32))
    own = tok_ref[...].astype(F32)
    blank = jnp.zeros((SIDE - EDGE, width), F32)
    pieces = []
    for i in range(ext_rows):
        if i < RADIUS:
            row = up[rows - RADIUS + i]
        elif i < RADIUS + rows:
            row = own[i - RADIUS]
        else:
            row = down[i - RADIUS - rows]
        edge = slice(i * EDGE, (i + 1) * EDGE)
        pieces += [blank, left[edge], row, right[edge], blank]
    x = jnp.concatenate(pieces, axis=0)
    x_ref[...] = x
    inverse = lax.rsqrt(jnp.mean(x * x, axis=1, keepdims=True) + EPS)
    unit = x * inverse
    normed32 = (unit * gain).astype(BF).astype(F32)
    normed = normed32.astype(BF)
    x_own = inner_tokens(x, rows, cols)
    kv = mm(normed, wqkv_ref[:, width:])
    key_raw = kv[:, :width]
    k_norm = lax.rsqrt(head_sum(key_raw * key_raw, ones_ref) + EPS)
    k_unit = key_raw * k_norm
    keys = k_unit.astype(BF)
    values = kv[:, width:].astype(BF)
    q_norm = q_norm_ref[...]
    q_unit = q_unit_ref[...]
    q_hat = (q_unit * scale_row).astype(BF).astype(F32)
    d_y = dy_ref[...]
    dy_b = d_y.astype(BF)
    d_attn = d_attn_ref[...].astype(F32)

    index = lax.broadcasted_iota(jnp.int32, (1, tokens), 1)
    q_row = jnp.zeros_like(index)
    for i in range(1, rows):
        q_row = q_row + (index >= i * cols).astype(jnp.int32)
    q_col = index - q_row * cols
    key_col = lax.broadcasted_iota(jnp.int32, (wide, tokens), 0) - SIDE
    near = (key_col - q_col <= RADIUS) & (key_col - q_col >= -RADIUS)
    near = near & (key_col + col_start >= 0) & (key_col + col_start < cols * n_col)
    near = jnp.where(near, 1.0, 0.0)
    parts = []
    for i in range(-RADIUS, rows + RADIUS):
        ok = (q_row - i <= RADIUS) & (q_row - i >= -RADIUS)
        ok = ok & (row_start + i >= first) & (row_start + i < first + image_rows)
        parts.append(near * jnp.where(ok, 1.0, 0.0))
    allowed = jnp.concatenate([jnp.concatenate(parts, axis=0)] * heads, axis=1)
    q_blocks = blocks(q_hat)
    g_blocks = blocks(d_attn)
    expo = jnp.exp(mm_t(keys, q_blocks)) * allowed
    prob = expo * (1.0 / jnp.sum(expo, axis=0, keepdims=True))
    weights = prob.astype(BF)
    d_w = mm_t(values, g_blocks)
    delta = jnp.sum(d_w * prob, axis=0, keepdims=True)
    d_s = (prob * (d_w - delta)).astype(BF)
    values_t = values.astype(F32).T.astype(BF)
    keys_t = keys.astype(F32).T.astype(BF)
    attn_t = []
    d_qhat_t = []
    for h in range(heads):
        feats = slice(h * head_dim, (h + 1) * head_dim)
        lanes = slice(h * tokens, (h + 1) * tokens)
        attn_t.append(mm(values_t[feats], weights[:, lanes]))
        d_qhat_t.append(mm(keys_t[feats], d_s[:, lanes]))
    attn_t = jnp.concatenate(attn_t, axis=0)
    d_qhat = jnp.concatenate(d_qhat_t, axis=0).T
    d_k = mm(d_s, q_blocks)
    d_v = mm(weights, g_blocks)

    attn = attn_t.T.astype(BF)
    y = (x_own + mm(attn, wout_ref[...])).astype(BF)
    y_ref[...] = y
    y32 = y.astype(F32)
    for part in range(width // LANES):
        yscr[part] = y32[:, part * LANES : (part + 1) * LANES].reshape(rows, cols, LANES)
    lines = []
    for i in range(rows // 2):
        pieces = []
        for pr in range(2):
            for pc in range(2):
                for part in range(width // LANES):
                    pieces.append(yscr[part, 2 * i + pr, pl.ds(pc, cols // 2, stride=2), :])
        lines.append(jnp.concatenate(pieces, axis=1))
    group = jnp.concatenate(lines, axis=0).astype(BF)
    group_ref[...] = group
    grad_out_ref[...] = mm(attn_t.astype(BF), dy_b)

    scale_part_ref[...] = jnp.broadcast_to(
        jnp.sum(q_unit * d_qhat, axis=0, keepdims=True), scale_part_ref.shape
    )
    g_unit = d_qhat * scale_row
    d_query_ref[...] = (q_norm * (g_unit - q_unit * head_sum(q_unit * g_unit, ones_ref))).astype(BF)
    d_key = k_norm * (d_k - k_unit * head_sum(k_unit * d_k, ones_ref))
    d_kv_ref[...] = jnp.concatenate([d_key, d_v], axis=1).astype(BF)


def inner_tokens(value, rows, cols):
    wide = cols + 2 * SIDE
    pieces = []
    for i in range(RADIUS, RADIUS + rows):
        pieces.append(value[i * wide + SIDE : i * wide + SIDE + cols])
    return jnp.concatenate(pieces, axis=0)


def output_kernel(y_ref, group_ref, wmerge_ref, skip_ref, merged_ref):
    skip_ref[...] = y_ref[...].reshape(skip_ref.shape)
    merged = mm(group_ref[...], wmerge_ref[...])
    merged_ref[...] = merged.astype(BF).reshape(merged_ref.shape)


def weights_kernel(
    sizes, x_ref, d_query_ref, d_kv_ref, grad_out_ref, group_ref, rows_ref, *refs
):
    rows, cols, width, n_row, n_dm = sizes
    dm_refs, dm_all_ref, sum_refs = (refs[:n_dm], refs[n_dm], refs[n_dm + 1 :])
    size = dm_all_ref.shape[0] // n_dm
    dm = [ref[...].reshape(size, dm_all_ref.shape[1]) for ref in dm_refs]
    dm_all_ref[...] = jnp.concatenate(dm[::-1], axis=0)
    x = x_ref[...]
    inverse = lax.rsqrt(jnp.mean(x * x, axis=1, keepdims=True) + EPS)
    normed32 = (x * inverse * rows_ref[0:1]).astype(BF).astype(F32)
    grad_q = mm(inner_tokens(normed32, rows, cols).T.astype(BF), d_query_ref[...])
    grad_kv = mm(normed32.T.astype(BF), d_kv_ref[...])
    sums = jnp.concatenate([grad_q, grad_kv, grad_out_ref[...]], axis=1)
    group = group_ref[...]
    if len(sum_refs) == 2:
        sum_refs[0][...] = sums.astype(BF)
        sum_refs[1][...] = group
        return
    send_ref, keep_ref, keep_group_ref = sum_refs
    per = width // n_row
    feats = 4 * width // n_row
    group = group.astype(F32)
    even = lax.rem(lax.axis_index("row"), 2) == 0
    for q in range(n_row // 2):
        parts = []
        for value, axis, size in ((sums, 0, per), (group, 1, feats)):
            first = lax.slice_in_dim(value, 2 * q * size, (2 * q + 1) * size, axis=axis)
            second = lax.slice_in_dim(value, (2 * q + 1) * size, (2 * q + 2) * size, axis=axis)
            parts.append((jnp.where(even, first, second), jnp.where(even, second, first)))
        (keep_ref[q], sums_send), (keep_group, group_send) = parts
        keep_group_ref[q] = keep_group.astype(BF)
        send_ref[q] = jnp.concatenate([sums_send, group_send], axis=1).astype(BF)


def norm_kernel(
    sizes, x_ref, d_query_ref, d_kv_ref, scale_part_ref, rows_ref, dy_ref, wqkv_ref, *refs
):
    rows, cols, width, heads = sizes
    gx_ref, side_near_ref, side_far_ref, small_ref = refs
    head_dim = width // heads
    wide = cols + 2 * SIDE
    ext_rows = rows + 2 * RADIUS
    gain = rows_ref[0:1]
    lane = lax.broadcasted_iota(jnp.int32, (1, width), 1)
    x = x_ref[...]
    inverse = lax.rsqrt(jnp.mean(x * x, axis=1, keepdims=True) + EPS)
    unit = x * inverse
    d_y = dy_ref[...]
    from_q = mm_t(d_query_ref[...], wqkv_ref[:, :width])
    d_normed = mm_t(d_kv_ref[...], wqkv_ref[:, width:])
    pieces = []
    side = jnp.zeros((SIDE, width), F32)
    for i in range(ext_rows):
        if RADIUS <= i < RADIUS + rows:
            at = (i - RADIUS) * cols
            pieces += [side, from_q[at : at + cols], side]
        else:
            pieces.append(jnp.zeros((wide, width), F32))
    d_normed = d_normed + jnp.concatenate(pieces, axis=0)
    gain_part = jnp.sum(unit * d_normed, axis=0, keepdims=True)
    scaled = gain * d_normed
    mean = jnp.mean(x * scaled, axis=1, keepdims=True)
    g_x = inverse * scaled - x * (inverse * inverse * inverse) * mean

    pieces = []
    left = []
    right = []
    for i in range(ext_rows):
        row = g_x[i * wide : (i + 1) * wide]
        middle = row[SIDE : SIDE + cols]
        if RADIUS <= i < RADIUS + rows:
            middle = middle + d_y[(i - RADIUS) * cols : (i - RADIUS + 1) * cols]
        pieces.append(middle)
        left.append(row[:SIDE][SIDE - EDGE :])
        right.append(row[SIDE + cols :][:EDGE])
    gx_ref[...] = jnp.concatenate(pieces, axis=0)
    left, right = [jnp.concatenate(part, axis=0) for part in (left, right)]
    far, near = by_side("col", right, left)
    side_near_ref[...] = near.astype(BF)
    side_far_ref[...] = far.astype(BF)
    scale_part = scale_part_ref[0:1]
    scale_lane = lax.broadcasted_iota(jnp.int32, (1, LANES), 1)
    scale_sums = jnp.zeros((1, LANES), F32)
    for h in range(heads):
        of_head = jnp.sum(jnp.where(lane // head_dim == h, scale_part, 0.0), axis=1, keepdims=True)
        scale_sums = jnp.where(scale_lane == h, of_head, scale_sums)
    small = [gain_part[:, i * LANES : (i + 1) * LANES] for i in range(width // LANES)] + [scale_sums]
    small = jnp.concatenate(small + [jnp.zeros((8 - len(small), LANES), F32)], axis=0)
    small_ref[...] = small


def small_rows(small):
    high = small.astype(BF).astype(F32)
    return jnp.concatenate([high[:4], (small - high)[:4]], axis=0)


def small_value(rows):
    value = rows.astype(BF).astype(F32)
    return value[:4] + value[4:]


def stacked(value):
    return jnp.concatenate(
        [value[:, i : i + LANES] for i in range(0, value.shape[1], LANES)], axis=0
    )


def unstacked(value, rows):
    return jnp.concatenate([value[i : i + rows] for i in range(0, value.shape[0], rows)], axis=1)


def core_sum_kernel(got_ref, keep_ref, keep_group_ref, small_ref, small_near_ref, *refs):
    *out_refs, own_ref, own_group_ref, small_sum_ref, blocks_ref = refs
    chips, per, width = keep_ref.shape
    feats = keep_group_ref.shape[2]
    small = small_ref[...] + small_near_ref[...]
    small_sum_ref[...] = small
    small = small_rows(small)
    chip = lax.axis_index("row") // 2
    own_ref[...] = keep_ref[chip] + got_ref[chip, :, :width].astype(F32)
    for q in range(chips):
        sums = keep_ref[q] + got_ref[q, :, :width].astype(F32)
        kept = keep_group_ref[q].astype(F32)
        first, second = in_order("row", kept, got_ref[q, :, width:].astype(F32))
        block = [stacked(sums), first, second, small]
        blocks_ref[q] = jnp.concatenate(block, axis=0).astype(BF)
    size = width // LANES * per
    own_group_ref[...] = blocks_ref[chip][size : size + 2 * per]
    for step, out_ref in enumerate(out_refs, 1):
        out_ref[...] = blocks_ref[partner(chip, step)]


def row_sum_kernel(sizes, *refs):
    rows, cols, width, n_col = sizes
    own_ref, own_group_ref, small_ref, *refs = refs
    got_refs, dm_ref, dm_near_ref, gx_ref, *refs = (refs[:3], *refs[3:])
    *out_refs, gx_sum_ref, slots_ref = refs
    gx_sum_ref[...] = gx_ref[...]
    per = own_ref.shape[0]
    feats = own_group_ref.shape[1]
    size = 4 * width // LANES * per

    def summed(first, part):
        fourth, third, second = [part(ref[...].astype(F32)) for ref in got_refs]
        return (first + second) + (third + fourth)

    sums = summed(stacked(own_ref[...]), lambda value: value[:size])
    sums = unstacked(sums, per)
    small = summed(small_value(small_rows(small_ref[...])), lambda value: small_value(value[size + 2 * per :]))
    group = [own_group_ref[...].astype(F32)]
    group += [ref[...].astype(F32)[size : size + 2 * per] for ref in got_refs[::-1]]
    group = [part[i * per : (i + 1) * per] for i in range(2) for part in group]
    group = jnp.concatenate(group, axis=0)
    own, near = (dm_ref[...].astype(F32), dm_near_ref[...].astype(F32))
    dm = jnp.concatenate(in_order("row", own, near), axis=0).astype(BF)
    merge = mm(group.T.astype(BF), dm)
    small = small_rows(small)
    col = lax.axis_index("col")
    third = 3 * width // n_col
    fourth = width // n_col
    depth = merge.shape[1] // n_col
    for slot in range(n_col):
        parts = [
            sums[:, slot * third : (slot + 1) * third],
            sums[:, 3 * width + slot * fourth : 3 * width + (slot + 1) * fourth],
        ]
        parts = [stacked(jnp.concatenate(parts, axis=1))]
        parts += [merge[:, slot * depth : (slot + 1) * depth], small]
        slots_ref[slot] = jnp.concatenate(parts, axis=0).astype(BF)
    for step, out_ref in enumerate(out_refs):
        out_ref[...] = slots_ref[partner(col, step)]


def partner(index, step):
    if step == 0:
        return index
    low = lax.rem(index, 2)
    if step == 1:
        return index + 1 - 2 * low
    if step == 2:
        return lax.rem(index + 2, 4)
    return 3 - index


def side_kernel(sizes, gx_ref, near_ref, far_ref, grad_ref, row_near_ref, row_far_ref):
    rows, cols, width = sizes
    ends = lax.axis_index("col")
    left, right = by_side("col", near_ref[...].astype(F32), far_ref[...].astype(F32))
    left = jnp.where(ends > 0, left, 0.0)
    right = jnp.where(ends < lax.axis_size("col") - 1, right, 0.0)
    blank = jnp.zeros((cols - 2 * EDGE, width), F32)
    pieces = []
    for i in range(rows + 2 * RADIUS):
        edge = slice(i * EDGE, (i + 1) * EDGE)
        pieces += [left[edge], blank, right[edge]]
    g_x = gx_ref[...] + jnp.concatenate(pieces, axis=0)
    reach = RADIUS * cols
    far, near = by_side("row", g_x[reach + rows * cols :], g_x[:reach])
    grad_ref[...] = g_x[reach : reach + rows * cols]
    row_near_ref[...] = near.astype(BF)
    row_far_ref[...] = far.astype(BF)


def col_sum_kernel(
    sizes,
    a_ref,
    d_ref,
    c_ref,
    b_ref,
    grad_ref,
    far_ref,
    near_ref,
    gqkv_ref,
    gout_ref,
    gmerge_ref,
    ggain_ref,
    gscale_ref,
    gtok_ref,
):
    rows, cols, width = sizes
    per, third = gqkv_ref.shape
    size = a_ref.shape[0] - 8

    def summed(part):
        first, second, third, fourth = [
            part(ref[...].astype(F32)) for ref in (a_ref, b_ref, c_ref, d_ref)
        ]
        return (first + second) + (third + fourth)

    total = summed(lambda value: value[:size])
    small = summed(lambda value: small_value(value[size:]))
    merge_at = size - gmerge_ref.shape[0]
    sums = unstacked(total[:merge_at], per)
    gqkv_ref[...] = sums[:, :third]
    gout_ref[...] = sums[:, third:]
    gmerge_ref[...] = total[merge_at:]
    ggain_ref[...] = jnp.concatenate([small[i : i + 1] for i in range(width // LANES)], axis=1)
    for h in range(gscale_ref.shape[0]):
        gscale_ref[h] = small[width // LANES, h]
    blank = jnp.zeros(((rows - RADIUS) * cols, width), F32)
    above, below = by_side("row", near_ref[...].astype(F32), far_ref[...].astype(F32))
    grad = grad_ref[...] + jnp.concatenate([above, blank], axis=0)
    grad = grad + jnp.concatenate([blank, below], axis=0)
    gtok_ref[...] = grad.astype(BF).reshape(rows, cols, width)


def plain_sums(width, sums, group, small, dm):
    sums = sums.astype(F32)
    merge = jnp.dot(group.T, dm, preferred_element_type=F32)
    outs = []
    for part in (sums[:, : 3 * width], sums[:, 3 * width :], merge):
        part = lax.psum_scatter(part, "row", scatter_dimension=0, tiled=True)
        outs.append(lax.psum_scatter(part, "col", scatter_dimension=1, tiled=True))
    small = lax.psum(small, ("row", "col"))
    return (*outs, small[: width // LANES].reshape(1, width), small[width // LANES])


def add_rows(grad, near, far, rows, cols):
    above, below = by_side("row", near.astype(F32), far.astype(F32))
    size = RADIUS * cols
    grad = grad.at[:size].add(above).at[rows * cols - size :].add(below)
    return grad.astype(BF).reshape(rows, cols, -1)


def swapped(near, far, axis):
    count = lax.axis_size(axis)
    first = [(i, i + 1) for i in range(0, count, 2)]
    second = [(i, (i + 1) % count) for i in range(1, count, 2)]
    first = first + [(j, i) for i, j in first]
    second = second + [(j, i) for i, j in second]
    return (lax.ppermute(near, axis, first), lax.ppermute(far, axis, second))


def swap(value, axis, step):
    count = lax.axis_size(axis)
    return lax.ppermute(value, axis, [(i, i ^ step) for i in range(count)])


def vmem(count):
    return [pl.BlockSpec(memory_space=pltpu.VMEM)] * count


def on_device(tokens, gain, w_qkv, head_scale, w_out, w_merge, d_merged, d_skip):
    rows, cols, width = tokens.shape
    heads = head_scale.shape[0]
    n_row, n_col = (lax.axis_size("row"), lax.axis_size("col"))
    g_rows, g_cols, depth = d_merged.shape
    groups = g_rows * g_cols
    wide = cols + 2 * SIDE
    ext_rows = rows + 2 * RADIUS
    shape = jax.ShapeDtypeStruct
    params = pltpu.CompilerParams(vmem_limit_bytes=24 * 1024 * 1024)
    less = pltpu.CompilerParams(vmem_limit_bytes=8 * 1024 * 1024)
    row_near, row_far = swapped(tokens, tokens, "row")
    edge = shape((ext_rows * EDGE, width), BF)
    ones, parity = pl.pallas_call(
        first_kernel,
        out_shape=(shape((width, width), BF), shape((2 * heads, LANES), F32)),
        out_specs=tuple(vmem(2)),
        compiler_params=less,
        cost_estimate=pl.CostEstimate(flops=10**10, bytes_accessed=10**5, transcendentals=0),
    )()
    dm = d_merged.reshape(groups, depth)
    tile = shape((rows * cols, width), F32)
    half = shape((rows * cols, width), BF)
    edges, two_rows, q_norm, q_unit, d_y, d_attn = pl.pallas_call(
        own_kernel,
        out_shape=(shape((2 * rows * EDGE, width), BF), shape((8, width), F32), tile, tile, tile, half),
        in_specs=vmem(10),
        out_specs=tuple(vmem(6)),
        scratch_shapes=[pltpu.VMEM((width // LANES, rows, cols, LANES), F32)],
        compiler_params=params,
        cost_estimate=pl.CostEstimate(flops=10**9, bytes_accessed=10**6, transcendentals=0),
    )(
        ones,
        parity,
        head_scale.reshape(1, heads),
        tokens,
        d_merged,
        d_skip,
        gain.reshape(1, width),
        w_qkv,
        w_out,
        w_merge,
    )
    edge_near, edge_far, dm_pair = pl.pallas_call(
        edge_kernel,
        out_shape=(edge, edge, shape((2 * groups, depth), BF)),
        in_specs=vmem(5),
        out_specs=tuple(vmem(3)),
        compiler_params=less,
    )(edges, row_far, row_near, d_merged, swap(dm, "row", 2))
    dms = [swap(dm_pair, "row", 4), dm_pair]
    col_near, col_far = swapped(edge_near, edge_far, "col")

    per = width // n_row
    feats = 4 * width // n_row
    packed = per % 16 == 0 and feats % LANES == 0 and groups == per
    packed = packed and width // LANES < 4 and feats == LANES and depth // n_col == LANES and n_col == 4 and n_row == 8
    if packed:
        sum_shapes = (
            shape((n_row // 2, per, 4 * width + feats), BF),
            shape((n_row // 2, per, 4 * width), F32),
            shape((n_row // 2, per, feats), BF),
        )
    else:
        sum_shapes = (
            shape((width, 4 * width), BF),
            shape((groups, 4 * width), BF),
        )
    sizes = (rows, cols, width, heads, n_row, n_col)
    tall = ext_rows * wide
    x, y, d_query, d_kv, grad_out, group, scale_part = pl.pallas_call(
        functools.partial(layer_kernel, sizes),
        out_shape=(
            shape((tall, width), F32),
            half,
            half,
            shape((tall, 2 * width), BF),
            shape((width, width), F32),
            shape((groups, 4 * width), BF),
            shape((8, width), F32),
        ),
        in_specs=vmem(13),
        out_specs=tuple(vmem(7)),
        scratch_shapes=[pltpu.VMEM((width // LANES, rows, cols, LANES), F32)],
        compiler_params=params,
        cost_estimate=pl.CostEstimate(flops=4 * 10**9, bytes_accessed=10**6, transcendentals=0),
    )(
        ones,
        tokens,
        row_far,
        row_near,
        col_near,
        col_far,
        two_rows,
        q_norm,
        q_unit,
        d_y,
        d_attn,
        w_qkv,
        w_out,
    )
    dm_core, *sums = pl.pallas_call(
        functools.partial(weights_kernel, (rows, cols, width, n_row, len(dms))),
        out_shape=(shape((2 * len(dms) * groups, depth), BF),) + sum_shapes,
        in_specs=vmem(6 + len(dms)),
        out_specs=tuple(vmem(1 + len(sum_shapes))),
        compiler_params=params,
        cost_estimate=pl.CostEstimate(flops=10**9, bytes_accessed=10**6, transcendentals=0),
    )(x, d_query, d_kv, grad_out, group, two_rows, *dms)
    gx, *sides = pl.pallas_call(
        functools.partial(norm_kernel, (rows, cols, width, heads)),
        out_shape=(shape((ext_rows * cols, width), F32), edge, edge, shape((8, LANES), F32)),
        in_specs=vmem(7),
        out_specs=tuple(vmem(4)),
        compiler_params=params,
        cost_estimate=pl.CostEstimate(flops=5 * 10**8, bytes_accessed=10**6, transcendentals=0),
    )(x, d_query, d_kv, scale_part, two_rows, d_y, w_qkv)
    *sides, small = sides
    sides = swapped(*sides, "col")
    skip_out, merged = pl.pallas_call(
        output_kernel,
        out_shape=(shape((rows, cols, width), BF), shape((g_rows, g_cols, depth), BF)),
        in_specs=vmem(3),
        out_specs=tuple(vmem(2)),
        compiler_params=less,
        cost_estimate=pl.CostEstimate(flops=10**9, bytes_accessed=10**6, transcendentals=0),
    )(y, group, w_merge)
    reach = shape((RADIUS * cols, width), BF)
    side_call = pl.pallas_call(
        functools.partial(side_kernel, (rows, cols, width)),
        out_shape=(tile, reach, reach),
        in_specs=vmem(3),
        out_specs=tuple(vmem(3)),
        compiler_params=less,
    )
    if not packed:
        grad, *rims = side_call(gx, *sides)
        grad_tokens = add_rows(grad, *swapped(*rims, "row"), rows, cols)
        g_qkv, g_out, g_merge, g_gain, g_scale = plain_sums(width, *sums, small, dm)
    else:
        send, *kept = sums
        block = shape((4 * width // LANES * per + 2 * per + 8, LANES), BF)
        *blocks, own, own_group, small = pl.pallas_call(
            core_sum_kernel,
            out_shape=(block, block, block)
            + (shape((per, 4 * width), F32), shape((2 * per, LANES), BF), shape((8, LANES), F32)),
            in_specs=vmem(5),
            out_specs=tuple(vmem(6)),
            scratch_shapes=[pltpu.VMEM((n_row // 2,) + block.shape, BF)],
            compiler_params=less,
            cost_estimate=pl.CostEstimate(flops=5 * 10**9, bytes_accessed=10**6, transcendentals=0),
        )(swap(send, "row", 1), *kept, small, swap(small, "row", 1))
        got = [swap(blocks[step - 1], "row", 2 * step) for step in (3, 2, 1)]
        slot = shape((4 * width // n_col // LANES * per + feats + 8, LANES), BF)
        *slots, gx = pl.pallas_call(
            functools.partial(row_sum_kernel, (rows, cols, width, n_col)),
            out_shape=(slot,) * n_col + (shape(gx.shape, F32),),
            in_specs=vmem(9),
            out_specs=tuple(vmem(n_col + 1)),
            scratch_shapes=[pltpu.VMEM((n_col,) + slot.shape, BF)],
            compiler_params=less,
        )(own, own_group, small, *got, dm_core, swap(dm_core, "row", 1), gx)
        got = [slots[0]] + [swap(slots[step], "col", step) for step in (3, 2, 1)]
        grad, *rims = side_call(gx, *sides)
        rims = swapped(*rims, "row")
        g_qkv, g_out, g_merge, g_gain, g_scale, grad_tokens = pl.pallas_call(
            functools.partial(col_sum_kernel, (rows, cols, width)),
            out_shape=(
                shape((per, 3 * width // n_col), F32),
                shape((per, width // n_col), F32),
                shape((feats, depth // n_col), F32),
                shape((1, width), F32),
                shape((heads,), F32),
                shape((rows, cols, width), BF),
            ),
            in_specs=vmem(7),
            out_specs=tuple(vmem(4)) + (pl.BlockSpec(memory_space=pltpu.SMEM), vmem(1)[0]),
            compiler_params=less,
        )(*got, grad, *rims[::-1])
    return (
        skip_out,
        merged,
        grad_tokens,
        g_qkv,
        g_out,
        g_merge,
        g_gain.reshape(width),
        g_scale[:heads],
    )


def solution(mesh):
    block = P("row", "col", None)
    return jax.shard_map(
        on_device,
        mesh=mesh,
        in_specs=(block, P(), P(), P(), P(), P(), block, block),
        out_specs=(block, block, block, P("row", "col"), P("row", "col"), P("row", "col"), P(), P()),
        check_vma=False,
    )
```

```python
import functools
import jax
import jax.numpy as jnp
from jax import lax
from jax.experimental import pallas as pl
from jax.experimental.pallas import tpu as pltpu
from jax.sharding import PartitionSpec as P

RADIUS = 3
IMG_MAX = 512
EPS = 1e-06
EDGE = 4
SIDE = 8
LANES = 128
BF = jnp.bfloat16
F32 = jnp.float32


def mm(a, b):
    return lax.dot_general(a, b, (((1,), (0,)), ((), ())), preferred_element_type=F32)


def mm_t(a, b):
    return lax.dot_general(a, b, (((1,), (1,)), ((), ())), preferred_element_type=F32)


def split_two(value):
    high = value.astype(BF)
    return (high, (value - high.astype(F32)).astype(BF))


def by_side(axis, near, far):
    even = lax.rem(lax.axis_index(axis), 2) == 0
    return (jnp.where(even, far, near), jnp.where(even, near, far))


def first_kernel(ones_ref, parity_ref):
    width = ones_ref.shape[0]
    head_dim = width // (parity_ref.shape[0] // 2)
    same_head = lax.broadcasted_iota(jnp.int32, (width, width), 0) // head_dim == (
        lax.broadcasted_iota(jnp.int32, (width, width), 1) // head_dim
    )
    ones_ref[...] = jnp.where(same_head, 1.0, 0.0).astype(BF)
    half = (parity_ref.shape[0] // 2, parity_ref.shape[1])
    parts = [
        jnp.where(lax.rem(lax.axis_index(axis), 2) == 0, jnp.ones(half, F32), jnp.zeros(half, F32))
        for axis in ("row", "col")
    ]
    parity_ref[...] = jnp.concatenate(parts, axis=0)


def edge_kernel(
    edges_ref, far_ref, near_ref, dm_ref, dm_next_ref, edge_near_ref, edge_far_ref, dm_pair_ref
):
    rows, cols, width = near_ref.shape
    size = dm_next_ref.shape[0]
    dm_pair_ref[...] = jnp.concatenate([dm_ref[...].reshape(size, -1), dm_next_ref[...]], axis=0)
    up, down = by_side("row", near_ref[...].astype(F32), far_ref[...].astype(F32))
    up = up[rows - RADIUS :]
    down = down[:RADIUS]
    halo = []
    for at in (0, cols - EDGE):
        parts = [part[:, at : at + EDGE].reshape(RADIUS * EDGE, width) for part in (up, down)]
        halo.append(jnp.concatenate(parts, axis=0))
    far, near = by_side("col", halo[1], halo[0])
    for out_ref, own_at, part in ((edge_near_ref, 0, near), (edge_far_ref, rows * EDGE, far)):
        own = edges_ref[own_at : own_at + rows * EDGE].astype(F32)
        size = RADIUS * EDGE
        out_ref[...] = jnp.concatenate([part[:size], own, part[size:]], axis=0).astype(BF)


def in_order(axis, own, partner):
    even = lax.rem(lax.axis_index(axis), 2) == 0
    return (jnp.where(even, own, partner), jnp.where(even, partner, own))


def head_sum(value, ones_ref):
    high, low = split_two(value)
    return mm(high, ones_ref[...]) + mm(low, ones_ref[...])


def own_kernel(
    ones_ref,
    parity_ref,
    scale_ref,
    tok_ref,
    dm_ref,
    dskip_ref,
    gain_ref,
    wqkv_ref,
    wout_ref,
    wmerge_ref,
    edges_ref,
    rows_ref,
    q_norm_ref,
    q_unit_ref,
    dy_ref,
    d_attn_ref,
    dscr,
):
    rows, cols, width = tok_ref.shape
    tokens = rows * cols
    tok = tok_ref[...].astype(F32)
    left = tok[:, :EDGE].reshape(rows * EDGE, width)
    right = tok[:, cols - EDGE :].reshape(rows * EDGE, width)
    heads = scale_ref.shape[1]
    even = parity_ref[heads : heads + 1, 0:1] > 0.5
    near, far = (jnp.where(even, right, left), jnp.where(even, left, right))
    edges_ref[...] = jnp.concatenate([near, far], axis=0).astype(BF)
    lane = lax.broadcasted_iota(jnp.int32, (1, width), 1)
    scale_row = jnp.zeros((1, width), F32)
    for h in range(heads):
        scale_row = jnp.where(lane // (width // heads) == h, scale_ref[:, h : h + 1], scale_row)
    blank = jnp.zeros((6, width), F32)
    rows_ref[...] = jnp.concatenate([gain_ref[...], scale_row, blank], axis=0)
    x = tok.reshape(tokens, width)
    inverse = lax.rsqrt(jnp.mean(x * x, axis=1, keepdims=True) + EPS)
    normed = (x * inverse * gain_ref[...]).astype(BF)
    query = mm(normed, wqkv_ref[:, :width])
    q_norm = lax.rsqrt(head_sum(query * query, ones_ref) + EPS)
    q_norm_ref[...] = q_norm
    q_unit_ref[...] = query * q_norm
    group_wide = cols // 2
    d_in = mm_t(dm_ref[...].reshape(-1, dm_ref.shape[2]), wmerge_ref[...])
    for i in range(rows // 2):
        for pr in range(2):
            for pc in range(2):
                for part in range(width // LANES):
                    at = (2 * pr + pc) * width + part * LANES
                    dscr[part, 2 * i + pr, pl.ds(pc, group_wide, stride=2), :] = d_in[
                        i * group_wide : (i + 1) * group_wide, at : at + LANES
                    ]
    d_group = jnp.concatenate(
        [dscr[part].reshape(tokens, LANES) for part in range(width // LANES)], axis=1
    )
    d_y = dskip_ref[...].reshape(tokens, width).astype(F32) + d_group
    dy_ref[...] = d_y
    d_attn_ref[...] = mm_t(d_y.astype(BF), wout_ref[...]).astype(BF)


def layer_kernel(
    sizes,
    ones_ref,
    tok_ref,
    row_far_ref,
    row_near_ref,
    col_near_ref,
    col_far_ref,
    rows_ref,
    q_norm_ref,
    q_unit_ref,
    dy_ref,
    d_attn_ref,
    wqkv_ref,
    wout_ref,
    x_ref,
    y_ref,
    d_query_ref,
    d_kv_ref,
    grad_out_ref,
    group_ref,
    scale_part_ref,
    yscr,
):
    rows, cols, width, heads, n_row, n_col = sizes
    head_dim = width // heads
    wide = cols + 2 * SIDE
    ext_rows = rows + 2 * RADIUS
    tokens = rows * cols
    image_rows = min(IMG_MAX, rows * n_row)
    row_start = lax.axis_index("row") * rows
    col_index = lax.axis_index("col")
    col_start = col_index * cols
    first = row_start // image_rows * image_rows

    lane = lax.broadcasted_iota(jnp.int32, (1, width), 1)
    def blocks(value):
        zero = jnp.zeros_like(value)
        kept = [jnp.where(lane // head_dim == h, value, zero) for h in range(heads)]
        return jnp.concatenate(kept, axis=0).astype(BF)

    gain = rows_ref[0:1]
    scale_row = rows_ref[1:2]
    up, down = by_side("row", row_near_ref[...].astype(F32), row_far_ref[...].astype(F32))
    left, right = by_side("col", col_near_ref[...].astype(F32), col_far_ref[...].astype(F32))
    own = tok_ref[...].astype(F32)
    blank = jnp.zeros((SIDE - EDGE, width), F32)
    pieces = []
    for i in range(ext_rows):
        if i < RADIUS:
            row = up[rows - RADIUS + i]
        elif i < RADIUS + rows:
            row = own[i - RADIUS]
        else:
            row = down[i - RADIUS - rows]
        edge = slice(i * EDGE, (i + 1) * EDGE)
        pieces += [blank, left[edge], row, right[edge], blank]
    x = jnp.concatenate(pieces, axis=0)
    x_ref[...] = x
    inverse = lax.rsqrt(jnp.mean(x * x, axis=1, keepdims=True) + EPS)
    unit = x * inverse
    normed32 = (unit * gain).astype(BF).astype(F32)
    normed = normed32.astype(BF)
    x_own = inner_tokens(x, rows, cols)
    kv = mm(normed, wqkv_ref[:, width:])
    key_raw = kv[:, :width]
    k_norm = lax.rsqrt(head_sum(key_raw * key_raw, ones_ref) + EPS)
    k_unit = key_raw * k_norm
    keys = k_unit.astype(BF)
    values = kv[:, width:].astype(BF)
    q_norm = q_norm_ref[...]
    q_unit = q_unit_ref[...]
    q_hat = (q_unit * scale_row).astype(BF).astype(F32)
    d_y = dy_ref[...]
    dy_b = d_y.astype(BF)
    d_attn = d_attn_ref[...].astype(F32)

    index = lax.broadcasted_iota(jnp.int32, (1, tokens), 1)
    q_row = jnp.zeros_like(index)
    for i in range(1, rows):
        q_row = q_row + (index >= i * cols).astype(jnp.int32)
    q_col = index - q_row * cols
    key_col = lax.broadcasted_iota(jnp.int32, (wide, tokens), 0) - SIDE
    near = (key_col - q_col <= RADIUS) & (key_col - q_col >= -RADIUS)
    near = near & (key_col + col_start >= 0) & (key_col + col_start < cols * n_col)
    near = jnp.where(near, 1.0, 0.0)
    parts = []
    for i in range(-RADIUS, rows + RADIUS):
        ok = (q_row - i <= RADIUS) & (q_row - i >= -RADIUS)
        ok = ok & (row_start + i >= first) & (row_start + i < first + image_rows)
        parts.append(near * jnp.where(ok, 1.0, 0.0))
    allowed = jnp.concatenate([jnp.concatenate(parts, axis=0)] * heads, axis=1)
    q_blocks = blocks(q_hat)
    g_blocks = blocks(d_attn)
    expo = jnp.exp(mm_t(keys, q_blocks)) * allowed
    prob = expo * (1.0 / jnp.sum(expo, axis=0, keepdims=True))
    weights = prob.astype(BF)
    d_w = mm_t(values, g_blocks)
    delta = jnp.sum(d_w * prob, axis=0, keepdims=True)
    d_s = (prob * (d_w - delta)).astype(BF)
    values_t = values.astype(F32).T.astype(BF)
    keys_t = keys.astype(F32).T.astype(BF)
    attn_t = []
    d_qhat_t = []
    for h in range(heads):
        feats = slice(h * head_dim, (h + 1) * head_dim)
        lanes = slice(h * tokens, (h + 1) * tokens)
        attn_t.append(mm(values_t[feats], weights[:, lanes]))
        d_qhat_t.append(mm(keys_t[feats], d_s[:, lanes]))
    attn_t = jnp.concatenate(attn_t, axis=0)
    d_qhat = jnp.concatenate(d_qhat_t, axis=0).T
    d_k = mm(d_s, q_blocks)
    d_v = mm(weights, g_blocks)

    attn = attn_t.T.astype(BF)
    y = (x_own + mm(attn, wout_ref[...])).astype(BF)
    y_ref[...] = y
    y32 = y.astype(F32)
    for part in range(width // LANES):
        yscr[part] = y32[:, part * LANES : (part + 1) * LANES].reshape(rows, cols, LANES)
    lines = []
    for i in range(rows // 2):
        pieces = []
        for pr in range(2):
            for pc in range(2):
                for part in range(width // LANES):
                    pieces.append(yscr[part, 2 * i + pr, pl.ds(pc, cols // 2, stride=2), :])
        lines.append(jnp.concatenate(pieces, axis=1))
    group = jnp.concatenate(lines, axis=0).astype(BF)
    group_ref[...] = group
    grad_out_ref[...] = mm(attn_t.astype(BF), dy_b)

    scale_part_ref[...] = jnp.broadcast_to(
        jnp.sum(q_unit * d_qhat, axis=0, keepdims=True), scale_part_ref.shape
    )
    g_unit = d_qhat * scale_row
    d_query_ref[...] = (q_norm * (g_unit - q_unit * head_sum(q_unit * g_unit, ones_ref))).astype(BF)
    d_key = k_norm * (d_k - k_unit * head_sum(k_unit * d_k, ones_ref))
    d_kv_ref[...] = jnp.concatenate([d_key, d_v], axis=1).astype(BF)


def inner_tokens(value, rows, cols):
    wide = cols + 2 * SIDE
    pieces = []
    for i in range(RADIUS, RADIUS + rows):
        pieces.append(value[i * wide + SIDE : i * wide + SIDE + cols])
    return jnp.concatenate(pieces, axis=0)


def output_kernel(y_ref, group_ref, wmerge_ref, skip_ref, merged_ref):
    skip_ref[...] = y_ref[...].reshape(skip_ref.shape)
    merged = mm(group_ref[...], wmerge_ref[...])
    merged_ref[...] = merged.astype(BF).reshape(merged_ref.shape)


def weights_kernel(
    sizes, x_ref, d_query_ref, d_kv_ref, grad_out_ref, group_ref, rows_ref, *refs
):
    rows, cols, width, n_row, n_dm = sizes
    dm_refs, dm_all_ref, sum_refs = (refs[:n_dm], refs[n_dm], refs[n_dm + 1 :])
    size = dm_all_ref.shape[0] // n_dm
    dm = [ref[...].reshape(size, dm_all_ref.shape[1]) for ref in dm_refs]
    dm_all_ref[...] = jnp.concatenate(dm[::-1], axis=0)
    x = x_ref[...]
    inverse = lax.rsqrt(jnp.mean(x * x, axis=1, keepdims=True) + EPS)
    normed32 = (x * inverse * rows_ref[0:1]).astype(BF).astype(F32)
    grad_q = mm(inner_tokens(normed32, rows, cols).T.astype(BF), d_query_ref[...])
    grad_kv = mm(normed32.T.astype(BF), d_kv_ref[...])
    sums = jnp.concatenate([grad_q, grad_kv, grad_out_ref[...]], axis=1)
    group = group_ref[...]
    if len(sum_refs) == 2:
        sum_refs[0][...] = sums.astype(BF)
        sum_refs[1][...] = group
        return
    send_ref, keep_ref, keep_group_ref = sum_refs
    per = width // n_row
    feats = 4 * width // n_row
    group = group.astype(F32)
    even = lax.rem(lax.axis_index("row"), 2) == 0
    for q in range(n_row // 2):
        parts = []
        for value, axis, size in ((sums, 0, per), (group, 1, feats)):
            first = lax.slice_in_dim(value, 2 * q * size, (2 * q + 1) * size, axis=axis)
            second = lax.slice_in_dim(value, (2 * q + 1) * size, (2 * q + 2) * size, axis=axis)
            parts.append((jnp.where(even, first, second), jnp.where(even, second, first)))
        (keep_ref[q], sums_send), (keep_group, group_send) = parts
        keep_group_ref[q] = keep_group.astype(BF)
        send_ref[q] = jnp.concatenate([sums_send, group_send], axis=1).astype(BF)


def norm_kernel(
    sizes, x_ref, d_query_ref, d_kv_ref, scale_part_ref, rows_ref, dy_ref, wqkv_ref, *refs
):
    rows, cols, width, heads = sizes
    gx_ref, side_near_ref, side_far_ref, small_ref = refs
    head_dim = width // heads
    wide = cols + 2 * SIDE
    ext_rows = rows + 2 * RADIUS
    gain = rows_ref[0:1]
    lane = lax.broadcasted_iota(jnp.int32, (1, width), 1)
    x = x_ref[...]
    inverse = lax.rsqrt(jnp.mean(x * x, axis=1, keepdims=True) + EPS)
    unit = x * inverse
    d_y = dy_ref[...]
    from_q = mm_t(d_query_ref[...], wqkv_ref[:, :width])
    d_normed = mm_t(d_kv_ref[...], wqkv_ref[:, width:])
    pieces = []
    side = jnp.zeros((SIDE, width), F32)
    for i in range(ext_rows):
        if RADIUS <= i < RADIUS + rows:
            at = (i - RADIUS) * cols
            pieces += [side, from_q[at : at + cols], side]
        else:
            pieces.append(jnp.zeros((wide, width), F32))
    d_normed = d_normed + jnp.concatenate(pieces, axis=0)
    gain_part = jnp.sum(unit * d_normed, axis=0, keepdims=True)
    scaled = gain * d_normed
    mean = jnp.mean(x * scaled, axis=1, keepdims=True)
    g_x = inverse * scaled - x * (inverse * inverse * inverse) * mean

    pieces = []
    left = []
    right = []
    for i in range(ext_rows):
        row = g_x[i * wide : (i + 1) * wide]
        middle = row[SIDE : SIDE + cols]
        if RADIUS <= i < RADIUS + rows:
            middle = middle + d_y[(i - RADIUS) * cols : (i - RADIUS + 1) * cols]
        pieces.append(middle)
        left.append(row[:SIDE][SIDE - EDGE :])
        right.append(row[SIDE + cols :][:EDGE])
    gx_ref[...] = jnp.concatenate(pieces, axis=0)
    left, right = [jnp.concatenate(part, axis=0) for part in (left, right)]
    far, near = by_side("col", right, left)
    side_near_ref[...] = near.astype(BF)
    side_far_ref[...] = far.astype(BF)
    scale_part = scale_part_ref[0:1]
    scale_lane = lax.broadcasted_iota(jnp.int32, (1, LANES), 1)
    scale_sums = jnp.zeros((1, LANES), F32)
    for h in range(heads):
        of_head = jnp.sum(jnp.where(lane // head_dim == h, scale_part, 0.0), axis=1, keepdims=True)
        scale_sums = jnp.where(scale_lane == h, of_head, scale_sums)
    small = [gain_part[:, i * LANES : (i + 1) * LANES] for i in range(width // LANES)] + [scale_sums]
    small = jnp.concatenate(small + [jnp.zeros((8 - len(small), LANES), F32)], axis=0)
    small_ref[...] = small


def small_rows(small):
    high = small.astype(BF).astype(F32)
    return jnp.concatenate([high[:4], (small - high)[:4]], axis=0)


def small_value(rows):
    value = rows.astype(BF).astype(F32)
    return value[:4] + value[4:]


def stacked(value):
    return jnp.concatenate(
        [value[:, i : i + LANES] for i in range(0, value.shape[1], LANES)], axis=0
    )


def unstacked(value, rows):
    return jnp.concatenate([value[i : i + rows] for i in range(0, value.shape[0], rows)], axis=1)


def core_sum_kernel(got_ref, keep_ref, keep_group_ref, small_ref, small_near_ref, *refs):
    *out_refs, own_ref, own_group_ref, small_sum_ref, blocks_ref = refs
    chips, per, width = keep_ref.shape
    feats = keep_group_ref.shape[2]
    small = small_ref[...] + small_near_ref[...]
    small_sum_ref[...] = small
    small = small_rows(small)
    chip = lax.axis_index("row") // 2
    own_ref[...] = keep_ref[chip] + got_ref[chip, :, :width].astype(F32)
    for q in range(chips):
        sums = keep_ref[q] + got_ref[q, :, :width].astype(F32)
        kept = keep_group_ref[q].astype(F32)
        first, second = in_order("row", kept, got_ref[q, :, width:].astype(F32))
        block = [stacked(sums), first, second, small]
        blocks_ref[q] = jnp.concatenate(block, axis=0).astype(BF)
    size = width // LANES * per
    own_group_ref[...] = blocks_ref[chip][size : size + 2 * per]
    for step, out_ref in enumerate(out_refs, 1):
        out_ref[...] = blocks_ref[partner(chip, step)]


def row_sum_kernel(sizes, *refs):
    rows, cols, width, n_col = sizes
    own_ref, own_group_ref, small_ref, *refs = refs
    got_refs, dm_ref, dm_near_ref, gx_ref, *refs = (refs[:3], *refs[3:])
    *out_refs, gx_sum_ref, slots_ref = refs
    gx_sum_ref[...] = gx_ref[...]
    per = own_ref.shape[0]
    feats = own_group_ref.shape[1]
    size = 4 * width // LANES * per

    def summed(first, part):
        fourth, third, second = [part(ref[...].astype(F32)) for ref in got_refs]
        return (first + second) + (third + fourth)

    sums = summed(stacked(own_ref[...]), lambda value: value[:size])
    sums = unstacked(sums, per)
    small = summed(small_value(small_rows(small_ref[...])), lambda value: small_value(value[size + 2 * per :]))
    group = [own_group_ref[...].astype(F32)]
    group += [ref[...].astype(F32)[size : size + 2 * per] for ref in got_refs[::-1]]
    group = [part[i * per : (i + 1) * per] for i in range(2) for part in group]
    group = jnp.concatenate(group, axis=0)
    own, near = (dm_ref[...].astype(F32), dm_near_ref[...].astype(F32))
    dm = jnp.concatenate(in_order("row", own, near), axis=0).astype(BF)
    merge = mm(group.T.astype(BF), dm)
    small = small_rows(small)
    col = lax.axis_index("col")
    third = 3 * width // n_col
    fourth = width // n_col
    depth = merge.shape[1] // n_col
    for slot in range(n_col):
        parts = [
            sums[:, slot * third : (slot + 1) * third],
            sums[:, 3 * width + slot * fourth : 3 * width + (slot + 1) * fourth],
        ]
        parts = [stacked(jnp.concatenate(parts, axis=1))]
        parts += [merge[:, slot * depth : (slot + 1) * depth], small]
        slots_ref[slot] = jnp.concatenate(parts, axis=0).astype(BF)
    for step, out_ref in enumerate(out_refs):
        out_ref[...] = slots_ref[partner(col, step)]


def partner(index, step):
    if step == 0:
        return index
    low = lax.rem(index, 2)
    if step == 1:
        return index + 1 - 2 * low
    if step == 2:
        return lax.rem(index + 2, 4)
    return 3 - index


def side_kernel(sizes, gx_ref, near_ref, far_ref, grad_ref, row_near_ref, row_far_ref):
    rows, cols, width = sizes
    ends = lax.axis_index("col")
    left, right = by_side("col", near_ref[...].astype(F32), far_ref[...].astype(F32))
    left = jnp.where(ends > 0, left, 0.0)
    right = jnp.where(ends < lax.axis_size("col") - 1, right, 0.0)
    blank = jnp.zeros((cols - 2 * EDGE, width), F32)
    pieces = []
    for i in range(rows + 2 * RADIUS):
        edge = slice(i * EDGE, (i + 1) * EDGE)
        pieces += [left[edge], blank, right[edge]]
    g_x = gx_ref[...] + jnp.concatenate(pieces, axis=0)
    reach = RADIUS * cols
    far, near = by_side("row", g_x[reach + rows * cols :], g_x[:reach])
    grad_ref[...] = g_x[reach : reach + rows * cols]
    row_near_ref[...] = near.astype(BF)
    row_far_ref[...] = far.astype(BF)


def col_sum_kernel(
    sizes,
    a_ref,
    d_ref,
    c_ref,
    b_ref,
    grad_ref,
    far_ref,
    near_ref,
    gqkv_ref,
    gout_ref,
    gmerge_ref,
    ggain_ref,
    gscale_ref,
    gtok_ref,
):
    rows, cols, width = sizes
    per, third = gqkv_ref.shape
    size = a_ref.shape[0] - 8

    def summed(part):
        first, second, third, fourth = [
            part(ref[...].astype(F32)) for ref in (a_ref, b_ref, c_ref, d_ref)
        ]
        return (first + second) + (third + fourth)

    total = summed(lambda value: value[:size])
    small = summed(lambda value: small_value(value[size:]))
    merge_at = size - gmerge_ref.shape[0]
    sums = unstacked(total[:merge_at], per)
    gqkv_ref[...] = sums[:, :third]
    gout_ref[...] = sums[:, third:]
    gmerge_ref[...] = total[merge_at:]
    ggain_ref[...] = jnp.concatenate([small[i : i + 1] for i in range(width // LANES)], axis=1)
    for h in range(gscale_ref.shape[0]):
        gscale_ref[h] = small[width // LANES, h]
    blank = jnp.zeros(((rows - RADIUS) * cols, width), F32)
    above, below = by_side("row", near_ref[...].astype(F32), far_ref[...].astype(F32))
    grad = grad_ref[...] + jnp.concatenate([above, blank], axis=0)
    grad = grad + jnp.concatenate([blank, below], axis=0)
    gtok_ref[...] = grad.astype(BF).reshape(rows, cols, width)


def plain_sums(width, sums, group, small, dm):
    sums = sums.astype(F32)
    merge = jnp.dot(group.T, dm, preferred_element_type=F32)
    outs = []
    for part in (sums[:, : 3 * width], sums[:, 3 * width :], merge):
        part = lax.psum_scatter(part, "row", scatter_dimension=0, tiled=True)
        outs.append(lax.psum_scatter(part, "col", scatter_dimension=1, tiled=True))
    small = lax.psum(small, ("row", "col"))
    return (*outs, small[: width // LANES].reshape(1, width), small[width // LANES])


def add_rows(grad, near, far, rows, cols):
    above, below = by_side("row", near.astype(F32), far.astype(F32))
    size = RADIUS * cols
    grad = grad.at[:size].add(above).at[rows * cols - size :].add(below)
    return grad.astype(BF).reshape(rows, cols, -1)


def swapped(near, far, axis):
    n_row, n_col = (lax.axis_size("row"), lax.axis_size("col"))
    pairs = []
    for row in range(n_row):
        for col in range(n_col):
            if axis == "row":
                other = row - 1 if row % 2 == 0 else row + 1
                target = (other, col) if 0 <= other < n_row else (row, col ^ 1)
            else:
                other = col - 1 if col % 2 == 0 else col + 1
                target = (row, other) if 0 <= other < n_col else (row ^ 1, col)
            pairs.append((row * n_col + col, target[0] * n_col + target[1]))
    return (swap(near, axis, 1), lax.ppermute(far, ("row", "col"), pairs))


def swap(value, axis, step):
    count = lax.axis_size(axis)
    return lax.ppermute(value, axis, [(i, i ^ step) for i in range(count)])


def vmem(count):
    return [pl.BlockSpec(memory_space=pltpu.VMEM)] * count


def on_device(tokens, gain, w_qkv, head_scale, w_out, w_merge, d_merged, d_skip):
    rows, cols, width = tokens.shape
    heads = head_scale.shape[0]
    n_row, n_col = (lax.axis_size("row"), lax.axis_size("col"))
    g_rows, g_cols, depth = d_merged.shape
    groups = g_rows * g_cols
    wide = cols + 2 * SIDE
    ext_rows = rows + 2 * RADIUS
    shape = jax.ShapeDtypeStruct
    params = pltpu.CompilerParams(vmem_limit_bytes=24 * 1024 * 1024)
    less = pltpu.CompilerParams(vmem_limit_bytes=8 * 1024 * 1024)
    row_near, row_far = swapped(tokens, tokens, "row")
    edge = shape((ext_rows * EDGE, width), BF)
    ones, parity = pl.pallas_call(
        first_kernel,
        out_shape=(shape((width, width), BF), shape((2 * heads, LANES), F32)),
        out_specs=tuple(vmem(2)),
        compiler_params=less,
        cost_estimate=pl.CostEstimate(flops=10**10, bytes_accessed=10**5, transcendentals=0),
    )()
    dm = d_merged.reshape(groups, depth)
    tile = shape((rows * cols, width), F32)
    half = shape((rows * cols, width), BF)
    edges, two_rows, q_norm, q_unit, d_y, d_attn = pl.pallas_call(
        own_kernel,
        out_shape=(shape((2 * rows * EDGE, width), BF), shape((8, width), F32), tile, tile, tile, half),
        in_specs=vmem(10),
        out_specs=tuple(vmem(6)),
        scratch_shapes=[pltpu.VMEM((width // LANES, rows, cols, LANES), F32)],
        compiler_params=params,
        cost_estimate=pl.CostEstimate(flops=10**9, bytes_accessed=10**6, transcendentals=0),
    )(
        ones,
        parity,
        head_scale.reshape(1, heads),
        tokens,
        d_merged,
        d_skip,
        gain.reshape(1, width),
        w_qkv,
        w_out,
        w_merge,
    )
    edge_near, edge_far, dm_pair = pl.pallas_call(
        edge_kernel,
        out_shape=(edge, edge, shape((2 * groups, depth), BF)),
        in_specs=vmem(5),
        out_specs=tuple(vmem(3)),
        compiler_params=less,
    )(edges, row_far, row_near, d_merged, swap(dm, "row", 2))
    dms = [swap(dm_pair, "row", 4), dm_pair]
    col_near, col_far = swapped(edge_near, edge_far, "col")

    per = width // n_row
    feats = 4 * width // n_row
    packed = per % 16 == 0 and feats % LANES == 0 and groups == per
    packed = packed and width // LANES < 4 and feats == LANES and depth // n_col == LANES and n_col == 4 and n_row == 8
    if packed:
        sum_shapes = (
            shape((n_row // 2, per, 4 * width + feats), BF),
            shape((n_row // 2, per, 4 * width), F32),
            shape((n_row // 2, per, feats), BF),
        )
    else:
        sum_shapes = (
            shape((width, 4 * width), BF),
            shape((groups, 4 * width), BF),
        )
    sizes = (rows, cols, width, heads, n_row, n_col)
    tall = ext_rows * wide
    x, y, d_query, d_kv, grad_out, group, scale_part = pl.pallas_call(
        functools.partial(layer_kernel, sizes),
        out_shape=(
            shape((tall, width), F32),
            half,
            half,
            shape((tall, 2 * width), BF),
            shape((width, width), F32),
            shape((groups, 4 * width), BF),
            shape((8, width), F32),
        ),
        in_specs=vmem(13),
        out_specs=tuple(vmem(7)),
        scratch_shapes=[pltpu.VMEM((width // LANES, rows, cols, LANES), F32)],
        compiler_params=params,
        cost_estimate=pl.CostEstimate(flops=4 * 10**9, bytes_accessed=10**6, transcendentals=0),
    )(
        ones,
        tokens,
        row_far,
        row_near,
        col_near,
        col_far,
        two_rows,
        q_norm,
        q_unit,
        d_y,
        d_attn,
        w_qkv,
        w_out,
    )
    dm_core, *sums = pl.pallas_call(
        functools.partial(weights_kernel, (rows, cols, width, n_row, len(dms))),
        out_shape=(shape((2 * len(dms) * groups, depth), BF),) + sum_shapes,
        in_specs=vmem(6 + len(dms)),
        out_specs=tuple(vmem(1 + len(sum_shapes))),
        compiler_params=params,
        cost_estimate=pl.CostEstimate(flops=10**9, bytes_accessed=10**6, transcendentals=0),
    )(x, d_query, d_kv, grad_out, group, two_rows, *dms)
    gx, *sides = pl.pallas_call(
        functools.partial(norm_kernel, (rows, cols, width, heads)),
        out_shape=(shape((ext_rows * cols, width), F32), edge, edge, shape((8, LANES), F32)),
        in_specs=vmem(7),
        out_specs=tuple(vmem(4)),
        compiler_params=params,
        cost_estimate=pl.CostEstimate(flops=5 * 10**8, bytes_accessed=10**6, transcendentals=0),
    )(x, d_query, d_kv, scale_part, two_rows, d_y, w_qkv)
    *sides, small = sides
    sides = swapped(*sides, "col")
    skip_out, merged = pl.pallas_call(
        output_kernel,
        out_shape=(shape((rows, cols, width), BF), shape((g_rows, g_cols, depth), BF)),
        in_specs=vmem(3),
        out_specs=tuple(vmem(2)),
        compiler_params=less,
        cost_estimate=pl.CostEstimate(flops=10**9, bytes_accessed=10**6, transcendentals=0),
    )(y, group, w_merge)
    reach = shape((RADIUS * cols, width), BF)
    side_call = pl.pallas_call(
        functools.partial(side_kernel, (rows, cols, width)),
        out_shape=(tile, reach, reach),
        in_specs=vmem(3),
        out_specs=tuple(vmem(3)),
        compiler_params=less,
    )
    if not packed:
        grad, *rims = side_call(gx, *sides)
        grad_tokens = add_rows(grad, *swapped(*rims, "row"), rows, cols)
        g_qkv, g_out, g_merge, g_gain, g_scale = plain_sums(width, *sums, small, dm)
    else:
        send, *kept = sums
        block = shape((4 * width // LANES * per + 2 * per + 8, LANES), BF)
        *blocks, own, own_group, small = pl.pallas_call(
            core_sum_kernel,
            out_shape=(block, block, block)
            + (shape((per, 4 * width), F32), shape((2 * per, LANES), BF), shape((8, LANES), F32)),
            in_specs=vmem(5),
            out_specs=tuple(vmem(6)),
            scratch_shapes=[pltpu.VMEM((n_row // 2,) + block.shape, BF)],
            compiler_params=less,
            cost_estimate=pl.CostEstimate(flops=5 * 10**9, bytes_accessed=10**6, transcendentals=0),
        )(swap(send, "row", 1), *kept, small, swap(small, "row", 1))
        got = [swap(blocks[step - 1], "row", 2 * step) for step in (3, 2, 1)]
        slot = shape((4 * width // n_col // LANES * per + feats + 8, LANES), BF)
        *slots, gx = pl.pallas_call(
            functools.partial(row_sum_kernel, (rows, cols, width, n_col)),
            out_shape=(slot,) * n_col + (shape(gx.shape, F32),),
            in_specs=vmem(9),
            out_specs=tuple(vmem(n_col + 1)),
            scratch_shapes=[pltpu.VMEM((n_col,) + slot.shape, BF)],
            compiler_params=less,
        )(own, own_group, small, *got, dm_core, swap(dm_core, "row", 1), gx)
        got = [slots[0]] + [swap(slots[step], "col", step) for step in (3, 2, 1)]
        grad, *rims = side_call(gx, *sides)
        rims = swapped(*rims, "row")
        g_qkv, g_out, g_merge, g_gain, g_scale, grad_tokens = pl.pallas_call(
            functools.partial(col_sum_kernel, (rows, cols, width)),
            out_shape=(
                shape((per, 3 * width // n_col), F32),
                shape((per, width // n_col), F32),
                shape((feats, depth // n_col), F32),
                shape((1, width), F32),
                shape((heads,), F32),
                shape((rows, cols, width), BF),
            ),
            in_specs=vmem(7),
            out_specs=tuple(vmem(4)) + (pl.BlockSpec(memory_space=pltpu.SMEM), vmem(1)[0]),
            compiler_params=less,
        )(*got, grad, *rims[::-1])
    return (
        skip_out,
        merged,
        grad_tokens,
        g_qkv,
        g_out,
        g_merge,
        g_gain.reshape(width),
        g_scale[:heads],
    )


def solution(mesh):
    block = P("row", "col", None)
    return jax.shard_map(
        on_device,
        mesh=mesh,
        in_specs=(block, P(), P(), P(), P(), P(), block, block),
        out_specs=(block, block, block, P("row", "col"), P("row", "col"), P("row", "col"), P(), P()),
        check_vma=False,
    )
```

```python
import functools
import jax
import jax.numpy as jnp
from jax import lax
from jax.experimental import pallas as pl
from jax.experimental.pallas import tpu as pltpu
from jax.sharding import PartitionSpec as P

RADIUS = 3
IMG_MAX = 512
EPS = 1e-06
EDGE = 4
SIDE = 8
LANES = 128
BF = jnp.bfloat16
F32 = jnp.float32


def mm(a, b):
    return lax.dot_general(a, b, (((1,), (0,)), ((), ())), preferred_element_type=F32)


def mm_t(a, b):
    return lax.dot_general(a, b, (((1,), (1,)), ((), ())), preferred_element_type=F32)


def split_two(value):
    high = value.astype(BF)
    return (high, (value - high.astype(F32)).astype(BF))


def by_side(axis, near, far):
    even = lax.rem(lax.axis_index(axis), 2) == 0
    return (jnp.where(even, far, near), jnp.where(even, near, far))


def first_kernel(ones_ref, parity_ref):
    width = ones_ref.shape[0]
    head_dim = width // (parity_ref.shape[0] // 2)
    same_head = lax.broadcasted_iota(jnp.int32, (width, width), 0) // head_dim == (
        lax.broadcasted_iota(jnp.int32, (width, width), 1) // head_dim
    )
    ones_ref[...] = jnp.where(same_head, 1.0, 0.0).astype(BF)
    half = (parity_ref.shape[0] // 2, parity_ref.shape[1])
    parts = [
        jnp.where(lax.rem(lax.axis_index(axis), 2) == 0, jnp.ones(half, F32), jnp.zeros(half, F32))
        for axis in ("row", "col")
    ]
    parity_ref[...] = jnp.concatenate(parts, axis=0)


def edge_kernel(edges_ref, near_ref, edge_near_ref, edge_far_ref):
    rows, cols, width = near_ref.shape
    near_row = near_ref[...].astype(F32)
    even = lax.rem(lax.axis_index("row"), 2) == 0
    near_row = jnp.where(even, near_row[:RADIUS], near_row[rows - RADIUS :])
    left, right = [
        near_row[:, at : at + EDGE].reshape(RADIUS * EDGE, width) for at in (0, cols - EDGE)
    ]
    far, near = by_side("col", right, left)
    for out_ref, own_at, part in ((edge_near_ref, 0, near), (edge_far_ref, rows * EDGE, far)):
        own = edges_ref[own_at : own_at + rows * EDGE].astype(F32)
        after = jnp.concatenate([own, part], axis=0)
        before = jnp.concatenate([part, own], axis=0)
        out_ref[...] = jnp.where(even, after, before).astype(BF)


def pair_kernel(dm_ref, dm_next_ref, dm_pair_ref):
    size = dm_next_ref.shape[0]
    dm_pair_ref[...] = jnp.concatenate([dm_ref[...].reshape(size, -1), dm_next_ref[...]], axis=0)


def in_order(axis, own, partner):
    even = lax.rem(lax.axis_index(axis), 2) == 0
    return (jnp.where(even, own, partner), jnp.where(even, partner, own))


def head_sum(value, ones_ref):
    high, low = split_two(value)
    return mm(high, ones_ref[...]) + mm(low, ones_ref[...])


def own_kernel(
    ones_ref,
    parity_ref,
    scale_ref,
    tok_ref,
    dm_ref,
    dskip_ref,
    gain_ref,
    wqkv_ref,
    wout_ref,
    wmerge_ref,
    edges_ref,
    corner_near_ref,
    corner_far_ref,
    rows_ref,
    q_norm_ref,
    q_unit_ref,
    dy_ref,
    d_attn_ref,
    dscr,
):
    rows, cols, width = tok_ref.shape
    tokens = rows * cols
    tok = tok_ref[...].astype(F32)
    left = tok[:, :EDGE].reshape(rows * EDGE, width)
    right = tok[:, cols - EDGE :].reshape(rows * EDGE, width)
    heads = scale_ref.shape[1]
    even = parity_ref[heads : heads + 1, 0:1] > 0.5
    near, far = (jnp.where(even, right, left), jnp.where(even, left, right))
    edges_ref[...] = jnp.concatenate([near, far], axis=0).astype(BF)
    even_row = parity_ref[0:1, 0:1] > 0.5
    reach = RADIUS * EDGE
    for out_ref, part in ((corner_near_ref, near), (corner_far_ref, far)):
        out_ref[...] = jnp.where(even_row, part[:reach], part[rows * EDGE - reach :]).astype(BF)
    lane = lax.broadcasted_iota(jnp.int32, (1, width), 1)
    scale_row = jnp.zeros((1, width), F32)
    for h in range(heads):
        scale_row = jnp.where(lane // (width // heads) == h, scale_ref[:, h : h + 1], scale_row)
    blank = jnp.zeros((6, width), F32)
    rows_ref[...] = jnp.concatenate([gain_ref[...], scale_row, blank], axis=0)
    x = tok.reshape(tokens, width)
    inverse = lax.rsqrt(jnp.mean(x * x, axis=1, keepdims=True) + EPS)
    normed = (x * inverse * gain_ref[...]).astype(BF)
    query = mm(normed, wqkv_ref[:, :width])
    q_norm = lax.rsqrt(head_sum(query * query, ones_ref) + EPS)
    q_norm_ref[...] = q_norm
    q_unit_ref[...] = query * q_norm
    group_wide = cols // 2
    d_in = mm_t(dm_ref[...].reshape(-1, dm_ref.shape[2]), wmerge_ref[...])
    for i in range(rows // 2):
        for pr in range(2):
            for pc in range(2):
                for part in range(width // LANES):
                    at = (2 * pr + pc) * width + part * LANES
                    dscr[part, 2 * i + pr, pl.ds(pc, group_wide, stride=2), :] = d_in[
                        i * group_wide : (i + 1) * group_wide, at : at + LANES
                    ]
    d_group = jnp.concatenate(
        [dscr[part].reshape(tokens, LANES) for part in range(width // LANES)], axis=1
    )
    d_y = dskip_ref[...].reshape(tokens, width).astype(F32) + d_group
    dy_ref[...] = d_y
    d_attn_ref[...] = mm_t(d_y.astype(BF), wout_ref[...]).astype(BF)


def layer_kernel(
    sizes,
    ones_ref,
    tok_ref,
    row_far_ref,
    row_near_ref,
    col_near_ref,
    col_far_ref,
    corner_near_ref,
    corner_far_ref,
    rows_ref,
    q_norm_ref,
    q_unit_ref,
    dy_ref,
    d_attn_ref,
    wqkv_ref,
    wout_ref,
    x_ref,
    y_ref,
    d_query_ref,
    d_kv_ref,
    grad_out_ref,
    group_ref,
    scale_part_ref,
    yscr,
):
    rows, cols, width, heads, n_row, n_col = sizes
    head_dim = width // heads
    wide = cols + 2 * SIDE
    ext_rows = rows + 2 * RADIUS
    tokens = rows * cols
    image_rows = min(IMG_MAX, rows * n_row)
    row_start = lax.axis_index("row") * rows
    col_index = lax.axis_index("col")
    col_start = col_index * cols
    first = row_start // image_rows * image_rows

    lane = lax.broadcasted_iota(jnp.int32, (1, width), 1)
    def blocks(value):
        zero = jnp.zeros_like(value)
        kept = [jnp.where(lane // head_dim == h, value, zero) for h in range(heads)]
        return jnp.concatenate(kept, axis=0).astype(BF)

    gain = rows_ref[0:1]
    scale_row = rows_ref[1:2]
    up, down = by_side("row", row_near_ref[...].astype(F32), row_far_ref[...].astype(F32))
    even = lax.rem(lax.axis_index("row"), 2) == 0
    sides = []
    for col_ref, corner_ref in ((col_near_ref, corner_near_ref), (col_far_ref, corner_far_ref)):
        col, corner = (col_ref[...].astype(F32), corner_ref[...].astype(F32))
        above = jnp.concatenate([corner, col], axis=0)
        below = jnp.concatenate([col, corner], axis=0)
        sides.append(jnp.where(even, above, below))
    left, right = by_side("col", *sides)
    own = tok_ref[...].astype(F32)
    blank = jnp.zeros((SIDE - EDGE, width), F32)
    pieces = []
    for i in range(ext_rows):
        if i < RADIUS:
            row = up[rows - RADIUS + i]
        elif i < RADIUS + rows:
            row = own[i - RADIUS]
        else:
            row = down[i - RADIUS - rows]
        edge = slice(i * EDGE, (i + 1) * EDGE)
        pieces += [blank, left[edge], row, right[edge], blank]
    x = jnp.concatenate(pieces, axis=0)
    x_ref[...] = x
    inverse = lax.rsqrt(jnp.mean(x * x, axis=1, keepdims=True) + EPS)
    unit = x * inverse
    normed32 = (unit * gain).astype(BF).astype(F32)
    normed = normed32.astype(BF)
    x_own = inner_tokens(x, rows, cols)
    kv = mm(normed, wqkv_ref[:, width:])
    key_raw = kv[:, :width]
    k_norm = lax.rsqrt(head_sum(key_raw * key_raw, ones_ref) + EPS)
    k_unit = key_raw * k_norm
    keys = k_unit.astype(BF)
    values = kv[:, width:].astype(BF)
    q_norm = q_norm_ref[...]
    q_unit = q_unit_ref[...]
    q_hat = (q_unit * scale_row).astype(BF).astype(F32)
    d_y = dy_ref[...]
    dy_b = d_y.astype(BF)
    d_attn = d_attn_ref[...].astype(F32)

    index = lax.broadcasted_iota(jnp.int32, (1, tokens), 1)
    q_row = jnp.zeros_like(index)
    for i in range(1, rows):
        q_row = q_row + (index >= i * cols).astype(jnp.int32)
    q_col = index - q_row * cols
    key_col = lax.broadcasted_iota(jnp.int32, (wide, tokens), 0) - SIDE
    near = (key_col - q_col <= RADIUS) & (key_col - q_col >= -RADIUS)
    near = near & (key_col + col_start >= 0) & (key_col + col_start < cols * n_col)
    near = jnp.where(near, 1.0, 0.0)
    parts = []
    for i in range(-RADIUS, rows + RADIUS):
        ok = (q_row - i <= RADIUS) & (q_row - i >= -RADIUS)
        ok = ok & (row_start + i >= first) & (row_start + i < first + image_rows)
        parts.append(near * jnp.where(ok, 1.0, 0.0))
    allowed = jnp.concatenate([jnp.concatenate(parts, axis=0)] * heads, axis=1)
    q_blocks = blocks(q_hat)
    g_blocks = blocks(d_attn)
    expo = jnp.exp(mm_t(keys, q_blocks)) * allowed
    prob = expo * (1.0 / jnp.sum(expo, axis=0, keepdims=True))
    weights = prob.astype(BF)
    d_w = mm_t(values, g_blocks)
    delta = jnp.sum(d_w * prob, axis=0, keepdims=True)
    d_s = (prob * (d_w - delta)).astype(BF)
    values_t = values.astype(F32).T.astype(BF)
    keys_t = keys.astype(F32).T.astype(BF)
    attn_t = []
    d_qhat_t = []
    for h in range(heads):
        feats = slice(h * head_dim, (h + 1) * head_dim)
        lanes = slice(h * tokens, (h + 1) * tokens)
        attn_t.append(mm(values_t[feats], weights[:, lanes]))
        d_qhat_t.append(mm(keys_t[feats], d_s[:, lanes]))
    attn_t = jnp.concatenate(attn_t, axis=0)
    d_qhat = jnp.concatenate(d_qhat_t, axis=0).T
    d_k = mm(d_s, q_blocks)
    d_v = mm(weights, g_blocks)

    attn = attn_t.T.astype(BF)
    y = (x_own + mm(attn, wout_ref[...])).astype(BF)
    y_ref[...] = y
    y32 = y.astype(F32)
    for part in range(width // LANES):
        yscr[part] = y32[:, part * LANES : (part + 1) * LANES].reshape(rows, cols, LANES)
    lines = []
    for i in range(rows // 2):
        pieces = []
        for pr in range(2):
            for pc in range(2):
                for part in range(width // LANES):
                    pieces.append(yscr[part, 2 * i + pr, pl.ds(pc, cols // 2, stride=2), :])
        lines.append(jnp.concatenate(pieces, axis=1))
    group = jnp.concatenate(lines, axis=0).astype(BF)
    group_ref[...] = group
    grad_out_ref[...] = mm(attn_t.astype(BF), dy_b)

    scale_part_ref[...] = jnp.broadcast_to(
        jnp.sum(q_unit * d_qhat, axis=0, keepdims=True), scale_part_ref.shape
    )
    g_unit = d_qhat * scale_row
    d_query_ref[...] = (q_norm * (g_unit - q_unit * head_sum(q_unit * g_unit, ones_ref))).astype(BF)
    d_key = k_norm * (d_k - k_unit * head_sum(k_unit * d_k, ones_ref))
    d_kv_ref[...] = jnp.concatenate([d_key, d_v], axis=1).astype(BF)


def inner_tokens(value, rows, cols):
    wide = cols + 2 * SIDE
    pieces = []
    for i in range(RADIUS, RADIUS + rows):
        pieces.append(value[i * wide + SIDE : i * wide + SIDE + cols])
    return jnp.concatenate(pieces, axis=0)


def output_kernel(y_ref, group_ref, wmerge_ref, skip_ref, merged_ref):
    skip_ref[...] = y_ref[...].reshape(skip_ref.shape)
    merged = mm(group_ref[...], wmerge_ref[...])
    merged_ref[...] = merged.astype(BF).reshape(merged_ref.shape)


def weights_kernel(
    sizes, x_ref, d_query_ref, d_kv_ref, grad_out_ref, group_ref, rows_ref, *refs
):
    rows, cols, width, n_row, n_dm = sizes
    dm_refs, dm_all_ref, sum_refs = (refs[:n_dm], refs[n_dm], refs[n_dm + 1 :])
    size = dm_all_ref.shape[0] // n_dm
    dm = [ref[...].reshape(size, dm_all_ref.shape[1]) for ref in dm_refs]
    dm_all_ref[...] = jnp.concatenate(dm[::-1], axis=0)
    x = x_ref[...]
    inverse = lax.rsqrt(jnp.mean(x * x, axis=1, keepdims=True) + EPS)
    normed32 = (x * inverse * rows_ref[0:1]).astype(BF).astype(F32)
    grad_q = mm(inner_tokens(normed32, rows, cols).T.astype(BF), d_query_ref[...])
    grad_kv = mm(normed32.T.astype(BF), d_kv_ref[...])
    sums = jnp.concatenate([grad_q, grad_kv, grad_out_ref[...]], axis=1)
    group = group_ref[...]
    if len(sum_refs) == 2:
        sum_refs[0][...] = sums.astype(BF)
        sum_refs[1][...] = group
        return
    send_ref, keep_ref, keep_group_ref = sum_refs
    per = width // n_row
    feats = 4 * width // n_row
    group = group.astype(F32)
    even = lax.rem(lax.axis_index("row"), 2) == 0
    for q in range(n_row // 2):
        parts = []
        for value, axis, size in ((sums, 0, per), (group, 1, feats)):
            first = lax.slice_in_dim(value, 2 * q * size, (2 * q + 1) * size, axis=axis)
            second = lax.slice_in_dim(value, (2 * q + 1) * size, (2 * q + 2) * size, axis=axis)
            parts.append((jnp.where(even, first, second), jnp.where(even, second, first)))
        (keep_ref[q], sums_send), (keep_group, group_send) = parts
        keep_group_ref[q] = keep_group.astype(BF)
        send_ref[q] = jnp.concatenate([sums_send, group_send], axis=1).astype(BF)


def norm_kernel(
    sizes, x_ref, d_query_ref, d_kv_ref, scale_part_ref, rows_ref, dy_ref, wqkv_ref, *refs
):
    rows, cols, width, heads = sizes
    gx_ref, side_near_ref, side_far_ref, small_ref = refs
    head_dim = width // heads
    wide = cols + 2 * SIDE
    ext_rows = rows + 2 * RADIUS
    gain = rows_ref[0:1]
    lane = lax.broadcasted_iota(jnp.int32, (1, width), 1)
    x = x_ref[...]
    inverse = lax.rsqrt(jnp.mean(x * x, axis=1, keepdims=True) + EPS)
    unit = x * inverse
    d_y = dy_ref[...]
    from_q = mm_t(d_query_ref[...], wqkv_ref[:, :width])
    d_normed = mm_t(d_kv_ref[...], wqkv_ref[:, width:])
    pieces = []
    side = jnp.zeros((SIDE, width), F32)
    for i in range(ext_rows):
        if RADIUS <= i < RADIUS + rows:
            at = (i - RADIUS) * cols
            pieces += [side, from_q[at : at + cols], side]
        else:
            pieces.append(jnp.zeros((wide, width), F32))
    d_normed = d_normed + jnp.concatenate(pieces, axis=0)
    gain_part = jnp.sum(unit * d_normed, axis=0, keepdims=True)
    scaled = gain * d_normed
    mean = jnp.mean(x * scaled, axis=1, keepdims=True)
    g_x = inverse * scaled - x * (inverse * inverse * inverse) * mean

    pieces = []
    left = []
    right = []
    for i in range(ext_rows):
        row = g_x[i * wide : (i + 1) * wide]
        middle = row[SIDE : SIDE + cols]
        if RADIUS <= i < RADIUS + rows:
            middle = middle + d_y[(i - RADIUS) * cols : (i - RADIUS + 1) * cols]
        pieces.append(middle)
        left.append(row[:SIDE][SIDE - EDGE :])
        right.append(row[SIDE + cols :][:EDGE])
    gx_ref[...] = jnp.concatenate(pieces, axis=0)
    left, right = [jnp.concatenate(part, axis=0) for part in (left, right)]
    far, near = by_side("col", right, left)
    side_near_ref[...] = near.astype(BF)
    side_far_ref[...] = far.astype(BF)
    scale_part = scale_part_ref[0:1]
    scale_lane = lax.broadcasted_iota(jnp.int32, (1, LANES), 1)
    scale_sums = jnp.zeros((1, LANES), F32)
    for h in range(heads):
        of_head = jnp.sum(jnp.where(lane // head_dim == h, scale_part, 0.0), axis=1, keepdims=True)
        scale_sums = jnp.where(scale_lane == h, of_head, scale_sums)
    small = [gain_part[:, i * LANES : (i + 1) * LANES] for i in range(width // LANES)] + [scale_sums]
    small = jnp.concatenate(small + [jnp.zeros((8 - len(small), LANES), F32)], axis=0)
    small_ref[...] = small


def small_rows(small):
    high = small.astype(BF).astype(F32)
    return jnp.concatenate([high[:4], (small - high)[:4]], axis=0)


def small_value(rows):
    value = rows.astype(BF).astype(F32)
    return value[:4] + value[4:]


def stacked(value):
    return jnp.concatenate(
        [value[:, i : i + LANES] for i in range(0, value.shape[1], LANES)], axis=0
    )


def unstacked(value, rows):
    return jnp.concatenate([value[i : i + rows] for i in range(0, value.shape[0], rows)], axis=1)


def core_sum_kernel(got_ref, keep_ref, keep_group_ref, small_ref, small_near_ref, *refs):
    *out_refs, own_ref, own_group_ref, small_sum_ref, blocks_ref = refs
    chips, per, width = keep_ref.shape
    feats = keep_group_ref.shape[2]
    small = small_ref[...] + small_near_ref[...]
    small_sum_ref[...] = small
    small = small_rows(small)
    chip = lax.axis_index("row") // 2
    own_ref[...] = keep_ref[chip] + got_ref[chip, :, :width].astype(F32)
    for q in range(chips):
        sums = keep_ref[q] + got_ref[q, :, :width].astype(F32)
        kept = keep_group_ref[q].astype(F32)
        first, second = in_order("row", kept, got_ref[q, :, width:].astype(F32))
        block = [stacked(sums), first, second, small]
        blocks_ref[q] = jnp.concatenate(block, axis=0).astype(BF)
    size = width // LANES * per
    own_group_ref[...] = blocks_ref[chip][size : size + 2 * per]
    for step, out_ref in enumerate(out_refs, 1):
        out_ref[...] = blocks_ref[partner(chip, step)]


def row_sum_kernel(sizes, *refs):
    rows, cols, width, n_col = sizes
    own_ref, own_group_ref, small_ref, *refs = refs
    got_refs, dm_ref, dm_near_ref, gx_ref, *refs = (refs[:3], *refs[3:])
    *out_refs, gx_sum_ref, slots_ref = refs
    gx_sum_ref[...] = gx_ref[...]
    per = own_ref.shape[0]
    feats = own_group_ref.shape[1]
    size = 4 * width // LANES * per

    def summed(first, part):
        fourth, third, second = [part(ref[...].astype(F32)) for ref in got_refs]
        return (first + second) + (third + fourth)

    sums = summed(stacked(own_ref[...]), lambda value: value[:size])
    sums = unstacked(sums, per)
    small = summed(small_value(small_rows(small_ref[...])), lambda value: small_value(value[size + 2 * per :]))
    group = [own_group_ref[...].astype(F32)]
    group += [ref[...].astype(F32)[size : size + 2 * per] for ref in got_refs[::-1]]
    group = [part[i * per : (i + 1) * per] for i in range(2) for part in group]
    group = jnp.concatenate(group, axis=0)
    own, near = (dm_ref[...].astype(F32), dm_near_ref[...].astype(F32))
    dm = jnp.concatenate(in_order("row", own, near), axis=0).astype(BF)
    merge = mm(group.T.astype(BF), dm)
    small = small_rows(small)
    col = lax.axis_index("col")
    third = 3 * width // n_col
    fourth = width // n_col
    depth = merge.shape[1] // n_col
    for slot in range(n_col):
        parts = [
            sums[:, slot * third : (slot + 1) * third],
            sums[:, 3 * width + slot * fourth : 3 * width + (slot + 1) * fourth],
        ]
        parts = [stacked(jnp.concatenate(parts, axis=1))]
        parts += [merge[:, slot * depth : (slot + 1) * depth], small]
        slots_ref[slot] = jnp.concatenate(parts, axis=0).astype(BF)
    for step, out_ref in enumerate(out_refs):
        out_ref[...] = slots_ref[partner(col, step)]


def partner(index, step):
    if step == 0:
        return index
    low = lax.rem(index, 2)
    if step == 1:
        return index + 1 - 2 * low
    if step == 2:
        return lax.rem(index + 2, 4)
    return 3 - index


def side_kernel(sizes, gx_ref, near_ref, far_ref, grad_ref, row_near_ref, row_far_ref):
    rows, cols, width = sizes
    ends = lax.axis_index("col")
    left, right = by_side("col", near_ref[...].astype(F32), far_ref[...].astype(F32))
    left = jnp.where(ends > 0, left, 0.0)
    right = jnp.where(ends < lax.axis_size("col") - 1, right, 0.0)
    blank = jnp.zeros((cols - 2 * EDGE, width), F32)
    pieces = []
    for i in range(rows + 2 * RADIUS):
        edge = slice(i * EDGE, (i + 1) * EDGE)
        pieces += [left[edge], blank, right[edge]]
    g_x = gx_ref[...] + jnp.concatenate(pieces, axis=0)
    reach = RADIUS * cols
    far, near = by_side("row", g_x[reach + rows * cols :], g_x[:reach])
    grad_ref[...] = g_x[reach : reach + rows * cols]
    row_near_ref[...] = near.astype(BF)
    row_far_ref[...] = far.astype(BF)


def col_sum_kernel(
    sizes,
    a_ref,
    d_ref,
    c_ref,
    b_ref,
    grad_ref,
    far_ref,
    near_ref,
    gqkv_ref,
    gout_ref,
    gmerge_ref,
    ggain_ref,
    gscale_ref,
    gtok_ref,
):
    rows, cols, width = sizes
    per, third = gqkv_ref.shape
    size = a_ref.shape[0] - 8

    def summed(part):
        first, second, third, fourth = [
            part(ref[...].astype(F32)) for ref in (a_ref, b_ref, c_ref, d_ref)
        ]
        return (first + second) + (third + fourth)

    total = summed(lambda value: value[:size])
    small = summed(lambda value: small_value(value[size:]))
    merge_at = size - gmerge_ref.shape[0]
    sums = unstacked(total[:merge_at], per)
    gqkv_ref[...] = sums[:, :third]
    gout_ref[...] = sums[:, third:]
    gmerge_ref[...] = total[merge_at:]
    ggain_ref[...] = jnp.concatenate([small[i : i + 1] for i in range(width // LANES)], axis=1)
    for h in range(gscale_ref.shape[0]):
        gscale_ref[h] = small[width // LANES, h]
    blank = jnp.zeros(((rows - RADIUS) * cols, width), F32)
    above, below = by_side("row", near_ref[...].astype(F32), far_ref[...].astype(F32))
    grad = grad_ref[...] + jnp.concatenate([above, blank], axis=0)
    grad = grad + jnp.concatenate([blank, below], axis=0)
    gtok_ref[...] = grad.astype(BF).reshape(rows, cols, width)


def plain_sums(width, sums, group, small, dm):
    sums = sums.astype(F32)
    merge = jnp.dot(group.T, dm, preferred_element_type=F32)
    outs = []
    for part in (sums[:, : 3 * width], sums[:, 3 * width :], merge):
        part = lax.psum_scatter(part, "row", scatter_dimension=0, tiled=True)
        outs.append(lax.psum_scatter(part, "col", scatter_dimension=1, tiled=True))
    small = lax.psum(small, ("row", "col"))
    return (*outs, small[: width // LANES].reshape(1, width), small[width // LANES])


def add_rows(grad, near, far, rows, cols):
    above, below = by_side("row", near.astype(F32), far.astype(F32))
    size = RADIUS * cols
    grad = grad.at[:size].add(above).at[rows * cols - size :].add(below)
    return grad.astype(BF).reshape(rows, cols, -1)


def swapped(near, far, axis):
    n_row, n_col = (lax.axis_size("row"), lax.axis_size("col"))
    pairs = []
    for row in range(n_row):
        for col in range(n_col):
            if axis == "row":
                other = row - 1 if row % 2 == 0 else row + 1
                target = (other, col) if 0 <= other < n_row else (row, col ^ 1)
            else:
                other = col - 1 if col % 2 == 0 else col + 1
                target = (row, other) if 0 <= other < n_col else (row ^ 1, col)
            pairs.append((row * n_col + col, target[0] * n_col + target[1]))
    return (swap(near, axis, 1), lax.ppermute(far, ("row", "col"), pairs))


def far_place(index, count):
    other = index - 1 if index % 2 == 0 else index + 1
    return other if 0 <= other < count else index


def corner_swapped(value, far_col):
    n_row, n_col = (lax.axis_size("row"), lax.axis_size("col"))
    pairs = []
    for row in range(n_row):
        for col in range(n_col):
            target = (far_place(row, n_row), far_place(col, n_col) if far_col else col ^ 1)
            if target == (row, col):
                target = (n_row - 1 - row, col)
            pairs.append((row * n_col + col, target[0] * n_col + target[1]))
    return lax.ppermute(value, ("row", "col"), pairs)


def swap(value, axis, step):
    count = lax.axis_size(axis)
    return lax.ppermute(value, axis, [(i, i ^ step) for i in range(count)])


def vmem(count):
    return [pl.BlockSpec(memory_space=pltpu.VMEM)] * count


def on_device(tokens, gain, w_qkv, head_scale, w_out, w_merge, d_merged, d_skip):
    rows, cols, width = tokens.shape
    heads = head_scale.shape[0]
    n_row, n_col = (lax.axis_size("row"), lax.axis_size("col"))
    g_rows, g_cols, depth = d_merged.shape
    groups = g_rows * g_cols
    wide = cols + 2 * SIDE
    ext_rows = rows + 2 * RADIUS
    shape = jax.ShapeDtypeStruct
    params = pltpu.CompilerParams(vmem_limit_bytes=24 * 1024 * 1024)
    less = pltpu.CompilerParams(vmem_limit_bytes=8 * 1024 * 1024)
    row_near, row_far = swapped(tokens, tokens, "row")
    edge = shape((ext_rows * EDGE, width), BF)
    ones, parity = pl.pallas_call(
        first_kernel,
        out_shape=(shape((width, width), BF), shape((2 * heads, LANES), F32)),
        out_specs=tuple(vmem(2)),
        compiler_params=less,
        cost_estimate=pl.CostEstimate(flops=10**10, bytes_accessed=10**5, transcendentals=0),
    )()
    dm = d_merged.reshape(groups, depth)
    tile = shape((rows * cols, width), F32)
    half = shape((rows * cols, width), BF)
    corner = shape((RADIUS * EDGE, width), BF)
    edges, *corners, two_rows, q_norm, q_unit, d_y, d_attn = pl.pallas_call(
        own_kernel,
        out_shape=(shape((2 * rows * EDGE, width), BF), corner, corner)
        + (shape((8, width), F32), tile, tile, tile, half),
        in_specs=vmem(10),
        out_specs=tuple(vmem(8)),
        scratch_shapes=[pltpu.VMEM((width // LANES, rows, cols, LANES), F32)],
        compiler_params=params,
        cost_estimate=pl.CostEstimate(flops=10**9, bytes_accessed=10**6, transcendentals=0),
    )(
        ones,
        parity,
        head_scale.reshape(1, heads),
        tokens,
        d_merged,
        d_skip,
        gain.reshape(1, width),
        w_qkv,
        w_out,
        w_merge,
    )
    half_edge = shape(((rows + RADIUS) * EDGE, width), BF)
    edge_near, edge_far = pl.pallas_call(
        edge_kernel,
        out_shape=(half_edge, half_edge),
        in_specs=vmem(2),
        out_specs=tuple(vmem(2)),
        compiler_params=less,
    )(edges, row_near)
    corners = [corner_swapped(value, bool(i)) for i, value in enumerate(corners)]
    dm_pair = pl.pallas_call(
        pair_kernel,
        out_shape=shape((2 * groups, depth), BF),
        in_specs=vmem(2),
        out_specs=vmem(1)[0],
        compiler_params=less,
    )(d_merged, swap(dm, "row", 2))
    dms = [swap(dm_pair, "row", 4), dm_pair]
    col_near, col_far = swapped(edge_near, edge_far, "col")

    per = width // n_row
    feats = 4 * width // n_row
    packed = per % 16 == 0 and feats % LANES == 0 and groups == per
    packed = packed and width // LANES < 4 and feats == LANES and depth // n_col == LANES and n_col == 4 and n_row == 8
    if packed:
        sum_shapes = (
            shape((n_row // 2, per, 4 * width + feats), BF),
            shape((n_row // 2, per, 4 * width), F32),
            shape((n_row // 2, per, feats), BF),
        )
    else:
        sum_shapes = (
            shape((width, 4 * width), BF),
            shape((groups, 4 * width), BF),
        )
    sizes = (rows, cols, width, heads, n_row, n_col)
    tall = ext_rows * wide
    x, y, d_query, d_kv, grad_out, group, scale_part = pl.pallas_call(
        functools.partial(layer_kernel, sizes),
        out_shape=(
            shape((tall, width), F32),
            half,
            half,
            shape((tall, 2 * width), BF),
            shape((width, width), F32),
            shape((groups, 4 * width), BF),
            shape((8, width), F32),
        ),
        in_specs=vmem(15),
        out_specs=tuple(vmem(7)),
        scratch_shapes=[pltpu.VMEM((width // LANES, rows, cols, LANES), F32)],
        compiler_params=params,
        cost_estimate=pl.CostEstimate(flops=4 * 10**9, bytes_accessed=10**6, transcendentals=0),
    )(
        ones,
        tokens,
        row_far,
        row_near,
        col_near,
        col_far,
        *corners,
        two_rows,
        q_norm,
        q_unit,
        d_y,
        d_attn,
        w_qkv,
        w_out,
    )
    dm_core, *sums = pl.pallas_call(
        functools.partial(weights_kernel, (rows, cols, width, n_row, len(dms))),
        out_shape=(shape((2 * len(dms) * groups, depth), BF),) + sum_shapes,
        in_specs=vmem(6 + len(dms)),
        out_specs=tuple(vmem(1 + len(sum_shapes))),
        compiler_params=params,
        cost_estimate=pl.CostEstimate(flops=10**9, bytes_accessed=10**6, transcendentals=0),
    )(x, d_query, d_kv, grad_out, group, two_rows, *dms)
    gx, *sides = pl.pallas_call(
        functools.partial(norm_kernel, (rows, cols, width, heads)),
        out_shape=(shape((ext_rows * cols, width), F32), edge, edge, shape((8, LANES), F32)),
        in_specs=vmem(7),
        out_specs=tuple(vmem(4)),
        compiler_params=params,
        cost_estimate=pl.CostEstimate(flops=5 * 10**8, bytes_accessed=10**6, transcendentals=0),
    )(x, d_query, d_kv, scale_part, two_rows, d_y, w_qkv)
    *sides, small = sides
    sides = swapped(*sides, "col")
    skip_out, merged = pl.pallas_call(
        output_kernel,
        out_shape=(shape((rows, cols, width), BF), shape((g_rows, g_cols, depth), BF)),
        in_specs=vmem(3),
        out_specs=tuple(vmem(2)),
        compiler_params=less,
        cost_estimate=pl.CostEstimate(flops=10**9, bytes_accessed=10**6, transcendentals=0),
    )(y, group, w_merge)
    reach = shape((RADIUS * cols, width), BF)
    side_call = pl.pallas_call(
        functools.partial(side_kernel, (rows, cols, width)),
        out_shape=(tile, reach, reach),
        in_specs=vmem(3),
        out_specs=tuple(vmem(3)),
        compiler_params=less,
    )
    if not packed:
        grad, *rims = side_call(gx, *sides)
        grad_tokens = add_rows(grad, *swapped(*rims, "row"), rows, cols)
        g_qkv, g_out, g_merge, g_gain, g_scale = plain_sums(width, *sums, small, dm)
    else:
        send, *kept = sums
        block = shape((4 * width // LANES * per + 2 * per + 8, LANES), BF)
        *blocks, own, own_group, small = pl.pallas_call(
            core_sum_kernel,
            out_shape=(block, block, block)
            + (shape((per, 4 * width), F32), shape((2 * per, LANES), BF), shape((8, LANES), F32)),
            in_specs=vmem(5),
            out_specs=tuple(vmem(6)),
            scratch_shapes=[pltpu.VMEM((n_row // 2,) + block.shape, BF)],
            compiler_params=less,
            cost_estimate=pl.CostEstimate(flops=5 * 10**9, bytes_accessed=10**6, transcendentals=0),
        )(swap(send, "row", 1), *kept, small, swap(small, "row", 1))
        got = [swap(blocks[step - 1], "row", 2 * step) for step in (3, 2, 1)]
        slot = shape((4 * width // n_col // LANES * per + feats + 8, LANES), BF)
        *slots, gx = pl.pallas_call(
            functools.partial(row_sum_kernel, (rows, cols, width, n_col)),
            out_shape=(slot,) * n_col + (shape(gx.shape, F32),),
            in_specs=vmem(9),
            out_specs=tuple(vmem(n_col + 1)),
            scratch_shapes=[pltpu.VMEM((n_col,) + slot.shape, BF)],
            compiler_params=less,
        )(own, own_group, small, *got, dm_core, swap(dm_core, "row", 1), gx)
        got = [slots[0]] + [swap(slots[step], "col", step) for step in (3, 2, 1)]
        grad, *rims = side_call(gx, *sides)
        rims = swapped(*rims, "row")
        g_qkv, g_out, g_merge, g_gain, g_scale, grad_tokens = pl.pallas_call(
            functools.partial(col_sum_kernel, (rows, cols, width)),
            out_shape=(
                shape((per, 3 * width // n_col), F32),
                shape((per, width // n_col), F32),
                shape((feats, depth // n_col), F32),
                shape((1, width), F32),
                shape((heads,), F32),
                shape((rows, cols, width), BF),
            ),
            in_specs=vmem(7),
            out_specs=tuple(vmem(4)) + (pl.BlockSpec(memory_space=pltpu.SMEM), vmem(1)[0]),
            compiler_params=less,
        )(*got, grad, *rims[::-1])
    return (
        skip_out,
        merged,
        grad_tokens,
        g_qkv,
        g_out,
        g_merge,
        g_gain.reshape(width),
        g_scale[:heads],
    )


def solution(mesh):
    block = P("row", "col", None)
    return jax.shard_map(
        on_device,
        mesh=mesh,
        in_specs=(block, P(), P(), P(), P(), P(), block, block),
        out_specs=(block, block, block, P("row", "col"), P("row", "col"), P("row", "col"), P(), P()),
        check_vma=False,
    )
```

```python
import functools
import jax
import jax.numpy as jnp
from jax import lax
from jax.experimental import pallas as pl
from jax.experimental.pallas import tpu as pltpu
from jax.sharding import PartitionSpec as P

RADIUS = 3
IMG_MAX = 512
EPS = 1e-06
EDGE = 4
SIDE = 8
LANES = 128
BF = jnp.bfloat16
F32 = jnp.float32


def mm(a, b):
    return lax.dot_general(a, b, (((1,), (0,)), ((), ())), preferred_element_type=F32)


def mm_t(a, b):
    return lax.dot_general(a, b, (((1,), (1,)), ((), ())), preferred_element_type=F32)


def split_two(value):
    high = value.astype(BF)
    return (high, (value - high.astype(F32)).astype(BF))


def by_side(axis, near, far):
    even = lax.rem(lax.axis_index(axis), 2) == 0
    return (jnp.where(even, far, near), jnp.where(even, near, far))


def first_kernel(ones_ref, parity_ref):
    width = ones_ref.shape[0]
    head_dim = width // (parity_ref.shape[0] // 2)
    same_head = lax.broadcasted_iota(jnp.int32, (width, width), 0) // head_dim == (
        lax.broadcasted_iota(jnp.int32, (width, width), 1) // head_dim
    )
    ones_ref[...] = jnp.where(same_head, 1.0, 0.0).astype(BF)
    half = (parity_ref.shape[0] // 2, parity_ref.shape[1])
    parts = [
        jnp.where(lax.rem(lax.axis_index(axis), 2) == 0, jnp.ones(half, F32), jnp.zeros(half, F32))
        for axis in ("row", "col")
    ]
    parity_ref[...] = jnp.concatenate(parts, axis=0)


def edge_kernel(
    edges_ref, far_ref, near_ref, dm_ref, dm_next_ref, edge_near_ref, edge_far_ref, dm_pair_ref
):
    rows, cols, width = near_ref.shape
    size = dm_next_ref.shape[0]
    dm_pair_ref[...] = jnp.concatenate([dm_ref[...].reshape(size, -1), dm_next_ref[...]], axis=0)
    up, down = by_side("row", near_ref[...].astype(F32), far_ref[...].astype(F32))
    up = up[rows - RADIUS :]
    down = down[:RADIUS]
    halo = []
    for at in (0, cols - EDGE):
        parts = [part[:, at : at + EDGE].reshape(RADIUS * EDGE, width) for part in (up, down)]
        halo.append(jnp.concatenate(parts, axis=0))
    far, near = by_side("col", halo[1], halo[0])
    for out_ref, own_at, part in ((edge_near_ref, 0, near), (edge_far_ref, rows * EDGE, far)):
        own = edges_ref[own_at : own_at + rows * EDGE].astype(F32)
        size = RADIUS * EDGE
        out_ref[...] = jnp.concatenate([part[:size], own, part[size:]], axis=0).astype(BF)


def in_order(axis, own, partner):
    even = lax.rem(lax.axis_index(axis), 2) == 0
    return (jnp.where(even, own, partner), jnp.where(even, partner, own))


def head_sum(value, ones_ref):
    high, low = split_two(value)
    return mm(high, ones_ref[...]) + mm(low, ones_ref[...])


def own_kernel(
    ones_ref,
    parity_ref,
    scale_ref,
    tok_ref,
    dm_ref,
    dskip_ref,
    gain_ref,
    wqkv_ref,
    wout_ref,
    wmerge_ref,
    edges_ref,
    rows_ref,
    q_norm_ref,
    q_unit_ref,
    dy_ref,
    d_attn_ref,
    dscr,
):
    rows, cols, width = tok_ref.shape
    tokens = rows * cols
    tok = tok_ref[...].astype(F32)
    left = tok[:, :EDGE].reshape(rows * EDGE, width)
    right = tok[:, cols - EDGE :].reshape(rows * EDGE, width)
    heads = scale_ref.shape[1]
    even = parity_ref[heads : heads + 1, 0:1] > 0.5
    near, far = (jnp.where(even, right, left), jnp.where(even, left, right))
    edges_ref[...] = jnp.concatenate([near, far], axis=0).astype(BF)
    lane = lax.broadcasted_iota(jnp.int32, (1, width), 1)
    scale_row = jnp.zeros((1, width), F32)
    for h in range(heads):
        scale_row = jnp.where(lane // (width // heads) == h, scale_ref[:, h : h + 1], scale_row)
    blank = jnp.zeros((6, width), F32)
    rows_ref[...] = jnp.concatenate([gain_ref[...], scale_row, blank], axis=0)
    x = tok.reshape(tokens, width)
    inverse = lax.rsqrt(jnp.mean(x * x, axis=1, keepdims=True) + EPS)
    normed = (x * inverse * gain_ref[...]).astype(BF)
    query = mm(normed, wqkv_ref[:, :width])
    q_norm = lax.rsqrt(head_sum(query * query, ones_ref) + EPS)
    q_norm_ref[...] = q_norm
    q_unit_ref[...] = query * q_norm
    group_wide = cols // 2
    d_in = mm_t(dm_ref[...].reshape(-1, dm_ref.shape[2]), wmerge_ref[...])
    for i in range(rows // 2):
        for pr in range(2):
            for pc in range(2):
                for part in range(width // LANES):
                    at = (2 * pr + pc) * width + part * LANES
                    dscr[part, 2 * i + pr, pl.ds(pc, group_wide, stride=2), :] = d_in[
                        i * group_wide : (i + 1) * group_wide, at : at + LANES
                    ]
    d_group = jnp.concatenate(
        [dscr[part].reshape(tokens, LANES) for part in range(width // LANES)], axis=1
    )
    d_y = dskip_ref[...].reshape(tokens, width).astype(F32) + d_group
    dy_ref[...] = d_y
    d_attn_ref[...] = mm_t(d_y.astype(BF), wout_ref[...]).astype(BF)


def layer_kernel(
    sizes,
    ones_ref,
    tok_ref,
    row_far_ref,
    row_near_ref,
    col_near_ref,
    col_far_ref,
    rows_ref,
    q_norm_ref,
    q_unit_ref,
    dy_ref,
    d_attn_ref,
    wqkv_ref,
    wout_ref,
    x_ref,
    y_ref,
    d_query_ref,
    d_kv_ref,
    grad_out_ref,
    group_ref,
    scale_part_ref,
    yscr,
):
    rows, cols, width, heads, n_row, n_col = sizes
    head_dim = width // heads
    wide = cols + 2 * SIDE
    ext_rows = rows + 2 * RADIUS
    tokens = rows * cols
    image_rows = min(IMG_MAX, rows * n_row)
    row_start = lax.axis_index("row") * rows
    col_index = lax.axis_index("col")
    col_start = col_index * cols
    first = row_start // image_rows * image_rows

    lane = lax.broadcasted_iota(jnp.int32, (1, width), 1)
    def blocks(value):
        zero = jnp.zeros_like(value)
        kept = [jnp.where(lane // head_dim == h, value, zero) for h in range(heads)]
        return jnp.concatenate(kept, axis=0).astype(BF)

    gain = rows_ref[0:1]
    scale_row = rows_ref[1:2]
    up, down = by_side("row", row_near_ref[...].astype(F32), row_far_ref[...].astype(F32))
    left, right = by_side("col", col_near_ref[...].astype(F32), col_far_ref[...].astype(F32))
    own = tok_ref[...].astype(F32)
    blank = jnp.zeros((SIDE - EDGE, width), F32)
    pieces = []
    for i in range(ext_rows):
        if i < RADIUS:
            row = up[rows - RADIUS + i]
        elif i < RADIUS + rows:
            row = own[i - RADIUS]
        else:
            row = down[i - RADIUS - rows]
        edge = slice(i * EDGE, (i + 1) * EDGE)
        pieces += [blank, left[edge], row, right[edge], blank]
    x = jnp.concatenate(pieces, axis=0)
    x_ref[...] = x
    inverse = lax.rsqrt(jnp.mean(x * x, axis=1, keepdims=True) + EPS)
    unit = x * inverse
    normed32 = (unit * gain).astype(BF).astype(F32)
    normed = normed32.astype(BF)
    x_own = inner_tokens(x, rows, cols)
    kv = mm(normed, wqkv_ref[:, width:])
    key_raw = kv[:, :width]
    k_norm = lax.rsqrt(head_sum(key_raw * key_raw, ones_ref) + EPS)
    k_unit = key_raw * k_norm
    keys = k_unit.astype(BF)
    values = kv[:, width:].astype(BF)
    q_norm = q_norm_ref[...]
    q_unit = q_unit_ref[...]
    q_hat = (q_unit * scale_row).astype(BF).astype(F32)
    d_y = dy_ref[...]
    dy_b = d_y.astype(BF)
    d_attn = d_attn_ref[...].astype(F32)

    index = lax.broadcasted_iota(jnp.int32, (1, tokens), 1)
    q_row = jnp.zeros_like(index)
    for i in range(1, rows):
        q_row = q_row + (index >= i * cols).astype(jnp.int32)
    q_col = index - q_row * cols
    key_col = lax.broadcasted_iota(jnp.int32, (wide, tokens), 0) - SIDE
    near = (key_col - q_col <= RADIUS) & (key_col - q_col >= -RADIUS)
    near = near & (key_col + col_start >= 0) & (key_col + col_start < cols * n_col)
    near = jnp.where(near, 1.0, 0.0)
    parts = []
    for i in range(-RADIUS, rows + RADIUS):
        ok = (q_row - i <= RADIUS) & (q_row - i >= -RADIUS)
        ok = ok & (row_start + i >= first) & (row_start + i < first + image_rows)
        parts.append(near * jnp.where(ok, 1.0, 0.0))
    allowed = jnp.concatenate([jnp.concatenate(parts, axis=0)] * heads, axis=1)
    q_blocks = blocks(q_hat)
    g_blocks = blocks(d_attn)
    expo = jnp.exp(mm_t(keys, q_blocks)) * allowed
    prob = expo * (1.0 / jnp.sum(expo, axis=0, keepdims=True))
    weights = prob.astype(BF)
    d_w = mm_t(values, g_blocks)
    delta = jnp.sum(d_w * prob, axis=0, keepdims=True)
    d_s = (prob * (d_w - delta)).astype(BF)
    values_t = values.astype(F32).T.astype(BF)
    keys_t = keys.astype(F32).T.astype(BF)
    attn_t = []
    d_qhat_t = []
    for h in range(heads):
        feats = slice(h * head_dim, (h + 1) * head_dim)
        lanes = slice(h * tokens, (h + 1) * tokens)
        attn_t.append(mm(values_t[feats], weights[:, lanes]))
        d_qhat_t.append(mm(keys_t[feats], d_s[:, lanes]))
    attn_t = jnp.concatenate(attn_t, axis=0)
    d_qhat = jnp.concatenate(d_qhat_t, axis=0).T
    d_k = mm(d_s, q_blocks)
    d_v = mm(weights, g_blocks)

    attn = attn_t.T.astype(BF)
    y = (x_own + mm(attn, wout_ref[...])).astype(BF)
    y_ref[...] = y
    y32 = y.astype(F32)
    for part in range(width // LANES):
        yscr[part] = y32[:, part * LANES : (part + 1) * LANES].reshape(rows, cols, LANES)
    lines = []
    for i in range(rows // 2):
        pieces = []
        for pr in range(2):
            for pc in range(2):
                for part in range(width // LANES):
                    pieces.append(yscr[part, 2 * i + pr, pl.ds(pc, cols // 2, stride=2), :])
        lines.append(jnp.concatenate(pieces, axis=1))
    group = jnp.concatenate(lines, axis=0).astype(BF)
    group_ref[...] = group
    grad_out_ref[...] = mm(attn_t.astype(BF), dy_b)

    scale_part_ref[...] = jnp.broadcast_to(
        jnp.sum(q_unit * d_qhat, axis=0, keepdims=True), scale_part_ref.shape
    )
    g_unit = d_qhat * scale_row
    d_query_ref[...] = (q_norm * (g_unit - q_unit * head_sum(q_unit * g_unit, ones_ref))).astype(BF)
    d_key = k_norm * (d_k - k_unit * head_sum(k_unit * d_k, ones_ref))
    d_kv_ref[...] = jnp.concatenate([d_key, d_v], axis=1).astype(BF)


def inner_tokens(value, rows, cols):
    wide = cols + 2 * SIDE
    pieces = []
    for i in range(RADIUS, RADIUS + rows):
        pieces.append(value[i * wide + SIDE : i * wide + SIDE + cols])
    return jnp.concatenate(pieces, axis=0)


def output_kernel(y_ref, group_ref, wmerge_ref, skip_ref, merged_ref):
    skip_ref[...] = y_ref[...].reshape(skip_ref.shape)
    merged = mm(group_ref[...], wmerge_ref[...])
    merged_ref[...] = merged.astype(BF).reshape(merged_ref.shape)


def weights_kernel(
    sizes, x_ref, d_query_ref, d_kv_ref, grad_out_ref, group_ref, rows_ref, *refs
):
    rows, cols, width, n_row, n_dm = sizes
    dm_refs, dm_all_ref, sum_refs = (refs[:n_dm], refs[n_dm], refs[n_dm + 1 :])
    size = dm_all_ref.shape[0] // n_dm
    dm = [ref[...].reshape(size, dm_all_ref.shape[1]) for ref in dm_refs]
    dm_all_ref[...] = jnp.concatenate(dm[::-1], axis=0)
    x = x_ref[...]
    inverse = lax.rsqrt(jnp.mean(x * x, axis=1, keepdims=True) + EPS)
    normed32 = (x * inverse * rows_ref[0:1]).astype(BF).astype(F32)
    grad_q = mm(inner_tokens(normed32, rows, cols).T.astype(BF), d_query_ref[...])
    grad_kv = mm(normed32.T.astype(BF), d_kv_ref[...])
    sums = jnp.concatenate([grad_q, grad_kv, grad_out_ref[...]], axis=1)
    group = group_ref[...]
    if len(sum_refs) == 2:
        sum_refs[0][...] = sums.astype(BF)
        sum_refs[1][...] = group
        return
    send_ref, send_own_ref, keep_ref, keep_group_ref, sends, keeps, keep_groups = sum_refs
    per = width // n_row
    feats = 4 * width // n_row
    group = group.astype(F32)
    even = lax.rem(lax.axis_index("row"), 2) == 0
    for q in range(n_row // 2):
        parts = []
        for value, axis, size in ((sums, 0, per), (group, 1, feats)):
            first = lax.slice_in_dim(value, 2 * q * size, (2 * q + 1) * size, axis=axis)
            second = lax.slice_in_dim(value, (2 * q + 1) * size, (2 * q + 2) * size, axis=axis)
            parts.append((jnp.where(even, first, second), jnp.where(even, second, first)))
        (keeps[q], sums_send), (keep_group, group_send) = parts
        keep_groups[q] = keep_group.astype(BF)
        sends[q] = jnp.concatenate([sums_send, group_send], axis=1).astype(BF)
    chip = lax.axis_index("row") // 2
    for step in range(n_row // 2):
        at = partner(chip, step)
        keep_ref[step] = keeps[at]
        keep_group_ref[step] = keep_groups[at]
        if step == 0:
            send_own_ref[...] = sends[at]
        else:
            send_ref[step - 1] = sends[at]


def gain_kernel(
    sizes,
    x_ref,
    d_query_ref,
    d_kv_ref,
    scale_part_ref,
    wqkv_ref,
    d_normed_ref,
    small_ref,
):
    rows, cols, width, heads = sizes
    head_dim = width // heads
    wide = cols + 2 * SIDE
    ext_rows = rows + 2 * RADIUS
    lane = lax.broadcasted_iota(jnp.int32, (1, width), 1)
    x = x_ref[...]
    unit = x * lax.rsqrt(jnp.mean(x * x, axis=1, keepdims=True) + EPS)
    from_q = mm_t(d_query_ref[...], wqkv_ref[:, :width])
    d_normed = mm_t(d_kv_ref[...], wqkv_ref[:, width:])
    pieces = []
    side = jnp.zeros((SIDE, width), F32)
    for i in range(ext_rows):
        if RADIUS <= i < RADIUS + rows:
            at = (i - RADIUS) * cols
            pieces += [side, from_q[at : at + cols], side]
        else:
            pieces.append(jnp.zeros((wide, width), F32))
    d_normed = d_normed + jnp.concatenate(pieces, axis=0)
    gain_part = jnp.sum(unit * d_normed, axis=0, keepdims=True)
    d_normed_ref[...] = d_normed
    scale_part = scale_part_ref[0:1]
    scale_lane = lax.broadcasted_iota(jnp.int32, (1, LANES), 1)
    scale_sums = jnp.zeros((1, LANES), F32)
    for h in range(heads):
        of_head = jnp.sum(jnp.where(lane // head_dim == h, scale_part, 0.0), axis=1, keepdims=True)
        scale_sums = jnp.where(scale_lane == h, of_head, scale_sums)
    small = [gain_part[:, i * LANES : (i + 1) * LANES] for i in range(width // LANES)] + [scale_sums]
    small = jnp.concatenate(small + [jnp.zeros((8 - len(small), LANES), F32)], axis=0)
    small_ref[...] = small


def norm_kernel(sizes, x_ref, d_normed_ref, rows_ref, dy_ref, *refs):
    rows, cols, width = sizes
    gx_ref, side_near_ref, side_far_ref = refs
    wide = cols + 2 * SIDE
    ext_rows = rows + 2 * RADIUS
    x = x_ref[...]
    inverse = lax.rsqrt(jnp.mean(x * x, axis=1, keepdims=True) + EPS)
    d_y = dy_ref[...]
    scaled = rows_ref[0:1] * d_normed_ref[...]
    mean = jnp.mean(x * scaled, axis=1, keepdims=True)
    g_x = inverse * scaled - x * (inverse * inverse * inverse) * mean

    pieces = []
    left = []
    right = []
    for i in range(ext_rows):
        row = g_x[i * wide : (i + 1) * wide]
        middle = row[SIDE : SIDE + cols]
        if RADIUS <= i < RADIUS + rows:
            middle = middle + d_y[(i - RADIUS) * cols : (i - RADIUS + 1) * cols]
        pieces.append(middle)
        left.append(row[:SIDE][SIDE - EDGE :])
        right.append(row[SIDE + cols :][:EDGE])
    gx_ref[...] = jnp.concatenate(pieces, axis=0)
    left, right = [jnp.concatenate(part, axis=0) for part in (left, right)]
    far, near = by_side("col", right, left)
    side_near_ref[...] = near.astype(BF)
    side_far_ref[...] = far.astype(BF)


def small_rows(small):
    high = small.astype(BF).astype(F32)
    return jnp.concatenate([high[:4], (small - high)[:4]], axis=0)


def small_value(rows):
    value = rows.astype(BF).astype(F32)
    return value[:4] + value[4:]


def stacked(value):
    return jnp.concatenate(
        [value[:, i : i + LANES] for i in range(0, value.shape[1], LANES)], axis=0
    )


def unstacked(value, rows):
    return jnp.concatenate([value[i : i + rows] for i in range(0, value.shape[0], rows)], axis=1)


def core_sum_kernel(got_ref, keep_ref, keep_group_ref, small_ref, small_near_ref, *refs):
    *out_refs, small_sum_ref = refs
    width = keep_ref.shape[2]
    small = small_ref[...] + small_near_ref[...]
    small_sum_ref[...] = small
    small = small_rows(small)
    for i, out_ref in enumerate(out_refs):
        sums = keep_ref[i + 1] + got_ref[i, :, :width].astype(F32)
        kept = keep_group_ref[i + 1].astype(F32)
        first, second = in_order("row", kept, got_ref[i, :, width:].astype(F32))
        out_ref[...] = jnp.concatenate([stacked(sums), first, second, small], axis=0).astype(BF)


def row_sum_kernel(sizes, *refs):
    rows, cols, width, n_col = sizes
    keep_ref, keep_group_ref, got_own_ref, small_ref, *refs = refs
    got_refs, dm_ref, dm_near_ref, gx_ref, *refs = (refs[:3], *refs[3:])
    *out_refs, gx_sum_ref, slots_ref = refs
    gx_sum_ref[...] = gx_ref[...]
    per, feats = keep_group_ref.shape[1:]
    got_own = got_own_ref[...].astype(F32)
    own = keep_ref[0] + got_own[:, : 4 * width]
    size = 4 * width // LANES * per

    def summed(first, part):
        fourth, third, second = [part(ref[...].astype(F32)) for ref in got_refs]
        return (first + second) + (third + fourth)

    sums = summed(stacked(own), lambda value: value[:size])
    sums = unstacked(sums, per)
    small = summed(small_value(small_rows(small_ref[...])), lambda value: small_value(value[size + 2 * per :]))
    own_group = in_order("row", keep_group_ref[0].astype(F32), got_own[:, 4 * width :])
    group = [jnp.concatenate(own_group, axis=0)]
    group += [ref[...].astype(F32)[size : size + 2 * per] for ref in got_refs[::-1]]
    group = [part[i * per : (i + 1) * per] for i in range(2) for part in group]
    group = jnp.concatenate(group, axis=0)
    own, near = (dm_ref[...].astype(F32), dm_near_ref[...].astype(F32))
    dm = jnp.concatenate(in_order("row", own, near), axis=0).astype(BF)
    merge = mm(group.T.astype(BF), dm)
    small = small_rows(small)
    col = lax.axis_index("col")
    third = 3 * width // n_col
    fourth = width // n_col
    depth = merge.shape[1] // n_col
    for slot in range(n_col):
        parts = [
            sums[:, slot * third : (slot + 1) * third],
            sums[:, 3 * width + slot * fourth : 3 * width + (slot + 1) * fourth],
        ]
        parts = [stacked(jnp.concatenate(parts, axis=1))]
        parts += [merge[:, slot * depth : (slot + 1) * depth], small]
        slots_ref[slot] = jnp.concatenate(parts, axis=0).astype(BF)
    for step, out_ref in enumerate(out_refs):
        out_ref[...] = slots_ref[partner(col, step)]


def partner(index, step):
    if step == 0:
        return index
    low = lax.rem(index, 2)
    if step == 1:
        return index + 1 - 2 * low
    if step == 2:
        return lax.rem(index + 2, 4)
    return 3 - index


def side_kernel(sizes, gx_ref, near_ref, far_ref, grad_ref, row_near_ref, row_far_ref):
    rows, cols, width = sizes
    ends = lax.axis_index("col")
    left, right = by_side("col", near_ref[...].astype(F32), far_ref[...].astype(F32))
    left = jnp.where(ends > 0, left, 0.0)
    right = jnp.where(ends < lax.axis_size("col") - 1, right, 0.0)
    blank = jnp.zeros((cols - 2 * EDGE, width), F32)
    pieces = []
    for i in range(rows + 2 * RADIUS):
        edge = slice(i * EDGE, (i + 1) * EDGE)
        pieces += [left[edge], blank, right[edge]]
    g_x = gx_ref[...] + jnp.concatenate(pieces, axis=0)
    reach = RADIUS * cols
    far, near = by_side("row", g_x[reach + rows * cols :], g_x[:reach])
    grad_ref[...] = g_x[reach : reach + rows * cols]
    row_near_ref[...] = near.astype(BF)
    row_far_ref[...] = far.astype(BF)


def col_sum_kernel(
    sizes,
    a_ref,
    d_ref,
    c_ref,
    b_ref,
    grad_ref,
    far_ref,
    near_ref,
    gqkv_ref,
    gout_ref,
    gmerge_ref,
    ggain_ref,
    gscale_ref,
    gtok_ref,
):
    rows, cols, width = sizes
    per, third = gqkv_ref.shape
    size = a_ref.shape[0] - 8

    def summed(part):
        first, second, third, fourth = [
            part(ref[...].astype(F32)) for ref in (a_ref, b_ref, c_ref, d_ref)
        ]
        return (first + second) + (third + fourth)

    total = summed(lambda value: value[:size])
    small = summed(lambda value: small_value(value[size:]))
    merge_at = size - gmerge_ref.shape[0]
    sums = unstacked(total[:merge_at], per)
    gqkv_ref[...] = sums[:, :third]
    gout_ref[...] = sums[:, third:]
    gmerge_ref[...] = total[merge_at:]
    ggain_ref[...] = jnp.concatenate([small[i : i + 1] for i in range(width // LANES)], axis=1)
    for h in range(gscale_ref.shape[0]):
        gscale_ref[h] = small[width // LANES, h]
    blank = jnp.zeros(((rows - RADIUS) * cols, width), F32)
    above, below = by_side("row", near_ref[...].astype(F32), far_ref[...].astype(F32))
    grad = grad_ref[...] + jnp.concatenate([above, blank], axis=0)
    grad = grad + jnp.concatenate([blank, below], axis=0)
    gtok_ref[...] = grad.astype(BF).reshape(rows, cols, width)


def plain_sums(width, sums, group, small, dm):
    sums = sums.astype(F32)
    merge = jnp.dot(group.T, dm, preferred_element_type=F32)
    outs = []
    for part in (sums[:, : 3 * width], sums[:, 3 * width :], merge):
        part = lax.psum_scatter(part, "row", scatter_dimension=0, tiled=True)
        outs.append(lax.psum_scatter(part, "col", scatter_dimension=1, tiled=True))
    small = lax.psum(small, ("row", "col"))
    return (*outs, small[: width // LANES].reshape(1, width), small[width // LANES])


def add_rows(grad, near, far, rows, cols):
    above, below = by_side("row", near.astype(F32), far.astype(F32))
    size = RADIUS * cols
    grad = grad.at[:size].add(above).at[rows * cols - size :].add(below)
    return grad.astype(BF).reshape(rows, cols, -1)


def swapped(near, far, axis):
    n_row, n_col = (lax.axis_size("row"), lax.axis_size("col"))
    pairs = []
    for row in range(n_row):
        for col in range(n_col):
            if axis == "row":
                other = row - 1 if row % 2 == 0 else row + 1
                target = (other, col) if 0 <= other < n_row else (row, col ^ 1)
            else:
                other = col - 1 if col % 2 == 0 else col + 1
                target = (row, other) if 0 <= other < n_col else (row ^ 1, col)
            pairs.append((row * n_col + col, target[0] * n_col + target[1]))
    return (swap(near, axis, 1), lax.ppermute(far, ("row", "col"), pairs))


def swap(value, axis, step):
    count = lax.axis_size(axis)
    return lax.ppermute(value, axis, [(i, i ^ step) for i in range(count)])


def vmem(count):
    return [pl.BlockSpec(memory_space=pltpu.VMEM)] * count


def on_device(tokens, gain, w_qkv, head_scale, w_out, w_merge, d_merged, d_skip):
    rows, cols, width = tokens.shape
    heads = head_scale.shape[0]
    n_row, n_col = (lax.axis_size("row"), lax.axis_size("col"))
    g_rows, g_cols, depth = d_merged.shape
    groups = g_rows * g_cols
    wide = cols + 2 * SIDE
    ext_rows = rows + 2 * RADIUS
    shape = jax.ShapeDtypeStruct
    params = pltpu.CompilerParams(vmem_limit_bytes=24 * 1024 * 1024)
    less = pltpu.CompilerParams(vmem_limit_bytes=8 * 1024 * 1024)
    row_near, row_far = swapped(tokens, tokens, "row")
    edge = shape((ext_rows * EDGE, width), BF)
    ones, parity = pl.pallas_call(
        first_kernel,
        out_shape=(shape((width, width), BF), shape((2 * heads, LANES), F32)),
        out_specs=tuple(vmem(2)),
        compiler_params=less,
        cost_estimate=pl.CostEstimate(flops=10**10, bytes_accessed=10**5, transcendentals=0),
    )()
    dm = d_merged.reshape(groups, depth)
    tile = shape((rows * cols, width), F32)
    half = shape((rows * cols, width), BF)
    edges, two_rows, q_norm, q_unit, d_y, d_attn = pl.pallas_call(
        own_kernel,
        out_shape=(shape((2 * rows * EDGE, width), BF), shape((8, width), F32), tile, tile, tile, half),
        in_specs=vmem(10),
        out_specs=tuple(vmem(6)),
        scratch_shapes=[pltpu.VMEM((width // LANES, rows, cols, LANES), F32)],
        compiler_params=params,
        cost_estimate=pl.CostEstimate(flops=10**9, bytes_accessed=10**6, transcendentals=0),
    )(
        ones,
        parity,
        head_scale.reshape(1, heads),
        tokens,
        d_merged,
        d_skip,
        gain.reshape(1, width),
        w_qkv,
        w_out,
        w_merge,
    )
    edge_near, edge_far, dm_pair = pl.pallas_call(
        edge_kernel,
        out_shape=(edge, edge, shape((2 * groups, depth), BF)),
        in_specs=vmem(5),
        out_specs=tuple(vmem(3)),
        compiler_params=less,
    )(edges, row_far, row_near, d_merged, swap(dm, "row", 2))
    dms = [swap(dm_pair, "row", 4), dm_pair]
    col_near, col_far = swapped(edge_near, edge_far, "col")

    per = width // n_row
    feats = 4 * width // n_row
    packed = per % 16 == 0 and feats % LANES == 0 and groups == per
    packed = packed and width // LANES < 4 and feats == LANES and depth // n_col == LANES and n_col == 4 and n_row == 8
    if packed:
        sum_shapes = (
            shape((n_row // 2 - 1, per, 4 * width + feats), BF),
            shape((per, 4 * width + feats), BF),
            shape((n_row // 2, per, 4 * width), F32),
            shape((n_row // 2, per, feats), BF),
        )
        sum_scratch = [
            pltpu.VMEM((n_row // 2, per, 4 * width + feats), BF),
            pltpu.VMEM((n_row // 2, per, 4 * width), F32),
            pltpu.VMEM((n_row // 2, per, feats), BF),
        ]
    else:
        sum_shapes = (
            shape((width, 4 * width), BF),
            shape((groups, 4 * width), BF),
        )
        sum_scratch = []
    sizes = (rows, cols, width, heads, n_row, n_col)
    tall = ext_rows * wide
    x, y, d_query, d_kv, grad_out, group, scale_part = pl.pallas_call(
        functools.partial(layer_kernel, sizes),
        out_shape=(
            shape((tall, width), F32),
            half,
            half,
            shape((tall, 2 * width), BF),
            shape((width, width), F32),
            shape((groups, 4 * width), BF),
            shape((8, width), F32),
        ),
        in_specs=vmem(13),
        out_specs=tuple(vmem(7)),
        scratch_shapes=[pltpu.VMEM((width // LANES, rows, cols, LANES), F32)],
        compiler_params=params,
        cost_estimate=pl.CostEstimate(flops=4 * 10**9, bytes_accessed=10**6, transcendentals=0),
    )(
        ones,
        tokens,
        row_far,
        row_near,
        col_near,
        col_far,
        two_rows,
        q_norm,
        q_unit,
        d_y,
        d_attn,
        w_qkv,
        w_out,
    )
    dm_core, *sums = pl.pallas_call(
        functools.partial(weights_kernel, (rows, cols, width, n_row, len(dms))),
        out_shape=(shape((2 * len(dms) * groups, depth), BF),) + sum_shapes,
        in_specs=vmem(6 + len(dms)),
        out_specs=tuple(vmem(1 + len(sum_shapes))),
        scratch_shapes=sum_scratch,
        compiler_params=params,
        cost_estimate=pl.CostEstimate(flops=10**9, bytes_accessed=10**6, transcendentals=0),
    )(x, d_query, d_kv, grad_out, group, two_rows, *dms)
    d_normed, small = pl.pallas_call(
        functools.partial(gain_kernel, (rows, cols, width, heads)),
        out_shape=(shape((tall, width), F32), shape((8, LANES), F32)),
        in_specs=vmem(5),
        out_specs=tuple(vmem(2)),
        compiler_params=params,
        cost_estimate=pl.CostEstimate(flops=3 * 10**8, bytes_accessed=10**6, transcendentals=0),
    )(x, d_query, d_kv, scale_part, w_qkv)
    gx, *sides = pl.pallas_call(
        functools.partial(norm_kernel, (rows, cols, width)),
        out_shape=(shape((ext_rows * cols, width), F32), edge, edge),
        in_specs=vmem(4),
        out_specs=tuple(vmem(3)),
        compiler_params=params,
        cost_estimate=pl.CostEstimate(flops=2 * 10**8, bytes_accessed=10**6, transcendentals=0),
    )(x, d_normed, two_rows, d_y)
    sides = swapped(*sides, "col")
    skip_out, merged = pl.pallas_call(
        output_kernel,
        out_shape=(shape((rows, cols, width), BF), shape((g_rows, g_cols, depth), BF)),
        in_specs=vmem(3),
        out_specs=tuple(vmem(2)),
        compiler_params=less,
        cost_estimate=pl.CostEstimate(flops=10**9, bytes_accessed=10**6, transcendentals=0),
    )(y, group, w_merge)
    reach = shape((RADIUS * cols, width), BF)
    side_call = pl.pallas_call(
        functools.partial(side_kernel, (rows, cols, width)),
        out_shape=(tile, reach, reach),
        in_specs=vmem(3),
        out_specs=tuple(vmem(3)),
        compiler_params=less,
    )
    if not packed:
        grad, *rims = side_call(gx, *sides)
        grad_tokens = add_rows(grad, *swapped(*rims, "row"), rows, cols)
        g_qkv, g_out, g_merge, g_gain, g_scale = plain_sums(width, *sums, small, dm)
    else:
        send, send_own, *kept = sums
        block = shape((4 * width // LANES * per + 2 * per + 8, LANES), BF)
        *blocks, small = pl.pallas_call(
            core_sum_kernel,
            out_shape=(block, block, block, shape((8, LANES), F32)),
            in_specs=vmem(5),
            out_specs=tuple(vmem(4)),
            compiler_params=less,
            cost_estimate=pl.CostEstimate(flops=5 * 10**9, bytes_accessed=10**6, transcendentals=0),
        )(swap(send, "row", 1), *kept, small, swap(small, "row", 1))
        got = [swap(blocks[step - 1], "row", 2 * step) for step in (3, 2, 1)]
        slot = shape((4 * width // n_col // LANES * per + feats + 8, LANES), BF)
        *slots, gx = pl.pallas_call(
            functools.partial(row_sum_kernel, (rows, cols, width, n_col)),
            out_shape=(slot,) * n_col + (shape(gx.shape, F32),),
            in_specs=vmem(10),
            out_specs=tuple(vmem(n_col + 1)),
            scratch_shapes=[pltpu.VMEM((n_col,) + slot.shape, BF)],
            compiler_params=less,
        )(*kept, swap(send_own, "row", 1), small, *got, dm_core, swap(dm_core, "row", 1), gx)
        got = [slots[0]] + [swap(slots[step], "col", step) for step in (3, 2, 1)]
        grad, *rims = side_call(gx, *sides)
        rims = swapped(*rims, "row")
        g_qkv, g_out, g_merge, g_gain, g_scale, grad_tokens = pl.pallas_call(
            functools.partial(col_sum_kernel, (rows, cols, width)),
            out_shape=(
                shape((per, 3 * width // n_col), F32),
                shape((per, width // n_col), F32),
                shape((feats, depth // n_col), F32),
                shape((1, width), F32),
                shape((heads,), F32),
                shape((rows, cols, width), BF),
            ),
            in_specs=vmem(7),
            out_specs=tuple(vmem(4)) + (pl.BlockSpec(memory_space=pltpu.SMEM), vmem(1)[0]),
            compiler_params=less,
        )(*got, grad, *rims[::-1])
    return (
        skip_out,
        merged,
        grad_tokens,
        g_qkv,
        g_out,
        g_merge,
        g_gain.reshape(width),
        g_scale[:heads],
    )


def solution(mesh):
    block = P("row", "col", None)
    return jax.shard_map(
        on_device,
        mesh=mesh,
        in_specs=(block, P(), P(), P(), P(), P(), block, block),
        out_specs=(block, block, block, P("row", "col"), P("row", "col"), P("row", "col"), P(), P()),
        check_vma=False,
    )
```

```python
import functools
import jax
import jax.numpy as jnp
from jax import lax
from jax.experimental import pallas as pl
from jax.experimental.pallas import tpu as pltpu
from jax.sharding import PartitionSpec as P

RADIUS = 3
IMG_MAX = 512
EPS = 1e-06
EDGE = 4
SIDE = 8
LANES = 128
BF = jnp.bfloat16
F32 = jnp.float32


def mm(a, b):
    return lax.dot_general(a, b, (((1,), (0,)), ((), ())), preferred_element_type=F32)


def mm_t(a, b):
    return lax.dot_general(a, b, (((1,), (1,)), ((), ())), preferred_element_type=F32)


def split_two(value):
    high = value.astype(BF)
    return (high, (value - high.astype(F32)).astype(BF))


def by_side(axis, near, far):
    even = lax.rem(lax.axis_index(axis), 2) == 0
    return (jnp.where(even, far, near), jnp.where(even, near, far))


def first_kernel(ones_ref, parity_ref):
    width = ones_ref.shape[0]
    head_dim = width // (parity_ref.shape[0] // 2)
    same_head = lax.broadcasted_iota(jnp.int32, (width, width), 0) // head_dim == (
        lax.broadcasted_iota(jnp.int32, (width, width), 1) // head_dim
    )
    ones_ref[...] = jnp.where(same_head, 1.0, 0.0).astype(BF)
    half = (parity_ref.shape[0] // 2, parity_ref.shape[1])
    parts = [
        jnp.where(lax.rem(lax.axis_index(axis), 2) == 0, jnp.ones(half, F32), jnp.zeros(half, F32))
        for axis in ("row", "col")
    ]
    parity_ref[...] = jnp.concatenate(parts, axis=0)


def pair_kernel(dm_ref, dm_next_ref, dm_pair_ref):
    size = dm_next_ref.shape[0]
    dm_pair_ref[...] = jnp.concatenate([dm_ref[...].reshape(size, -1), dm_next_ref[...]], axis=0)


def edge_kernel(edges_ref, far_ref, near_ref, edge_near_ref, edge_far_ref):
    rows, cols, width = near_ref.shape
    up, down = by_side("row", near_ref[...].astype(F32), far_ref[...].astype(F32))
    up = up[rows - RADIUS :]
    down = down[:RADIUS]
    halo = []
    for at in (0, cols - EDGE):
        parts = [part[:, at : at + EDGE].reshape(RADIUS * EDGE, width) for part in (up, down)]
        halo.append(jnp.concatenate(parts, axis=0))
    far, near = by_side("col", halo[1], halo[0])
    for out_ref, own_at, part in ((edge_near_ref, 0, near), (edge_far_ref, rows * EDGE, far)):
        own = edges_ref[own_at : own_at + rows * EDGE].astype(F32)
        size = RADIUS * EDGE
        out_ref[...] = jnp.concatenate([part[:size], own, part[size:]], axis=0).astype(BF)


def in_order(axis, own, partner):
    even = lax.rem(lax.axis_index(axis), 2) == 0
    return (jnp.where(even, own, partner), jnp.where(even, partner, own))


def head_sum(value, ones_ref):
    high, low = split_two(value)
    return mm(high, ones_ref[...]) + mm(low, ones_ref[...])


def own_kernel(
    ones_ref,
    parity_ref,
    scale_ref,
    tok_ref,
    dm_ref,
    dskip_ref,
    gain_ref,
    wqkv_ref,
    wout_ref,
    wmerge_ref,
    edges_ref,
    rows_ref,
    q_norm_ref,
    q_unit_ref,
    dy_ref,
    d_attn_ref,
    dscr,
):
    rows, cols, width = tok_ref.shape
    tokens = rows * cols
    tok = tok_ref[...].astype(F32)
    left = tok[:, :EDGE].reshape(rows * EDGE, width)
    right = tok[:, cols - EDGE :].reshape(rows * EDGE, width)
    heads = scale_ref.shape[1]
    even = parity_ref[heads : heads + 1, 0:1] > 0.5
    near, far = (jnp.where(even, right, left), jnp.where(even, left, right))
    edges_ref[...] = jnp.concatenate([near, far], axis=0).astype(BF)
    lane = lax.broadcasted_iota(jnp.int32, (1, width), 1)
    scale_row = jnp.zeros((1, width), F32)
    for h in range(heads):
        scale_row = jnp.where(lane // (width // heads) == h, scale_ref[:, h : h + 1], scale_row)
    blank = jnp.zeros((6, width), F32)
    rows_ref[...] = jnp.concatenate([gain_ref[...], scale_row, blank], axis=0)
    x = tok.reshape(tokens, width)
    inverse = lax.rsqrt(jnp.mean(x * x, axis=1, keepdims=True) + EPS)
    normed = (x * inverse * gain_ref[...]).astype(BF)
    query = mm(normed, wqkv_ref[:, :width])
    q_norm = lax.rsqrt(head_sum(query * query, ones_ref) + EPS)
    q_norm_ref[...] = q_norm
    q_unit_ref[...] = query * q_norm
    group_wide = cols // 2
    d_in = mm_t(dm_ref[...].reshape(-1, dm_ref.shape[2]), wmerge_ref[...])
    for i in range(rows // 2):
        for pr in range(2):
            for pc in range(2):
                for part in range(width // LANES):
                    at = (2 * pr + pc) * width + part * LANES
                    dscr[part, 2 * i + pr, pl.ds(pc, group_wide, stride=2), :] = d_in[
                        i * group_wide : (i + 1) * group_wide, at : at + LANES
                    ]
    d_group = jnp.concatenate(
        [dscr[part].reshape(tokens, LANES) for part in range(width // LANES)], axis=1
    )
    d_y = dskip_ref[...].reshape(tokens, width).astype(F32) + d_group
    dy_ref[...] = d_y
    d_attn_ref[...] = mm_t(d_y.astype(BF), wout_ref[...]).astype(BF)


def layer_kernel(
    sizes,
    ones_ref,
    tok_ref,
    row_far_ref,
    row_near_ref,
    col_near_ref,
    col_far_ref,
    rows_ref,
    q_norm_ref,
    q_unit_ref,
    dy_ref,
    d_attn_ref,
    wqkv_ref,
    wout_ref,
    x_ref,
    y_ref,
    d_query_ref,
    d_kv_ref,
    grad_out_ref,
    group_ref,
    scale_part_ref,
    yscr,
):
    rows, cols, width, heads, n_row, n_col = sizes
    head_dim = width // heads
    wide = cols + 2 * SIDE
    ext_rows = rows + 2 * RADIUS
    tokens = rows * cols
    image_rows = min(IMG_MAX, rows * n_row)
    row_start = lax.axis_index("row") * rows
    col_index = lax.axis_index("col")
    col_start = col_index * cols
    first = row_start // image_rows * image_rows

    lane = lax.broadcasted_iota(jnp.int32, (1, width), 1)
    def blocks(value):
        zero = jnp.zeros_like(value)
        kept = [jnp.where(lane // head_dim == h, value, zero) for h in range(heads)]
        return jnp.concatenate(kept, axis=0).astype(BF)

    gain = rows_ref[0:1]
    scale_row = rows_ref[1:2]
    up, down = by_side("row", row_near_ref[...].astype(F32), row_far_ref[...].astype(F32))
    left, right = by_side("col", col_near_ref[...].astype(F32), col_far_ref[...].astype(F32))
    own = tok_ref[...].astype(F32)
    blank = jnp.zeros((SIDE - EDGE, width), F32)
    pieces = []
    for i in range(ext_rows):
        if i < RADIUS:
            row = up[rows - RADIUS + i]
        elif i < RADIUS + rows:
            row = own[i - RADIUS]
        else:
            row = down[i - RADIUS - rows]
        edge = slice(i * EDGE, (i + 1) * EDGE)
        pieces += [blank, left[edge], row, right[edge], blank]
    x = jnp.concatenate(pieces, axis=0)
    x_ref[...] = x
    inverse = lax.rsqrt(jnp.mean(x * x, axis=1, keepdims=True) + EPS)
    unit = x * inverse
    normed32 = (unit * gain).astype(BF).astype(F32)
    normed = normed32.astype(BF)
    x_own = inner_tokens(x, rows, cols)
    kv = mm(normed, wqkv_ref[:, width:])
    key_raw = kv[:, :width]
    k_norm = lax.rsqrt(head_sum(key_raw * key_raw, ones_ref) + EPS)
    k_unit = key_raw * k_norm
    keys = k_unit.astype(BF)
    values = kv[:, width:].astype(BF)
    q_norm = q_norm_ref[...]
    q_unit = q_unit_ref[...]
    q_hat = (q_unit * scale_row).astype(BF).astype(F32)
    d_y = dy_ref[...]
    dy_b = d_y.astype(BF)
    d_attn = d_attn_ref[...].astype(F32)

    index = lax.broadcasted_iota(jnp.int32, (1, tokens), 1)
    q_row = jnp.zeros_like(index)
    for i in range(1, rows):
        q_row = q_row + (index >= i * cols).astype(jnp.int32)
    q_col = index - q_row * cols
    key_col = lax.broadcasted_iota(jnp.int32, (wide, tokens), 0) - SIDE
    near = (key_col - q_col <= RADIUS) & (key_col - q_col >= -RADIUS)
    near = near & (key_col + col_start >= 0) & (key_col + col_start < cols * n_col)
    near = jnp.where(near, 1.0, 0.0)
    parts = []
    for i in range(-RADIUS, rows + RADIUS):
        ok = (q_row - i <= RADIUS) & (q_row - i >= -RADIUS)
        ok = ok & (row_start + i >= first) & (row_start + i < first + image_rows)
        parts.append(near * jnp.where(ok, 1.0, 0.0))
    allowed = jnp.concatenate([jnp.concatenate(parts, axis=0)] * heads, axis=1)
    q_blocks = blocks(q_hat)
    g_blocks = blocks(d_attn)
    expo = jnp.exp(mm_t(keys, q_blocks)) * allowed
    prob = expo * (1.0 / jnp.sum(expo, axis=0, keepdims=True))
    weights = prob.astype(BF)
    d_w = mm_t(values, g_blocks)
    delta = jnp.sum(d_w * prob, axis=0, keepdims=True)
    d_s = (prob * (d_w - delta)).astype(BF)
    values_t = values.astype(F32).T.astype(BF)
    keys_t = keys.astype(F32).T.astype(BF)
    attn_t = []
    d_qhat_t = []
    for h in range(heads):
        feats = slice(h * head_dim, (h + 1) * head_dim)
        lanes = slice(h * tokens, (h + 1) * tokens)
        attn_t.append(mm(values_t[feats], weights[:, lanes]))
        d_qhat_t.append(mm(keys_t[feats], d_s[:, lanes]))
    attn_t = jnp.concatenate(attn_t, axis=0)
    d_qhat = jnp.concatenate(d_qhat_t, axis=0).T
    d_k = mm(d_s, q_blocks)
    d_v = mm(weights, g_blocks)

    attn = attn_t.T.astype(BF)
    y = (x_own + mm(attn, wout_ref[...])).astype(BF)
    y_ref[...] = y
    y32 = y.astype(F32)
    for part in range(width // LANES):
        yscr[part] = y32[:, part * LANES : (part + 1) * LANES].reshape(rows, cols, LANES)
    lines = []
    for i in range(rows // 2):
        pieces = []
        for pr in range(2):
            for pc in range(2):
                for part in range(width // LANES):
                    pieces.append(yscr[part, 2 * i + pr, pl.ds(pc, cols // 2, stride=2), :])
        lines.append(jnp.concatenate(pieces, axis=1))
    group = jnp.concatenate(lines, axis=0).astype(BF)
    group_ref[...] = group
    grad_out_ref[...] = mm(attn_t.astype(BF), dy_b)

    scale_part_ref[...] = jnp.broadcast_to(
        jnp.sum(q_unit * d_qhat, axis=0, keepdims=True), scale_part_ref.shape
    )
    g_unit = d_qhat * scale_row
    d_query_ref[...] = (q_norm * (g_unit - q_unit * head_sum(q_unit * g_unit, ones_ref))).astype(BF)
    d_key = k_norm * (d_k - k_unit * head_sum(k_unit * d_k, ones_ref))
    d_kv_ref[...] = jnp.concatenate([d_key, d_v], axis=1).astype(BF)


def inner_tokens(value, rows, cols):
    wide = cols + 2 * SIDE
    pieces = []
    for i in range(RADIUS, RADIUS + rows):
        pieces.append(value[i * wide + SIDE : i * wide + SIDE + cols])
    return jnp.concatenate(pieces, axis=0)


def output_kernel(y_ref, group_ref, wmerge_ref, skip_ref, merged_ref):
    skip_ref[...] = y_ref[...].reshape(skip_ref.shape)
    merged = mm(group_ref[...], wmerge_ref[...])
    merged_ref[...] = merged.astype(BF).reshape(merged_ref.shape)


def weights_kernel(
    sizes, x_ref, d_query_ref, d_kv_ref, grad_out_ref, group_ref, rows_ref, *refs
):
    rows, cols, width, n_row, n_dm = sizes
    dm_refs, dm_all_ref, sum_refs = (refs[:n_dm], refs[n_dm], refs[n_dm + 1 :])
    size = dm_all_ref.shape[0] // n_dm
    dm = [ref[...].reshape(size, dm_all_ref.shape[1]) for ref in dm_refs]
    dm_all_ref[...] = jnp.concatenate(dm[::-1], axis=0)
    x = x_ref[...]
    inverse = lax.rsqrt(jnp.mean(x * x, axis=1, keepdims=True) + EPS)
    normed32 = (x * inverse * rows_ref[0:1]).astype(BF).astype(F32)
    grad_q = mm(inner_tokens(normed32, rows, cols).T.astype(BF), d_query_ref[...])
    grad_kv = mm(normed32.T.astype(BF), d_kv_ref[...])
    sums = jnp.concatenate([grad_q, grad_kv, grad_out_ref[...]], axis=1)
    group = group_ref[...]
    if len(sum_refs) == 2:
        sum_refs[0][...] = sums.astype(BF)
        sum_refs[1][...] = group
        return
    send_ref, keep_ref, keep_group_ref = sum_refs
    per = width // n_row
    feats = 4 * width // n_row
    group = group.astype(F32)
    even = lax.rem(lax.axis_index("row"), 2) == 0
    for q in range(n_row // 2):
        parts = []
        for value, axis, size in ((sums, 0, per), (group, 1, feats)):
            first = lax.slice_in_dim(value, 2 * q * size, (2 * q + 1) * size, axis=axis)
            second = lax.slice_in_dim(value, (2 * q + 1) * size, (2 * q + 2) * size, axis=axis)
            parts.append((jnp.where(even, first, second), jnp.where(even, second, first)))
        (keep_ref[q], sums_send), (keep_group, group_send) = parts
        keep_group_ref[q] = keep_group.astype(BF)
        send_ref[q] = jnp.concatenate([sums_send, group_send], axis=1).astype(BF)


def norm_kernel(
    sizes, x_ref, d_query_ref, d_kv_ref, scale_part_ref, rows_ref, dy_ref, wqkv_ref, *refs
):
    rows, cols, width, heads = sizes
    gx_ref, side_near_ref, side_far_ref, small_ref = refs
    head_dim = width // heads
    wide = cols + 2 * SIDE
    ext_rows = rows + 2 * RADIUS
    gain = rows_ref[0:1]
    lane = lax.broadcasted_iota(jnp.int32, (1, width), 1)
    x = x_ref[...]
    inverse = lax.rsqrt(jnp.mean(x * x, axis=1, keepdims=True) + EPS)
    unit = x * inverse
    d_y = dy_ref[...]
    from_q = mm_t(d_query_ref[...], wqkv_ref[:, :width])
    d_normed = mm_t(d_kv_ref[...], wqkv_ref[:, width:])
    pieces = []
    side = jnp.zeros((SIDE, width), F32)
    for i in range(ext_rows):
        if RADIUS <= i < RADIUS + rows:
            at = (i - RADIUS) * cols
            pieces += [side, from_q[at : at + cols], side]
        else:
            pieces.append(jnp.zeros((wide, width), F32))
    d_normed = d_normed + jnp.concatenate(pieces, axis=0)
    gain_part = jnp.sum(unit * d_normed, axis=0, keepdims=True)
    scaled = gain * d_normed
    mean = jnp.mean(x * scaled, axis=1, keepdims=True)
    g_x = inverse * scaled - x * (inverse * inverse * inverse) * mean

    pieces = []
    left = []
    right = []
    for i in range(ext_rows):
        row = g_x[i * wide : (i + 1) * wide]
        middle = row[SIDE : SIDE + cols]
        if RADIUS <= i < RADIUS + rows:
            middle = middle + d_y[(i - RADIUS) * cols : (i - RADIUS + 1) * cols]
        pieces.append(middle)
        left.append(row[:SIDE][SIDE - EDGE :])
        right.append(row[SIDE + cols :][:EDGE])
    gx_ref[...] = jnp.concatenate(pieces, axis=0)
    left, right = [jnp.concatenate(part, axis=0) for part in (left, right)]
    far, near = by_side("col", right, left)
    side_near_ref[...] = near.astype(BF)
    side_far_ref[...] = far.astype(BF)
    scale_part = scale_part_ref[0:1]
    scale_lane = lax.broadcasted_iota(jnp.int32, (1, LANES), 1)
    scale_sums = jnp.zeros((1, LANES), F32)
    for h in range(heads):
        of_head = jnp.sum(jnp.where(lane // head_dim == h, scale_part, 0.0), axis=1, keepdims=True)
        scale_sums = jnp.where(scale_lane == h, of_head, scale_sums)
    small = [gain_part[:, i * LANES : (i + 1) * LANES] for i in range(width // LANES)] + [scale_sums]
    small = jnp.concatenate(small + [jnp.zeros((8 - len(small), LANES), F32)], axis=0)
    small_ref[...] = small


def small_rows(small):
    high = small.astype(BF).astype(F32)
    return jnp.concatenate([high[:4], (small - high)[:4]], axis=0)


def small_value(rows):
    value = rows.astype(BF).astype(F32)
    return value[:4] + value[4:]


def stacked(value):
    return jnp.concatenate(
        [value[:, i : i + LANES] for i in range(0, value.shape[1], LANES)], axis=0
    )


def unstacked(value, rows):
    return jnp.concatenate([value[i : i + rows] for i in range(0, value.shape[0], rows)], axis=1)


def core_sum_kernel(got_ref, keep_ref, keep_group_ref, small_ref, small_near_ref, *refs):
    *out_refs, own_ref, own_group_ref, small_sum_ref, blocks_ref = refs
    chips, per, width = keep_ref.shape
    feats = keep_group_ref.shape[2]
    small = small_ref[...] + small_near_ref[...]
    small_sum_ref[...] = small
    small = small_rows(small)
    chip = lax.axis_index("row") // 2
    own_ref[...] = keep_ref[chip] + got_ref[chip, :, :width].astype(F32)
    for q in range(chips):
        sums = keep_ref[q] + got_ref[q, :, :width].astype(F32)
        kept = keep_group_ref[q].astype(F32)
        first, second = in_order("row", kept, got_ref[q, :, width:].astype(F32))
        block = [stacked(sums), first, second, small]
        blocks_ref[q] = jnp.concatenate(block, axis=0).astype(BF)
    size = width // LANES * per
    own_group_ref[...] = blocks_ref[chip][size : size + 2 * per]
    for step, out_ref in enumerate(out_refs, 1):
        out_ref[...] = blocks_ref[partner(chip, step)]


def row_sum_kernel(sizes, *refs):
    rows, cols, width, n_col = sizes
    own_ref, own_group_ref, small_ref, *refs = refs
    got_refs, dm_ref, dm_near_ref, gx_ref, *refs = (refs[:3], *refs[3:])
    *out_refs, gx_sum_ref, slots_ref = refs
    gx_sum_ref[...] = gx_ref[...]
    per = own_ref.shape[0]
    feats = own_group_ref.shape[1]
    size = 4 * width // LANES * per

    def summed(first, part):
        fourth, third, second = [part(ref[...].astype(F32)) for ref in got_refs]
        return (first + second) + (third + fourth)

    sums = summed(stacked(own_ref[...]), lambda value: value[:size])
    sums = unstacked(sums, per)
    small = summed(small_value(small_rows(small_ref[...])), lambda value: small_value(value[size + 2 * per :]))
    group = [own_group_ref[...].astype(F32)]
    group += [ref[...].astype(F32)[size : size + 2 * per] for ref in got_refs[::-1]]
    group = [part[i * per : (i + 1) * per] for i in range(2) for part in group]
    group = jnp.concatenate(group, axis=0)
    own, near = (dm_ref[...].astype(F32), dm_near_ref[...].astype(F32))
    dm = jnp.concatenate(in_order("row", own, near), axis=0).astype(BF)
    merge = mm(group.T.astype(BF), dm)
    small = small_rows(small)
    col = lax.axis_index("col")
    third = 3 * width // n_col
    fourth = width // n_col
    depth = merge.shape[1] // n_col
    for slot in range(n_col):
        parts = [
            sums[:, slot * third : (slot + 1) * third],
            sums[:, 3 * width + slot * fourth : 3 * width + (slot + 1) * fourth],
        ]
        parts = [stacked(jnp.concatenate(parts, axis=1))]
        parts += [merge[:, slot * depth : (slot + 1) * depth], small]
        slots_ref[slot] = jnp.concatenate(parts, axis=0).astype(BF)
    for step, out_ref in enumerate(out_refs):
        out_ref[...] = slots_ref[partner(col, step)]


def partner(index, step):
    if step == 0:
        return index
    low = lax.rem(index, 2)
    if step == 1:
        return index + 1 - 2 * low
    if step == 2:
        return lax.rem(index + 2, 4)
    return 3 - index


def side_kernel(sizes, gx_ref, near_ref, far_ref, grad_ref, row_near_ref, row_far_ref):
    rows, cols, width = sizes
    ends = lax.axis_index("col")
    left, right = by_side("col", near_ref[...].astype(F32), far_ref[...].astype(F32))
    left = jnp.where(ends > 0, left, 0.0)
    right = jnp.where(ends < lax.axis_size("col") - 1, right, 0.0)
    blank = jnp.zeros((cols - 2 * EDGE, width), F32)
    pieces = []
    for i in range(rows + 2 * RADIUS):
        edge = slice(i * EDGE, (i + 1) * EDGE)
        pieces += [left[edge], blank, right[edge]]
    g_x = gx_ref[...] + jnp.concatenate(pieces, axis=0)
    reach = RADIUS * cols
    far, near = by_side("row", g_x[reach + rows * cols :], g_x[:reach])
    grad_ref[...] = g_x[reach : reach + rows * cols]
    row_near_ref[...] = near.astype(BF)
    row_far_ref[...] = far.astype(BF)


def col_sum_kernel(
    sizes,
    a_ref,
    d_ref,
    c_ref,
    b_ref,
    grad_ref,
    far_ref,
    near_ref,
    gqkv_ref,
    gout_ref,
    gmerge_ref,
    ggain_ref,
    gscale_ref,
    gtok_ref,
):
    rows, cols, width = sizes
    per, third = gqkv_ref.shape
    size = a_ref.shape[0] - 8

    def summed(part):
        first, second, third, fourth = [
            part(ref[...].astype(F32)) for ref in (a_ref, b_ref, c_ref, d_ref)
        ]
        return (first + second) + (third + fourth)

    total = summed(lambda value: value[:size])
    small = summed(lambda value: small_value(value[size:]))
    merge_at = size - gmerge_ref.shape[0]
    sums = unstacked(total[:merge_at], per)
    gqkv_ref[...] = sums[:, :third]
    gout_ref[...] = sums[:, third:]
    gmerge_ref[...] = total[merge_at:]
    ggain_ref[...] = jnp.concatenate([small[i : i + 1] for i in range(width // LANES)], axis=1)
    for h in range(gscale_ref.shape[0]):
        gscale_ref[h] = small[width // LANES, h]
    blank = jnp.zeros(((rows - RADIUS) * cols, width), F32)
    above, below = by_side("row", near_ref[...].astype(F32), far_ref[...].astype(F32))
    grad = grad_ref[...] + jnp.concatenate([above, blank], axis=0)
    grad = grad + jnp.concatenate([blank, below], axis=0)
    gtok_ref[...] = grad.astype(BF).reshape(rows, cols, width)


def plain_sums(width, sums, group, small, dm):
    sums = sums.astype(F32)
    merge = jnp.dot(group.T, dm, preferred_element_type=F32)
    outs = []
    for part in (sums[:, : 3 * width], sums[:, 3 * width :], merge):
        part = lax.psum_scatter(part, "row", scatter_dimension=0, tiled=True)
        outs.append(lax.psum_scatter(part, "col", scatter_dimension=1, tiled=True))
    small = lax.psum(small, ("row", "col"))
    return (*outs, small[: width // LANES].reshape(1, width), small[width // LANES])


def add_rows(grad, near, far, rows, cols):
    above, below = by_side("row", near.astype(F32), far.astype(F32))
    size = RADIUS * cols
    grad = grad.at[:size].add(above).at[rows * cols - size :].add(below)
    return grad.astype(BF).reshape(rows, cols, -1)


def swapped(near, far, axis):
    n_row, n_col = (lax.axis_size("row"), lax.axis_size("col"))
    pairs = []
    for row in range(n_row):
        for col in range(n_col):
            if axis == "row":
                other = row - 1 if row % 2 == 0 else row + 1
                target = (other, col) if 0 <= other < n_row else (row, col ^ 1)
            else:
                other = col - 1 if col % 2 == 0 else col + 1
                target = (row, other) if 0 <= other < n_col else (row ^ 1, col)
            pairs.append((row * n_col + col, target[0] * n_col + target[1]))
    return (swap(near, axis, 1), lax.ppermute(far, ("row", "col"), pairs))


def swap(value, axis, step):
    count = lax.axis_size(axis)
    return lax.ppermute(value, axis, [(i, i ^ step) for i in range(count)])


def vmem(count):
    return [pl.BlockSpec(memory_space=pltpu.VMEM)] * count


def on_device(tokens, gain, w_qkv, head_scale, w_out, w_merge, d_merged, d_skip):
    rows, cols, width = tokens.shape
    heads = head_scale.shape[0]
    n_row, n_col = (lax.axis_size("row"), lax.axis_size("col"))
    g_rows, g_cols, depth = d_merged.shape
    groups = g_rows * g_cols
    wide = cols + 2 * SIDE
    ext_rows = rows + 2 * RADIUS
    shape = jax.ShapeDtypeStruct
    params = pltpu.CompilerParams(vmem_limit_bytes=24 * 1024 * 1024)
    less = pltpu.CompilerParams(vmem_limit_bytes=8 * 1024 * 1024)
    row_near, row_far = swapped(tokens, tokens, "row")
    edge = shape((ext_rows * EDGE, width), BF)
    ones, parity = pl.pallas_call(
        first_kernel,
        out_shape=(shape((width, width), BF), shape((2 * heads, LANES), F32)),
        out_specs=tuple(vmem(2)),
        compiler_params=less,
        cost_estimate=pl.CostEstimate(flops=10**10, bytes_accessed=10**5, transcendentals=0),
    )()
    dm = d_merged.reshape(groups, depth)
    tile = shape((rows * cols, width), F32)
    half = shape((rows * cols, width), BF)
    edges, two_rows, q_norm, q_unit, d_y, d_attn = pl.pallas_call(
        own_kernel,
        out_shape=(shape((2 * rows * EDGE, width), BF), shape((8, width), F32), tile, tile, tile, half),
        in_specs=vmem(10),
        out_specs=tuple(vmem(6)),
        scratch_shapes=[pltpu.VMEM((width // LANES, rows, cols, LANES), F32)],
        compiler_params=params,
        cost_estimate=pl.CostEstimate(flops=10**9, bytes_accessed=10**6, transcendentals=0),
    )(
        ones,
        parity,
        head_scale.reshape(1, heads),
        tokens,
        d_merged,
        d_skip,
        gain.reshape(1, width),
        w_qkv,
        w_out,
        w_merge,
    )
    edge_near, edge_far = pl.pallas_call(
        edge_kernel,
        out_shape=(edge, edge),
        in_specs=vmem(3),
        out_specs=tuple(vmem(2)),
        compiler_params=less,
    )(edges, row_far, row_near)
    dm_pair = pl.pallas_call(
        pair_kernel,
        out_shape=shape((2 * groups, depth), BF),
        in_specs=vmem(2),
        out_specs=vmem(1)[0],
        compiler_params=less,
    )(d_merged, swap(dm, "row", 2))
    dms = [swap(dm_pair, "row", 4), dm_pair]
    col_near, col_far = swapped(edge_near, edge_far, "col")

    per = width // n_row
    feats = 4 * width // n_row
    packed = per % 16 == 0 and feats % LANES == 0 and groups == per
    packed = packed and width // LANES < 4 and feats == LANES and depth // n_col == LANES and n_col == 4 and n_row == 8
    if packed:
        sum_shapes = (
            shape((n_row // 2, per, 4 * width + feats), BF),
            shape((n_row // 2, per, 4 * width), F32),
            shape((n_row // 2, per, feats), BF),
        )
    else:
        sum_shapes = (
            shape((width, 4 * width), BF),
            shape((groups, 4 * width), BF),
        )
    sizes = (rows, cols, width, heads, n_row, n_col)
    tall = ext_rows * wide
    x, y, d_query, d_kv, grad_out, group, scale_part = pl.pallas_call(
        functools.partial(layer_kernel, sizes),
        out_shape=(
            shape((tall, width), F32),
            half,
            half,
            shape((tall, 2 * width), BF),
            shape((width, width), F32),
            shape((groups, 4 * width), BF),
            shape((8, width), F32),
        ),
        in_specs=vmem(13),
        out_specs=tuple(vmem(7)),
        scratch_shapes=[pltpu.VMEM((width // LANES, rows, cols, LANES), F32)],
        compiler_params=params,
        cost_estimate=pl.CostEstimate(flops=4 * 10**9, bytes_accessed=10**6, transcendentals=0),
    )(
        ones,
        tokens,
        row_far,
        row_near,
        col_near,
        col_far,
        two_rows,
        q_norm,
        q_unit,
        d_y,
        d_attn,
        w_qkv,
        w_out,
    )
    dm_core, *sums = pl.pallas_call(
        functools.partial(weights_kernel, (rows, cols, width, n_row, len(dms))),
        out_shape=(shape((2 * len(dms) * groups, depth), BF),) + sum_shapes,
        in_specs=vmem(6 + len(dms)),
        out_specs=tuple(vmem(1 + len(sum_shapes))),
        compiler_params=params,
        cost_estimate=pl.CostEstimate(flops=10**9, bytes_accessed=10**6, transcendentals=0),
    )(x, d_query, d_kv, grad_out, group, two_rows, *dms)
    gx, *sides = pl.pallas_call(
        functools.partial(norm_kernel, (rows, cols, width, heads)),
        out_shape=(shape((ext_rows * cols, width), F32), edge, edge, shape((8, LANES), F32)),
        in_specs=vmem(7),
        out_specs=tuple(vmem(4)),
        compiler_params=params,
        cost_estimate=pl.CostEstimate(flops=5 * 10**8, bytes_accessed=10**6, transcendentals=0),
    )(x, d_query, d_kv, scale_part, two_rows, d_y, w_qkv)
    *sides, small = sides
    sides = swapped(*sides, "col")
    skip_out, merged = pl.pallas_call(
        output_kernel,
        out_shape=(shape((rows, cols, width), BF), shape((g_rows, g_cols, depth), BF)),
        in_specs=vmem(3),
        out_specs=tuple(vmem(2)),
        compiler_params=less,
        cost_estimate=pl.CostEstimate(flops=10**9, bytes_accessed=10**6, transcendentals=0),
    )(y, group, w_merge)
    reach = shape((RADIUS * cols, width), BF)
    side_call = pl.pallas_call(
        functools.partial(side_kernel, (rows, cols, width)),
        out_shape=(tile, reach, reach),
        in_specs=vmem(3),
        out_specs=tuple(vmem(3)),
        compiler_params=less,
    )
    if not packed:
        grad, *rims = side_call(gx, *sides)
        grad_tokens = add_rows(grad, *swapped(*rims, "row"), rows, cols)
        g_qkv, g_out, g_merge, g_gain, g_scale = plain_sums(width, *sums, small, dm)
    else:
        send, *kept = sums
        block = shape((4 * width // LANES * per + 2 * per + 8, LANES), BF)
        *blocks, own, own_group, small = pl.pallas_call(
            core_sum_kernel,
            out_shape=(block, block, block)
            + (shape((per, 4 * width), F32), shape((2 * per, LANES), BF), shape((8, LANES), F32)),
            in_specs=vmem(5),
            out_specs=tuple(vmem(6)),
            scratch_shapes=[pltpu.VMEM((n_row // 2,) + block.shape, BF)],
            compiler_params=less,
            cost_estimate=pl.CostEstimate(flops=5 * 10**9, bytes_accessed=10**6, transcendentals=0),
        )(swap(send, "row", 1), *kept, small, swap(small, "row", 1))
        got = [swap(blocks[step - 1], "row", 2 * step) for step in (3, 2, 1)]
        slot = shape((4 * width // n_col // LANES * per + feats + 8, LANES), BF)
        *slots, gx = pl.pallas_call(
            functools.partial(row_sum_kernel, (rows, cols, width, n_col)),
            out_shape=(slot,) * n_col + (shape(gx.shape, F32),),
            in_specs=vmem(9),
            out_specs=tuple(vmem(n_col + 1)),
            scratch_shapes=[pltpu.VMEM((n_col,) + slot.shape, BF)],
            compiler_params=less,
        )(own, own_group, small, *got, dm_core, swap(dm_core, "row", 1), gx)
        got = [slots[0]] + [swap(slots[step], "col", step) for step in (3, 2, 1)]
        grad, *rims = side_call(gx, *sides)
        rims = swapped(*rims, "row")
        g_qkv, g_out, g_merge, g_gain, g_scale, grad_tokens = pl.pallas_call(
            functools.partial(col_sum_kernel, (rows, cols, width)),
            out_shape=(
                shape((per, 3 * width // n_col), F32),
                shape((per, width // n_col), F32),
                shape((feats, depth // n_col), F32),
                shape((1, width), F32),
                shape((heads,), F32),
                shape((rows, cols, width), BF),
            ),
            in_specs=vmem(7),
            out_specs=tuple(vmem(4)) + (pl.BlockSpec(memory_space=pltpu.SMEM), vmem(1)[0]),
            compiler_params=less,
        )(*got, grad, *rims[::-1])
    return (
        skip_out,
        merged,
        grad_tokens,
        g_qkv,
        g_out,
        g_merge,
        g_gain.reshape(width),
        g_scale[:heads],
    )


def solution(mesh):
    block = P("row", "col", None)
    return jax.shard_map(
        on_device,
        mesh=mesh,
        in_specs=(block, P(), P(), P(), P(), P(), block, block),
        out_specs=(block, block, block, P("row", "col"), P("row", "col"), P("row", "col"), P(), P()),
        check_vma=False,
    )
```

```python
import functools
import jax
import jax.numpy as jnp
from jax import lax
from jax.experimental import pallas as pl
from jax.experimental.pallas import tpu as pltpu
from jax.sharding import PartitionSpec as P

RADIUS = 3
IMG_MAX = 512
EPS = 1e-06
EDGE = 4
SIDE = 8
LANES = 128
BF = jnp.bfloat16
F32 = jnp.float32


def mm(a, b):
    return lax.dot_general(a, b, (((1,), (0,)), ((), ())), preferred_element_type=F32)


def mm_t(a, b):
    return lax.dot_general(a, b, (((1,), (1,)), ((), ())), preferred_element_type=F32)


def split_two(value):
    high = value.astype(BF)
    return (high, (value - high.astype(F32)).astype(BF))


def by_side(axis, near, far):
    even = lax.rem(lax.axis_index(axis), 2) == 0
    return (jnp.where(even, far, near), jnp.where(even, near, far))


def first_kernel(ones_ref, parity_ref):
    width = ones_ref.shape[0]
    head_dim = width // (parity_ref.shape[0] // 2)
    same_head = lax.broadcasted_iota(jnp.int32, (width, width), 0) // head_dim == (
        lax.broadcasted_iota(jnp.int32, (width, width), 1) // head_dim
    )
    ones_ref[...] = jnp.where(same_head, 1.0, 0.0).astype(BF)
    half = (parity_ref.shape[0] // 2, parity_ref.shape[1])
    parts = [
        jnp.where(lax.rem(lax.axis_index(axis), 2) == 0, jnp.ones(half, F32), jnp.zeros(half, F32))
        for axis in ("row", "col")
    ]
    parity_ref[...] = jnp.concatenate(parts, axis=0)


def pair_kernel(dm_ref, dm_next_ref, dm_pair_ref):
    size = dm_next_ref.shape[0]
    dm_pair_ref[...] = jnp.concatenate([dm_ref[...].reshape(size, -1), dm_next_ref[...]], axis=0)


def edge_kernel(edges_ref, far_ref, near_ref, edge_near_ref, edge_far_ref):
    rows, cols, width = near_ref.shape
    up, down = by_side("row", near_ref[...].astype(F32), far_ref[...].astype(F32))
    up = up[rows - RADIUS :]
    down = down[:RADIUS]
    halo = []
    for at in (0, cols - EDGE):
        parts = [part[:, at : at + EDGE].reshape(RADIUS * EDGE, width) for part in (up, down)]
        halo.append(jnp.concatenate(parts, axis=0))
    far, near = by_side("col", halo[1], halo[0])
    for out_ref, own_at, part in ((edge_near_ref, 0, near), (edge_far_ref, rows * EDGE, far)):
        own = edges_ref[own_at : own_at + rows * EDGE].astype(F32)
        size = RADIUS * EDGE
        out_ref[...] = jnp.concatenate([part[:size], own, part[size:]], axis=0).astype(BF)


def in_order(axis, own, partner):
    even = lax.rem(lax.axis_index(axis), 2) == 0
    return (jnp.where(even, own, partner), jnp.where(even, partner, own))


def head_sum(value, ones_ref):
    high, low = split_two(value)
    return mm(high, ones_ref[...]) + mm(low, ones_ref[...])


def own_kernel(
    ones_ref,
    parity_ref,
    scale_ref,
    tok_ref,
    gain_ref,
    wqkv_ref,
    edges_ref,
    rows_ref,
    q_norm_ref,
    q_unit_ref,
):
    rows, cols, width = tok_ref.shape
    tokens = rows * cols
    tok = tok_ref[...].astype(F32)
    left = tok[:, :EDGE].reshape(rows * EDGE, width)
    right = tok[:, cols - EDGE :].reshape(rows * EDGE, width)
    heads = scale_ref.shape[1]
    even = parity_ref[heads : heads + 1, 0:1] > 0.5
    near, far = (jnp.where(even, right, left), jnp.where(even, left, right))
    edges_ref[...] = jnp.concatenate([near, far], axis=0).astype(BF)
    lane = lax.broadcasted_iota(jnp.int32, (1, width), 1)
    scale_row = jnp.zeros((1, width), F32)
    for h in range(heads):
        scale_row = jnp.where(lane // (width // heads) == h, scale_ref[:, h : h + 1], scale_row)
    blank = jnp.zeros((6, width), F32)
    rows_ref[...] = jnp.concatenate([gain_ref[...], scale_row, blank], axis=0)
    x = tok.reshape(tokens, width)
    inverse = lax.rsqrt(jnp.mean(x * x, axis=1, keepdims=True) + EPS)
    normed = (x * inverse * gain_ref[...]).astype(BF)
    query = mm(normed, wqkv_ref[:, :width])
    q_norm = lax.rsqrt(head_sum(query * query, ones_ref) + EPS)
    q_norm_ref[...] = q_norm
    q_unit_ref[...] = query * q_norm


def cotangent_kernel(dm_ref, dskip_ref, wout_ref, wmerge_ref, dy_ref, d_attn_ref, dscr):
    rows, cols, width = dskip_ref.shape
    tokens = rows * cols
    group_wide = cols // 2
    d_in = mm_t(dm_ref[...].reshape(-1, dm_ref.shape[2]), wmerge_ref[...])
    for i in range(rows // 2):
        for pr in range(2):
            for pc in range(2):
                for part in range(width // LANES):
                    at = (2 * pr + pc) * width + part * LANES
                    dscr[part, 2 * i + pr, pl.ds(pc, group_wide, stride=2), :] = d_in[
                        i * group_wide : (i + 1) * group_wide, at : at + LANES
                    ]
    d_group = jnp.concatenate(
        [dscr[part].reshape(tokens, LANES) for part in range(width // LANES)], axis=1
    )
    d_y = dskip_ref[...].reshape(tokens, width).astype(F32) + d_group
    dy_ref[...] = d_y
    d_attn_ref[...] = mm_t(d_y.astype(BF), wout_ref[...]).astype(BF)


def layer_kernel(
    sizes,
    ones_ref,
    tok_ref,
    row_far_ref,
    row_near_ref,
    col_near_ref,
    col_far_ref,
    rows_ref,
    q_norm_ref,
    q_unit_ref,
    dy_ref,
    d_attn_ref,
    wqkv_ref,
    wout_ref,
    x_ref,
    y_ref,
    d_query_ref,
    d_kv_ref,
    grad_out_ref,
    group_ref,
    scale_part_ref,
    yscr,
):
    rows, cols, width, heads, n_row, n_col = sizes
    head_dim = width // heads
    wide = cols + 2 * SIDE
    ext_rows = rows + 2 * RADIUS
    tokens = rows * cols
    image_rows = min(IMG_MAX, rows * n_row)
    row_start = lax.axis_index("row") * rows
    col_index = lax.axis_index("col")
    col_start = col_index * cols
    first = row_start // image_rows * image_rows

    lane = lax.broadcasted_iota(jnp.int32, (1, width), 1)
    def blocks(value):
        zero = jnp.zeros_like(value)
        kept = [jnp.where(lane // head_dim == h, value, zero) for h in range(heads)]
        return jnp.concatenate(kept, axis=0).astype(BF)

    gain = rows_ref[0:1]
    scale_row = rows_ref[1:2]
    up, down = by_side("row", row_near_ref[...].astype(F32), row_far_ref[...].astype(F32))
    left, right = by_side("col", col_near_ref[...].astype(F32), col_far_ref[...].astype(F32))
    own = tok_ref[...].astype(F32)
    blank = jnp.zeros((SIDE - EDGE, width), F32)
    pieces = []
    for i in range(ext_rows):
        if i < RADIUS:
            row = up[rows - RADIUS + i]
        elif i < RADIUS + rows:
            row = own[i - RADIUS]
        else:
            row = down[i - RADIUS - rows]
        edge = slice(i * EDGE, (i + 1) * EDGE)
        pieces += [blank, left[edge], row, right[edge], blank]
    x = jnp.concatenate(pieces, axis=0)
    x_ref[...] = x
    inverse = lax.rsqrt(jnp.mean(x * x, axis=1, keepdims=True) + EPS)
    unit = x * inverse
    normed32 = (unit * gain).astype(BF).astype(F32)
    normed = normed32.astype(BF)
    x_own = inner_tokens(x, rows, cols)
    kv = mm(normed, wqkv_ref[:, width:])
    key_raw = kv[:, :width]
    k_norm = lax.rsqrt(head_sum(key_raw * key_raw, ones_ref) + EPS)
    k_unit = key_raw * k_norm
    keys = k_unit.astype(BF)
    values = kv[:, width:].astype(BF)
    q_norm = q_norm_ref[...]
    q_unit = q_unit_ref[...]
    q_hat = (q_unit * scale_row).astype(BF).astype(F32)
    d_y = dy_ref[...]
    dy_b = d_y.astype(BF)
    d_attn = d_attn_ref[...].astype(F32)

    index = lax.broadcasted_iota(jnp.int32, (1, tokens), 1)
    q_row = jnp.zeros_like(index)
    for i in range(1, rows):
        q_row = q_row + (index >= i * cols).astype(jnp.int32)
    q_col = index - q_row * cols
    key_col = lax.broadcasted_iota(jnp.int32, (wide, tokens), 0) - SIDE
    near = (key_col - q_col <= RADIUS) & (key_col - q_col >= -RADIUS)
    near = near & (key_col + col_start >= 0) & (key_col + col_start < cols * n_col)
    near = jnp.where(near, 1.0, 0.0)
    parts = []
    for i in range(-RADIUS, rows + RADIUS):
        ok = (q_row - i <= RADIUS) & (q_row - i >= -RADIUS)
        ok = ok & (row_start + i >= first) & (row_start + i < first + image_rows)
        parts.append(near * jnp.where(ok, 1.0, 0.0))
    allowed = jnp.concatenate([jnp.concatenate(parts, axis=0)] * heads, axis=1)
    q_blocks = blocks(q_hat)
    g_blocks = blocks(d_attn)
    expo = jnp.exp(mm_t(keys, q_blocks)) * allowed
    prob = expo * (1.0 / jnp.sum(expo, axis=0, keepdims=True))
    weights = prob.astype(BF)
    d_w = mm_t(values, g_blocks)
    delta = jnp.sum(d_w * prob, axis=0, keepdims=True)
    d_s = (prob * (d_w - delta)).astype(BF)
    values_t = values.astype(F32).T.astype(BF)
    keys_t = keys.astype(F32).T.astype(BF)
    attn_t = []
    d_qhat_t = []
    for h in range(heads):
        feats = slice(h * head_dim, (h + 1) * head_dim)
        lanes = slice(h * tokens, (h + 1) * tokens)
        attn_t.append(mm(values_t[feats], weights[:, lanes]))
        d_qhat_t.append(mm(keys_t[feats], d_s[:, lanes]))
    attn_t = jnp.concatenate(attn_t, axis=0)
    d_qhat = jnp.concatenate(d_qhat_t, axis=0).T
    d_k = mm(d_s, q_blocks)
    d_v = mm(weights, g_blocks)

    attn = attn_t.T.astype(BF)
    y = (x_own + mm(attn, wout_ref[...])).astype(BF)
    y_ref[...] = y
    y32 = y.astype(F32)
    for part in range(width // LANES):
        yscr[part] = y32[:, part * LANES : (part + 1) * LANES].reshape(rows, cols, LANES)
    lines = []
    for i in range(rows // 2):
        pieces = []
        for pr in range(2):
            for pc in range(2):
                for part in range(width // LANES):
                    pieces.append(yscr[part, 2 * i + pr, pl.ds(pc, cols // 2, stride=2), :])
        lines.append(jnp.concatenate(pieces, axis=1))
    group = jnp.concatenate(lines, axis=0).astype(BF)
    group_ref[...] = group
    grad_out_ref[...] = mm(attn_t.astype(BF), dy_b)

    scale_part_ref[...] = jnp.broadcast_to(
        jnp.sum(q_unit * d_qhat, axis=0, keepdims=True), scale_part_ref.shape
    )
    g_unit = d_qhat * scale_row
    d_query_ref[...] = (q_norm * (g_unit - q_unit * head_sum(q_unit * g_unit, ones_ref))).astype(BF)
    d_key = k_norm * (d_k - k_unit * head_sum(k_unit * d_k, ones_ref))
    d_kv_ref[...] = jnp.concatenate([d_key, d_v], axis=1).astype(BF)


def inner_tokens(value, rows, cols):
    wide = cols + 2 * SIDE
    pieces = []
    for i in range(RADIUS, RADIUS + rows):
        pieces.append(value[i * wide + SIDE : i * wide + SIDE + cols])
    return jnp.concatenate(pieces, axis=0)


def output_kernel(y_ref, group_ref, wmerge_ref, skip_ref, merged_ref):
    skip_ref[...] = y_ref[...].reshape(skip_ref.shape)
    merged = mm(group_ref[...], wmerge_ref[...])
    merged_ref[...] = merged.astype(BF).reshape(merged_ref.shape)


def weights_kernel(
    sizes, x_ref, d_query_ref, d_kv_ref, grad_out_ref, group_ref, rows_ref, *refs
):
    rows, cols, width, n_row, n_dm = sizes
    dm_refs, dm_all_ref, sum_refs = (refs[:n_dm], refs[n_dm], refs[n_dm + 1 :])
    size = dm_all_ref.shape[0] // n_dm
    dm = [ref[...].reshape(size, dm_all_ref.shape[1]) for ref in dm_refs]
    dm_all_ref[...] = jnp.concatenate(dm[::-1], axis=0)
    x = x_ref[...]
    inverse = lax.rsqrt(jnp.mean(x * x, axis=1, keepdims=True) + EPS)
    normed32 = (x * inverse * rows_ref[0:1]).astype(BF).astype(F32)
    grad_q = mm(inner_tokens(normed32, rows, cols).T.astype(BF), d_query_ref[...])
    grad_kv = mm(normed32.T.astype(BF), d_kv_ref[...])
    sums = jnp.concatenate([grad_q, grad_kv, grad_out_ref[...]], axis=1)
    group = group_ref[...]
    if len(sum_refs) == 2:
        sum_refs[0][...] = sums.astype(BF)
        sum_refs[1][...] = group
        return
    send_ref, keep_ref, keep_group_ref = sum_refs
    per = width // n_row
    feats = 4 * width // n_row
    group = group.astype(F32)
    even = lax.rem(lax.axis_index("row"), 2) == 0
    for q in range(n_row // 2):
        parts = []
        for value, axis, size in ((sums, 0, per), (group, 1, feats)):
            first = lax.slice_in_dim(value, 2 * q * size, (2 * q + 1) * size, axis=axis)
            second = lax.slice_in_dim(value, (2 * q + 1) * size, (2 * q + 2) * size, axis=axis)
            parts.append((jnp.where(even, first, second), jnp.where(even, second, first)))
        (keep_ref[q], sums_send), (keep_group, group_send) = parts
        keep_group_ref[q] = keep_group.astype(BF)
        send_ref[q] = jnp.concatenate([sums_send, group_send], axis=1).astype(BF)


def norm_kernel(
    sizes, x_ref, d_query_ref, d_kv_ref, scale_part_ref, rows_ref, dy_ref, wqkv_ref, *refs
):
    rows, cols, width, heads = sizes
    gx_ref, side_near_ref, side_far_ref, small_ref = refs
    head_dim = width // heads
    wide = cols + 2 * SIDE
    ext_rows = rows + 2 * RADIUS
    gain = rows_ref[0:1]
    lane = lax.broadcasted_iota(jnp.int32, (1, width), 1)
    x = x_ref[...]
    inverse = lax.rsqrt(jnp.mean(x * x, axis=1, keepdims=True) + EPS)
    unit = x * inverse
    d_y = dy_ref[...]
    from_q = mm_t(d_query_ref[...], wqkv_ref[:, :width])
    d_normed = mm_t(d_kv_ref[...], wqkv_ref[:, width:])
    pieces = []
    side = jnp.zeros((SIDE, width), F32)
    for i in range(ext_rows):
        if RADIUS <= i < RADIUS + rows:
            at = (i - RADIUS) * cols
            pieces += [side, from_q[at : at + cols], side]
        else:
            pieces.append(jnp.zeros((wide, width), F32))
    d_normed = d_normed + jnp.concatenate(pieces, axis=0)
    gain_part = jnp.sum(unit * d_normed, axis=0, keepdims=True)
    scaled = gain * d_normed
    mean = jnp.mean(x * scaled, axis=1, keepdims=True)
    g_x = inverse * scaled - x * (inverse * inverse * inverse) * mean

    pieces = []
    left = []
    right = []
    for i in range(ext_rows):
        row = g_x[i * wide : (i + 1) * wide]
        middle = row[SIDE : SIDE + cols]
        if RADIUS <= i < RADIUS + rows:
            middle = middle + d_y[(i - RADIUS) * cols : (i - RADIUS + 1) * cols]
        pieces.append(middle)
        left.append(row[:SIDE][SIDE - EDGE :])
        right.append(row[SIDE + cols :][:EDGE])
    gx_ref[...] = jnp.concatenate(pieces, axis=0)
    left, right = [jnp.concatenate(part, axis=0) for part in (left, right)]
    far, near = by_side("col", right, left)
    side_near_ref[...] = near.astype(BF)
    side_far_ref[...] = far.astype(BF)
    scale_part = scale_part_ref[0:1]
    scale_lane = lax.broadcasted_iota(jnp.int32, (1, LANES), 1)
    scale_sums = jnp.zeros((1, LANES), F32)
    for h in range(heads):
        of_head = jnp.sum(jnp.where(lane // head_dim == h, scale_part, 0.0), axis=1, keepdims=True)
        scale_sums = jnp.where(scale_lane == h, of_head, scale_sums)
    small = [gain_part[:, i * LANES : (i + 1) * LANES] for i in range(width // LANES)] + [scale_sums]
    small = jnp.concatenate(small + [jnp.zeros((8 - len(small), LANES), F32)], axis=0)
    small_ref[...] = small


def small_rows(small):
    high = small.astype(BF).astype(F32)
    return jnp.concatenate([high[:4], (small - high)[:4]], axis=0)


def small_value(rows):
    value = rows.astype(BF).astype(F32)
    return value[:4] + value[4:]


def stacked(value):
    return jnp.concatenate(
        [value[:, i : i + LANES] for i in range(0, value.shape[1], LANES)], axis=0
    )


def unstacked(value, rows):
    return jnp.concatenate([value[i : i + rows] for i in range(0, value.shape[0], rows)], axis=1)


def core_sum_kernel(got_ref, keep_ref, keep_group_ref, small_ref, small_near_ref, *refs):
    *out_refs, own_ref, own_group_ref, small_sum_ref, blocks_ref = refs
    chips, per, width = keep_ref.shape
    feats = keep_group_ref.shape[2]
    small = small_ref[...] + small_near_ref[...]
    small_sum_ref[...] = small
    small = small_rows(small)
    chip = lax.axis_index("row") // 2
    own_ref[...] = keep_ref[chip] + got_ref[chip, :, :width].astype(F32)
    for q in range(chips):
        sums = keep_ref[q] + got_ref[q, :, :width].astype(F32)
        kept = keep_group_ref[q].astype(F32)
        first, second = in_order("row", kept, got_ref[q, :, width:].astype(F32))
        block = [stacked(sums), first, second, small]
        blocks_ref[q] = jnp.concatenate(block, axis=0).astype(BF)
    size = width // LANES * per
    own_group_ref[...] = blocks_ref[chip][size : size + 2 * per]
    for step, out_ref in enumerate(out_refs, 1):
        out_ref[...] = blocks_ref[partner(chip, step)]


def row_sum_kernel(sizes, *refs):
    rows, cols, width, n_col = sizes
    own_ref, own_group_ref, small_ref, *refs = refs
    got_refs, dm_ref, dm_near_ref, gx_ref, *refs = (refs[:3], *refs[3:])
    *out_refs, gx_sum_ref, slots_ref = refs
    gx_sum_ref[...] = gx_ref[...]
    per = own_ref.shape[0]
    feats = own_group_ref.shape[1]
    size = 4 * width // LANES * per

    def summed(first, part):
        fourth, third, second = [part(ref[...].astype(F32)) for ref in got_refs]
        return (first + second) + (third + fourth)

    sums = summed(stacked(own_ref[...]), lambda value: value[:size])
    sums = unstacked(sums, per)
    small = summed(small_value(small_rows(small_ref[...])), lambda value: small_value(value[size + 2 * per :]))
    group = [own_group_ref[...].astype(F32)]
    group += [ref[...].astype(F32)[size : size + 2 * per] for ref in got_refs[::-1]]
    group = [part[i * per : (i + 1) * per] for i in range(2) for part in group]
    group = jnp.concatenate(group, axis=0)
    own, near = (dm_ref[...].astype(F32), dm_near_ref[...].astype(F32))
    dm = jnp.concatenate(in_order("row", own, near), axis=0).astype(BF)
    merge = mm(group.T.astype(BF), dm)
    small = small_rows(small)
    col = lax.axis_index("col")
    third = 3 * width // n_col
    fourth = width // n_col
    depth = merge.shape[1] // n_col
    for slot in range(n_col):
        parts = [
            sums[:, slot * third : (slot + 1) * third],
            sums[:, 3 * width + slot * fourth : 3 * width + (slot + 1) * fourth],
        ]
        parts = [stacked(jnp.concatenate(parts, axis=1))]
        parts += [merge[:, slot * depth : (slot + 1) * depth], small]
        slots_ref[slot] = jnp.concatenate(parts, axis=0).astype(BF)
    for step, out_ref in enumerate(out_refs):
        out_ref[...] = slots_ref[partner(col, step)]


def partner(index, step):
    if step == 0:
        return index
    low = lax.rem(index, 2)
    if step == 1:
        return index + 1 - 2 * low
    if step == 2:
        return lax.rem(index + 2, 4)
    return 3 - index


def side_kernel(sizes, gx_ref, near_ref, far_ref, grad_ref, row_near_ref, row_far_ref):
    rows, cols, width = sizes
    ends = lax.axis_index("col")
    left, right = by_side("col", near_ref[...].astype(F32), far_ref[...].astype(F32))
    left = jnp.where(ends > 0, left, 0.0)
    right = jnp.where(ends < lax.axis_size("col") - 1, right, 0.0)
    blank = jnp.zeros((cols - 2 * EDGE, width), F32)
    pieces = []
    for i in range(rows + 2 * RADIUS):
        edge = slice(i * EDGE, (i + 1) * EDGE)
        pieces += [left[edge], blank, right[edge]]
    g_x = gx_ref[...] + jnp.concatenate(pieces, axis=0)
    reach = RADIUS * cols
    far, near = by_side("row", g_x[reach + rows * cols :], g_x[:reach])
    grad_ref[...] = g_x[reach : reach + rows * cols]
    row_near_ref[...] = near.astype(BF)
    row_far_ref[...] = far.astype(BF)


def col_sum_kernel(
    sizes,
    a_ref,
    d_ref,
    c_ref,
    b_ref,
    grad_ref,
    far_ref,
    near_ref,
    gqkv_ref,
    gout_ref,
    gmerge_ref,
    ggain_ref,
    gscale_ref,
    gtok_ref,
):
    rows, cols, width = sizes
    per, third = gqkv_ref.shape
    size = a_ref.shape[0] - 8

    def summed(part):
        first, second, third, fourth = [
            part(ref[...].astype(F32)) for ref in (a_ref, b_ref, c_ref, d_ref)
        ]
        return (first + second) + (third + fourth)

    total = summed(lambda value: value[:size])
    small = summed(lambda value: small_value(value[size:]))
    merge_at = size - gmerge_ref.shape[0]
    sums = unstacked(total[:merge_at], per)
    gqkv_ref[...] = sums[:, :third]
    gout_ref[...] = sums[:, third:]
    gmerge_ref[...] = total[merge_at:]
    ggain_ref[...] = jnp.concatenate([small[i : i + 1] for i in range(width // LANES)], axis=1)
    for h in range(gscale_ref.shape[0]):
        gscale_ref[h] = small[width // LANES, h]
    blank = jnp.zeros(((rows - RADIUS) * cols, width), F32)
    above, below = by_side("row", near_ref[...].astype(F32), far_ref[...].astype(F32))
    grad = grad_ref[...] + jnp.concatenate([above, blank], axis=0)
    grad = grad + jnp.concatenate([blank, below], axis=0)
    gtok_ref[...] = grad.astype(BF).reshape(rows, cols, width)


def plain_sums(width, sums, group, small, dm):
    sums = sums.astype(F32)
    merge = jnp.dot(group.T, dm, preferred_element_type=F32)
    outs = []
    for part in (sums[:, : 3 * width], sums[:, 3 * width :], merge):
        part = lax.psum_scatter(part, "row", scatter_dimension=0, tiled=True)
        outs.append(lax.psum_scatter(part, "col", scatter_dimension=1, tiled=True))
    small = lax.psum(small, ("row", "col"))
    return (*outs, small[: width // LANES].reshape(1, width), small[width // LANES])


def add_rows(grad, near, far, rows, cols):
    above, below = by_side("row", near.astype(F32), far.astype(F32))
    size = RADIUS * cols
    grad = grad.at[:size].add(above).at[rows * cols - size :].add(below)
    return grad.astype(BF).reshape(rows, cols, -1)


def swapped(near, far, axis):
    n_row, n_col = (lax.axis_size("row"), lax.axis_size("col"))
    pairs = []
    for row in range(n_row):
        for col in range(n_col):
            if axis == "row":
                other = row - 1 if row % 2 == 0 else row + 1
                target = (other, col) if 0 <= other < n_row else (row, col ^ 1)
            else:
                other = col - 1 if col % 2 == 0 else col + 1
                target = (row, other) if 0 <= other < n_col else (row ^ 1, col)
            pairs.append((row * n_col + col, target[0] * n_col + target[1]))
    return (swap(near, axis, 1), lax.ppermute(far, ("row", "col"), pairs))


def swap(value, axis, step):
    count = lax.axis_size(axis)
    return lax.ppermute(value, axis, [(i, i ^ step) for i in range(count)])


def vmem(count):
    return [pl.BlockSpec(memory_space=pltpu.VMEM)] * count


def on_device(tokens, gain, w_qkv, head_scale, w_out, w_merge, d_merged, d_skip):
    rows, cols, width = tokens.shape
    heads = head_scale.shape[0]
    n_row, n_col = (lax.axis_size("row"), lax.axis_size("col"))
    g_rows, g_cols, depth = d_merged.shape
    groups = g_rows * g_cols
    wide = cols + 2 * SIDE
    ext_rows = rows + 2 * RADIUS
    shape = jax.ShapeDtypeStruct
    params = pltpu.CompilerParams(vmem_limit_bytes=24 * 1024 * 1024)
    less = pltpu.CompilerParams(vmem_limit_bytes=8 * 1024 * 1024)
    row_near, row_far = swapped(tokens, tokens, "row")
    edge = shape((ext_rows * EDGE, width), BF)
    ones, parity = pl.pallas_call(
        first_kernel,
        out_shape=(shape((width, width), BF), shape((2 * heads, LANES), F32)),
        out_specs=tuple(vmem(2)),
        compiler_params=less,
        cost_estimate=pl.CostEstimate(flops=10**10, bytes_accessed=10**5, transcendentals=0),
    )()
    dm = d_merged.reshape(groups, depth)
    tile = shape((rows * cols, width), F32)
    half = shape((rows * cols, width), BF)
    edges, two_rows, q_norm, q_unit = pl.pallas_call(
        own_kernel,
        out_shape=(shape((2 * rows * EDGE, width), BF), shape((8, width), F32), tile, tile),
        in_specs=vmem(6),
        out_specs=tuple(vmem(4)),
        compiler_params=params,
        cost_estimate=pl.CostEstimate(flops=5 * 10**8, bytes_accessed=10**6, transcendentals=0),
    )(ones, parity, head_scale.reshape(1, heads), tokens, gain.reshape(1, width), w_qkv)
    d_y, d_attn = pl.pallas_call(
        cotangent_kernel,
        out_shape=(tile, half),
        in_specs=vmem(4),
        out_specs=tuple(vmem(2)),
        scratch_shapes=[pltpu.VMEM((width // LANES, rows, cols, LANES), F32)],
        compiler_params=params,
        cost_estimate=pl.CostEstimate(flops=5 * 10**8, bytes_accessed=10**6, transcendentals=0),
    )(d_merged, d_skip, w_out, w_merge)
    edge_near, edge_far = pl.pallas_call(
        edge_kernel,
        out_shape=(edge, edge),
        in_specs=vmem(3),
        out_specs=tuple(vmem(2)),
        compiler_params=less,
    )(edges, row_far, row_near)
    dm_pair = pl.pallas_call(
        pair_kernel,
        out_shape=shape((2 * groups, depth), BF),
        in_specs=vmem(2),
        out_specs=vmem(1)[0],
        compiler_params=less,
    )(d_merged, swap(dm, "row", 2))
    dms = [swap(dm_pair, "row", 4), dm_pair]
    col_near, col_far = swapped(edge_near, edge_far, "col")

    per = width // n_row
    feats = 4 * width // n_row
    packed = per % 16 == 0 and feats % LANES == 0 and groups == per
    packed = packed and width // LANES < 4 and feats == LANES and depth // n_col == LANES and n_col == 4 and n_row == 8
    if packed:
        sum_shapes = (
            shape((n_row // 2, per, 4 * width + feats), BF),
            shape((n_row // 2, per, 4 * width), F32),
            shape((n_row // 2, per, feats), BF),
        )
    else:
        sum_shapes = (
            shape((width, 4 * width), BF),
            shape((groups, 4 * width), BF),
        )
    sizes = (rows, cols, width, heads, n_row, n_col)
    tall = ext_rows * wide
    x, y, d_query, d_kv, grad_out, group, scale_part = pl.pallas_call(
        functools.partial(layer_kernel, sizes),
        out_shape=(
            shape((tall, width), F32),
            half,
            half,
            shape((tall, 2 * width), BF),
            shape((width, width), F32),
            shape((groups, 4 * width), BF),
            shape((8, width), F32),
        ),
        in_specs=vmem(13),
        out_specs=tuple(vmem(7)),
        scratch_shapes=[pltpu.VMEM((width // LANES, rows, cols, LANES), F32)],
        compiler_params=params,
        cost_estimate=pl.CostEstimate(flops=4 * 10**9, bytes_accessed=10**6, transcendentals=0),
    )(
        ones,
        tokens,
        row_far,
        row_near,
        col_near,
        col_far,
        two_rows,
        q_norm,
        q_unit,
        d_y,
        d_attn,
        w_qkv,
        w_out,
    )
    dm_core, *sums = pl.pallas_call(
        functools.partial(weights_kernel, (rows, cols, width, n_row, len(dms))),
        out_shape=(shape((2 * len(dms) * groups, depth), BF),) + sum_shapes,
        in_specs=vmem(6 + len(dms)),
        out_specs=tuple(vmem(1 + len(sum_shapes))),
        compiler_params=params,
        cost_estimate=pl.CostEstimate(flops=10**9, bytes_accessed=10**6, transcendentals=0),
    )(x, d_query, d_kv, grad_out, group, two_rows, *dms)
    gx, *sides = pl.pallas_call(
        functools.partial(norm_kernel, (rows, cols, width, heads)),
        out_shape=(shape((ext_rows * cols, width), F32), edge, edge, shape((8, LANES), F32)),
        in_specs=vmem(7),
        out_specs=tuple(vmem(4)),
        compiler_params=params,
        cost_estimate=pl.CostEstimate(flops=5 * 10**8, bytes_accessed=10**6, transcendentals=0),
    )(x, d_query, d_kv, scale_part, two_rows, d_y, w_qkv)
    *sides, small = sides
    sides = swapped(*sides, "col")
    skip_out, merged = pl.pallas_call(
        output_kernel,
        out_shape=(shape((rows, cols, width), BF), shape((g_rows, g_cols, depth), BF)),
        in_specs=vmem(3),
        out_specs=tuple(vmem(2)),
        compiler_params=less,
        cost_estimate=pl.CostEstimate(flops=10**9, bytes_accessed=10**6, transcendentals=0),
    )(y, group, w_merge)
    reach = shape((RADIUS * cols, width), BF)
    side_call = pl.pallas_call(
        functools.partial(side_kernel, (rows, cols, width)),
        out_shape=(tile, reach, reach),
        in_specs=vmem(3),
        out_specs=tuple(vmem(3)),
        compiler_params=less,
    )
    if not packed:
        grad, *rims = side_call(gx, *sides)
        grad_tokens = add_rows(grad, *swapped(*rims, "row"), rows, cols)
        g_qkv, g_out, g_merge, g_gain, g_scale = plain_sums(width, *sums, small, dm)
    else:
        send, *kept = sums
        block = shape((4 * width // LANES * per + 2 * per + 8, LANES), BF)
        *blocks, own, own_group, small = pl.pallas_call(
            core_sum_kernel,
            out_shape=(block, block, block)
            + (shape((per, 4 * width), F32), shape((2 * per, LANES), BF), shape((8, LANES), F32)),
            in_specs=vmem(5),
            out_specs=tuple(vmem(6)),
            scratch_shapes=[pltpu.VMEM((n_row // 2,) + block.shape, BF)],
            compiler_params=less,
            cost_estimate=pl.CostEstimate(flops=5 * 10**9, bytes_accessed=10**6, transcendentals=0),
        )(swap(send, "row", 1), *kept, small, swap(small, "row", 1))
        got = [swap(blocks[step - 1], "row", 2 * step) for step in (3, 2, 1)]
        slot = shape((4 * width // n_col // LANES * per + feats + 8, LANES), BF)
        *slots, gx = pl.pallas_call(
            functools.partial(row_sum_kernel, (rows, cols, width, n_col)),
            out_shape=(slot,) * n_col + (shape(gx.shape, F32),),
            in_specs=vmem(9),
            out_specs=tuple(vmem(n_col + 1)),
            scratch_shapes=[pltpu.VMEM((n_col,) + slot.shape, BF)],
            compiler_params=less,
        )(own, own_group, small, *got, dm_core, swap(dm_core, "row", 1), gx)
        got = [slots[0]] + [swap(slots[step], "col", step) for step in (3, 2, 1)]
        grad, *rims = side_call(gx, *sides)
        rims = swapped(*rims, "row")
        g_qkv, g_out, g_merge, g_gain, g_scale, grad_tokens = pl.pallas_call(
            functools.partial(col_sum_kernel, (rows, cols, width)),
            out_shape=(
                shape((per, 3 * width // n_col), F32),
                shape((per, width // n_col), F32),
                shape((feats, depth // n_col), F32),
                shape((1, width), F32),
                shape((heads,), F32),
                shape((rows, cols, width), BF),
            ),
            in_specs=vmem(7),
            out_specs=tuple(vmem(4)) + (pl.BlockSpec(memory_space=pltpu.SMEM), vmem(1)[0]),
            compiler_params=less,
        )(*got, grad, *rims[::-1])
    return (
        skip_out,
        merged,
        grad_tokens,
        g_qkv,
        g_out,
        g_merge,
        g_gain.reshape(width),
        g_scale[:heads],
    )


def solution(mesh):
    block = P("row", "col", None)
    return jax.shard_map(
        on_device,
        mesh=mesh,
        in_specs=(block, P(), P(), P(), P(), P(), block, block),
        out_specs=(block, block, block, P("row", "col"), P("row", "col"), P("row", "col"), P(), P()),
        check_vma=False,
    )
```

```python
import functools
import jax
import jax.numpy as jnp
from jax import lax
from jax.experimental import pallas as pl
from jax.experimental.pallas import tpu as pltpu
from jax.sharding import PartitionSpec as P

RADIUS = 3
IMG_MAX = 512
EPS = 1e-06
EDGE = 4
SIDE = 8
LANES = 128
BF = jnp.bfloat16
F32 = jnp.float32


def mm(a, b):
    return lax.dot_general(a, b, (((1,), (0,)), ((), ())), preferred_element_type=F32)


def mm_t(a, b):
    return lax.dot_general(a, b, (((1,), (1,)), ((), ())), preferred_element_type=F32)


def split_two(value):
    high = value.astype(BF)
    return (high, (value - high.astype(F32)).astype(BF))


def by_side(axis, near, far):
    even = lax.rem(lax.axis_index(axis), 2) == 0
    return (jnp.where(even, far, near), jnp.where(even, near, far))


def first_kernel(ones_ref, parity_ref):
    width = ones_ref.shape[0]
    head_dim = width // (parity_ref.shape[0] // 2)
    same_head = lax.broadcasted_iota(jnp.int32, (width, width), 0) // head_dim == (
        lax.broadcasted_iota(jnp.int32, (width, width), 1) // head_dim
    )
    ones_ref[...] = jnp.where(same_head, 1.0, 0.0).astype(BF)
    half = (parity_ref.shape[0] // 2, parity_ref.shape[1])
    parts = [
        jnp.where(lax.rem(lax.axis_index(axis), 2) == 0, jnp.ones(half, F32), jnp.zeros(half, F32))
        for axis in ("row", "col")
    ]
    parity_ref[...] = jnp.concatenate(parts, axis=0)


def pair_kernel(dm_ref, dm_next_ref, dm_pair_ref):
    size = dm_next_ref.shape[0]
    dm_pair_ref[...] = jnp.concatenate([dm_ref[...].reshape(size, -1), dm_next_ref[...]], axis=0)


def edge_kernel(edges_ref, far_ref, near_ref, edge_near_ref, edge_far_ref):
    rows, cols, width = near_ref.shape
    up, down = by_side("row", near_ref[...].astype(F32), far_ref[...].astype(F32))
    up = up[rows - RADIUS :]
    down = down[:RADIUS]
    halo = []
    for at in (0, cols - EDGE):
        parts = [part[:, at : at + EDGE].reshape(RADIUS * EDGE, width) for part in (up, down)]
        halo.append(jnp.concatenate(parts, axis=0))
    far, near = by_side("col", halo[1], halo[0])
    for out_ref, own_at, part in ((edge_near_ref, 0, near), (edge_far_ref, rows * EDGE, far)):
        own = edges_ref[own_at : own_at + rows * EDGE].astype(F32)
        size = RADIUS * EDGE
        out_ref[...] = jnp.concatenate([part[:size], own, part[size:]], axis=0).astype(BF)


def in_order(axis, own, partner):
    even = lax.rem(lax.axis_index(axis), 2) == 0
    return (jnp.where(even, own, partner), jnp.where(even, partner, own))


def head_sum(value, ones_ref):
    high, low = split_two(value)
    return mm(high, ones_ref[...]) + mm(low, ones_ref[...])


def own_kernel(
    ones_ref,
    parity_ref,
    scale_ref,
    tok_ref,
    dm_ref,
    dskip_ref,
    gain_ref,
    wqkv_ref,
    wout_ref,
    wmerge_ref,
    edges_ref,
    rows_ref,
    q_norm_ref,
    q_unit_ref,
    dy_ref,
    d_attn_ref,
    dscr,
):
    rows, cols, width = tok_ref.shape
    tokens = rows * cols
    tok = tok_ref[...].astype(F32)
    left = tok[:, :EDGE].reshape(rows * EDGE, width)
    right = tok[:, cols - EDGE :].reshape(rows * EDGE, width)
    heads = scale_ref.shape[1]
    even = parity_ref[heads : heads + 1, 0:1] > 0.5
    near, far = (jnp.where(even, right, left), jnp.where(even, left, right))
    edges_ref[...] = jnp.concatenate([near, far], axis=0).astype(BF)
    lane = lax.broadcasted_iota(jnp.int32, (1, width), 1)
    scale_row = jnp.zeros((1, width), F32)
    for h in range(heads):
        scale_row = jnp.where(lane // (width // heads) == h, scale_ref[:, h : h + 1], scale_row)
    blank = jnp.zeros((6, width), F32)
    rows_ref[...] = jnp.concatenate([gain_ref[...], scale_row, blank], axis=0)
    x = tok.reshape(tokens, width)
    inverse = lax.rsqrt(jnp.mean(x * x, axis=1, keepdims=True) + EPS)
    normed = (x * inverse * gain_ref[...]).astype(BF)
    query = mm(normed, wqkv_ref[:, :width])
    q_norm = lax.rsqrt(head_sum(query * query, ones_ref) + EPS)
    q_norm_ref[...] = q_norm
    q_unit_ref[...] = query * q_norm
    group_wide = cols // 2
    d_in = mm_t(dm_ref[...].reshape(-1, dm_ref.shape[2]), wmerge_ref[...])
    for i in range(rows // 2):
        for pr in range(2):
            for pc in range(2):
                for part in range(width // LANES):
                    at = (2 * pr + pc) * width + part * LANES
                    dscr[part, 2 * i + pr, pl.ds(pc, group_wide, stride=2), :] = d_in[
                        i * group_wide : (i + 1) * group_wide, at : at + LANES
                    ]
    d_group = jnp.concatenate(
        [dscr[part].reshape(tokens, LANES) for part in range(width // LANES)], axis=1
    )
    d_y = dskip_ref[...].reshape(tokens, width).astype(F32) + d_group
    dy_ref[...] = d_y
    d_attn_ref[...] = mm_t(d_y.astype(BF), wout_ref[...]).astype(BF)


def layer_kernel(
    sizes,
    ones_ref,
    tok_ref,
    row_far_ref,
    row_near_ref,
    col_near_ref,
    col_far_ref,
    rows_ref,
    q_norm_ref,
    q_unit_ref,
    dy_ref,
    d_attn_ref,
    wqkv_ref,
    wout_ref,
    x_ref,
    y_ref,
    d_query_ref,
    d_kv_ref,
    grad_out_ref,
    group_ref,
    scale_part_ref,
    yscr,
):
    rows, cols, width, heads, n_row, n_col = sizes
    head_dim = width // heads
    wide = cols + 2 * SIDE
    ext_rows = rows + 2 * RADIUS
    tokens = rows * cols
    image_rows = min(IMG_MAX, rows * n_row)
    row_start = lax.axis_index("row") * rows
    col_index = lax.axis_index("col")
    col_start = col_index * cols
    first = row_start // image_rows * image_rows

    lane = lax.broadcasted_iota(jnp.int32, (1, width), 1)
    def blocks(value):
        zero = jnp.zeros_like(value)
        kept = [jnp.where(lane // head_dim == h, value, zero) for h in range(heads)]
        return jnp.concatenate(kept, axis=0).astype(BF)

    gain = rows_ref[0:1]
    scale_row = rows_ref[1:2]
    up, down = by_side("row", row_near_ref[...].astype(F32), row_far_ref[...].astype(F32))
    left, right = by_side("col", col_near_ref[...].astype(F32), col_far_ref[...].astype(F32))
    own = tok_ref[...].astype(F32)
    blank = jnp.zeros((SIDE - EDGE, width), F32)
    pieces = []
    for i in range(ext_rows):
        if i < RADIUS:
            row = up[rows - RADIUS + i]
        elif i < RADIUS + rows:
            row = own[i - RADIUS]
        else:
            row = down[i - RADIUS - rows]
        edge = slice(i * EDGE, (i + 1) * EDGE)
        pieces += [blank, left[edge], row, right[edge], blank]
    x = jnp.concatenate(pieces, axis=0)
    x_ref[...] = x
    inverse = lax.rsqrt(jnp.mean(x * x, axis=1, keepdims=True) + EPS)
    unit = x * inverse
    normed32 = (unit * gain).astype(BF).astype(F32)
    normed = normed32.astype(BF)
    x_own = inner_tokens(x, rows, cols)
    kv = mm(normed, wqkv_ref[:, width:])
    key_raw = kv[:, :width]
    k_norm = lax.rsqrt(head_sum(key_raw * key_raw, ones_ref) + EPS)
    k_unit = key_raw * k_norm
    keys = k_unit.astype(BF)
    values = kv[:, width:].astype(BF)
    q_norm = q_norm_ref[...]
    q_unit = q_unit_ref[...]
    q_hat = (q_unit * scale_row).astype(BF).astype(F32)
    d_y = dy_ref[...]
    dy_b = d_y.astype(BF)
    d_attn = d_attn_ref[...].astype(F32)

    index = lax.broadcasted_iota(jnp.int32, (1, tokens), 1)
    q_row = jnp.zeros_like(index)
    for i in range(1, rows):
        q_row = q_row + (index >= i * cols).astype(jnp.int32)
    q_col = index - q_row * cols
    key_col = lax.broadcasted_iota(jnp.int32, (wide, tokens), 0) - SIDE
    near = (key_col - q_col <= RADIUS) & (key_col - q_col >= -RADIUS)
    near = near & (key_col + col_start >= 0) & (key_col + col_start < cols * n_col)
    near = jnp.where(near, 1.0, 0.0)
    parts = []
    for i in range(-RADIUS, rows + RADIUS):
        ok = (q_row - i <= RADIUS) & (q_row - i >= -RADIUS)
        ok = ok & (row_start + i >= first) & (row_start + i < first + image_rows)
        parts.append(near * jnp.where(ok, 1.0, 0.0))
    allowed = jnp.concatenate([jnp.concatenate(parts, axis=0)] * heads, axis=1)
    q_blocks = blocks(q_hat)
    g_blocks = blocks(d_attn)
    expo = jnp.exp(mm_t(keys, q_blocks)) * allowed
    prob = expo * (1.0 / jnp.sum(expo, axis=0, keepdims=True))
    weights = prob.astype(BF)
    d_w = mm_t(values, g_blocks)
    delta = jnp.sum(d_w * prob, axis=0, keepdims=True)
    d_s = (prob * (d_w - delta)).astype(BF)
    values_t = values.astype(F32).T.astype(BF)
    keys_t = keys.astype(F32).T.astype(BF)
    attn_t = []
    d_qhat_t = []
    for h in range(heads):
        feats = slice(h * head_dim, (h + 1) * head_dim)
        lanes = slice(h * tokens, (h + 1) * tokens)
        attn_t.append(mm(values_t[feats], weights[:, lanes]))
        d_qhat_t.append(mm(keys_t[feats], d_s[:, lanes]))
    attn_t = jnp.concatenate(attn_t, axis=0)
    d_qhat = jnp.concatenate(d_qhat_t, axis=0).T
    d_k = mm(d_s, q_blocks)
    d_v = mm(weights, g_blocks)

    attn = attn_t.T.astype(BF)
    y = (x_own + mm(attn, wout_ref[...])).astype(BF)
    y_ref[...] = y
    y32 = y.astype(F32)
    for part in range(width // LANES):
        yscr[part] = y32[:, part * LANES : (part + 1) * LANES].reshape(rows, cols, LANES)
    lines = []
    for i in range(rows // 2):
        pieces = []
        for pr in range(2):
            for pc in range(2):
                for part in range(width // LANES):
                    pieces.append(yscr[part, 2 * i + pr, pl.ds(pc, cols // 2, stride=2), :])
        lines.append(jnp.concatenate(pieces, axis=1))
    group = jnp.concatenate(lines, axis=0).astype(BF)
    group_ref[...] = group
    grad_out_ref[...] = mm(attn_t.astype(BF), dy_b)

    scale_part_ref[...] = jnp.broadcast_to(
        jnp.sum(q_unit * d_qhat, axis=0, keepdims=True), scale_part_ref.shape
    )
    g_unit = d_qhat * scale_row
    d_query_ref[...] = (q_norm * (g_unit - q_unit * head_sum(q_unit * g_unit, ones_ref))).astype(BF)
    d_key = k_norm * (d_k - k_unit * head_sum(k_unit * d_k, ones_ref))
    d_kv_ref[...] = jnp.concatenate([d_key, d_v], axis=1).astype(BF)


def inner_tokens(value, rows, cols):
    wide = cols + 2 * SIDE
    pieces = []
    for i in range(RADIUS, RADIUS + rows):
        pieces.append(value[i * wide + SIDE : i * wide + SIDE + cols])
    return jnp.concatenate(pieces, axis=0)


def output_kernel(y_ref, group_ref, wmerge_ref, skip_ref, merged_ref):
    skip_ref[...] = y_ref[...].reshape(skip_ref.shape)
    merged = mm(group_ref[...], wmerge_ref[...])
    merged_ref[...] = merged.astype(BF).reshape(merged_ref.shape)


def weights_kernel(
    sizes, x_ref, d_query_ref, d_kv_ref, grad_out_ref, group_ref, rows_ref, *refs
):
    rows, cols, width, n_row, n_dm = sizes
    dm_refs, dm_all_ref, sum_refs = (refs[:n_dm], refs[n_dm], refs[n_dm + 1 :])
    size = dm_all_ref.shape[0] // n_dm
    dm = [ref[...].reshape(size, dm_all_ref.shape[1]) for ref in dm_refs]
    dm_all_ref[...] = jnp.concatenate(dm[::-1], axis=0)
    x = x_ref[...]
    inverse = lax.rsqrt(jnp.mean(x * x, axis=1, keepdims=True) + EPS)
    normed32 = (x * inverse * rows_ref[0:1]).astype(BF).astype(F32)
    grad_q = mm(inner_tokens(normed32, rows, cols).T.astype(BF), d_query_ref[...])
    grad_kv = mm(normed32.T.astype(BF), d_kv_ref[...])
    sums = jnp.concatenate([grad_q, grad_kv, grad_out_ref[...]], axis=1)
    group = group_ref[...]
    if len(sum_refs) == 2:
        sum_refs[0][...] = sums.astype(BF)
        sum_refs[1][...] = group
        return
    send_ref, keep_ref, keep_group_ref = sum_refs
    per = width // n_row
    feats = 4 * width // n_row
    group = group.astype(F32)
    even = lax.rem(lax.axis_index("row"), 2) == 0
    for q in range(n_row // 2):
        parts = []
        for value, axis, size in ((sums, 0, per), (group, 1, feats)):
            first = lax.slice_in_dim(value, 2 * q * size, (2 * q + 1) * size, axis=axis)
            second = lax.slice_in_dim(value, (2 * q + 1) * size, (2 * q + 2) * size, axis=axis)
            parts.append((jnp.where(even, first, second), jnp.where(even, second, first)))
        (keep_ref[q], sums_send), (keep_group, group_send) = parts
        keep_group_ref[q] = keep_group.astype(BF)
        send_ref[q] = jnp.concatenate([sums_send, group_send], axis=1).astype(BF)


def norm_kernel(
    sizes, x_ref, d_query_ref, d_kv_ref, scale_part_ref, rows_ref, dy_ref, wqkv_ref, *refs
):
    rows, cols, width, heads = sizes
    gx_ref, side_near_ref, side_far_ref, small_ref = refs
    head_dim = width // heads
    wide = cols + 2 * SIDE
    ext_rows = rows + 2 * RADIUS
    gain = rows_ref[0:1]
    lane = lax.broadcasted_iota(jnp.int32, (1, width), 1)
    x = x_ref[...]
    inverse = lax.rsqrt(jnp.mean(x * x, axis=1, keepdims=True) + EPS)
    unit = x * inverse
    d_y = dy_ref[...]
    from_q = mm_t(d_query_ref[...], wqkv_ref[:, :width])
    d_normed = mm_t(d_kv_ref[...], wqkv_ref[:, width:])
    pieces = []
    side = jnp.zeros((SIDE, width), F32)
    for i in range(ext_rows):
        if RADIUS <= i < RADIUS + rows:
            at = (i - RADIUS) * cols
            pieces += [side, from_q[at : at + cols], side]
        else:
            pieces.append(jnp.zeros((wide, width), F32))
    d_normed = d_normed + jnp.concatenate(pieces, axis=0)
    gain_part = jnp.sum(unit * d_normed, axis=0, keepdims=True)
    scaled = gain * d_normed
    mean = jnp.mean(x * scaled, axis=1, keepdims=True)
    g_x = inverse * scaled - x * (inverse * inverse * inverse) * mean

    pieces = []
    left = []
    right = []
    for i in range(ext_rows):
        row = g_x[i * wide : (i + 1) * wide]
        middle = row[SIDE : SIDE + cols]
        if RADIUS <= i < RADIUS + rows:
            middle = middle + d_y[(i - RADIUS) * cols : (i - RADIUS + 1) * cols]
        pieces.append(middle)
        left.append(row[:SIDE][SIDE - EDGE :])
        right.append(row[SIDE + cols :][:EDGE])
    gx_ref[...] = jnp.concatenate(pieces, axis=0)
    left, right = [jnp.concatenate(part, axis=0) for part in (left, right)]
    far, near = by_side("col", right, left)
    side_near_ref[...] = near.astype(BF)
    side_far_ref[...] = far.astype(BF)
    scale_part = scale_part_ref[0:1]
    scale_lane = lax.broadcasted_iota(jnp.int32, (1, LANES), 1)
    scale_sums = jnp.zeros((1, LANES), F32)
    for h in range(heads):
        of_head = jnp.sum(jnp.where(lane // head_dim == h, scale_part, 0.0), axis=1, keepdims=True)
        scale_sums = jnp.where(scale_lane == h, of_head, scale_sums)
    small = [gain_part[:, i * LANES : (i + 1) * LANES] for i in range(width // LANES)] + [scale_sums]
    small = jnp.concatenate(small + [jnp.zeros((8 - len(small), LANES), F32)], axis=0)
    small_ref[...] = small


def small_rows(small):
    high = small.astype(BF).astype(F32)
    return jnp.concatenate([high[:4], (small - high)[:4]], axis=0)


def small_value(rows):
    value = rows.astype(BF).astype(F32)
    return value[:4] + value[4:]


def stacked(value):
    return jnp.concatenate(
        [value[:, i : i + LANES] for i in range(0, value.shape[1], LANES)], axis=0
    )


def unstacked(value, rows):
    return jnp.concatenate([value[i : i + rows] for i in range(0, value.shape[0], rows)], axis=1)


def core_sum_kernel(got_ref, keep_ref, keep_group_ref, small_ref, small_near_ref, *refs):
    *out_refs, own_ref, own_group_ref, small_sum_ref, blocks_ref = refs
    chips, per, width = keep_ref.shape
    feats = keep_group_ref.shape[2]
    small = small_ref[...] + small_near_ref[...]
    small_sum_ref[...] = small
    small = small_rows(small)
    chip = lax.axis_index("row") // 2
    own_ref[...] = keep_ref[chip] + got_ref[chip, :, :width].astype(F32)
    for q in range(chips):
        sums = keep_ref[q] + got_ref[q, :, :width].astype(F32)
        kept = keep_group_ref[q].astype(F32)
        first, second = in_order("row", kept, got_ref[q, :, width:].astype(F32))
        block = [stacked(sums), first, second, small]
        blocks_ref[q] = jnp.concatenate(block, axis=0).astype(BF)
    size = width // LANES * per
    own_group_ref[...] = blocks_ref[chip][size : size + 2 * per]
    for step, out_ref in enumerate(out_refs, 1):
        out_ref[...] = blocks_ref[partner(chip, step)]


def row_sum_kernel(sizes, *refs):
    rows, cols, width, n_col = sizes
    own_ref, own_group_ref, small_ref, *refs = refs
    got_refs, dm_ref, dm_near_ref, *refs = (refs[:3], *refs[3:])
    *out_refs, slots_ref = refs
    per = own_ref.shape[0]
    feats = own_group_ref.shape[1]
    size = 4 * width // LANES * per

    def summed(first, part):
        fourth, third, second = [part(ref[...].astype(F32)) for ref in got_refs]
        return (first + second) + (third + fourth)

    sums = summed(stacked(own_ref[...]), lambda value: value[:size])
    sums = unstacked(sums, per)
    small = summed(small_value(small_rows(small_ref[...])), lambda value: small_value(value[size + 2 * per :]))
    group = [own_group_ref[...].astype(F32)]
    group += [ref[...].astype(F32)[size : size + 2 * per] for ref in got_refs[::-1]]
    group = [part[i * per : (i + 1) * per] for i in range(2) for part in group]
    group = jnp.concatenate(group, axis=0)
    own, near = (dm_ref[...].astype(F32), dm_near_ref[...].astype(F32))
    dm = jnp.concatenate(in_order("row", own, near), axis=0).astype(BF)
    merge = mm(group.T.astype(BF), dm)
    small = small_rows(small)
    col = lax.axis_index("col")
    third = 3 * width // n_col
    fourth = width // n_col
    depth = merge.shape[1] // n_col
    for slot in range(n_col):
        parts = [
            sums[:, slot * third : (slot + 1) * third],
            sums[:, 3 * width + slot * fourth : 3 * width + (slot + 1) * fourth],
        ]
        parts = [stacked(jnp.concatenate(parts, axis=1))]
        parts += [merge[:, slot * depth : (slot + 1) * depth], small]
        slots_ref[slot] = jnp.concatenate(parts, axis=0).astype(BF)
    for step, out_ref in enumerate(out_refs):
        out_ref[...] = slots_ref[partner(col, step)]


def partner(index, step):
    if step == 0:
        return index
    low = lax.rem(index, 2)
    if step == 1:
        return index + 1 - 2 * low
    if step == 2:
        return lax.rem(index + 2, 4)
    return 3 - index


def side_kernel(sizes, gx_ref, near_ref, far_ref, grad_ref, row_near_ref, row_far_ref):
    rows, cols, width = sizes
    ends = lax.axis_index("col")
    left, right = by_side("col", near_ref[...].astype(F32), far_ref[...].astype(F32))
    left = jnp.where(ends > 0, left, 0.0)
    right = jnp.where(ends < lax.axis_size("col") - 1, right, 0.0)
    blank = jnp.zeros((cols - 2 * EDGE, width), F32)
    pieces = []
    for i in range(rows + 2 * RADIUS):
        edge = slice(i * EDGE, (i + 1) * EDGE)
        pieces += [left[edge], blank, right[edge]]
    g_x = gx_ref[...] + jnp.concatenate(pieces, axis=0)
    reach = RADIUS * cols
    far, near = by_side("row", g_x[reach + rows * cols :], g_x[:reach])
    grad_ref[...] = g_x[reach : reach + rows * cols]
    row_near_ref[...] = near.astype(BF)
    row_far_ref[...] = far.astype(BF)


def col_sum_kernel(
    sizes,
    a_ref,
    d_ref,
    c_ref,
    b_ref,
    grad_ref,
    far_ref,
    near_ref,
    gqkv_ref,
    gout_ref,
    gmerge_ref,
    ggain_ref,
    gscale_ref,
    gtok_ref,
):
    rows, cols, width = sizes
    per, third = gqkv_ref.shape
    size = a_ref.shape[0] - 8

    def summed(part):
        first, second, third, fourth = [
            part(ref[...].astype(F32)) for ref in (a_ref, b_ref, c_ref, d_ref)
        ]
        return (first + second) + (third + fourth)

    total = summed(lambda value: value[:size])
    small = summed(lambda value: small_value(value[size:]))
    merge_at = size - gmerge_ref.shape[0]
    sums = unstacked(total[:merge_at], per)
    gqkv_ref[...] = sums[:, :third]
    gout_ref[...] = sums[:, third:]
    gmerge_ref[...] = total[merge_at:]
    ggain_ref[...] = jnp.concatenate([small[i : i + 1] for i in range(width // LANES)], axis=1)
    for h in range(gscale_ref.shape[0]):
        gscale_ref[h] = small[width // LANES, h]
    blank = jnp.zeros(((rows - RADIUS) * cols, width), F32)
    above, below = by_side("row", near_ref[...].astype(F32), far_ref[...].astype(F32))
    grad = grad_ref[...] + jnp.concatenate([above, blank], axis=0)
    grad = grad + jnp.concatenate([blank, below], axis=0)
    gtok_ref[...] = grad.astype(BF).reshape(rows, cols, width)


def plain_sums(width, sums, group, small, dm):
    sums = sums.astype(F32)
    merge = jnp.dot(group.T, dm, preferred_element_type=F32)
    outs = []
    for part in (sums[:, : 3 * width], sums[:, 3 * width :], merge):
        part = lax.psum_scatter(part, "row", scatter_dimension=0, tiled=True)
        outs.append(lax.psum_scatter(part, "col", scatter_dimension=1, tiled=True))
    small = lax.psum(small, ("row", "col"))
    return (*outs, small[: width // LANES].reshape(1, width), small[width // LANES])


def add_rows(grad, near, far, rows, cols):
    above, below = by_side("row", near.astype(F32), far.astype(F32))
    size = RADIUS * cols
    grad = grad.at[:size].add(above).at[rows * cols - size :].add(below)
    return grad.astype(BF).reshape(rows, cols, -1)


def swapped(near, far, axis):
    n_row, n_col = (lax.axis_size("row"), lax.axis_size("col"))
    pairs = []
    for row in range(n_row):
        for col in range(n_col):
            if axis == "row":
                other = row - 1 if row % 2 == 0 else row + 1
                target = (other, col) if 0 <= other < n_row else (row, col ^ 1)
            else:
                other = col - 1 if col % 2 == 0 else col + 1
                target = (row, other) if 0 <= other < n_col else (row ^ 1, col)
            pairs.append((row * n_col + col, target[0] * n_col + target[1]))
    return (swap(near, axis, 1), lax.ppermute(far, ("row", "col"), pairs))


def swap(value, axis, step):
    count = lax.axis_size(axis)
    return lax.ppermute(value, axis, [(i, i ^ step) for i in range(count)])


def vmem(count):
    return [pl.BlockSpec(memory_space=pltpu.VMEM)] * count


def on_device(tokens, gain, w_qkv, head_scale, w_out, w_merge, d_merged, d_skip):
    rows, cols, width = tokens.shape
    heads = head_scale.shape[0]
    n_row, n_col = (lax.axis_size("row"), lax.axis_size("col"))
    g_rows, g_cols, depth = d_merged.shape
    groups = g_rows * g_cols
    wide = cols + 2 * SIDE
    ext_rows = rows + 2 * RADIUS
    shape = jax.ShapeDtypeStruct
    params = pltpu.CompilerParams(vmem_limit_bytes=24 * 1024 * 1024)
    less = pltpu.CompilerParams(vmem_limit_bytes=8 * 1024 * 1024)
    row_near, row_far = swapped(tokens, tokens, "row")
    edge = shape((ext_rows * EDGE, width), BF)
    ones, parity = pl.pallas_call(
        first_kernel,
        out_shape=(shape((width, width), BF), shape((2 * heads, LANES), F32)),
        out_specs=tuple(vmem(2)),
        compiler_params=less,
        cost_estimate=pl.CostEstimate(flops=10**10, bytes_accessed=10**5, transcendentals=0),
    )()
    dm = d_merged.reshape(groups, depth)
    tile = shape((rows * cols, width), F32)
    half = shape((rows * cols, width), BF)
    edges, two_rows, q_norm, q_unit, d_y, d_attn = pl.pallas_call(
        own_kernel,
        out_shape=(shape((2 * rows * EDGE, width), BF), shape((8, width), F32), tile, tile, tile, half),
        in_specs=vmem(10),
        out_specs=tuple(vmem(6)),
        scratch_shapes=[pltpu.VMEM((width // LANES, rows, cols, LANES), F32)],
        compiler_params=params,
        cost_estimate=pl.CostEstimate(flops=10**9, bytes_accessed=10**6, transcendentals=0),
    )(
        ones,
        parity,
        head_scale.reshape(1, heads),
        tokens,
        d_merged,
        d_skip,
        gain.reshape(1, width),
        w_qkv,
        w_out,
        w_merge,
    )
    edge_near, edge_far = pl.pallas_call(
        edge_kernel,
        out_shape=(edge, edge),
        in_specs=vmem(3),
        out_specs=tuple(vmem(2)),
        compiler_params=less,
    )(edges, row_far, row_near)
    dm_pair = pl.pallas_call(
        pair_kernel,
        out_shape=shape((2 * groups, depth), BF),
        in_specs=vmem(2),
        out_specs=vmem(1)[0],
        compiler_params=less,
    )(d_merged, swap(dm, "row", 2))
    dms = [swap(dm_pair, "row", 4), dm_pair]
    col_near, col_far = swapped(edge_near, edge_far, "col")

    per = width // n_row
    feats = 4 * width // n_row
    packed = per % 16 == 0 and feats % LANES == 0 and groups == per
    packed = packed and width // LANES < 4 and feats == LANES and depth // n_col == LANES and n_col == 4 and n_row == 8
    if packed:
        sum_shapes = (
            shape((n_row // 2, per, 4 * width + feats), BF),
            shape((n_row // 2, per, 4 * width), F32),
            shape((n_row // 2, per, feats), BF),
        )
    else:
        sum_shapes = (
            shape((width, 4 * width), BF),
            shape((groups, 4 * width), BF),
        )
    sizes = (rows, cols, width, heads, n_row, n_col)
    tall = ext_rows * wide
    x, y, d_query, d_kv, grad_out, group, scale_part = pl.pallas_call(
        functools.partial(layer_kernel, sizes),
        out_shape=(
            shape((tall, width), F32),
            half,
            half,
            shape((tall, 2 * width), BF),
            shape((width, width), F32),
            shape((groups, 4 * width), BF),
            shape((8, width), F32),
        ),
        in_specs=vmem(13),
        out_specs=tuple(vmem(7)),
        scratch_shapes=[pltpu.VMEM((width // LANES, rows, cols, LANES), F32)],
        compiler_params=params,
        cost_estimate=pl.CostEstimate(flops=4 * 10**9, bytes_accessed=10**6, transcendentals=0),
    )(
        ones,
        tokens,
        row_far,
        row_near,
        col_near,
        col_far,
        two_rows,
        q_norm,
        q_unit,
        d_y,
        d_attn,
        w_qkv,
        w_out,
    )
    dm_core, *sums = pl.pallas_call(
        functools.partial(weights_kernel, (rows, cols, width, n_row, len(dms))),
        out_shape=(shape((2 * len(dms) * groups, depth), BF),) + sum_shapes,
        in_specs=vmem(6 + len(dms)),
        out_specs=tuple(vmem(1 + len(sum_shapes))),
        compiler_params=params,
        cost_estimate=pl.CostEstimate(flops=10**9, bytes_accessed=10**6, transcendentals=0),
    )(x, d_query, d_kv, grad_out, group, two_rows, *dms)
    gx, *sides = pl.pallas_call(
        functools.partial(norm_kernel, (rows, cols, width, heads)),
        out_shape=(shape((ext_rows * cols, width), F32), edge, edge, shape((8, LANES), F32)),
        in_specs=vmem(7),
        out_specs=tuple(vmem(4)),
        compiler_params=params,
        cost_estimate=pl.CostEstimate(flops=5 * 10**8, bytes_accessed=10**6, transcendentals=0),
    )(x, d_query, d_kv, scale_part, two_rows, d_y, w_qkv)
    *sides, small = sides
    sides = swapped(*sides, "col")
    skip_out, merged = pl.pallas_call(
        output_kernel,
        out_shape=(shape((rows, cols, width), BF), shape((g_rows, g_cols, depth), BF)),
        in_specs=vmem(3),
        out_specs=tuple(vmem(2)),
        compiler_params=less,
        cost_estimate=pl.CostEstimate(flops=10**9, bytes_accessed=10**6, transcendentals=0),
    )(y, group, w_merge)
    reach = shape((RADIUS * cols, width), BF)
    side_call = pl.pallas_call(
        functools.partial(side_kernel, (rows, cols, width)),
        out_shape=(tile, reach, reach),
        in_specs=vmem(3),
        out_specs=tuple(vmem(3)),
        compiler_params=less,
    )
    if not packed:
        grad, *rims = side_call(gx, *sides)
        grad_tokens = add_rows(grad, *swapped(*rims, "row"), rows, cols)
        g_qkv, g_out, g_merge, g_gain, g_scale = plain_sums(width, *sums, small, dm)
    else:
        send, *kept = sums
        block = shape((4 * width // LANES * per + 2 * per + 8, LANES), BF)
        *blocks, own, own_group, small = pl.pallas_call(
            core_sum_kernel,
            out_shape=(block, block, block)
            + (shape((per, 4 * width), F32), shape((2 * per, LANES), BF), shape((8, LANES), F32)),
            in_specs=vmem(5),
            out_specs=tuple(vmem(6)),
            scratch_shapes=[pltpu.VMEM((n_row // 2,) + block.shape, BF)],
            compiler_params=less,
            cost_estimate=pl.CostEstimate(flops=5 * 10**9, bytes_accessed=10**6, transcendentals=0),
        )(swap(send, "row", 1), *kept, small, swap(small, "row", 1))
        got = [swap(blocks[step - 1], "row", 2 * step) for step in (3, 2, 1)]
        slot = shape((4 * width // n_col // LANES * per + feats + 8, LANES), BF)
        slots = pl.pallas_call(
            functools.partial(row_sum_kernel, (rows, cols, width, n_col)),
            out_shape=(slot,) * n_col,
            in_specs=vmem(8),
            out_specs=tuple(vmem(n_col)),
            scratch_shapes=[pltpu.VMEM((n_col,) + slot.shape, BF)],
            compiler_params=less,
        )(own, own_group, small, *got, dm_core, swap(dm_core, "row", 1))
        got = [slots[0]] + [swap(slots[step], "col", step) for step in (3, 2, 1)]
        grad, *rims = side_call(gx, *sides)
        rims = swapped(*rims, "row")
        g_qkv, g_out, g_merge, g_gain, g_scale, grad_tokens = pl.pallas_call(
            functools.partial(col_sum_kernel, (rows, cols, width)),
            out_shape=(
                shape((per, 3 * width // n_col), F32),
                shape((per, width // n_col), F32),
                shape((feats, depth // n_col), F32),
                shape((1, width), F32),
                shape((heads,), F32),
                shape((rows, cols, width), BF),
            ),
            in_specs=vmem(7),
            out_specs=tuple(vmem(4)) + (pl.BlockSpec(memory_space=pltpu.SMEM), vmem(1)[0]),
            compiler_params=less,
        )(*got, grad, *rims[::-1])
    return (
        skip_out,
        merged,
        grad_tokens,
        g_qkv,
        g_out,
        g_merge,
        g_gain.reshape(width),
        g_scale[:heads],
    )


def solution(mesh):
    block = P("row", "col", None)
    return jax.shard_map(
        on_device,
        mesh=mesh,
        in_specs=(block, P(), P(), P(), P(), P(), block, block),
        out_specs=(block, block, block, P("row", "col"), P("row", "col"), P("row", "col"), P(), P()),
        check_vma=False,
    )
```

```python
import functools
import jax
import jax.numpy as jnp
from jax import lax
from jax.experimental import pallas as pl
from jax.experimental.pallas import tpu as pltpu
from jax.sharding import PartitionSpec as P

RADIUS = 3
IMG_MAX = 512
EPS = 1e-06
EDGE = 4
SIDE = 8
LANES = 128
BF = jnp.bfloat16
F32 = jnp.float32


def mm(a, b):
    return lax.dot_general(a, b, (((1,), (0,)), ((), ())), preferred_element_type=F32)


def mm_t(a, b):
    return lax.dot_general(a, b, (((1,), (1,)), ((), ())), preferred_element_type=F32)


def split_two(value):
    high = value.astype(BF)
    return (high, (value - high.astype(F32)).astype(BF))


def by_side(axis, near, far):
    even = lax.rem(lax.axis_index(axis), 2) == 0
    return (jnp.where(even, far, near), jnp.where(even, near, far))


def first_kernel(ones_ref, parity_ref):
    width = ones_ref.shape[0]
    head_dim = width // (parity_ref.shape[0] // 2)
    same_head = lax.broadcasted_iota(jnp.int32, (width, width), 0) // head_dim == (
        lax.broadcasted_iota(jnp.int32, (width, width), 1) // head_dim
    )
    ones_ref[...] = jnp.where(same_head, 1.0, 0.0).astype(BF)
    half = (parity_ref.shape[0] // 2, parity_ref.shape[1])
    parts = [
        jnp.where(lax.rem(lax.axis_index(axis), 2) == 0, jnp.ones(half, F32), jnp.zeros(half, F32))
        for axis in ("row", "col")
    ]
    parity_ref[...] = jnp.concatenate(parts, axis=0)


def pair_kernel(dm_ref, dm_next_ref, dm_pair_ref):
    size = dm_next_ref.shape[0]
    dm_pair_ref[...] = jnp.concatenate([dm_ref[...].reshape(size, -1), dm_next_ref[...]], axis=0)


def edge_kernel(edges_ref, far_ref, near_ref, edge_near_ref, edge_far_ref):
    rows, cols, width = near_ref.shape
    up, down = by_side("row", near_ref[...].astype(F32), far_ref[...].astype(F32))
    up = up[rows - RADIUS :]
    down = down[:RADIUS]
    halo = []
    for at in (0, cols - EDGE):
        parts = [part[:, at : at + EDGE].reshape(RADIUS * EDGE, width) for part in (up, down)]
        halo.append(jnp.concatenate(parts, axis=0))
    far, near = by_side("col", halo[1], halo[0])
    for out_ref, own_at, part in ((edge_near_ref, 0, near), (edge_far_ref, rows * EDGE, far)):
        own = edges_ref[own_at : own_at + rows * EDGE].astype(F32)
        size = RADIUS * EDGE
        out_ref[...] = jnp.concatenate([part[:size], own, part[size:]], axis=0).astype(BF)


def in_order(axis, own, partner):
    even = lax.rem(lax.axis_index(axis), 2) == 0
    return (jnp.where(even, own, partner), jnp.where(even, partner, own))


def head_sum(value, ones_ref):
    high, low = split_two(value)
    return mm(high, ones_ref[...]) + mm(low, ones_ref[...])


def own_kernel(
    ones_ref,
    parity_ref,
    scale_ref,
    tok_ref,
    dm_ref,
    dskip_ref,
    gain_ref,
    wqkv_ref,
    wout_ref,
    wmerge_ref,
    edges_ref,
    rows_ref,
    q_norm_ref,
    q_unit_ref,
    dy_ref,
    d_attn_ref,
    dscr,
):
    rows, cols, width = tok_ref.shape
    tokens = rows * cols
    tok = tok_ref[...].astype(F32)
    left = tok[:, :EDGE].reshape(rows * EDGE, width)
    right = tok[:, cols - EDGE :].reshape(rows * EDGE, width)
    heads = scale_ref.shape[1]
    even = parity_ref[heads : heads + 1, 0:1] > 0.5
    near, far = (jnp.where(even, right, left), jnp.where(even, left, right))
    edges_ref[...] = jnp.concatenate([near, far], axis=0).astype(BF)
    lane = lax.broadcasted_iota(jnp.int32, (1, width), 1)
    scale_row = jnp.zeros((1, width), F32)
    for h in range(heads):
        scale_row = jnp.where(lane // (width // heads) == h, scale_ref[:, h : h + 1], scale_row)
    blank = jnp.zeros((6, width), F32)
    rows_ref[...] = jnp.concatenate([gain_ref[...], scale_row, blank], axis=0)
    x = tok.reshape(tokens, width)
    inverse = lax.rsqrt(jnp.mean(x * x, axis=1, keepdims=True) + EPS)
    normed = (x * inverse * gain_ref[...]).astype(BF)
    query = mm(normed, wqkv_ref[:, :width])
    q_norm = lax.rsqrt(head_sum(query * query, ones_ref) + EPS)
    q_norm_ref[...] = q_norm
    q_unit_ref[...] = query * q_norm
    group_wide = cols // 2
    d_in = mm_t(dm_ref[...].reshape(-1, dm_ref.shape[2]), wmerge_ref[...])
    for i in range(rows // 2):
        for pr in range(2):
            for pc in range(2):
                for part in range(width // LANES):
                    at = (2 * pr + pc) * width + part * LANES
                    dscr[part, 2 * i + pr, pl.ds(pc, group_wide, stride=2), :] = d_in[
                        i * group_wide : (i + 1) * group_wide, at : at + LANES
                    ]
    d_group = jnp.concatenate(
        [dscr[part].reshape(tokens, LANES) for part in range(width // LANES)], axis=1
    )
    d_y = dskip_ref[...].reshape(tokens, width).astype(F32) + d_group
    dy_ref[...] = d_y
    d_attn_ref[...] = mm_t(d_y.astype(BF), wout_ref[...]).astype(BF)


def layer_kernel(
    sizes,
    ones_ref,
    tok_ref,
    row_far_ref,
    row_near_ref,
    col_near_ref,
    col_far_ref,
    rows_ref,
    q_norm_ref,
    q_unit_ref,
    dy_ref,
    d_attn_ref,
    wqkv_ref,
    wout_ref,
    x_ref,
    y_ref,
    d_query_ref,
    d_kv_ref,
    grad_out_ref,
    group_ref,
    scale_part_ref,
    yscr,
):
    rows, cols, width, heads, n_row, n_col = sizes
    head_dim = width // heads
    wide = cols + 2 * SIDE
    ext_rows = rows + 2 * RADIUS
    tokens = rows * cols
    image_rows = min(IMG_MAX, rows * n_row)
    row_start = lax.axis_index("row") * rows
    col_index = lax.axis_index("col")
    col_start = col_index * cols
    first = row_start // image_rows * image_rows

    lane = lax.broadcasted_iota(jnp.int32, (1, width), 1)
    def blocks(value):
        zero = jnp.zeros_like(value)
        kept = [jnp.where(lane // head_dim == h, value, zero) for h in range(heads)]
        return jnp.concatenate(kept, axis=0).astype(BF)

    gain = rows_ref[0:1]
    scale_row = rows_ref[1:2]
    up, down = by_side("row", row_near_ref[...].astype(F32), row_far_ref[...].astype(F32))
    left, right = by_side("col", col_near_ref[...].astype(F32), col_far_ref[...].astype(F32))
    own = tok_ref[...].astype(F32)
    blank = jnp.zeros((SIDE - EDGE, width), F32)
    pieces = []
    for i in range(ext_rows):
        if i < RADIUS:
            row = up[rows - RADIUS + i]
        elif i < RADIUS + rows:
            row = own[i - RADIUS]
        else:
            row = down[i - RADIUS - rows]
        edge = slice(i * EDGE, (i + 1) * EDGE)
        pieces += [blank, left[edge], row, right[edge], blank]
    x = jnp.concatenate(pieces, axis=0)
    x_ref[...] = x
    inverse = lax.rsqrt(jnp.mean(x * x, axis=1, keepdims=True) + EPS)
    unit = x * inverse
    normed32 = (unit * gain).astype(BF).astype(F32)
    normed = normed32.astype(BF)
    x_own = inner_tokens(x, rows, cols)
    kv = mm(normed, wqkv_ref[:, width:])
    key_raw = kv[:, :width]
    k_norm = lax.rsqrt(head_sum(key_raw * key_raw, ones_ref) + EPS)
    k_unit = key_raw * k_norm
    keys = k_unit.astype(BF)
    values = kv[:, width:].astype(BF)
    q_norm = q_norm_ref[...]
    q_unit = q_unit_ref[...]
    q_hat = (q_unit * scale_row).astype(BF).astype(F32)
    d_y = dy_ref[...]
    dy_b = d_y.astype(BF)
    d_attn = d_attn_ref[...].astype(F32)

    index = lax.broadcasted_iota(jnp.int32, (1, tokens), 1)
    q_row = jnp.zeros_like(index)
    for i in range(1, rows):
        q_row = q_row + (index >= i * cols).astype(jnp.int32)
    q_col = index - q_row * cols
    key_col = lax.broadcasted_iota(jnp.int32, (wide, tokens), 0) - SIDE
    near = (key_col - q_col <= RADIUS) & (key_col - q_col >= -RADIUS)
    near = near & (key_col + col_start >= 0) & (key_col + col_start < cols * n_col)
    near = jnp.where(near, 1.0, 0.0)
    parts = []
    for i in range(-RADIUS, rows + RADIUS):
        ok = (q_row - i <= RADIUS) & (q_row - i >= -RADIUS)
        ok = ok & (row_start + i >= first) & (row_start + i < first + image_rows)
        parts.append(near * jnp.where(ok, 1.0, 0.0))
    allowed = jnp.concatenate([jnp.concatenate(parts, axis=0)] * heads, axis=1)
    q_blocks = blocks(q_hat)
    g_blocks = blocks(d_attn)
    expo = jnp.exp(mm_t(keys, q_blocks)) * allowed
    prob = expo * (1.0 / jnp.sum(expo, axis=0, keepdims=True))
    weights = prob.astype(BF)
    d_w = mm_t(values, g_blocks)
    delta = jnp.sum(d_w * prob, axis=0, keepdims=True)
    d_s = (prob * (d_w - delta)).astype(BF)
    values_t = values.astype(F32).T.astype(BF)
    keys_t = keys.astype(F32).T.astype(BF)
    attn_t = []
    d_qhat_t = []
    for h in range(heads):
        feats = slice(h * head_dim, (h + 1) * head_dim)
        lanes = slice(h * tokens, (h + 1) * tokens)
        attn_t.append(mm(values_t[feats], weights[:, lanes]))
        d_qhat_t.append(mm(keys_t[feats], d_s[:, lanes]))
    attn_t = jnp.concatenate(attn_t, axis=0)
    d_qhat = jnp.concatenate(d_qhat_t, axis=0).T
    d_k = mm(d_s, q_blocks)
    d_v = mm(weights, g_blocks)

    attn = attn_t.T.astype(BF)
    y = (x_own + mm(attn, wout_ref[...])).astype(BF)
    y_ref[...] = y
    y32 = y.astype(F32)
    for part in range(width // LANES):
        yscr[part] = y32[:, part * LANES : (part + 1) * LANES].reshape(rows, cols, LANES)
    lines = []
    for i in range(rows // 2):
        pieces = []
        for pr in range(2):
            for pc in range(2):
                for part in range(width // LANES):
                    pieces.append(yscr[part, 2 * i + pr, pl.ds(pc, cols // 2, stride=2), :])
        lines.append(jnp.concatenate(pieces, axis=1))
    group = jnp.concatenate(lines, axis=0).astype(BF)
    group_ref[...] = group
    grad_out_ref[...] = mm(attn_t.astype(BF), dy_b)

    scale_part_ref[...] = jnp.broadcast_to(
        jnp.sum(q_unit * d_qhat, axis=0, keepdims=True), scale_part_ref.shape
    )
    g_unit = d_qhat * scale_row
    d_query_ref[...] = (q_norm * (g_unit - q_unit * head_sum(q_unit * g_unit, ones_ref))).astype(BF)
    d_key = k_norm * (d_k - k_unit * head_sum(k_unit * d_k, ones_ref))
    d_kv_ref[...] = jnp.concatenate([d_key, d_v], axis=1).astype(BF)


def inner_tokens(value, rows, cols):
    wide = cols + 2 * SIDE
    pieces = []
    for i in range(RADIUS, RADIUS + rows):
        pieces.append(value[i * wide + SIDE : i * wide + SIDE + cols])
    return jnp.concatenate(pieces, axis=0)


def output_kernel(y_ref, group_ref, wmerge_ref, skip_ref, merged_ref):
    skip_ref[...] = y_ref[...].reshape(skip_ref.shape)
    merged = mm(group_ref[...], wmerge_ref[...])
    merged_ref[...] = merged.astype(BF).reshape(merged_ref.shape)


def weights_kernel(
    sizes, x_ref, d_query_ref, d_kv_ref, grad_out_ref, group_ref, rows_ref, *refs
):
    rows, cols, width, n_row, n_dm = sizes
    dm_refs, dm_all_ref, sum_refs = (refs[:n_dm], refs[n_dm], refs[n_dm + 1 :])
    size = dm_all_ref.shape[0] // n_dm
    dm = [ref[...].reshape(size, dm_all_ref.shape[1]) for ref in dm_refs]
    dm_all_ref[...] = jnp.concatenate(dm[::-1], axis=0)
    x = x_ref[...]
    inverse = lax.rsqrt(jnp.mean(x * x, axis=1, keepdims=True) + EPS)
    normed32 = (x * inverse * rows_ref[0:1]).astype(BF).astype(F32)
    grad_q = mm(inner_tokens(normed32, rows, cols).T.astype(BF), d_query_ref[...])
    grad_kv = mm(normed32.T.astype(BF), d_kv_ref[...])
    sums = jnp.concatenate([grad_q, grad_kv, grad_out_ref[...]], axis=1)
    group = group_ref[...]
    if len(sum_refs) == 2:
        sum_refs[0][...] = sums.astype(BF)
        sum_refs[1][...] = group
        return
    send_ref, send_own_ref, keep_ref, keep_group_ref, sends, keeps, keep_groups = sum_refs
    per = width // n_row
    feats = 4 * width // n_row
    group = group.astype(F32)
    even = lax.rem(lax.axis_index("row"), 2) == 0
    for q in range(n_row // 2):
        parts = []
        for value, axis, size in ((sums, 0, per), (group, 1, feats)):
            first = lax.slice_in_dim(value, 2 * q * size, (2 * q + 1) * size, axis=axis)
            second = lax.slice_in_dim(value, (2 * q + 1) * size, (2 * q + 2) * size, axis=axis)
            parts.append((jnp.where(even, first, second), jnp.where(even, second, first)))
        (keeps[q], sums_send), (keep_group, group_send) = parts
        keep_groups[q] = keep_group.astype(BF)
        sends[q] = jnp.concatenate([sums_send, group_send], axis=1).astype(BF)
    chip = lax.axis_index("row") // 2
    for step in range(n_row // 2):
        at = partner(chip, step)
        keep_ref[step] = keeps[at]
        keep_group_ref[step] = keep_groups[at]
        if step == 0:
            send_own_ref[...] = sends[at]
        else:
            send_ref[step - 1] = sends[at]


def gain_kernel(
    sizes,
    x_ref,
    d_query_ref,
    d_kv_ref,
    scale_part_ref,
    wqkv_ref,
    d_normed_ref,
    small_ref,
):
    rows, cols, width, heads = sizes
    head_dim = width // heads
    wide = cols + 2 * SIDE
    ext_rows = rows + 2 * RADIUS
    lane = lax.broadcasted_iota(jnp.int32, (1, width), 1)
    x = x_ref[...]
    unit = x * lax.rsqrt(jnp.mean(x * x, axis=1, keepdims=True) + EPS)
    from_q = mm_t(d_query_ref[...], wqkv_ref[:, :width])
    d_normed = mm_t(d_kv_ref[...], wqkv_ref[:, width:])
    pieces = []
    side = jnp.zeros((SIDE, width), F32)
    for i in range(ext_rows):
        if RADIUS <= i < RADIUS + rows:
            at = (i - RADIUS) * cols
            pieces += [side, from_q[at : at + cols], side]
        else:
            pieces.append(jnp.zeros((wide, width), F32))
    d_normed = d_normed + jnp.concatenate(pieces, axis=0)
    gain_part = jnp.sum(unit * d_normed, axis=0, keepdims=True)
    d_normed_ref[...] = d_normed
    scale_part = scale_part_ref[0:1]
    scale_lane = lax.broadcasted_iota(jnp.int32, (1, LANES), 1)
    scale_sums = jnp.zeros((1, LANES), F32)
    for h in range(heads):
        of_head = jnp.sum(jnp.where(lane // head_dim == h, scale_part, 0.0), axis=1, keepdims=True)
        scale_sums = jnp.where(scale_lane == h, of_head, scale_sums)
    small = [gain_part[:, i * LANES : (i + 1) * LANES] for i in range(width // LANES)] + [scale_sums]
    small = jnp.concatenate(small + [jnp.zeros((8 - len(small), LANES), F32)], axis=0)
    small_ref[...] = small


def norm_kernel(sizes, x_ref, d_normed_ref, rows_ref, dy_ref, *refs):
    rows, cols, width = sizes
    gx_ref, side_near_ref, side_far_ref = refs
    wide = cols + 2 * SIDE
    ext_rows = rows + 2 * RADIUS
    x = x_ref[...]
    inverse = lax.rsqrt(jnp.mean(x * x, axis=1, keepdims=True) + EPS)
    d_y = dy_ref[...]
    scaled = rows_ref[0:1] * d_normed_ref[...]
    mean = jnp.mean(x * scaled, axis=1, keepdims=True)
    g_x = inverse * scaled - x * (inverse * inverse * inverse) * mean

    pieces = []
    left = []
    right = []
    for i in range(ext_rows):
        row = g_x[i * wide : (i + 1) * wide]
        middle = row[SIDE : SIDE + cols]
        if RADIUS <= i < RADIUS + rows:
            middle = middle + d_y[(i - RADIUS) * cols : (i - RADIUS + 1) * cols]
        pieces.append(middle)
        left.append(row[:SIDE][SIDE - EDGE :])
        right.append(row[SIDE + cols :][:EDGE])
    gx_ref[...] = jnp.concatenate(pieces, axis=0)
    left, right = [jnp.concatenate(part, axis=0) for part in (left, right)]
    far, near = by_side("col", right, left)
    side_near_ref[...] = near.astype(BF)
    side_far_ref[...] = far.astype(BF)


def small_rows(small):
    high = small.astype(BF).astype(F32)
    return jnp.concatenate([high[:4], (small - high)[:4]], axis=0)


def small_value(rows):
    value = rows.astype(BF).astype(F32)
    return value[:4] + value[4:]


def stacked(value):
    return jnp.concatenate(
        [value[:, i : i + LANES] for i in range(0, value.shape[1], LANES)], axis=0
    )


def unstacked(value, rows):
    return jnp.concatenate([value[i : i + rows] for i in range(0, value.shape[0], rows)], axis=1)


def core_sum_kernel(got_ref, keep_ref, keep_group_ref, small_ref, small_near_ref, *refs):
    *out_refs, small_sum_ref = refs
    width = keep_ref.shape[2]
    small = small_ref[...] + small_near_ref[...]
    small_sum_ref[...] = small
    small = small_rows(small)
    for i, out_ref in enumerate(out_refs):
        sums = keep_ref[i + 1] + got_ref[i, :, :width].astype(F32)
        kept = keep_group_ref[i + 1].astype(F32)
        first, second = in_order("row", kept, got_ref[i, :, width:].astype(F32))
        out_ref[...] = jnp.concatenate([stacked(sums), first, second, small], axis=0).astype(BF)


def row_sum_kernel(sizes, *refs):
    rows, cols, width, n_col = sizes
    keep_ref, keep_group_ref, got_own_ref, small_ref, *refs = refs
    got_refs, dm_ref, dm_near_ref, gx_ref, *refs = (refs[:3], *refs[3:])
    *out_refs, gx_sum_ref, slots_ref = refs
    gx_sum_ref[...] = gx_ref[...]
    per, feats = keep_group_ref.shape[1:]
    got_own = got_own_ref[...].astype(F32)
    own = keep_ref[0] + got_own[:, : 4 * width]
    size = 4 * width // LANES * per

    def summed(first, part):
        fourth, third, second = [part(ref[...].astype(F32)) for ref in got_refs]
        return (first + second) + (third + fourth)

    sums = summed(stacked(own), lambda value: value[:size])
    sums = unstacked(sums, per)
    small = summed(small_value(small_rows(small_ref[...])), lambda value: small_value(value[size + 2 * per :]))
    own_group = in_order("row", keep_group_ref[0].astype(F32), got_own[:, 4 * width :])
    group = [jnp.concatenate(own_group, axis=0)]
    group += [ref[...].astype(F32)[size : size + 2 * per] for ref in got_refs[::-1]]
    group = [part[i * per : (i + 1) * per] for i in range(2) for part in group]
    group = jnp.concatenate(group, axis=0)
    own, near = (dm_ref[...].astype(F32), dm_near_ref[...].astype(F32))
    dm = jnp.concatenate(in_order("row", own, near), axis=0).astype(BF)
    merge = mm(group.T.astype(BF), dm)
    small = small_rows(small)
    col = lax.axis_index("col")
    third = 3 * width // n_col
    fourth = width // n_col
    depth = merge.shape[1] // n_col
    for slot in range(n_col):
        parts = [
            sums[:, slot * third : (slot + 1) * third],
            sums[:, 3 * width + slot * fourth : 3 * width + (slot + 1) * fourth],
        ]
        parts = [stacked(jnp.concatenate(parts, axis=1))]
        parts += [merge[:, slot * depth : (slot + 1) * depth], small]
        slots_ref[slot] = jnp.concatenate(parts, axis=0).astype(BF)
    for step, out_ref in enumerate(out_refs):
        out_ref[...] = slots_ref[partner(col, step)]


def partner(index, step):
    if step == 0:
        return index
    low = lax.rem(index, 2)
    if step == 1:
        return index + 1 - 2 * low
    if step == 2:
        return lax.rem(index + 2, 4)
    return 3 - index


def side_kernel(sizes, gx_ref, near_ref, far_ref, grad_ref, row_near_ref, row_far_ref):
    rows, cols, width = sizes
    ends = lax.axis_index("col")
    left, right = by_side("col", near_ref[...].astype(F32), far_ref[...].astype(F32))
    left = jnp.where(ends > 0, left, 0.0)
    right = jnp.where(ends < lax.axis_size("col") - 1, right, 0.0)
    blank = jnp.zeros((cols - 2 * EDGE, width), F32)
    pieces = []
    for i in range(rows + 2 * RADIUS):
        edge = slice(i * EDGE, (i + 1) * EDGE)
        pieces += [left[edge], blank, right[edge]]
    g_x = gx_ref[...] + jnp.concatenate(pieces, axis=0)
    reach = RADIUS * cols
    far, near = by_side("row", g_x[reach + rows * cols :], g_x[:reach])
    grad_ref[...] = g_x[reach : reach + rows * cols]
    row_near_ref[...] = near.astype(BF)
    row_far_ref[...] = far.astype(BF)


def col_sum_kernel(
    sizes,
    a_ref,
    d_ref,
    c_ref,
    b_ref,
    grad_ref,
    far_ref,
    near_ref,
    gqkv_ref,
    gout_ref,
    gmerge_ref,
    ggain_ref,
    gscale_ref,
    gtok_ref,
):
    rows, cols, width = sizes
    per, third = gqkv_ref.shape
    size = a_ref.shape[0] - 8

    def summed(part):
        first, second, third, fourth = [
            part(ref[...].astype(F32)) for ref in (a_ref, b_ref, c_ref, d_ref)
        ]
        return (first + second) + (third + fourth)

    total = summed(lambda value: value[:size])
    small = summed(lambda value: small_value(value[size:]))
    merge_at = size - gmerge_ref.shape[0]
    sums = unstacked(total[:merge_at], per)
    gqkv_ref[...] = sums[:, :third]
    gout_ref[...] = sums[:, third:]
    gmerge_ref[...] = total[merge_at:]
    ggain_ref[...] = jnp.concatenate([small[i : i + 1] for i in range(width // LANES)], axis=1)
    for h in range(gscale_ref.shape[0]):
        gscale_ref[h] = small[width // LANES, h]
    blank = jnp.zeros(((rows - RADIUS) * cols, width), F32)
    above, below = by_side("row", near_ref[...].astype(F32), far_ref[...].astype(F32))
    grad = grad_ref[...] + jnp.concatenate([above, blank], axis=0)
    grad = grad + jnp.concatenate([blank, below], axis=0)
    gtok_ref[...] = grad.astype(BF).reshape(rows, cols, width)


def plain_sums(width, sums, group, small, dm):
    sums = sums.astype(F32)
    merge = jnp.dot(group.T, dm, preferred_element_type=F32)
    outs = []
    for part in (sums[:, : 3 * width], sums[:, 3 * width :], merge):
        part = lax.psum_scatter(part, "row", scatter_dimension=0, tiled=True)
        outs.append(lax.psum_scatter(part, "col", scatter_dimension=1, tiled=True))
    small = lax.psum(small, ("row", "col"))
    return (*outs, small[: width // LANES].reshape(1, width), small[width // LANES])


def add_rows(grad, near, far, rows, cols):
    above, below = by_side("row", near.astype(F32), far.astype(F32))
    size = RADIUS * cols
    grad = grad.at[:size].add(above).at[rows * cols - size :].add(below)
    return grad.astype(BF).reshape(rows, cols, -1)


def swapped(near, far, axis):
    n_row, n_col = (lax.axis_size("row"), lax.axis_size("col"))
    pairs = []
    for row in range(n_row):
        for col in range(n_col):
            if axis == "row":
                other = row - 1 if row % 2 == 0 else row + 1
                target = (other, col) if 0 <= other < n_row else (row, col ^ 1)
            else:
                other = col - 1 if col % 2 == 0 else col + 1
                target = (row, other) if 0 <= other < n_col else (row ^ 1, col)
            pairs.append((row * n_col + col, target[0] * n_col + target[1]))
    return (swap(near, axis, 1), lax.ppermute(far, ("row", "col"), pairs))


def swap(value, axis, step):
    count = lax.axis_size(axis)
    return lax.ppermute(value, axis, [(i, i ^ step) for i in range(count)])


def vmem(count):
    return [pl.BlockSpec(memory_space=pltpu.VMEM)] * count


def on_device(tokens, gain, w_qkv, head_scale, w_out, w_merge, d_merged, d_skip):
    rows, cols, width = tokens.shape
    heads = head_scale.shape[0]
    n_row, n_col = (lax.axis_size("row"), lax.axis_size("col"))
    g_rows, g_cols, depth = d_merged.shape
    groups = g_rows * g_cols
    wide = cols + 2 * SIDE
    ext_rows = rows + 2 * RADIUS
    shape = jax.ShapeDtypeStruct
    params = pltpu.CompilerParams(vmem_limit_bytes=24 * 1024 * 1024)
    less = pltpu.CompilerParams(vmem_limit_bytes=8 * 1024 * 1024)
    row_near, row_far = swapped(tokens, tokens, "row")
    edge = shape((ext_rows * EDGE, width), BF)
    ones, parity = pl.pallas_call(
        first_kernel,
        out_shape=(shape((width, width), BF), shape((2 * heads, LANES), F32)),
        out_specs=tuple(vmem(2)),
        compiler_params=less,
        cost_estimate=pl.CostEstimate(flops=10**10, bytes_accessed=10**5, transcendentals=0),
    )()
    dm = d_merged.reshape(groups, depth)
    tile = shape((rows * cols, width), F32)
    half = shape((rows * cols, width), BF)
    edges, two_rows, q_norm, q_unit, d_y, d_attn = pl.pallas_call(
        own_kernel,
        out_shape=(shape((2 * rows * EDGE, width), BF), shape((8, width), F32), tile, tile, tile, half),
        in_specs=vmem(10),
        out_specs=tuple(vmem(6)),
        scratch_shapes=[pltpu.VMEM((width // LANES, rows, cols, LANES), F32)],
        compiler_params=params,
        cost_estimate=pl.CostEstimate(flops=10**9, bytes_accessed=10**6, transcendentals=0),
    )(
        ones,
        parity,
        head_scale.reshape(1, heads),
        tokens,
        d_merged,
        d_skip,
        gain.reshape(1, width),
        w_qkv,
        w_out,
        w_merge,
    )
    edge_near, edge_far = pl.pallas_call(
        edge_kernel,
        out_shape=(edge, edge),
        in_specs=vmem(3),
        out_specs=tuple(vmem(2)),
        compiler_params=less,
    )(edges, row_far, row_near)
    dm_pair = pl.pallas_call(
        pair_kernel,
        out_shape=shape((2 * groups, depth), BF),
        in_specs=vmem(2),
        out_specs=vmem(1)[0],
        compiler_params=less,
    )(d_merged, swap(dm, "row", 2))
    dms = [swap(dm_pair, "row", 4), dm_pair]
    col_near, col_far = swapped(edge_near, edge_far, "col")

    per = width // n_row
    feats = 4 * width // n_row
    packed = per % 16 == 0 and feats % LANES == 0 and groups == per
    packed = packed and width // LANES < 4 and feats == LANES and depth // n_col == LANES and n_col == 4 and n_row == 8
    if packed:
        sum_shapes = (
            shape((n_row // 2 - 1, per, 4 * width + feats), BF),
            shape((per, 4 * width + feats), BF),
            shape((n_row // 2, per, 4 * width), F32),
            shape((n_row // 2, per, feats), BF),
        )
        sum_scratch = [
            pltpu.VMEM((n_row // 2, per, 4 * width + feats), BF),
            pltpu.VMEM((n_row // 2, per, 4 * width), F32),
            pltpu.VMEM((n_row // 2, per, feats), BF),
        ]
    else:
        sum_shapes = (
            shape((width, 4 * width), BF),
            shape((groups, 4 * width), BF),
        )
        sum_scratch = []
    sizes = (rows, cols, width, heads, n_row, n_col)
    tall = ext_rows * wide
    x, y, d_query, d_kv, grad_out, group, scale_part = pl.pallas_call(
        functools.partial(layer_kernel, sizes),
        out_shape=(
            shape((tall, width), F32),
            half,
            half,
            shape((tall, 2 * width), BF),
            shape((width, width), F32),
            shape((groups, 4 * width), BF),
            shape((8, width), F32),
        ),
        in_specs=vmem(13),
        out_specs=tuple(vmem(7)),
        scratch_shapes=[pltpu.VMEM((width // LANES, rows, cols, LANES), F32)],
        compiler_params=params,
        cost_estimate=pl.CostEstimate(flops=4 * 10**9, bytes_accessed=10**6, transcendentals=0),
    )(
        ones,
        tokens,
        row_far,
        row_near,
        col_near,
        col_far,
        two_rows,
        q_norm,
        q_unit,
        d_y,
        d_attn,
        w_qkv,
        w_out,
    )
    dm_core, *sums = pl.pallas_call(
        functools.partial(weights_kernel, (rows, cols, width, n_row, len(dms))),
        out_shape=(shape((2 * len(dms) * groups, depth), BF),) + sum_shapes,
        in_specs=vmem(6 + len(dms)),
        out_specs=tuple(vmem(1 + len(sum_shapes))),
        scratch_shapes=sum_scratch,
        compiler_params=params,
        cost_estimate=pl.CostEstimate(flops=10**9, bytes_accessed=10**6, transcendentals=0),
    )(x, d_query, d_kv, grad_out, group, two_rows, *dms)
    d_normed, small = pl.pallas_call(
        functools.partial(gain_kernel, (rows, cols, width, heads)),
        out_shape=(shape((tall, width), F32), shape((8, LANES), F32)),
        in_specs=vmem(5),
        out_specs=tuple(vmem(2)),
        compiler_params=params,
        cost_estimate=pl.CostEstimate(flops=3 * 10**8, bytes_accessed=10**6, transcendentals=0),
    )(x, d_query, d_kv, scale_part, w_qkv)
    gx, *sides = pl.pallas_call(
        functools.partial(norm_kernel, (rows, cols, width)),
        out_shape=(shape((ext_rows * cols, width), F32), edge, edge),
        in_specs=vmem(4),
        out_specs=tuple(vmem(3)),
        compiler_params=params,
        cost_estimate=pl.CostEstimate(flops=2 * 10**8, bytes_accessed=10**6, transcendentals=0),
    )(x, d_normed, two_rows, d_y)
    sides = swapped(*sides, "col")
    skip_out, merged = pl.pallas_call(
        output_kernel,
        out_shape=(shape((rows, cols, width), BF), shape((g_rows, g_cols, depth), BF)),
        in_specs=vmem(3),
        out_specs=tuple(vmem(2)),
        compiler_params=less,
        cost_estimate=pl.CostEstimate(flops=10**9, bytes_accessed=10**6, transcendentals=0),
    )(y, group, w_merge)
    reach = shape((RADIUS * cols, width), BF)
    side_call = pl.pallas_call(
        functools.partial(side_kernel, (rows, cols, width)),
        out_shape=(tile, reach, reach),
        in_specs=vmem(3),
        out_specs=tuple(vmem(3)),
        compiler_params=less,
    )
    if not packed:
        grad, *rims = side_call(gx, *sides)
        grad_tokens = add_rows(grad, *swapped(*rims, "row"), rows, cols)
        g_qkv, g_out, g_merge, g_gain, g_scale = plain_sums(width, *sums, small, dm)
    else:
        send, send_own, *kept = sums
        block = shape((4 * width // LANES * per + 2 * per + 8, LANES), BF)
        *blocks, small = pl.pallas_call(
            core_sum_kernel,
            out_shape=(block, block, block, shape((8, LANES), F32)),
            in_specs=vmem(5),
            out_specs=tuple(vmem(4)),
            compiler_params=less,
            cost_estimate=pl.CostEstimate(flops=5 * 10**9, bytes_accessed=10**6, transcendentals=0),
        )(swap(send, "row", 1), *kept, small, swap(small, "row", 1))
        got = [swap(blocks[step - 1], "row", 2 * step) for step in (3, 2, 1)]
        slot = shape((4 * width // n_col // LANES * per + feats + 8, LANES), BF)
        *slots, gx = pl.pallas_call(
            functools.partial(row_sum_kernel, (rows, cols, width, n_col)),
            out_shape=(slot,) * n_col + (shape(gx.shape, F32),),
            in_specs=vmem(10),
            out_specs=tuple(vmem(n_col + 1)),
            scratch_shapes=[pltpu.VMEM((n_col,) + slot.shape, BF)],
            compiler_params=less,
        )(*kept, swap(send_own, "row", 1), small, *got, dm_core, swap(dm_core, "row", 1), gx)
        got = [slots[0]] + [swap(slots[step], "col", step) for step in (3, 2, 1)]
        grad, *rims = side_call(gx, *sides)
        rims = swapped(*rims, "row")
        g_qkv, g_out, g_merge, g_gain, g_scale, grad_tokens = pl.pallas_call(
            functools.partial(col_sum_kernel, (rows, cols, width)),
            out_shape=(
                shape((per, 3 * width // n_col), F32),
                shape((per, width // n_col), F32),
                shape((feats, depth // n_col), F32),
                shape((1, width), F32),
                shape((heads,), F32),
                shape((rows, cols, width), BF),
            ),
            in_specs=vmem(7),
            out_specs=tuple(vmem(4)) + (pl.BlockSpec(memory_space=pltpu.SMEM), vmem(1)[0]),
            compiler_params=less,
        )(*got, grad, *rims[::-1])
    return (
        skip_out,
        merged,
        grad_tokens,
        g_qkv,
        g_out,
        g_merge,
        g_gain.reshape(width),
        g_scale[:heads],
    )


def solution(mesh):
    block = P("row", "col", None)
    return jax.shard_map(
        on_device,
        mesh=mesh,
        in_specs=(block, P(), P(), P(), P(), P(), block, block),
        out_specs=(block, block, block, P("row", "col"), P("row", "col"), P("row", "col"), P(), P()),
        check_vma=False,
    )
```
